32 devices in a mesh: group: 2 (over y), aperture: 8 (over z, x), wave: 2 (over core).
Axes of the slice: x: 2, y: 2, z: 4, core: 2. Of those that a mesh axis runs over, the one named last changes fastest.
Arguments:
- widths: float32 [512, 4096], P(('group', 'aperture')), parts along dimension 0, may hold values from -0.95 to 0.95
- coef_table: float32 [256, 16], replicated, may hold values from -3 to 3
- wave_ids: int32 [8], P(('group', 'wave')), parts along dimension 0, may hold values from 0 to 255
- angle_ids: int32 [8], P(('group', 'wave')), parts along dimension 0, may hold values from 0 to 3
- targets: int32 [8, 2], P(('group', 'wave')), parts along dimension 0, may hold values from 32 to 223
Outputs:
- width_grad: float32 [512, 4096], P(('group', 'aperture'), 'wave'), parts along dimension 0
- efficiency: float32 [8], P(('group', 'wave')), parts along dimension 0
The draws below stay inside these ranges and needn't reach their ends.
There are 2 independent parts, one for each index of `group`. The reference program is written for one: setup_inputs(seed, part) draws one part's arguments, and reference() takes and returns one part's arrays. A program takes and returns all parts, laid end to end along the dimension named above; an argument that names none is the same for every part. Nothing has to cross between parts.
All inputs are finite; a program needn't handle non-finite values.
Results may differ from the reference program's by a relative error of at most 0.0045.
The reference program's roundings to bfloat16 on the way count: a program that leaves them out, or rounds other values in their place, can miss the bound.
Values may be sent and summed in bfloat16 or wider, within the bound.
No kernel may reach another device: no remote copies, remote signals or barrier semaphores. Data moves between devices by JAX's collectives and lax.ppermute only.
A program may use at most 64 MiB of HBM per device.

```python
import math
import jax
import jax.numpy as jnp
from jax import lax

COLS = 4096
ROWS = 256
FOCAL = 256
WAVES = 256
ANGLES = 4
DEGREE = 8
SPOT = 4
SHIFT = 32
PAIRS = 4


def grating_sum(key, count, height, rough):
    keys = jax.random.split(key, 5)
    low = FOCAL / 8.0
    high = FOCAL / 4.0
    row_freq = jax.random.uniform(keys[0], (count,), jnp.float32, low, high)
    row_sign = jnp.where(jax.random.bernoulli(keys[1], 0.5, (count,)), 1.0, -1.0)
    row_freq = row_freq * row_sign
    col_freq = jax.random.uniform(keys[2], (count,), jnp.float32, low, high)
    offsets = jax.random.uniform(keys[3], (count,), jnp.float32, 0.0, 1.0)
    row_frac = jnp.arange(ROWS, dtype=jnp.float32) / ROWS
    col_frac = jnp.arange(COLS, dtype=jnp.float32) / COLS
    total = jnp.zeros((ROWS, COLS), jnp.float32)
    for index in range(count):
        turns = row_freq[index] * row_frac[:, None] + col_freq[index] * col_frac[None, :] + offsets[index]
        turns = turns - jnp.floor(turns)
        total = total + height * jnp.cos(2.0 * math.pi * turns)
    noise = jax.random.uniform(keys[4], (ROWS, COLS), jnp.float32, -rough, rough)
    return total + noise


def draw_widths(key, part):
    key = jax.random.fold_in(key, 11)
    values = grating_sum(key, 2, 0.35, 0.2)
    return values.astype(jnp.float32)


def with_ends(array, stream_key, low, top_value):
    longest = array.shape.index(max(array.shape))
    spots = []
    for shift in (0, 1):
        where = [jax.random.randint(jax.random.fold_in(stream_key, axis), (), 0, length) for axis, length in enumerate(array.shape)]
        where[longest] = (where[longest] + shift) % array.shape[longest]
        spots.append(tuple(where))
    return array.at[spots[0]].set(low).at[spots[1]].set(top_value)


def scatter_about(stream_key, extent, spread, reach, kind=jnp.bfloat16):
    result = jax.random.normal(stream_key, extent, jnp.float32) * spread
    return jnp.minimum(jnp.maximum(result, -reach), reach).astype(kind)


def setup_inputs(seed: int = 0, part: int = 0) -> dict:
    streams_of = jax.random.split(jax.random.key(seed), 6)
    own_keys = jax.random.split(jax.random.fold_in(streams_of[5], part), 6)
    return {
        "widths": draw_widths(jax.random.fold_in(jax.random.fold_in(streams_of[5], part), 71), part),
        "coef_table": scatter_about(streams_of[1], (WAVES, 2 * DEGREE), 0.5, 3.0, jnp.float32),
        "wave_ids": with_ends(jax.random.randint(own_keys[2], (PAIRS,), 0, WAVES), jax.random.fold_in(own_keys[2], 1), 0, WAVES - 1).astype(jnp.int32),
        "angle_ids": with_ends(jax.random.randint(own_keys[3], (PAIRS,), 0, ANGLES), jax.random.fold_in(own_keys[3], 1), 0, ANGLES - 1).astype(jnp.int32),
        "targets": with_ends(jax.random.randint(own_keys[4], (PAIRS, 2), FOCAL // 8, FOCAL - FOCAL // 8), jax.random.fold_in(own_keys[4], 1), FOCAL // 8, (FOCAL - FOCAL // 8) - 1).astype(jnp.int32),
    }


def phase_table(positions, frequencies, period):
    turns = jnp.mod(positions[:, None] * frequencies[None, :], period)
    angle = turns.astype(jnp.float32) * (2.0 * math.pi / period)
    return jnp.concatenate([jnp.cos(angle), -jnp.sin(angle)], axis=1).astype(jnp.bfloat16)

def near_field(widths, coef):
    order_count = coef.shape[0] // 2
    before, current = (jnp.ones_like(widths), widths)
    real = coef[0] * before + coef[1] * current
    imag = coef[order_count] * before + coef[order_count + 1] * current
    for order in range(2, order_count):
        before, current = (current, 2.0 * widths * current - before)
        real = real + coef[order] * current
        imag = imag + coef[order_count + order] * current
    return (real, imag)

def near_slope(widths, coef):
    order_count = coef.shape[0] // 2
    before, current = (jnp.zeros_like(widths), jnp.ones_like(widths))
    real = jnp.zeros_like(widths)
    imag = jnp.zeros_like(widths)
    for order in range(1, order_count):
        real = real + order * coef[order] * current
        imag = imag + order * coef[order_count + order] * current
        before, current = (current, 2.0 * widths * current - before)
    return (real, imag)

def spot_map(target, first_row, count):
    rows_off = (first_row + jnp.arange(count, dtype=jnp.int32) - target[0]).astype(jnp.float32)
    cols_off = (jnp.arange(FOCAL, dtype=jnp.int32) - target[1]).astype(jnp.float32)
    return jnp.exp(-(rows_off[:, None] ** 2 + cols_off[None, :] ** 2) / (2.0 * SPOT * SPOT))

def reference(widths, coef_table, wave_ids, angle_ids, targets):
    rows, cols = widths.shape
    focal_pos = jnp.arange(FOCAL, dtype=jnp.int32) - FOCAL // 2
    row_pos = jnp.arange(rows, dtype=jnp.int32) - rows // 2
    col_pos = jnp.arange(cols, dtype=jnp.int32) - cols // 2
    total = jnp.zeros((rows, cols), jnp.float32)
    scores = []
    for pair in range(PAIRS):
        wave = wave_ids[pair]
        wave_freq = 256 + wave
        coef = coef_table[wave]
        row_tab = phase_table(row_pos, focal_pos * wave_freq, 256 * rows)
        col_tab = phase_table(col_pos, (focal_pos + SHIFT * angle_ids[pair]) * wave_freq, 256 * cols)
        real_near, imag_near = near_field(widths, coef)
        near = jnp.concatenate([real_near, imag_near], axis=0).astype(jnp.bfloat16)
        section = jnp.dot(near, col_tab, preferred_element_type=jnp.float32)
        section_r = section[:rows, :FOCAL] - section[rows:, FOCAL:]
        section_i = section[:rows, FOCAL:] + section[rows:, :FOCAL]
        section_cat = jnp.concatenate([section_r, section_i], axis=1).astype(jnp.bfloat16)
        mixed = lax.dot_general(row_tab, section_cat, (((0,), (0,)), ((), ())), preferred_element_type=jnp.float32)
        field_r = mixed[:FOCAL, :FOCAL] - mixed[FOCAL:, FOCAL:]
        field_i = mixed[:FOCAL, FOCAL:] + mixed[FOCAL:, :FOCAL]
        intensity = field_r * field_r + field_i * field_i
        spot = spot_map(targets[pair], 0, FOCAL)
        spot_power = jnp.sum(spot * intensity)
        all_power = jnp.sum(intensity) + 1e-06
        ratio = spot_power / all_power
        factor = FOCAL * FOCAL / jnp.sum(spot)
        scores.append(ratio * factor)
        weight = factor * 2.0 * (spot - ratio) / all_power
        seed_r = (weight * field_r).astype(jnp.bfloat16)
        seed_i = (weight * field_i).astype(jnp.bfloat16)
        seed_mat = jnp.concatenate([jnp.concatenate([seed_r, seed_i], axis=1), jnp.concatenate([seed_i, -seed_r], axis=1)], axis=0)
        back = jnp.dot(row_tab, seed_mat, preferred_element_type=jnp.float32).astype(jnp.bfloat16)
        left = jnp.concatenate([back, jnp.concatenate([back[:, FOCAL:], -back[:, :FOCAL]], axis=1)], axis=0)
        grad_near = lax.dot_general(left, col_tab, (((1,), (1,)), ((), ())), preferred_element_type=jnp.float32)
        slope_r, slope_i = near_slope(widths, coef)
        total = total + grad_near[:rows] * slope_r + grad_near[rows:] * slope_i
    return (total * math.sqrt(rows * cols), jnp.stack(scores))
```

```python
import functools
import math

import jax
import jax.numpy as jnp
from jax import lax
from jax.experimental import pallas as pl
from jax.experimental.pallas import tpu as pltpu
from jax.sharding import PartitionSpec as P

FOCAL = 256
SPOT = 4
SHIFT = 32
TERMS = 8
BLOCK = 256
GRAIN = 16
VMEM_LIMIT = 24 * 1024 * 1024

COS = (
    1.0, -19.7392088015709, 64.93939395773512, -85.45681453397417, 60.24458621302471,
    -26.425616460281425, 7.8991596631575085, -1.6968741456712442, 0.2437618617467591,
)
SIN = (
    6.2831853071792665, -41.34170224019464, 81.60524925425943, -76.70585885700535,
    42.05867547580699, -15.094428387947755, 3.818490079304055, -0.7122771247541972,
    0.09149844789363434,
)


def horner(terms, u):
    value = terms[-1] * u + terms[-2]
    for term in terms[-3::-1]:
        value = value * u + term
    return value


def unit_waves(counts, period):
    half = period // 2
    centred = ((counts + half) & (period - 1)) - half
    t = centred.astype(jnp.float32) * (1.0 / period)
    u = t * t
    return horner(COS, u), -(t * horner(SIN, u))


def iota(shape, axis):
    return lax.broadcasted_iota(jnp.int32, shape, axis)


def pick_coef(table_ref, wave):
    table = table_ref[...]
    chosen = jnp.where(iota(table.shape, 1) == wave, table, 0.0)
    return jnp.sum(chosen, axis=1, keepdims=True)


def column_freq(wave, angle):
    return (iota((1, FOCAL), 1) - FOCAL // 2 + SHIFT * angle) * (BLOCK + wave)


def fill_base(freq, shift, period, base_ref, centre_ref):
    low_r, low_i = unit_waves(iota((GRAIN, 1), 0) * freq, period)
    steps = BLOCK // GRAIN
    high_r, high_i = unit_waves((iota((steps, 1), 0) * GRAIN - BLOCK // 2 + shift) * freq, period)
    for step in range(steps):
        one_r, one_i = high_r[step : step + 1], high_i[step : step + 1]
        rows = slice(step * GRAIN, (step + 1) * GRAIN)
        base_ref[0, rows, :] = one_r * low_r - one_i * low_i
        base_ref[1, rows, :] = one_r * low_i + one_i * low_r
    count = centre_ref.shape[1]
    cent_r, cent_i = unit_waves((iota((count, 1), 0) * BLOCK + BLOCK // 2) * freq, period)
    centre_ref[0] = cent_r
    centre_ref[1] = cent_i


def block_pair(base_ref, centre_ref, index):
    cent_r = centre_ref[0, pl.ds(index, 1), :]
    cent_i = centre_ref[1, pl.ds(index, 1), :]
    base_r, base_i = base_ref[0], base_ref[1]
    rr, ii = base_r * cent_r, base_i * cent_i
    ri, ir = base_r * cent_i, base_i * cent_r
    before = ((rr + ii).astype(jnp.bfloat16), (ir - ri).astype(jnp.bfloat16))
    after = ((rr - ii).astype(jnp.bfloat16), (ir + ri).astype(jnp.bfloat16))
    return before, after


def near_fields(s, coefs):
    outs = [[c[0:1] + c[1:2] * s, c[TERMS : TERMS + 1] + c[TERMS + 1 : TERMS + 2] * s] for c in coefs]
    twice = s + s
    before, current = jnp.ones_like(s), s
    for order in range(2, TERMS):
        before, current = current, twice * current - before
        for out, c in zip(outs, coefs):
            out[0] = out[0] + c[order : order + 1] * current
            out[1] = out[1] + c[TERMS + order : TERMS + order + 1] * current
    return outs


def near_slopes(s, coefs):
    outs = [[jnp.broadcast_to(c[1:2], s.shape), jnp.broadcast_to(c[TERMS + 1 : TERMS + 2], s.shape)] for c in coefs]
    twice = s + s
    before, current = jnp.ones_like(s), twice
    for order in range(2, TERMS):
        for out, c in zip(outs, coefs):
            out[0] = out[0] + c[order : order + 1] * current
            out[1] = out[1] + c[TERMS + order : TERMS + order + 1] * current
        before, current = current, twice * current - before
    return outs


def forward_kernel(wave_ref, angle_ref, coef_ref, width_ref, out_ref, base_ref, centre_ref, acc_ref):
    rows_dev, cols = width_ref.shape
    pairs = wave_ref.shape[0]
    period = 256 * cols
    peers, _, lanes = out_ref.shape
    width = lanes // (2 * pairs)
    coefs = [pick_coef(coef_ref, wave_ref[pair]) for pair in range(pairs)]
    for pair in range(pairs):
        freq = column_freq(wave_ref[pair], angle_ref[pair])
        fill_base(freq, 0, period, base_ref.at[pair], centre_ref.at[pair])
    acc_ref[...] = jnp.zeros_like(acc_ref)

    def step(index, carry):
        left = pl.multiple_of(cols // 2 - (index + 1) * BLOCK, BLOCK)
        right = pl.multiple_of(cols // 2 + index * BLOCK, BLOCK)
        nears = []
        for start in (left, right):
            outs = near_fields(width_ref[:, pl.ds(start, BLOCK)], coefs)
            nears.append([jnp.concatenate(out, axis=0).astype(jnp.bfloat16) for out in outs])
        for pair in range(pairs):
            before, after = block_pair(base_ref.at[pair], centre_ref.at[pair], index)
            near = jnp.concatenate([nears[0][pair], nears[1][pair]], axis=1)
            for part in range(2):
                table = jnp.concatenate([before[part], after[part]], axis=0)
                acc_ref[pair, part] += jnp.dot(near, table, preferred_element_type=jnp.float32)
        return carry

    lax.fori_loop(0, cols // (2 * BLOCK), step, 0)
    sections = []
    for pair in range(pairs):
        sections.append(acc_ref[pair, 0, :rows_dev] - acc_ref[pair, 1, rows_dev:])
        sections.append(acc_ref[pair, 1, :rows_dev] + acc_ref[pair, 0, rows_dev:])
    for peer in range(peers):
        part = [section[:, peer * width : (peer + 1) * width] for section in sections]
        out_ref[peer] = jnp.concatenate(part, axis=1).astype(jnp.bfloat16)


def row_kernel(wave_ref, flat_ref, tall_ref):
    pairs, rows, _ = flat_ref.shape
    period = 256 * rows
    size = min(rows, FOCAL)
    for pair in range(pairs):
        freq = BLOCK + wave_ref[pair]

        def step(index, carry):
            start = pl.multiple_of(index * size, size)
            first = start - rows // 2
            focal = (iota((1, FOCAL), 1) - FOCAL // 2) * freq
            real, imag = unit_waves((iota((size, 1), 0) + first) * focal, period)
            flat_ref[pair, pl.ds(start, size), :FOCAL] = real.astype(jnp.bfloat16)
            flat_ref[pair, pl.ds(start, size), FOCAL:] = imag.astype(jnp.bfloat16)
            if rows != FOCAL:
                focal = (iota((FOCAL, 1), 0) - FOCAL // 2) * freq
                real, imag = unit_waves((iota((1, size), 1) + first) * focal, period)
            tall_ref[pair, :FOCAL, pl.ds(start, size)] = real.astype(jnp.bfloat16)
            tall_ref[pair, FOCAL:, pl.ds(start, size)] = imag.astype(jnp.bfloat16)
            return carry

        if rows == size:
            step(0, 0)
        else:
            lax.fori_loop(0, rows // size, step, 0)


def lane_facts(lanes, pairs):
    width = lanes // (2 * pairs)
    lane = iota((1, lanes), 1)
    second = lane >= 2 * width
    imag = (lane % (2 * width)) >= width
    return width, lane, second, imag


def swap_parts(value, width, imag):
    lanes = value.shape[1]
    ahead = pltpu.roll(value, lanes - width, 1)
    behind = pltpu.roll(value, width, 1)
    return jnp.where(imag, behind, -ahead)


def spot_lanes(aim_ref, first_col, lanes, pairs):
    width, lane, second, _ = lane_facts(lanes, pairs)
    col = first_col + lane % width
    aim_row = jnp.where(second, aim_ref[1, 0], aim_ref[0, 0])
    aim_col = jnp.where(second, aim_ref[1, 1], aim_ref[0, 1])
    rows_off = (iota((FOCAL, lanes), 0) - aim_row).astype(jnp.float32)
    cols_off = (col - aim_col).astype(jnp.float32)
    return jnp.exp(-(rows_off * rows_off + cols_off * cols_off) / (2.0 * SPOT * SPOT))


def field_kernel(aim_ref, sect_ref, tall_ref, field_ref, power_ref):
    peers, rows_dev, lanes = sect_ref.shape
    pairs = tall_ref.shape[0]
    width, _, second, imag = lane_facts(lanes, pairs)
    sect = sect_ref[...].reshape(peers * rows_dev, lanes)
    mixed = [
        jnp.dot(tall_ref[pair], sect, preferred_element_type=jnp.float32) for pair in range(pairs)
    ]
    mixed = jnp.where(second, mixed[1], mixed[0])
    field = mixed[:FOCAL] + swap_parts(mixed[FOCAL:], width, imag)
    spot = spot_lanes(aim_ref, lax.axis_index("aperture") * width, lanes, pairs)
    power = field * field
    spot_power = jnp.sum(spot * power, axis=0, keepdims=True)
    all_power = jnp.sum(power, axis=0, keepdims=True)
    both = jnp.concatenate([spot_power, all_power, jnp.zeros((6, lanes), jnp.float32)], axis=0)
    field_ref[...] = field
    power_ref[...] = jnp.broadcast_to(both[None], power_ref.shape)


def seed_kernel(aim_ref, power_ref, field_ref, flat_ref, back_ref, score_ref):
    lanes = field_ref.shape[1]
    pairs, rows, _ = flat_ref.shape
    peers, copies, rows_dev, _ = back_ref.shape
    width, _, second, imag = lane_facts(lanes, pairs)
    total = jnp.sum(power_ref[...], axis=0)
    ratios, scales = [], []
    for pair in range(pairs):
        mine = jnp.where(second == (pair == 1), total, 0.0)
        sums = jnp.sum(mine, axis=1, keepdims=True)
        all_power = sums[1:2] + 1e-06
        ratio = sums[0:1] / all_power
        place = iota((1, FOCAL), 1)
        spans = []
        for axis in range(2):
            off = (place - aim_ref[pair, axis]).astype(jnp.float32)
            spans.append(jnp.sum(jnp.exp(-(off * off) / (2.0 * SPOT * SPOT)), axis=1, keepdims=True))
        factor = FOCAL * FOCAL / (spans[0] * spans[1])
        ratios.append(ratio)
        scales.append(factor * 2.0 / all_power)
        score_ref[pair] = jnp.sum(ratio * factor)
    spot = spot_lanes(aim_ref, lax.axis_index("aperture") * width, lanes, pairs)
    ratio = jnp.where(second, ratios[1], ratios[0])
    scale = jnp.where(second, scales[1], scales[0])
    seed = (scale * (spot - ratio)) * field_ref[...]
    turned = -swap_parts(seed, width, imag)
    stack = jnp.concatenate([seed, turned], axis=0).astype(jnp.bfloat16)
    backs = [
        jnp.dot(flat_ref[pair], stack, preferred_element_type=jnp.float32) for pair in range(pairs)
    ]
    back = jnp.where(second, backs[1], backs[0]).astype(jnp.bfloat16)
    back = back.reshape(peers, rows_dev, lanes)
    for copy in range(copies):
        back_ref[:, copy] = back


def table_kernel(scale, wave_ref, angle_ref, far_ref, coef_ref, width_ref, table_ref, slope_ref, base_ref, centre_ref):
    rows_dev, cols = width_ref.shape
    near_pairs = wave_ref.shape[0]
    pairs, own_cols, _ = table_ref.shape
    period = 256 * cols
    first = lax.axis_index("wave") * own_cols
    middle = own_cols // 2
    coefs = []
    for pair in range(pairs):
        if pair < near_pairs:
            wave, angle = wave_ref[pair], angle_ref[pair]
        else:
            wave, angle = far_ref[0, pair - near_pairs], far_ref[1, pair - near_pairs]
        coef = pick_coef(coef_ref, wave)
        order = (iota(coef.shape, 0) % TERMS).astype(jnp.float32) * scale
        coefs.append(coef * order)
        shift = first + middle - cols // 2
        fill_base(column_freq(wave, angle), shift, period, base_ref.at[pair], centre_ref.at[pair])

    def step(index, carry):
        left = pl.multiple_of(middle - (index + 1) * BLOCK, BLOCK)
        right = pl.multiple_of(middle + index * BLOCK, BLOCK)
        for pair in range(pairs):
            tables = block_pair(base_ref.at[pair], centre_ref.at[pair], index)
            for start, table in zip((left, right), tables):
                table_ref[pair, pl.ds(start, BLOCK), :FOCAL] = table[0]
                table_ref[pair, pl.ds(start, BLOCK), FOCAL:] = table[1]
        for start in (left, right):
            whole = pl.multiple_of(first + start, BLOCK)
            slopes = near_slopes(width_ref[:, pl.ds(whole, BLOCK)], coefs)
            for pair in range(pairs):
                slope_ref[pair, 0, :, pl.ds(start, BLOCK)] = slopes[pair][0]
                slope_ref[pair, 1, :, pl.ds(start, BLOCK)] = slopes[pair][1]
        return carry

    lax.fori_loop(0, own_cols // (2 * BLOCK), step, 0)


def grad_kernel(peers, back_ref, table_ref, slope_ref, out_ref, left_ref):
    rows_dev, own_cols = out_ref.shape
    pairs = table_ref.shape[0]
    copies = back_ref.shape[0] // peers
    pairs_dev = pairs // copies
    lanes = back_ref.shape[2]
    width = lanes // (2 * pairs_dev)
    me = lax.axis_index("wave")
    for pair in range(pairs):
        wave = lax.rem(me + pair // pairs_dev, copies)
        lane = (pair % pairs_dev) * 2 * width
        parts = [back_ref[peer * copies + wave] for peer in range(peers)]
        real = jnp.concatenate([part[:, lane : lane + width] for part in parts], axis=1)
        imag = jnp.concatenate([part[:, lane + width : lane + 2 * width] for part in parts], axis=1)
        left_ref[pair, :rows_dev, :FOCAL] = real
        left_ref[pair, :rows_dev, FOCAL:] = imag
        left_ref[pair, rows_dev:, :FOCAL] = imag
        left_ref[pair, rows_dev:, FOCAL:] = -real
    size = 2 * BLOCK

    def step(index, carry):
        start = pl.multiple_of(index * size, size)
        total = jnp.zeros((rows_dev, size), jnp.float32)
        for pair in range(pairs):
            grad = lax.dot_general(
                left_ref[pair],
                table_ref[pair, pl.ds(start, size), :],
                (((1,), (1,)), ((), ())),
                preferred_element_type=jnp.float32,
            )
            total += grad[:rows_dev] * slope_ref[pair, 0, :, pl.ds(start, size)]
            total += grad[rows_dev:] * slope_ref[pair, 1, :, pl.ds(start, size)]
        out_ref[:, pl.ds(start, size)] = total
        return carry

    lax.fori_loop(0, own_cols // size, step, 0)


VMEM = pl.BlockSpec(memory_space=pltpu.VMEM)
SMEM = pl.BlockSpec(memory_space=pltpu.SMEM)


def call(kernel, name, outs, in_specs, out_specs, scratch, flops, moved):
    return pl.pallas_call(
        kernel,
        name=name,
        out_shape=outs,
        in_specs=in_specs,
        out_specs=out_specs,
        scratch_shapes=scratch,
        cost_estimate=pl.CostEstimate(flops=flops, bytes_accessed=moved, transcendentals=0),
        compiler_params=pltpu.CompilerParams(vmem_limit_bytes=VMEM_LIMIT),
    )


def on_device(widths, coef_table, wave_ids, angle_ids, targets):
    rows_dev, cols = widths.shape
    pairs_dev = wave_ids.shape[0]
    peers = lax.axis_size("aperture")
    copies = lax.axis_size("wave")
    rows = rows_dev * peers
    pairs = pairs_dev * copies
    lanes = 2 * pairs_dev * FOCAL // peers
    own_cols = cols // copies
    f32, bf16 = jnp.float32, jnp.bfloat16
    coefs = coef_table.T
    ring = [(index, (index + 1) % copies) for index in range(copies)]
    far_ids = lax.ppermute(jnp.stack([wave_ids, angle_ids]), "wave", ring)

    sections = call(
        forward_kernel, "forward", jax.ShapeDtypeStruct((peers, rows_dev, lanes), bf16),
        [SMEM, SMEM, VMEM, VMEM], VMEM,
        [
            pltpu.VMEM((pairs_dev, 2, BLOCK, FOCAL), f32),
            pltpu.VMEM((pairs_dev, 2, cols // (2 * BLOCK), FOCAL), f32),
            pltpu.VMEM((pairs_dev, 2, 2 * rows_dev, FOCAL), f32),
        ],
        10**9, 10**7,
    )(wave_ids, angle_ids, coefs, widths)
    sections = lax.all_to_all(sections, "aperture", 0, 0, tiled=True)

    flat, tall = call(
        row_kernel, "row_tables",
        (pltpu.VMEM((pairs_dev, rows, 2 * FOCAL), bf16), pltpu.VMEM((pairs_dev, 2 * FOCAL, rows), bf16)),
        [SMEM], (VMEM, VMEM), [], 10**8, 10**6,
    )(wave_ids)
    tables, slopes = call(
        functools.partial(table_kernel, math.sqrt(rows * cols)), "column_tables",
        (pltpu.VMEM((pairs, own_cols, 2 * FOCAL), bf16), pltpu.VMEM((pairs, 2, rows_dev, own_cols), f32)),
        [SMEM, SMEM, SMEM, VMEM, VMEM], (VMEM, VMEM),
        [
            pltpu.VMEM((pairs, 2, BLOCK, FOCAL), f32),
            pltpu.VMEM((pairs, 2, own_cols // (2 * BLOCK), FOCAL), f32),
        ],
        10**9, 10**7,
    )(wave_ids, angle_ids, far_ids, coefs, widths)

    field, power = call(
        field_kernel, "field",
        (pltpu.VMEM((FOCAL, lanes), f32), jax.ShapeDtypeStruct((peers, 8, lanes), f32)),
        [SMEM, VMEM, VMEM], (VMEM, VMEM), [], 10**8, 10**6,
    )(targets, sections, tall)
    power = lax.all_to_all(power, "aperture", 0, 0, tiled=True)
    backs, scores = call(
        seed_kernel, "seed",
        (jax.ShapeDtypeStruct((peers, copies, rows_dev, lanes), bf16), jax.ShapeDtypeStruct((pairs_dev,), f32)),
        [SMEM, VMEM, VMEM, VMEM], (VMEM, SMEM), [], 10**8, 10**6,
    )(targets, power, field, flat)
    backs = backs.reshape(peers * copies, rows_dev, lanes)
    backs = lax.all_to_all(backs, ("aperture", "wave"), 0, 0, tiled=True)
    grad = call(
        functools.partial(grad_kernel, peers), "gradient",
        jax.ShapeDtypeStruct((rows_dev, own_cols), f32),
        [VMEM, VMEM, VMEM], VMEM,
        [pltpu.VMEM((pairs, 2 * rows_dev, 2 * FOCAL), bf16)],
        10**9, 10**7,
    )(backs, tables, slopes)
    return grad, scores


def solution(mesh):
    in_specs = (
        P(("group", "aperture"), None),
        P(),
        P(("group", "wave")),
        P(("group", "wave")),
        P(("group", "wave"), None),
    )
    out_specs = (P(("group", "aperture"), "wave"), P(("group", "wave")))
    return jax.shard_map(
        on_device, mesh=mesh, in_specs=in_specs, out_specs=out_specs, check_vma=False
    )
```

```python
import functools
import math

import jax
import jax.numpy as jnp
from jax import lax
from jax.experimental import pallas as pl
from jax.experimental.pallas import tpu as pltpu
from jax.sharding import PartitionSpec as P

FOCAL = 256
SPOT = 4
SHIFT = 32
TERMS = 8
BLOCK = 256
GRAIN = 16
VMEM_LIMIT = 16 * 1024 * 1024
HALF = FOCAL // 2
WAVE_ROW, ANGLE_ROW, AIM_ROW, INFO_ROWS = 16, 17, 18, 24
DIRECT = 16

COS = (
    1.0, -19.7392088015709, 64.93939395773512, -85.45681453397417, 60.24458621302471,
    -26.425616460281425, 7.8991596631575085, -1.6968741456712442, 0.2437618617467591,
)
SIN = (
    6.2831853071792665, -41.34170224019464, 81.60524925425943, -76.70585885700535,
    42.05867547580699, -15.094428387947755, 3.818490079304055, -0.7122771247541972,
    0.09149844789363434,
)


def horner(terms, u):
    value = terms[-1] * u + terms[-2]
    for term in terms[-3::-1]:
        value = value * u + term
    return value


def unit_waves(counts, period):
    half = period // 2
    centred = ((counts + half) & (period - 1)) - half
    t = centred.astype(jnp.float32) * (1.0 / period)
    u = t * t
    return horner(COS, u), -(t * horner(SIN, u))


def iota(shape, axis):
    return lax.broadcasted_iota(jnp.int32, shape, axis)


def pick_coef(table, wave):
    chosen = jnp.where(iota(table.shape, 1) == wave, table, 0.0)
    return jnp.sum(chosen, axis=1, keepdims=True)


def own_half():
    return lax.axis_index("aperture") % 2


def column_freq(info_ref, pair, first):
    wave = info_ref[pair, WAVE_ROW : WAVE_ROW + 1, :].astype(jnp.int32)
    angle = info_ref[pair, ANGLE_ROW : ANGLE_ROW + 1, :].astype(jnp.int32)
    focal = (iota((1, FOCAL), 1) + first) & (FOCAL - 1)
    return (focal - FOCAL // 2 + SHIFT * angle) * (BLOCK + wave)


def fill_base(freq, shift, period, base_ref, centre_ref):
    low_r, low_i = unit_waves(iota((GRAIN, 1), 0) * freq, period)
    steps = BLOCK // GRAIN
    high_r, high_i = unit_waves((iota((steps, 1), 0) * GRAIN - BLOCK // 2 + shift) * freq, period)
    for step in range(steps):
        one_r, one_i = high_r[step : step + 1], high_i[step : step + 1]
        rows = slice(step * GRAIN, (step + 1) * GRAIN)
        base_ref[0, rows, :] = one_r * low_r - one_i * low_i
        base_ref[1, rows, :] = one_r * low_i + one_i * low_r
    count = centre_ref.shape[1]
    cent_r, cent_i = unit_waves((iota((count, 1), 0) * BLOCK + BLOCK // 2) * freq, period)
    centre_ref[0] = cent_r
    centre_ref[1] = cent_i


def block_pair(base_ref, centre_ref, index):
    cent_r = centre_ref[0, index : index + 1, :]
    cent_i = centre_ref[1, index : index + 1, :]
    base_r, base_i = base_ref[0], base_ref[1]
    rr, ii = base_r * cent_r, base_i * cent_i
    ri, ir = base_r * cent_i, base_i * cent_r
    before = ((rr + ii).astype(jnp.bfloat16), (ir - ri).astype(jnp.bfloat16))
    after = ((rr - ii).astype(jnp.bfloat16), (ir + ri).astype(jnp.bfloat16))
    return before, after


def near_fields(s, info_ref, pairs):
    def coef(pair, row):
        return info_ref[pair, row : row + 1, :]

    outs = [[coef(p, k) + coef(p, k + 1) * s for k in (0, TERMS)] for p in range(pairs)]
    twice = s + s
    before, current = jnp.ones_like(s), s
    for order in range(2, TERMS):
        before, current = current, twice * current - before
        for pair, out in enumerate(outs):
            out[0] = out[0] + coef(pair, order) * current
            out[1] = out[1] + coef(pair, TERMS + order) * current
    return outs


def near_slopes(s, scale, info_ref, pairs):
    def coef(pair, row):
        return info_ref[pair, row : row + 1, :] * (scale * (row % TERMS))

    twice = s + s
    before, current = jnp.ones_like(s), twice
    outs = [[coef(p, k) + coef(p, k + 1) * twice for k in (1, TERMS + 1)] for p in range(pairs)]
    for order in range(3, TERMS):
        before, current = current, twice * current - before
        for pair, out in enumerate(outs):
            out[0] = out[0] + coef(pair, order) * current
            out[1] = out[1] + coef(pair, TERMS + order) * current
    return outs


def forward_kernel(
    wave_hbm, angle_hbm, aim_hbm, coef_hbm, width_hbm, mine_ref, other_ref, info_ref, own_ref,
    wave_ref, angle_ref, aim_ref, coef_ref, width_ref, base_ref, centre_ref, acc_ref, sems,
):
    rows_dev, cols = width_ref.shape
    pairs = wave_ref.shape[0]
    period = 256 * cols
    moves = [
        pltpu.make_async_copy(source, target, sems.at[index])
        for index, (source, target) in enumerate((
            (wave_hbm, wave_ref), (angle_hbm, angle_ref), (aim_hbm, aim_ref),
            (coef_hbm, coef_ref), (width_hbm, width_ref),
        ))
    ]
    for move in moves:
        move.start()
    for move in moves[:4]:
        move.wait()
    for pair in range(pairs):
        coef = pick_coef(coef_ref[...], wave_ref[pair])
        info_ref[pair, :WAVE_ROW, :] = jnp.broadcast_to(coef, (WAVE_ROW, FOCAL))
        row = iota((INFO_ROWS - WAVE_ROW, FOCAL), 0) + WAVE_ROW
        ids = jnp.where(row == WAVE_ROW, wave_ref[pair], 0)
        ids = jnp.where(row == ANGLE_ROW, angle_ref[pair], ids)
        ids = jnp.where(row == AIM_ROW, aim_ref[pair, 0], ids)
        ids = jnp.where(row == AIM_ROW + 1, aim_ref[pair, 1], ids)
        info_ref[pair, WAVE_ROW:, :] = ids.astype(jnp.float32)
    for pair in range(pairs):
        fill_base(column_freq(info_ref, pair, 0), 0, period, base_ref.at[pair], centre_ref.at[pair])
    acc_ref[...] = jnp.zeros_like(acc_ref)
    moves[4].wait()
    for index in range(cols // (2 * BLOCK)):
        left = cols // 2 - (index + 1) * BLOCK
        right = cols // 2 + index * BLOCK
        nears = []
        for start in (left, right):
            outs = near_fields(width_ref[:, start : start + BLOCK], info_ref, pairs)
            nears.append([jnp.concatenate(out, axis=0).astype(jnp.bfloat16) for out in outs])
        for pair in range(pairs):
            before, after = block_pair(base_ref.at[pair], centre_ref.at[pair], index)
            near = jnp.concatenate([nears[0][pair], nears[1][pair]], axis=1)
            for part in range(2):
                table = jnp.concatenate([before[part], after[part]], axis=0)
                acc_ref[pair, part] += jnp.dot(near, table, preferred_element_type=jnp.float32)
    own_cols = own_ref.shape[1]
    first = pl.multiple_of(lax.axis_index("wave") * own_cols, own_cols)
    own_ref[...] = width_ref[:, pl.ds(first, own_cols)]
    even = own_half() == 0
    for pair in range(pairs):
        real = acc_ref[pair, 0, :rows_dev] - acc_ref[pair, 1, rows_dev:]
        imag = acc_ref[pair, 1, :rows_dev] + acc_ref[pair, 0, rows_dev:]
        for part, value in enumerate((real, imag)):
            lanes = slice((2 * pair + part) * HALF, (2 * pair + part + 1) * HALF)
            mine_ref[:, lanes] = jnp.where(even, value[:, :HALF], value[:, HALF:]).astype(jnp.bfloat16)
            other_ref[:, lanes] = jnp.where(even, value[:, HALF:], value[:, :HALF]).astype(jnp.bfloat16)


def row_kernel(info_ref, tall_ref, flat_ref):
    pairs, _, rows = tall_ref.shape
    rows_dev = flat_ref.shape[1] // 2
    period = 256 * rows
    size = min(rows, FOCAL)
    me = lax.axis_index("aperture")
    for pair in range(pairs):
        wave = info_ref[pair, WAVE_ROW : WAVE_ROW + 1, :].astype(jnp.int32) + BLOCK
        focal = (iota((FOCAL, 1), 0) - FOCAL // 2) * wave

        def step(index, carry):
            start = pl.multiple_of(index * size, size)
            place = iota((1, size), 1) + (start - rows // 2)
            real, imag = unit_waves(focal[:, :size] * place, period)
            tall_ref[pair, :FOCAL, pl.ds(start, size)] = real.astype(jnp.bfloat16)
            tall_ref[pair, FOCAL:, pl.ds(start, size)] = imag.astype(jnp.bfloat16)
            return carry

        if rows == size:
            step(0, 0)
        else:
            lax.fori_loop(0, rows // size, step, 0)
        focal = (iota((1, FOCAL), 1) - FOCAL // 2) * wave
        for copy in range(2):
            first = (me ^ copy) * rows_dev - rows // 2
            real, imag = unit_waves((iota((rows_dev, 1), 0) + first) * focal, period)
            lines = slice(copy * rows_dev, (copy + 1) * rows_dev)
            flat_ref[pair, lines, :FOCAL] = real.astype(jnp.bfloat16)
            flat_ref[pair, lines, FOCAL:] = imag.astype(jnp.bfloat16)


def spot_half(info_ref, pair):
    aims = [info_ref[pair, row : row + 1, :HALF] for row in (AIM_ROW, AIM_ROW + 1)]
    rows_off = iota((FOCAL, HALF), 0).astype(jnp.float32) - aims[0]
    cols_off = (iota((1, HALF), 1) + own_half() * HALF).astype(jnp.float32) - aims[1]
    return jnp.exp(-(rows_off * rows_off + cols_off * cols_off) / (2.0 * SPOT * SPOT))


def field_kernel(info_ref, tall_ref, *refs):
    *sect_refs, field_ref, power_ref, rows_ref = refs
    pairs = tall_ref.shape[0]
    rows_dev = sect_refs[0].shape[0]
    if len(sect_refs) == 1:
        sect_ref = sect_refs[0]
    else:
        sect_ref = rows_ref
        me = lax.axis_index("aperture")
        for step, ref in enumerate(sect_refs):
            start = pl.multiple_of((me ^ step) * rows_dev, rows_dev)
            rows_ref[pl.ds(start, rows_dev), :] = ref[...]
    sums = []
    for pair in range(pairs):
        lanes = slice(pair * FOCAL, (pair + 1) * FOCAL)
        mixed = jnp.dot(tall_ref[pair], sect_ref[:, lanes], preferred_element_type=jnp.float32)
        real = mixed[:FOCAL, :HALF] - mixed[FOCAL:, HALF:]
        imag = mixed[:FOCAL, HALF:] + mixed[FOCAL:, :HALF]
        field_ref[pair, 0] = real
        field_ref[pair, 1] = imag
        power = real * real + imag * imag
        spot = spot_half(info_ref, pair)
        sums.append(jnp.sum(spot * power, axis=0, keepdims=True))
        sums.append(jnp.sum(power, axis=0, keepdims=True))
    sums.append(jnp.zeros((8 - len(sums), HALF), jnp.float32))
    power_ref[...] = jnp.concatenate(sums, axis=0)


def seed_kernel(info_ref, power_ref, far_ref, field_ref, flat_ref, mine_ref, other_ref, score_ref):
    rows_dev = mine_ref.shape[0]
    pairs = flat_ref.shape[0]
    sums = jnp.sum(power_ref[...] + far_ref[...], axis=1, keepdims=True)
    place = iota((1, FOCAL), 1).astype(jnp.float32)
    for pair in range(pairs):
        all_power = sums[2 * pair + 1 : 2 * pair + 2] + 1e-06
        ratio = sums[2 * pair : 2 * pair + 1] / all_power
        spans = []
        for row in (AIM_ROW, AIM_ROW + 1):
            off = place - info_ref[pair, row : row + 1, :]
            spans.append(jnp.sum(jnp.exp(-(off * off) / (2.0 * SPOT * SPOT)), axis=1, keepdims=True))
        factor = FOCAL * FOCAL / (spans[0] * spans[1])
        score_ref[pair] = jnp.sum(ratio * factor)
        weight = (factor * 2.0 / all_power) * (spot_half(info_ref, pair) - ratio)
        real = (weight * field_ref[pair, 0]).astype(jnp.bfloat16)
        imag = (weight * field_ref[pair, 1]).astype(jnp.bfloat16)
        stack = jnp.concatenate(
            [jnp.concatenate([real, imag], axis=1), jnp.concatenate([imag, -real], axis=1)], axis=0
        )
        back = jnp.dot(flat_ref[pair], stack, preferred_element_type=jnp.float32).astype(jnp.bfloat16)
        lanes = slice(pair * FOCAL, (pair + 1) * FOCAL)
        mine_ref[:, lanes] = back[:rows_dev]
        other_ref[:, lanes] = back[rows_dev:]


def table_kernel(scale, cols, info_ref, width_ref, *refs):
    *out_refs, base_ref, centre_ref = refs
    pairs = base_ref.shape[0]
    table_refs, slope_refs = out_refs[:pairs], out_refs[pairs:]
    own_cols = width_ref.shape[1]
    period = 256 * cols
    middle = own_cols // 2
    shift = lax.axis_index("wave") * own_cols + middle - cols // 2
    for pair in range(pairs):
        freq = column_freq(info_ref, pair, own_half() * HALF)
        fill_base(freq, shift, period, base_ref.at[pair], centre_ref.at[pair])
    for index in range(own_cols // (2 * BLOCK)):
        left = middle - (index + 1) * BLOCK
        right = middle + index * BLOCK
        for pair in range(pairs):
            tables = block_pair(base_ref.at[pair], centre_ref.at[pair], index)
            for start, table in zip((left, right), tables):
                table_refs[pair][start : start + BLOCK, :FOCAL] = table[0]
                table_refs[pair][start : start + BLOCK, FOCAL:] = table[1]
        for start in (left, right):
            slopes = near_slopes(width_ref[:, start : start + BLOCK], scale, info_ref, pairs)
            for pair in range(pairs):
                slope_refs[pair][0, :, start : start + BLOCK] = slopes[pair][0]
                slope_refs[pair][1, :, start : start + BLOCK] = slopes[pair][1]


def grad_kernel(pairs_dev, *refs):
    *in_refs, out_ref, left_ref = refs
    rows_dev, own_cols = out_ref.shape
    pairs = left_ref.shape[0]
    back_refs, in_refs = in_refs[: 2 * pairs // pairs_dev], in_refs[2 * pairs // pairs_dev :]
    table_refs, slope_refs = in_refs[:pairs], in_refs[pairs:]
    for pair in range(pairs):
        halves = back_refs[2 * (pair // pairs_dev) : 2 * (pair // pairs_dev) + 2]
        for half, ref in enumerate(halves):
            lane = (pair % pairs_dev) * FOCAL
            real, imag = ref[:, lane : lane + HALF], ref[:, lane + HALF : lane + FOCAL]
            for part, rows, value in ((0, 0, real), (1, 0, imag), (0, 1, imag), (1, 1, -real)):
                start = part * FOCAL + half * HALF
                left_ref[pair, rows * rows_dev : (rows + 1) * rows_dev, start : start + HALF] = value
    size = 2 * BLOCK
    for start in range(0, own_cols, size):
        total = jnp.zeros((rows_dev, size), jnp.float32)
        for pair in range(pairs):
            grad = lax.dot_general(
                left_ref[pair],
                table_refs[pair][start : start + size, :],
                (((1,), (1,)), ((), ())),
                preferred_element_type=jnp.float32,
            )
            total += grad[:rows_dev] * slope_refs[pair][0, :, start : start + size]
            total += grad[rows_dev:] * slope_refs[pair][1, :, start : start + size]
        out_ref[:, start : start + size] = total


VMEM = pl.BlockSpec(memory_space=pltpu.VMEM)
SMEM = pl.BlockSpec(memory_space=pltpu.SMEM)
HBM = pl.BlockSpec(memory_space=pltpu.HBM)


def call(kernel, name, outs, in_specs, out_specs, scratch, flops, moved):
    return pl.pallas_call(
        kernel,
        name=name,
        out_shape=outs,
        in_specs=in_specs,
        out_specs=out_specs,
        scratch_shapes=scratch,
        cost_estimate=pl.CostEstimate(flops=flops, bytes_accessed=moved, transcendentals=0),
        compiler_params=pltpu.CompilerParams(vmem_limit_bytes=VMEM_LIMIT),
    )


def on_device(widths, coef_table, wave_ids, angle_ids, targets):
    rows_dev, cols = widths.shape
    pairs_dev = wave_ids.shape[0]
    peers = lax.axis_size("aperture")
    copies = lax.axis_size("wave")
    rows = rows_dev * peers
    own_cols = cols // copies
    lanes = 2 * pairs_dev * HALF
    f32, bf16 = jnp.float32, jnp.bfloat16
    shape = jax.ShapeDtypeStruct

    def in_hbm(value):
        return pltpu.with_memory_space_constraint(value, pltpu.HBM)

    def exchange(value, step):
        return lax.ppermute(value, "aperture", [(index, index ^ step) for index in range(peers)])

    def to_core(value):
        return lax.ppermute(value, "wave", [(index, (index + 1) % copies) for index in range(copies)])

    def to_corner(value):
        places = [(index, core) for index in range(peers) for core in range(copies)]
        pairs = [
            (index * copies + core, (index ^ 1) * copies + (core + 1) % copies) for index, core in places
        ]
        return lax.ppermute(value, ("aperture", "wave"), pairs)

    mine, other, info, own = call(
        forward_kernel, "forward",
        (
            shape((rows_dev, lanes), bf16), shape((rows_dev, lanes), bf16),
            shape((pairs_dev, INFO_ROWS, FOCAL), f32), shape((rows_dev, own_cols), f32),
        ),
        [HBM] * 5, (VMEM,) * 4,
        [
            pltpu.SMEM(wave_ids.shape, jnp.int32),
            pltpu.SMEM(angle_ids.shape, jnp.int32),
            pltpu.SMEM(targets.shape, jnp.int32),
            pltpu.VMEM(coef_table.shape[::-1], f32),
            pltpu.VMEM(widths.shape, f32),
            pltpu.VMEM((pairs_dev, 2, BLOCK, FOCAL), f32),
            pltpu.VMEM((pairs_dev, 2, cols // (2 * BLOCK), FOCAL), f32),
            pltpu.VMEM((pairs_dev, 2, 2 * rows_dev, FOCAL), f32),
            pltpu.SemaphoreType.DMA((5,)),
        ],
        10**9, 10**7,
    )(*(in_hbm(value) for value in (wave_ids, angle_ids, targets, coef_table.T, widths)))
    far_info = to_core(info)
    if peers <= DIRECT:
        sections = [mine] + [exchange(other if step % 2 else mine, step) for step in range(1, peers)]
    else:
        even = lax.axis_index("aperture") % 2 == 0
        blocks = jnp.stack([jnp.where(even, mine, other), jnp.where(even, other, mine)])
        blocks = jnp.tile(blocks, (peers // 2, 1, 1))
        blocks = lax.all_to_all(blocks, "aperture", 0, 0, tiled=True)
        sections = [blocks.reshape(rows, lanes)]

    tall, flat = call(
        row_kernel, "row_tables",
        (shape((pairs_dev, 2 * FOCAL, rows), bf16), shape((pairs_dev, 2 * rows_dev, 2 * FOCAL), bf16)),
        [VMEM], (VMEM, VMEM), [], 10**8, 10**6,
    )(info)

    def column_tables(info, name):
        outs = [shape((own_cols, 2 * FOCAL), bf16)] * pairs_dev
        outs += [shape((2, rows_dev, own_cols), f32)] * pairs_dev
        got = call(
            functools.partial(table_kernel, math.sqrt(rows * cols), cols), name,
            outs, [VMEM, VMEM], [VMEM] * len(outs),
            [
                pltpu.VMEM((pairs_dev, 2, BLOCK, FOCAL), f32),
                pltpu.VMEM((pairs_dev, 2, own_cols // (2 * BLOCK), FOCAL), f32),
            ],
            10**9, 10**7,
        )(info, own)
        return got[:pairs_dev], got[pairs_dev:]

    tables, slopes = column_tables(info, "own_tables")
    far_tables, far_slopes = column_tables(far_info, "far_tables")

    field, power = call(
        field_kernel, "field",
        (shape((pairs_dev, 2, FOCAL, HALF), f32), shape((8, HALF), f32)),
        [VMEM] * (2 + len(sections)), (VMEM, VMEM), [pltpu.VMEM((rows, lanes), bf16)], 10**8, 10**6,
    )(info, tall, *sections)
    mine, other, scores = call(
        seed_kernel, "seed",
        (shape((rows_dev, lanes), bf16), shape((rows_dev, lanes), bf16), shape((pairs_dev,), f32)),
        [VMEM] * 5, (VMEM, VMEM, SMEM), [], 10**8, 10**6,
    )(info, power, exchange(power, 1), field, flat)
    backs = [mine, exchange(other, 1), to_core(mine), to_corner(other)]
    ins = [*backs, *tables, *far_tables, *slopes, *far_slopes]
    grad = call(
        functools.partial(grad_kernel, pairs_dev), "gradient",
        shape((rows_dev, own_cols), f32), [VMEM] * len(ins), VMEM,
        [pltpu.VMEM((copies * pairs_dev, 2 * rows_dev, 2 * FOCAL), bf16)],
        10**9, 10**7,
    )(*ins)
    return grad, scores


def solution(mesh):
    in_specs = (
        P(("group", "aperture"), None),
        P(),
        P(("group", "wave")),
        P(("group", "wave")),
        P(("group", "wave"), None),
    )
    out_specs = (P(("group", "aperture"), "wave"), P(("group", "wave")))
    return jax.shard_map(
        on_device, mesh=mesh, in_specs=in_specs, out_specs=out_specs, check_vma=False
    )
```

```python
import functools
import math

import jax
import jax.numpy as jnp
from jax import lax
from jax.experimental import pallas as pl
from jax.experimental.pallas import tpu as pltpu
from jax.sharding import PartitionSpec as P

FOCAL = 256
SPOT = 4
SHIFT = 32
TERMS = 8
BLOCK = 256
GRAIN = 16
VMEM_LIMIT = 16 * 1024 * 1024
HALF = FOCAL // 2
WAVE_ROW, ANGLE_ROW, AIM_ROW, INFO_ROWS = 16, 17, 18, 24
DIRECT = 16

COS = (
    1.0, -19.7392088015709, 64.93939395773512, -85.45681453397417, 60.24458621302471,
    -26.425616460281425, 7.8991596631575085, -1.6968741456712442, 0.2437618617467591,
)
SIN = (
    6.2831853071792665, -41.34170224019464, 81.60524925425943, -76.70585885700535,
    42.05867547580699, -15.094428387947755, 3.818490079304055, -0.7122771247541972,
    0.09149844789363434,
)


def horner(terms, u):
    value = terms[-1] * u + terms[-2]
    for term in terms[-3::-1]:
        value = value * u + term
    return value


def unit_waves(counts, period):
    half = period // 2
    centred = ((counts + half) & (period - 1)) - half
    t = centred.astype(jnp.float32) * (1.0 / period)
    u = t * t
    return horner(COS, u), -(t * horner(SIN, u))


def iota(shape, axis):
    return lax.broadcasted_iota(jnp.int32, shape, axis)


def pick_coef(table, wave):
    chosen = jnp.where(iota(table.shape, 1) == wave, table, 0.0)
    return jnp.sum(chosen, axis=1, keepdims=True)


def own_half():
    return lax.axis_index("aperture") % 2


def column_freq(info_ref, pair, first):
    wave = info_ref[pair, WAVE_ROW : WAVE_ROW + 1, :].astype(jnp.int32)
    angle = info_ref[pair, ANGLE_ROW : ANGLE_ROW + 1, :].astype(jnp.int32)
    focal = (iota((1, FOCAL), 1) + first) & (FOCAL - 1)
    return (focal - FOCAL // 2 + SHIFT * angle) * (BLOCK + wave)


def fill_base(freq, shift, period, base_ref, centre_ref):
    low_r, low_i = unit_waves(iota((GRAIN, 1), 0) * freq, period)
    steps = BLOCK // GRAIN
    high_r, high_i = unit_waves((iota((steps, 1), 0) * GRAIN - BLOCK // 2 + shift) * freq, period)
    for step in range(steps):
        one_r, one_i = high_r[step : step + 1], high_i[step : step + 1]
        rows = slice(step * GRAIN, (step + 1) * GRAIN)
        base_ref[0, rows, :] = one_r * low_r - one_i * low_i
        base_ref[1, rows, :] = one_r * low_i + one_i * low_r
    count = centre_ref.shape[1]
    cent_r, cent_i = unit_waves((iota((count, 1), 0) * BLOCK + BLOCK // 2) * freq, period)
    centre_ref[0] = cent_r
    centre_ref[1] = cent_i


def block_pair(base_ref, centre_ref, index):
    cent_r = centre_ref[0, index : index + 1, :]
    cent_i = centre_ref[1, index : index + 1, :]
    base_r, base_i = base_ref[0], base_ref[1]
    rr, ii = base_r * cent_r, base_i * cent_i
    ri, ir = base_r * cent_i, base_i * cent_r
    before = ((rr + ii).astype(jnp.bfloat16), (ir - ri).astype(jnp.bfloat16))
    after = ((rr - ii).astype(jnp.bfloat16), (ir + ri).astype(jnp.bfloat16))
    return before, after


def near_fields(s, info_ref, pairs):
    def coef(pair, row):
        return info_ref[pair, row : row + 1, :]

    outs = [[coef(p, k) + coef(p, k + 1) * s for k in (0, TERMS)] for p in range(pairs)]
    twice = s + s
    before, current = jnp.ones_like(s), s
    for order in range(2, TERMS):
        before, current = current, twice * current - before
        for pair, out in enumerate(outs):
            out[0] = out[0] + coef(pair, order) * current
            out[1] = out[1] + coef(pair, TERMS + order) * current
    return outs


def near_slopes(s, scale, info_ref, pairs):
    def coef(pair, row):
        return info_ref[pair, row : row + 1, :] * (scale * (row % TERMS))

    twice = s + s
    before, current = jnp.ones_like(s), twice
    outs = [[coef(p, k) + coef(p, k + 1) * twice for k in (1, TERMS + 1)] for p in range(pairs)]
    for order in range(3, TERMS):
        before, current = current, twice * current - before
        for pair, out in enumerate(outs):
            out[0] = out[0] + coef(pair, order) * current
            out[1] = out[1] + coef(pair, TERMS + order) * current
    return outs


def forward_kernel(
    wave_hbm, angle_hbm, aim_hbm, coef_hbm, width_hbm, mine_ref, other_ref, info_ref, own_ref,
    wave_ref, angle_ref, aim_ref, coef_ref, width_ref, base_ref, centre_ref, acc_ref, sems,
):
    rows_dev, cols = width_ref.shape
    pairs = wave_ref.shape[0]
    period = 256 * cols
    moves = [
        pltpu.make_async_copy(source, target, sems.at[index])
        for index, (source, target) in enumerate((
            (wave_hbm, wave_ref), (angle_hbm, angle_ref), (aim_hbm, aim_ref),
            (coef_hbm, coef_ref), (width_hbm, width_ref),
        ))
    ]
    for move in moves:
        move.start()
    for move in moves[:4]:
        move.wait()
    for pair in range(pairs):
        coef = pick_coef(coef_ref[...], wave_ref[pair])
        info_ref[pair, :WAVE_ROW, :] = jnp.broadcast_to(coef, (WAVE_ROW, FOCAL))
        row = iota((INFO_ROWS - WAVE_ROW, FOCAL), 0) + WAVE_ROW
        ids = jnp.where(row == WAVE_ROW, wave_ref[pair], 0)
        ids = jnp.where(row == ANGLE_ROW, angle_ref[pair], ids)
        ids = jnp.where(row == AIM_ROW, aim_ref[pair, 0], ids)
        ids = jnp.where(row == AIM_ROW + 1, aim_ref[pair, 1], ids)
        info_ref[pair, WAVE_ROW:, :] = ids.astype(jnp.float32)
    for pair in range(pairs):
        fill_base(column_freq(info_ref, pair, 0), 0, period, base_ref.at[pair], centre_ref.at[pair])
    acc_ref[...] = jnp.zeros_like(acc_ref)
    moves[4].wait()
    for index in range(cols // (2 * BLOCK)):
        left = cols // 2 - (index + 1) * BLOCK
        right = cols // 2 + index * BLOCK
        nears = []
        for start in (left, right):
            outs = near_fields(width_ref[:, start : start + BLOCK], info_ref, pairs)
            nears.append([jnp.concatenate(out, axis=0).astype(jnp.bfloat16) for out in outs])
        for pair in range(pairs):
            before, after = block_pair(base_ref.at[pair], centre_ref.at[pair], index)
            near = jnp.concatenate([nears[0][pair], nears[1][pair]], axis=1)
            for part in range(2):
                table = jnp.concatenate([before[part], after[part]], axis=0)
                acc_ref[pair, part] += jnp.dot(near, table, preferred_element_type=jnp.float32)
    own_cols = own_ref.shape[1]
    first = pl.multiple_of(lax.axis_index("wave") * own_cols, own_cols)
    own_ref[...] = width_ref[:, pl.ds(first, own_cols)]
    even = own_half() == 0
    for pair in range(pairs):
        real = acc_ref[pair, 0, :rows_dev] - acc_ref[pair, 1, rows_dev:]
        imag = acc_ref[pair, 1, :rows_dev] + acc_ref[pair, 0, rows_dev:]
        for part, value in enumerate((real, imag)):
            lanes = slice((2 * pair + part) * HALF, (2 * pair + part + 1) * HALF)
            mine_ref[:, lanes] = jnp.where(even, value[:, :HALF], value[:, HALF:]).astype(jnp.bfloat16)
            other_ref[:, lanes] = jnp.where(even, value[:, HALF:], value[:, :HALF]).astype(jnp.bfloat16)


def row_kernel(info_ref, tall_ref, flat_ref):
    pairs, _, rows = tall_ref.shape
    rows_dev = flat_ref.shape[1] // 2
    period = 256 * rows
    size = min(rows, FOCAL)
    me = lax.axis_index("aperture")
    for pair in range(pairs):
        wave = info_ref[pair, WAVE_ROW : WAVE_ROW + 1, :].astype(jnp.int32) + BLOCK
        focal = (iota((FOCAL, 1), 0) - FOCAL // 2) * wave

        def step(index, carry):
            start = pl.multiple_of(index * size, size)
            place = iota((1, size), 1) + (start - rows // 2)
            real, imag = unit_waves(focal[:, :size] * place, period)
            tall_ref[pair, :FOCAL, pl.ds(start, size)] = real.astype(jnp.bfloat16)
            tall_ref[pair, FOCAL:, pl.ds(start, size)] = imag.astype(jnp.bfloat16)
            return carry

        if rows == size:
            step(0, 0)
        else:
            lax.fori_loop(0, rows // size, step, 0)
        focal = (iota((1, FOCAL), 1) - FOCAL // 2) * wave
        for copy in range(2):
            first = (me ^ copy) * rows_dev - rows // 2
            real, imag = unit_waves((iota((rows_dev, 1), 0) + first) * focal, period)
            lines = slice(copy * rows_dev, (copy + 1) * rows_dev)
            flat_ref[pair, lines, :FOCAL] = real.astype(jnp.bfloat16)
            flat_ref[pair, lines, FOCAL:] = imag.astype(jnp.bfloat16)


def spot_half(info_ref, pair):
    aims = [info_ref[pair, row : row + 1, :HALF] for row in (AIM_ROW, AIM_ROW + 1)]
    rows_off = iota((FOCAL, HALF), 0).astype(jnp.float32) - aims[0]
    cols_off = (iota((1, HALF), 1) + own_half() * HALF).astype(jnp.float32) - aims[1]
    return jnp.exp(-(rows_off * rows_off + cols_off * cols_off) / (2.0 * SPOT * SPOT))


def merge_kernel(mine_ref, near_ref, after_ref, out_ref):
    del after_ref
    rows_dev = mine_ref.shape[0]
    place = own_half()
    out_ref[pl.ds(pl.multiple_of(place * rows_dev, rows_dev), rows_dev), :] = mine_ref[...]
    out_ref[pl.ds(pl.multiple_of((1 - place) * rows_dev, rows_dev), rows_dev), :] = near_ref[...]


def field_kernel(info_ref, tall_ref, after_ref, *refs):
    del after_ref
    *sect_refs, field_ref, power_ref, rows_ref = refs
    pairs = tall_ref.shape[0]
    count = sect_refs[0].shape[0]
    if len(sect_refs) == 1:
        sect_ref = sect_refs[0]
    else:
        sect_ref = rows_ref
        me = lax.axis_index("aperture") // 2
        for step, ref in enumerate(sect_refs):
            start = pl.multiple_of((me ^ step) * count, count)
            rows_ref[pl.ds(start, count), :] = ref[...]
    sums = []
    for pair in range(pairs):
        lanes = slice(pair * FOCAL, (pair + 1) * FOCAL)
        mixed = jnp.dot(tall_ref[pair], sect_ref[:, lanes], preferred_element_type=jnp.float32)
        real = mixed[:FOCAL, :HALF] - mixed[FOCAL:, HALF:]
        imag = mixed[:FOCAL, HALF:] + mixed[FOCAL:, :HALF]
        field_ref[pair, 0] = real
        field_ref[pair, 1] = imag
        power = real * real + imag * imag
        spot = spot_half(info_ref, pair)
        sums.append(jnp.sum(spot * power, axis=0, keepdims=True))
        sums.append(jnp.sum(power, axis=0, keepdims=True))
    sums.append(jnp.zeros((8 - len(sums), HALF), jnp.float32))
    power_ref[...] = jnp.concatenate(sums, axis=0)


def seed_kernel(info_ref, power_ref, far_ref, field_ref, flat_ref, mine_ref, other_ref, score_ref):
    rows_dev = mine_ref.shape[0]
    pairs = flat_ref.shape[0]
    sums = jnp.sum(power_ref[...] + far_ref[...], axis=1, keepdims=True)
    place = iota((1, FOCAL), 1).astype(jnp.float32)
    for pair in range(pairs):
        all_power = sums[2 * pair + 1 : 2 * pair + 2] + 1e-06
        ratio = sums[2 * pair : 2 * pair + 1] / all_power
        spans = []
        for row in (AIM_ROW, AIM_ROW + 1):
            off = place - info_ref[pair, row : row + 1, :]
            spans.append(jnp.sum(jnp.exp(-(off * off) / (2.0 * SPOT * SPOT)), axis=1, keepdims=True))
        factor = FOCAL * FOCAL / (spans[0] * spans[1])
        score_ref[pair] = jnp.sum(ratio * factor)
        weight = (factor * 2.0 / all_power) * (spot_half(info_ref, pair) - ratio)
        real = (weight * field_ref[pair, 0]).astype(jnp.bfloat16)
        imag = (weight * field_ref[pair, 1]).astype(jnp.bfloat16)
        stack = jnp.concatenate(
            [jnp.concatenate([real, imag], axis=1), jnp.concatenate([imag, -real], axis=1)], axis=0
        )
        back = jnp.dot(flat_ref[pair], stack, preferred_element_type=jnp.float32).astype(jnp.bfloat16)
        lanes = slice(pair * FOCAL, (pair + 1) * FOCAL)
        mine_ref[:, lanes] = back[:rows_dev]
        other_ref[:, lanes] = back[rows_dev:]


def table_kernel(scale, cols, info_ref, width_ref, after_ref, *refs):
    del after_ref
    *out_refs, base_ref, centre_ref = refs
    pairs = base_ref.shape[0]
    table_refs, slope_refs = out_refs[:pairs], out_refs[pairs:]
    own_cols = width_ref.shape[1]
    period = 256 * cols
    middle = own_cols // 2
    shift = lax.axis_index("wave") * own_cols + middle - cols // 2
    for pair in range(pairs):
        freq = column_freq(info_ref, pair, own_half() * HALF)
        fill_base(freq, shift, period, base_ref.at[pair], centre_ref.at[pair])
    for index in range(own_cols // (2 * BLOCK)):
        left = middle - (index + 1) * BLOCK
        right = middle + index * BLOCK
        for pair in range(pairs):
            tables = block_pair(base_ref.at[pair], centre_ref.at[pair], index)
            for start, table in zip((left, right), tables):
                table_refs[pair][start : start + BLOCK, :FOCAL] = table[0]
                table_refs[pair][start : start + BLOCK, FOCAL:] = table[1]
        for start in (left, right):
            slopes = near_slopes(width_ref[:, start : start + BLOCK], scale, info_ref, pairs)
            for pair in range(pairs):
                slope_refs[pair][0, :, start : start + BLOCK] = slopes[pair][0]
                slope_refs[pair][1, :, start : start + BLOCK] = slopes[pair][1]


def grad_kernel(pairs_dev, *refs):
    *in_refs, out_ref, left_ref = refs
    rows_dev, own_cols = out_ref.shape
    pairs = left_ref.shape[0]
    back_refs, in_refs = in_refs[: 2 * pairs // pairs_dev], in_refs[2 * pairs // pairs_dev :]
    table_refs, slope_refs = in_refs[:pairs], in_refs[pairs:]
    for pair in range(pairs):
        halves = back_refs[2 * (pair // pairs_dev) : 2 * (pair // pairs_dev) + 2]
        for half, ref in enumerate(halves):
            lane = (pair % pairs_dev) * FOCAL
            real, imag = ref[:, lane : lane + HALF], ref[:, lane + HALF : lane + FOCAL]
            for part, rows, value in ((0, 0, real), (1, 0, imag), (0, 1, imag), (1, 1, -real)):
                start = part * FOCAL + half * HALF
                left_ref[pair, rows * rows_dev : (rows + 1) * rows_dev, start : start + HALF] = value
    size = 2 * BLOCK
    for start in range(0, own_cols, size):
        total = jnp.zeros((rows_dev, size), jnp.float32)
        for pair in range(pairs):
            grad = lax.dot_general(
                left_ref[pair],
                table_refs[pair][start : start + size, :],
                (((1,), (1,)), ((), ())),
                preferred_element_type=jnp.float32,
            )
            total += grad[:rows_dev] * slope_refs[pair][0, :, start : start + size]
            total += grad[rows_dev:] * slope_refs[pair][1, :, start : start + size]
        out_ref[:, start : start + size] = total


VMEM = pl.BlockSpec(memory_space=pltpu.VMEM)
SMEM = pl.BlockSpec(memory_space=pltpu.SMEM)
ANY = pl.BlockSpec(memory_space=pl.ANY)
HBM = pl.BlockSpec(memory_space=pltpu.HBM)


def call(kernel, name, outs, in_specs, out_specs, scratch, flops, moved):
    return pl.pallas_call(
        kernel,
        name=name,
        out_shape=outs,
        in_specs=in_specs,
        out_specs=out_specs,
        scratch_shapes=scratch,
        cost_estimate=pl.CostEstimate(flops=flops, bytes_accessed=moved, transcendentals=0),
        compiler_params=pltpu.CompilerParams(vmem_limit_bytes=VMEM_LIMIT),
    )


def on_device(widths, coef_table, wave_ids, angle_ids, targets):
    rows_dev, cols = widths.shape
    pairs_dev = wave_ids.shape[0]
    peers = lax.axis_size("aperture")
    copies = lax.axis_size("wave")
    rows = rows_dev * peers
    own_cols = cols // copies
    lanes = 2 * pairs_dev * HALF
    f32, bf16 = jnp.float32, jnp.bfloat16
    shape = jax.ShapeDtypeStruct

    def in_hbm(value):
        return pltpu.with_memory_space_constraint(value, pltpu.HBM)

    def exchange(value, step):
        return lax.ppermute(value, "aperture", [(index, index ^ step) for index in range(peers)])

    def to_core(value):
        return lax.ppermute(value, "wave", [(index, (index + 1) % copies) for index in range(copies)])

    def to_corner(value):
        places = [(index, core) for index in range(peers) for core in range(copies)]
        pairs = [
            (index * copies + core, (index ^ 1) * copies + (core + 1) % copies) for index, core in places
        ]
        return lax.ppermute(value, ("aperture", "wave"), pairs)

    mine, other, info, own = call(
        forward_kernel, "forward",
        (
            shape((rows_dev, lanes), bf16), shape((rows_dev, lanes), bf16),
            shape((pairs_dev, INFO_ROWS, FOCAL), f32), shape((rows_dev, own_cols), f32),
        ),
        [HBM] * 5, (VMEM,) * 4,
        [
            pltpu.SMEM(wave_ids.shape, jnp.int32),
            pltpu.SMEM(angle_ids.shape, jnp.int32),
            pltpu.SMEM(targets.shape, jnp.int32),
            pltpu.VMEM(coef_table.shape[::-1], f32),
            pltpu.VMEM(widths.shape, f32),
            pltpu.VMEM((pairs_dev, 2, BLOCK, FOCAL), f32),
            pltpu.VMEM((pairs_dev, 2, cols // (2 * BLOCK), FOCAL), f32),
            pltpu.VMEM((pairs_dev, 2, 2 * rows_dev, FOCAL), f32),
            pltpu.SemaphoreType.DMA((5,)),
        ],
        10**9, 10**7,
    )(*(in_hbm(value) for value in (wave_ids, angle_ids, targets, coef_table.T, widths)))
    far_info = to_core(info)
    tall, flat = call(
        row_kernel, "row_tables",
        (shape((pairs_dev, 2 * FOCAL, rows), bf16), shape((pairs_dev, 2 * rows_dev, 2 * FOCAL), bf16)),
        [VMEM], (VMEM, VMEM), [], 10**8, 10**6,
    )(info)
    if peers <= DIRECT:
        merged = call(
            merge_kernel, "merge", shape((2 * rows_dev, lanes), bf16), [VMEM, VMEM, ANY], VMEM, [], 10**6, 10**6
        )(mine, exchange(other, 1), flat)
        sections = [merged] + [exchange(merged, step) for step in range(2, peers, 2)]
    else:
        even = lax.axis_index("aperture") % 2 == 0
        blocks = jnp.stack([jnp.where(even, mine, other), jnp.where(even, other, mine)])
        blocks = jnp.tile(blocks, (peers // 2, 1, 1))
        blocks = lax.all_to_all(blocks, "aperture", 0, 0, tiled=True)
        sections = [blocks.reshape(rows, lanes)]

    def column_tables(info, after, name):
        outs = [shape((own_cols, 2 * FOCAL), bf16)] * pairs_dev
        outs += [shape((2, rows_dev, own_cols), f32)] * pairs_dev
        got = call(
            functools.partial(table_kernel, math.sqrt(rows * cols), cols), name,
            outs, [VMEM, VMEM, ANY], [VMEM] * len(outs),
            [
                pltpu.VMEM((pairs_dev, 2, BLOCK, FOCAL), f32),
                pltpu.VMEM((pairs_dev, 2, own_cols // (2 * BLOCK), FOCAL), f32),
            ],
            10**9, 10**7,
        )(info, own, after)
        return got[:pairs_dev], got[pairs_dev:]

    tables, slopes = column_tables(info, sections[0], "own_tables")
    field, power = call(
        field_kernel, "field",
        (shape((pairs_dev, 2, FOCAL, HALF), f32), shape((8, HALF), f32)),
        [VMEM, VMEM, ANY] + [VMEM] * len(sections), (VMEM, VMEM), [pltpu.VMEM((rows, lanes), bf16)], 10**8, 10**6,
    )(info, tall, slopes[0], *sections)
    far_tables, far_slopes = column_tables(far_info, power, "far_tables")
    mine, other, scores = call(
        seed_kernel, "seed",
        (shape((rows_dev, lanes), bf16), shape((rows_dev, lanes), bf16), shape((pairs_dev,), f32)),
        [VMEM] * 5, (VMEM, VMEM, SMEM), [], 10**8, 10**6,
    )(info, power, exchange(power, 1), field, flat)
    backs = [mine, exchange(other, 1), to_core(mine), to_corner(other)]
    ins = [*backs, *tables, *far_tables, *slopes, *far_slopes]
    grad = call(
        functools.partial(grad_kernel, pairs_dev), "gradient",
        shape((rows_dev, own_cols), f32), [VMEM] * len(ins), VMEM,
        [pltpu.VMEM((copies * pairs_dev, 2 * rows_dev, 2 * FOCAL), bf16)],
        10**9, 10**7,
    )(*ins)
    return grad, scores


def solution(mesh):
    in_specs = (
        P(("group", "aperture"), None),
        P(),
        P(("group", "wave")),
        P(("group", "wave")),
        P(("group", "wave"), None),
    )
    out_specs = (P(("group", "aperture"), "wave"), P(("group", "wave")))
    return jax.shard_map(
        on_device, mesh=mesh, in_specs=in_specs, out_specs=out_specs, check_vma=False
    )
```

```python
import functools
import math

import jax
import jax.numpy as jnp
from jax import lax
from jax.experimental import pallas as pl
from jax.experimental.pallas import tpu as pltpu
from jax.sharding import PartitionSpec as P

FOCAL = 256
SPOT = 4
SHIFT = 32
TERMS = 8
BLOCK = 256
GRAIN = 16
VMEM_LIMIT = 16 * 1024 * 1024
HALF = FOCAL // 2
WAVE_ROW, ANGLE_ROW, AIM_ROW, INFO_ROWS = 16, 17, 18, 24
DIRECT = 16

COS = (
    1.0, -19.7392088015709, 64.93939395773512, -85.45681453397417, 60.24458621302471,
    -26.425616460281425, 7.8991596631575085, -1.6968741456712442, 0.2437618617467591,
)
SIN = (
    6.2831853071792665, -41.34170224019464, 81.60524925425943, -76.70585885700535,
    42.05867547580699, -15.094428387947755, 3.818490079304055, -0.7122771247541972,
    0.09149844789363434,
)


def horner(terms, u):
    value = terms[-1] * u + terms[-2]
    for term in terms[-3::-1]:
        value = value * u + term
    return value


def unit_waves(counts, period):
    half = period // 2
    centred = ((counts + half) & (period - 1)) - half
    t = centred.astype(jnp.float32) * (1.0 / period)
    u = t * t
    return horner(COS, u), -(t * horner(SIN, u))


def iota(shape, axis):
    return lax.broadcasted_iota(jnp.int32, shape, axis)


def pick_coef(table, wave):
    chosen = jnp.where(iota(table.shape, 1) == wave, table, 0.0)
    return jnp.sum(chosen, axis=1, keepdims=True)


def own_half():
    return lax.axis_index("aperture") % 2


def column_freq(info_ref, pair, first):
    wave = info_ref[pair, WAVE_ROW : WAVE_ROW + 1, :].astype(jnp.int32)
    angle = info_ref[pair, ANGLE_ROW : ANGLE_ROW + 1, :].astype(jnp.int32)
    focal = (iota((1, FOCAL), 1) + first) & (FOCAL - 1)
    return (focal - FOCAL // 2 + SHIFT * angle) * (BLOCK + wave)


def fill_base(freq, shift, period, base_ref, centre_ref):
    low_r, low_i = unit_waves(iota((GRAIN, 1), 0) * freq, period)
    steps = BLOCK // GRAIN
    high_r, high_i = unit_waves((iota((steps, 1), 0) * GRAIN - BLOCK // 2 + shift) * freq, period)
    for step in range(steps):
        one_r, one_i = high_r[step : step + 1], high_i[step : step + 1]
        rows = slice(step * GRAIN, (step + 1) * GRAIN)
        base_ref[0, rows, :] = one_r * low_r - one_i * low_i
        base_ref[1, rows, :] = one_r * low_i + one_i * low_r
    count = centre_ref.shape[1]
    cent_r, cent_i = unit_waves((iota((count, 1), 0) * BLOCK + BLOCK // 2) * freq, period)
    centre_ref[0] = cent_r
    centre_ref[1] = cent_i


def block_pair(base_ref, centre_ref, index):
    cent_r = centre_ref[0, index : index + 1, :]
    cent_i = centre_ref[1, index : index + 1, :]
    base_r, base_i = base_ref[0], base_ref[1]
    rr, ii = base_r * cent_r, base_i * cent_i
    ri, ir = base_r * cent_i, base_i * cent_r
    before = ((rr + ii).astype(jnp.bfloat16), (ir - ri).astype(jnp.bfloat16))
    after = ((rr - ii).astype(jnp.bfloat16), (ir + ri).astype(jnp.bfloat16))
    return before, after


def near_fields(s, info_ref, pairs):
    def coef(pair, row):
        return info_ref[pair, row : row + 1, :]

    outs = [[coef(p, k) + coef(p, k + 1) * s for k in (0, TERMS)] for p in range(pairs)]
    twice = s + s
    before, current = jnp.ones_like(s), s
    for order in range(2, TERMS):
        before, current = current, twice * current - before
        for pair, out in enumerate(outs):
            out[0] = out[0] + coef(pair, order) * current
            out[1] = out[1] + coef(pair, TERMS + order) * current
    return outs


def near_slopes(s, scale, info_ref, pairs):
    def coef(pair, row):
        return info_ref[pair, row : row + 1, :] * (scale * (row % TERMS))

    twice = s + s
    before, current = jnp.ones_like(s), twice
    outs = [[coef(p, k) + coef(p, k + 1) * twice for k in (1, TERMS + 1)] for p in range(pairs)]
    for order in range(3, TERMS):
        before, current = current, twice * current - before
        for pair, out in enumerate(outs):
            out[0] = out[0] + coef(pair, order) * current
            out[1] = out[1] + coef(pair, TERMS + order) * current
    return outs


def forward_kernel(
    wave_hbm, angle_hbm, aim_hbm, coef_hbm, width_hbm, mine_ref, other_ref, info_ref, own_ref,
    wave_ref, angle_ref, aim_ref, coef_ref, width_ref, base_ref, centre_ref, acc_ref, sems,
):
    rows_dev, cols = width_ref.shape
    pairs = wave_ref.shape[0]
    period = 256 * cols
    moves = [
        pltpu.make_async_copy(source, target, sems.at[index])
        for index, (source, target) in enumerate((
            (wave_hbm, wave_ref), (angle_hbm, angle_ref), (aim_hbm, aim_ref),
            (coef_hbm, coef_ref), (width_hbm, width_ref),
        ))
    ]
    for move in moves:
        move.start()
    for move in moves[:4]:
        move.wait()
    for pair in range(pairs):
        coef = pick_coef(coef_ref[...], wave_ref[pair])
        info_ref[pair, :WAVE_ROW, :] = jnp.broadcast_to(coef, (WAVE_ROW, FOCAL))
        row = iota((INFO_ROWS - WAVE_ROW, FOCAL), 0) + WAVE_ROW
        ids = jnp.where(row == WAVE_ROW, wave_ref[pair], 0)
        ids = jnp.where(row == ANGLE_ROW, angle_ref[pair], ids)
        ids = jnp.where(row == AIM_ROW, aim_ref[pair, 0], ids)
        ids = jnp.where(row == AIM_ROW + 1, aim_ref[pair, 1], ids)
        info_ref[pair, WAVE_ROW:, :] = ids.astype(jnp.float32)
    for pair in range(pairs):
        fill_base(column_freq(info_ref, pair, 0), 0, period, base_ref.at[pair], centre_ref.at[pair])
    acc_ref[...] = jnp.zeros_like(acc_ref)
    moves[4].wait()
    for index in range(cols // (2 * BLOCK)):
        left = cols // 2 - (index + 1) * BLOCK
        right = cols // 2 + index * BLOCK
        nears = []
        for start in (left, right):
            outs = near_fields(width_ref[:, start : start + BLOCK], info_ref, pairs)
            nears.append([jnp.concatenate(out, axis=0).astype(jnp.bfloat16) for out in outs])
        for pair in range(pairs):
            before, after = block_pair(base_ref.at[pair], centre_ref.at[pair], index)
            near = jnp.concatenate([nears[0][pair], nears[1][pair]], axis=1)
            for part in range(2):
                table = jnp.concatenate([before[part], after[part]], axis=0)
                acc_ref[pair, part] += jnp.dot(near, table, preferred_element_type=jnp.float32)
    own_cols = own_ref.shape[1]
    first = pl.multiple_of(lax.axis_index("wave") * own_cols, own_cols)
    own_ref[...] = width_ref[:, pl.ds(first, own_cols)]
    even = own_half() == 0
    for pair in range(pairs):
        real = acc_ref[pair, 0, :rows_dev] - acc_ref[pair, 1, rows_dev:]
        imag = acc_ref[pair, 1, :rows_dev] + acc_ref[pair, 0, rows_dev:]
        for part, value in enumerate((real, imag)):
            lanes = slice((2 * pair + part) * HALF, (2 * pair + part + 1) * HALF)
            mine_ref[:, lanes] = jnp.where(even, value[:, :HALF], value[:, HALF:]).astype(jnp.bfloat16)
            other_ref[:, lanes] = jnp.where(even, value[:, HALF:], value[:, :HALF]).astype(jnp.bfloat16)


def row_kernel(info_ref, tall_ref, flat_ref):
    pairs, _, rows = tall_ref.shape
    rows_dev = flat_ref.shape[1] // 2
    period = 256 * rows
    size = min(rows, FOCAL)
    me = lax.axis_index("aperture")
    for pair in range(pairs):
        wave = info_ref[pair, WAVE_ROW : WAVE_ROW + 1, :].astype(jnp.int32) + BLOCK
        focal = (iota((FOCAL, 1), 0) - FOCAL // 2) * wave

        def step(index, carry):
            start = pl.multiple_of(index * size, size)
            place = iota((1, size), 1) + (start - rows // 2)
            real, imag = unit_waves(focal[:, :size] * place, period)
            tall_ref[pair, :FOCAL, pl.ds(start, size)] = real.astype(jnp.bfloat16)
            tall_ref[pair, FOCAL:, pl.ds(start, size)] = imag.astype(jnp.bfloat16)
            return carry

        if rows == size:
            step(0, 0)
        else:
            lax.fori_loop(0, rows // size, step, 0)
        focal = (iota((1, FOCAL), 1) - FOCAL // 2) * wave
        for copy in range(2):
            first = (me ^ copy) * rows_dev - rows // 2
            real, imag = unit_waves((iota((rows_dev, 1), 0) + first) * focal, period)
            lines = slice(copy * rows_dev, (copy + 1) * rows_dev)
            flat_ref[pair, lines, :FOCAL] = real.astype(jnp.bfloat16)
            flat_ref[pair, lines, FOCAL:] = imag.astype(jnp.bfloat16)


def spot_half(info_ref, pair):
    aims = [info_ref[pair, row : row + 1, :HALF] for row in (AIM_ROW, AIM_ROW + 1)]
    rows_off = iota((FOCAL, HALF), 0).astype(jnp.float32) - aims[0]
    cols_off = (iota((1, HALF), 1) + own_half() * HALF).astype(jnp.float32) - aims[1]
    return jnp.exp(-(rows_off * rows_off + cols_off * cols_off) / (2.0 * SPOT * SPOT))


def merge_kernel(mine_ref, near_ref, after_ref, out_ref):
    del after_ref
    rows_dev = mine_ref.shape[0]
    place = own_half()
    out_ref[pl.ds(pl.multiple_of(place * rows_dev, rows_dev), rows_dev), :] = mine_ref[...]
    out_ref[pl.ds(pl.multiple_of((1 - place) * rows_dev, rows_dev), rows_dev), :] = near_ref[...]


def field_kernel(info_ref, tall_ref, after_ref, *refs):
    del after_ref
    *sect_refs, field_ref, power_ref, rows_ref = refs
    pairs = tall_ref.shape[0]
    count = sect_refs[0].shape[0]
    if len(sect_refs) == 1:
        sect_ref = sect_refs[0]
    else:
        sect_ref = rows_ref
        me = lax.axis_index("aperture") // 2
        for step, ref in enumerate(sect_refs):
            start = pl.multiple_of((me ^ step) * count, count)
            rows_ref[pl.ds(start, count), :] = ref[...]
    sums = []
    for pair in range(pairs):
        lanes = slice(pair * FOCAL, (pair + 1) * FOCAL)
        mixed = jnp.dot(tall_ref[pair], sect_ref[:, lanes], preferred_element_type=jnp.float32)
        real = mixed[:FOCAL, :HALF] - mixed[FOCAL:, HALF:]
        imag = mixed[:FOCAL, HALF:] + mixed[FOCAL:, :HALF]
        field_ref[pair, 0] = real
        field_ref[pair, 1] = imag
        power = real * real + imag * imag
        spot = spot_half(info_ref, pair)
        sums.append(jnp.sum(spot * power, axis=0, keepdims=True))
        sums.append(jnp.sum(power, axis=0, keepdims=True))
    sums.append(jnp.zeros((8 - len(sums), HALF), jnp.float32))
    power_ref[...] = jnp.concatenate(sums, axis=0)


def seed_kernel(
    info_ref, power_ref, far_ref, field_ref, flat_ref, after_ref, mine_ref, other_ref, score_ref
):
    del after_ref
    rows_dev = mine_ref.shape[0]
    pairs = flat_ref.shape[0]
    sums = jnp.sum(power_ref[...] + far_ref[...], axis=1, keepdims=True)
    place = iota((1, FOCAL), 1).astype(jnp.float32)
    for pair in range(pairs):
        all_power = sums[2 * pair + 1 : 2 * pair + 2] + 1e-06
        ratio = sums[2 * pair : 2 * pair + 1] / all_power
        spans = []
        for row in (AIM_ROW, AIM_ROW + 1):
            off = place - info_ref[pair, row : row + 1, :]
            spans.append(jnp.sum(jnp.exp(-(off * off) / (2.0 * SPOT * SPOT)), axis=1, keepdims=True))
        factor = FOCAL * FOCAL / (spans[0] * spans[1])
        score_ref[pair] = jnp.sum(ratio * factor)
        weight = (factor * 2.0 / all_power) * (spot_half(info_ref, pair) - ratio)
        real = (weight * field_ref[pair, 0]).astype(jnp.bfloat16)
        imag = (weight * field_ref[pair, 1]).astype(jnp.bfloat16)
        stack = jnp.concatenate(
            [jnp.concatenate([real, imag], axis=1), jnp.concatenate([imag, -real], axis=1)], axis=0
        )
        back = jnp.dot(flat_ref[pair], stack, preferred_element_type=jnp.float32).astype(jnp.bfloat16)
        lanes = slice(pair * FOCAL, (pair + 1) * FOCAL)
        mine_ref[:, lanes] = back[:rows_dev]
        other_ref[:, lanes] = back[rows_dev:]


def table_kernel(scale, cols, info_ref, width_ref, after_ref, *refs):
    del after_ref
    *out_refs, base_ref, centre_ref, turned_ref = refs
    pairs = base_ref.shape[0]
    table_refs, slope_refs = out_refs[:pairs], out_refs[pairs:]
    own_cols = width_ref.shape[1]
    period = 256 * cols
    middle = own_cols // 2
    shift = lax.axis_index("wave") * own_cols + middle - cols // 2
    for pair in range(pairs):
        freq = column_freq(info_ref, pair, own_half() * HALF)
        fill_base(freq, shift, period, base_ref.at[pair], centre_ref.at[pair])
        for part in range(2):
            turned_ref[pair, part] = base_ref[pair, part].T
    centres = [[centre_ref[pair, part].T for part in range(2)] for pair in range(pairs)]
    for index in range(own_cols // (2 * BLOCK)):
        left = middle - (index + 1) * BLOCK
        right = middle + index * BLOCK
        for pair in range(pairs):
            cent_r, cent_i = (centre[:, index : index + 1] for centre in centres[pair])
            for half in range(2):
                lines = slice(half * HALF, (half + 1) * HALF)
                one_r, one_i = cent_r[lines], cent_i[lines]
                base_r, base_i = turned_ref[pair, 0, lines, :], turned_ref[pair, 1, lines, :]
                rr, ii = base_r * one_r, base_i * one_i
                ri, ir = base_r * one_i, base_i * one_r
                for start, values in ((left, (rr + ii, ir - ri)), (right, (rr - ii, ir + ri))):
                    for part, value in enumerate(values):
                        row = (2 * half + part) * HALF
                        table_refs[pair][row : row + HALF, start : start + BLOCK] = value.astype(jnp.bfloat16)
        for start in (left, right):
            slopes = near_slopes(width_ref[:, start : start + BLOCK], scale, info_ref, pairs)
            for pair in range(pairs):
                slope_refs[pair][0, :, start : start + BLOCK] = slopes[pair][0]
                slope_refs[pair][1, :, start : start + BLOCK] = slopes[pair][1]


def grad_kernel(pairs, half, back_ref, *refs):
    *in_refs, out_ref = refs
    table_refs, slope_refs, total_ref = in_refs[:pairs], in_refs[pairs : 2 * pairs], in_refs[2 * pairs :]
    rows_dev, own_cols = out_ref.shape
    lefts = []
    for pair in range(pairs):
        lane = pair * FOCAL
        real, imag = back_ref[:, lane : lane + HALF], back_ref[:, lane + HALF : lane + FOCAL]
        lefts.append(
            jnp.concatenate(
                [jnp.concatenate([real, imag], axis=1), jnp.concatenate([imag, -real], axis=1)], axis=0
            )
        )
    size = 2 * BLOCK
    lines = slice(half * FOCAL, (half + 1) * FOCAL)
    for start in range(0, own_cols, size):
        place = slice(start, start + size)
        total = total_ref[0][:, place] if total_ref else jnp.zeros((rows_dev, size), jnp.float32)
        for pair in range(pairs):
            grad = jnp.dot(lefts[pair], table_refs[pair][lines, place], preferred_element_type=jnp.float32)
            total += grad[:rows_dev] * slope_refs[pair][0, :, place]
            total += grad[rows_dev:] * slope_refs[pair][1, :, place]
        out_ref[:, place] = total


VMEM = pl.BlockSpec(memory_space=pltpu.VMEM)
SMEM = pl.BlockSpec(memory_space=pltpu.SMEM)
ANY = pl.BlockSpec(memory_space=pl.ANY)
HBM = pl.BlockSpec(memory_space=pltpu.HBM)


def call(kernel, name, outs, in_specs, out_specs, scratch, flops, moved):
    return pl.pallas_call(
        kernel,
        name=name,
        out_shape=outs,
        in_specs=in_specs,
        out_specs=out_specs,
        scratch_shapes=scratch,
        cost_estimate=pl.CostEstimate(flops=flops, bytes_accessed=moved, transcendentals=0),
        compiler_params=pltpu.CompilerParams(vmem_limit_bytes=VMEM_LIMIT),
    )


def on_device(widths, coef_table, wave_ids, angle_ids, targets):
    rows_dev, cols = widths.shape
    pairs_dev = wave_ids.shape[0]
    peers = lax.axis_size("aperture")
    copies = lax.axis_size("wave")
    rows = rows_dev * peers
    own_cols = cols // copies
    lanes = 2 * pairs_dev * HALF
    f32, bf16 = jnp.float32, jnp.bfloat16
    shape = jax.ShapeDtypeStruct

    def in_hbm(value):
        return pltpu.with_memory_space_constraint(value, pltpu.HBM)

    def exchange(value, step):
        return lax.ppermute(value, "aperture", [(index, index ^ step) for index in range(peers)])

    def to_core(value):
        return lax.ppermute(value, "wave", [(index, (index + 1) % copies) for index in range(copies)])

    mine, other, info, own = call(
        forward_kernel, "forward",
        (
            shape((rows_dev, lanes), bf16), shape((rows_dev, lanes), bf16),
            shape((pairs_dev, INFO_ROWS, FOCAL), f32), shape((rows_dev, own_cols), f32),
        ),
        [HBM] * 5, (VMEM,) * 4,
        [
            pltpu.SMEM(wave_ids.shape, jnp.int32),
            pltpu.SMEM(angle_ids.shape, jnp.int32),
            pltpu.SMEM(targets.shape, jnp.int32),
            pltpu.VMEM(coef_table.shape[::-1], f32),
            pltpu.VMEM(widths.shape, f32),
            pltpu.VMEM((pairs_dev, 2, BLOCK, FOCAL), f32),
            pltpu.VMEM((pairs_dev, 2, cols // (2 * BLOCK), FOCAL), f32),
            pltpu.VMEM((pairs_dev, 2, 2 * rows_dev, FOCAL), f32),
            pltpu.SemaphoreType.DMA((5,)),
        ],
        10**9, 10**7,
    )(*(in_hbm(value) for value in (wave_ids, angle_ids, targets, coef_table.T, widths)))
    far_info = to_core(info)
    tall, flat = call(
        row_kernel, "row_tables",
        (shape((pairs_dev, 2 * FOCAL, rows), bf16), shape((pairs_dev, 2 * rows_dev, 2 * FOCAL), bf16)),
        [VMEM], (VMEM, VMEM), [], 10**8, 10**6,
    )(info)
    if peers <= DIRECT:
        merged = call(
            merge_kernel, "merge", shape((2 * rows_dev, lanes), bf16), [VMEM, VMEM, ANY], VMEM, [], 10**6, 10**6
        )(mine, exchange(other, 1), flat)
        sections = [merged] + [exchange(merged, step) for step in range(2, peers, 2)]
    else:
        even = lax.axis_index("aperture") % 2 == 0
        blocks = jnp.stack([jnp.where(even, mine, other), jnp.where(even, other, mine)])
        blocks = jnp.tile(blocks, (peers // 2, 1, 1))
        blocks = lax.all_to_all(blocks, "aperture", 0, 0, tiled=True)
        sections = [blocks.reshape(rows, lanes)]

    def column_tables(info, after, name):
        outs = [shape((2 * FOCAL, own_cols), bf16)] * pairs_dev
        outs += [shape((2, rows_dev, own_cols), f32)] * pairs_dev
        got = call(
            functools.partial(table_kernel, math.sqrt(rows * cols), cols), name,
            outs, [VMEM, VMEM, ANY], [VMEM] * len(outs),
            [
                pltpu.VMEM((pairs_dev, 2, BLOCK, FOCAL), f32),
                pltpu.VMEM((pairs_dev, 2, own_cols // (2 * BLOCK), FOCAL), f32),
                pltpu.VMEM((pairs_dev, 2, FOCAL, BLOCK), f32),
            ],
            10**9, 10**7,
        )(info, own, after)
        return got[:pairs_dev], got[pairs_dev:]

    tables, slopes = column_tables(info, sections[0], "own_tables")
    field, power = call(
        field_kernel, "field",
        (shape((pairs_dev, 2, FOCAL, HALF), f32), shape((8, HALF), f32)),
        [VMEM, VMEM, ANY] + [VMEM] * len(sections), (VMEM, VMEM), [pltpu.VMEM((rows, lanes), bf16)], 10**8, 10**6,
    )(info, tall, slopes[0], *sections)
    far_tables, far_slopes = column_tables(far_info, power, "far_tables")
    mine, other, scores = call(
        seed_kernel, "seed",
        (shape((rows_dev, lanes), bf16), shape((rows_dev, lanes), bf16), shape((pairs_dev,), f32)),
        [VMEM] * 5 + [ANY], (VMEM, VMEM, SMEM), [], 10**8, 10**6,
    )(info, power, exchange(power, 1), field, flat, far_slopes[0])

    def add_grad(back, half, tables, slopes, name, *total):
        ins = [back, *tables, *slopes, *total]
        return call(
            functools.partial(grad_kernel, pairs_dev, half), name,
            shape((rows_dev, own_cols), f32), [VMEM] * len(ins), VMEM, [], 10**9, 10**7,
        )(*ins)

    from_core = to_core(mine)
    from_near = exchange(other, 1)
    grad = add_grad(mine, 0, tables, slopes, "gradient_own")
    grad = add_grad(from_core, 0, far_tables, far_slopes, "gradient_core", grad)
    from_near, grad = lax.optimization_barrier((from_near, grad))
    grad = add_grad(from_near, 1, tables, slopes, "gradient_near", grad)
    grad = add_grad(to_core(from_near), 1, far_tables, far_slopes, "gradient_last", grad)
    return grad, scores


def solution(mesh):
    in_specs = (
        P(("group", "aperture"), None),
        P(),
        P(("group", "wave")),
        P(("group", "wave")),
        P(("group", "wave"), None),
    )
    out_specs = (P(("group", "aperture"), "wave"), P(("group", "wave")))
    return jax.shard_map(
        on_device, mesh=mesh, in_specs=in_specs, out_specs=out_specs, check_vma=False
    )
```

```python
import functools
import math

import jax
import jax.numpy as jnp
from jax import lax
from jax.experimental import pallas as pl
from jax.experimental.pallas import tpu as pltpu
from jax.sharding import PartitionSpec as P

FOCAL = 256
SPOT = 4
SHIFT = 32
TERMS = 8
BLOCK = 256
GRAIN = 16
VMEM_LIMIT = 16 * 1024 * 1024
WAVE_ROW, ANGLE_ROW, AIM_ROW, INFO_ROWS = 16, 17, 18, 24
DIRECT = 16

COS = (
    1.0, -19.7392088015709, 64.93939395773512, -85.45681453397417, 60.24458621302471,
    -26.425616460281425, 7.8991596631575085, -1.6968741456712442, 0.2437618617467591,
)
SIN = (
    6.2831853071792665, -41.34170224019464, 81.60524925425943, -76.70585885700535,
    42.05867547580699, -15.094428387947755, 3.818490079304055, -0.7122771247541972,
    0.09149844789363434,
)


def horner(terms, u):
    value = terms[-1] * u + terms[-2]
    for term in terms[-3::-1]:
        value = value * u + term
    return value


def unit_waves(counts, period):
    half = period // 2
    centred = ((counts + half) & (period - 1)) - half
    t = centred.astype(jnp.float32) * (1.0 / period)
    u = t * t
    return horner(COS, u), -(t * horner(SIN, u))


def iota(shape, axis):
    return lax.broadcasted_iota(jnp.int32, shape, axis)


def pick_coef(table, wave):
    chosen = jnp.where(iota(table.shape, 1) == wave, table, 0.0)
    return jnp.sum(chosen, axis=1, keepdims=True)


def column_freq(info_ref, pair):
    wave = info_ref[pair, WAVE_ROW : WAVE_ROW + 1, :].astype(jnp.int32)
    angle = info_ref[pair, ANGLE_ROW : ANGLE_ROW + 1, :].astype(jnp.int32)
    return (iota((1, FOCAL), 1) - FOCAL // 2 + SHIFT * angle) * (BLOCK + wave)


def fill_base(freq, shift, period, base_ref, centre_ref):
    low_r, low_i = unit_waves(iota((GRAIN, 1), 0) * freq, period)
    steps = BLOCK // GRAIN
    high_r, high_i = unit_waves((iota((steps, 1), 0) * GRAIN - BLOCK // 2 + shift) * freq, period)
    for step in range(steps):
        one_r, one_i = high_r[step : step + 1], high_i[step : step + 1]
        rows = slice(step * GRAIN, (step + 1) * GRAIN)
        base_ref[0, rows, :] = one_r * low_r - one_i * low_i
        base_ref[1, rows, :] = one_r * low_i + one_i * low_r
    count = centre_ref.shape[1]
    cent_r, cent_i = unit_waves((iota((count, 1), 0) * BLOCK + BLOCK // 2) * freq, period)
    centre_ref[0] = cent_r
    centre_ref[1] = cent_i


def block_pair(base_ref, centre_ref, index):
    cent_r = centre_ref[0, index : index + 1, :]
    cent_i = centre_ref[1, index : index + 1, :]
    base_r, base_i = base_ref[0], base_ref[1]
    rr, ii = base_r * cent_r, base_i * cent_i
    ri, ir = base_r * cent_i, base_i * cent_r
    before = ((rr + ii).astype(jnp.bfloat16), (ir - ri).astype(jnp.bfloat16))
    after = ((rr - ii).astype(jnp.bfloat16), (ir + ri).astype(jnp.bfloat16))
    return before, after


def near_fields(s, info_ref, pairs):
    def coef(pair, row):
        return info_ref[pair, row : row + 1, :]

    outs = [[coef(p, k) + coef(p, k + 1) * s for k in (0, TERMS)] for p in range(pairs)]
    twice = s + s
    before, current = jnp.ones_like(s), s
    for order in range(2, TERMS):
        before, current = current, twice * current - before
        for pair, out in enumerate(outs):
            out[0] = out[0] + coef(pair, order) * current
            out[1] = out[1] + coef(pair, TERMS + order) * current
    return outs


def near_slopes(s, scale, info_ref, pairs):
    def coef(pair, row):
        return info_ref[pair, row : row + 1, :] * (scale * (row % TERMS))

    twice = s + s
    before, current = jnp.ones_like(s), twice
    outs = [[coef(p, k) + coef(p, k + 1) * twice for k in (1, TERMS + 1)] for p in range(pairs)]
    for order in range(3, TERMS):
        before, current = current, twice * current - before
        for pair, out in enumerate(outs):
            out[0] = out[0] + coef(pair, order) * current
            out[1] = out[1] + coef(pair, TERMS + order) * current
    return outs


def forward_kernel(
    wave_hbm, angle_hbm, aim_hbm, coef_hbm, width_hbm, mine_ref, info_ref, own_ref,
    wave_ref, angle_ref, aim_ref, coef_ref, width_ref, base_ref, centre_ref, acc_ref, sems,
):
    rows_dev, cols = width_ref.shape
    pairs = wave_ref.shape[0]
    period = 256 * cols
    moves = [
        pltpu.make_async_copy(source, target, sems.at[index])
        for index, (source, target) in enumerate((
            (wave_hbm, wave_ref), (angle_hbm, angle_ref), (aim_hbm, aim_ref),
            (coef_hbm, coef_ref), (width_hbm, width_ref),
        ))
    ]
    for move in moves:
        move.start()
    for move in moves[:4]:
        move.wait()
    for pair in range(pairs):
        coef = pick_coef(coef_ref[...], wave_ref[pair])
        info_ref[pair, :WAVE_ROW, :] = jnp.broadcast_to(coef, (WAVE_ROW, FOCAL))
        row = iota((INFO_ROWS - WAVE_ROW, FOCAL), 0) + WAVE_ROW
        ids = jnp.where(row == WAVE_ROW, wave_ref[pair], 0)
        ids = jnp.where(row == ANGLE_ROW, angle_ref[pair], ids)
        ids = jnp.where(row == AIM_ROW, aim_ref[pair, 0], ids)
        ids = jnp.where(row == AIM_ROW + 1, aim_ref[pair, 1], ids)
        info_ref[pair, WAVE_ROW:, :] = ids.astype(jnp.float32)
    for pair in range(pairs):
        fill_base(column_freq(info_ref, pair), 0, period, base_ref.at[pair], centre_ref.at[pair])
    acc_ref[...] = jnp.zeros_like(acc_ref)
    moves[4].wait()
    for index in range(cols // (2 * BLOCK)):
        left = cols // 2 - (index + 1) * BLOCK
        right = cols // 2 + index * BLOCK
        nears = []
        for start in (left, right):
            outs = near_fields(width_ref[:, start : start + BLOCK], info_ref, pairs)
            nears.append([jnp.concatenate(out, axis=0).astype(jnp.bfloat16) for out in outs])
        for pair in range(pairs):
            before, after = block_pair(base_ref.at[pair], centre_ref.at[pair], index)
            near = jnp.concatenate([nears[0][pair], nears[1][pair]], axis=1)
            for part in range(2):
                table = jnp.concatenate([before[part], after[part]], axis=0)
                acc_ref[pair, part] += jnp.dot(near, table, preferred_element_type=jnp.float32)
    own_cols = own_ref.shape[1]
    first = pl.multiple_of(lax.axis_index("wave") * own_cols, own_cols)
    own_ref[...] = width_ref[:, pl.ds(first, own_cols)]
    for pair in range(pairs):
        real = acc_ref[pair, 0, :rows_dev] - acc_ref[pair, 1, rows_dev:]
        imag = acc_ref[pair, 1, :rows_dev] + acc_ref[pair, 0, rows_dev:]
        for part, value in enumerate((real, imag)):
            lane = (2 * pair + part) * FOCAL
            mine_ref[:, lane : lane + FOCAL] = value.astype(jnp.bfloat16)


def row_kernel(info_ref, after_ref, tall_ref, flat_ref):
    del after_ref
    pairs, _, rows = tall_ref.shape
    rows_dev = flat_ref.shape[1]
    period = 256 * rows
    size = min(rows, FOCAL)
    for pair in range(pairs):
        wave = info_ref[pair, WAVE_ROW : WAVE_ROW + 1, :].astype(jnp.int32) + BLOCK
        focal = (iota((FOCAL, 1), 0) - FOCAL // 2) * wave

        def step(index, carry):
            start = pl.multiple_of(index * size, size)
            place = iota((1, size), 1) + (start - rows // 2)
            real, imag = unit_waves(focal[:, :size] * place, period)
            tall_ref[pair, :FOCAL, pl.ds(start, size)] = real.astype(jnp.bfloat16)
            tall_ref[pair, FOCAL:, pl.ds(start, size)] = imag.astype(jnp.bfloat16)
            return carry

        if rows == size:
            step(0, 0)
        else:
            lax.fori_loop(0, rows // size, step, 0)
        focal = (iota((1, FOCAL), 1) - FOCAL // 2) * wave
        first = lax.axis_index("aperture") * rows_dev - rows // 2
        real, imag = unit_waves((iota((rows_dev, 1), 0) + first) * focal, period)
        flat_ref[pair, :, :FOCAL] = real.astype(jnp.bfloat16)
        flat_ref[pair, :, FOCAL:] = imag.astype(jnp.bfloat16)


def spot_map(info_ref, pair):
    aims = [info_ref[pair, row : row + 1, :] for row in (AIM_ROW, AIM_ROW + 1)]
    rows_off = iota((FOCAL, FOCAL), 0).astype(jnp.float32) - aims[0]
    cols_off = iota((1, FOCAL), 1).astype(jnp.float32) - aims[1]
    return jnp.exp(-(rows_off * rows_off + cols_off * cols_off) / (2.0 * SPOT * SPOT))


def join_kernel(*refs):
    *in_refs, out_ref = refs
    count = in_refs[0].shape[0]
    for index, ref in enumerate(in_refs):
        out_ref[index * count : (index + 1) * count, :] = ref[...]


def total_of(value):
    return jnp.sum(jnp.sum(value, axis=0, keepdims=True), axis=1, keepdims=True)


def focus_kernel(steps, info_ref, tall_ref, flat_ref, after_ref, *refs):
    del after_ref
    *sect_refs, back_ref, score_ref, rows_ref = refs
    pairs = tall_ref.shape[0]
    rows_dev = back_ref.shape[0]
    if steps is None:
        rows_ref = sect_refs[0]
    else:
        me = lax.axis_index("aperture")
        blocks = [
            ref[index * rows_dev : (index + 1) * rows_dev, :]
            for ref in sect_refs
            for index in range(ref.shape[0] // rows_dev)
        ]
        for step, block in zip(steps, blocks, strict=True):
            start = pl.multiple_of((me ^ step) * rows_dev, rows_dev)
            rows_ref[pl.ds(start, rows_dev), :] = block
    for pair in range(pairs):
        lane = 2 * pair * FOCAL
        section = rows_ref[:, lane : lane + 2 * FOCAL]
        mixed = jnp.dot(tall_ref[pair], section, preferred_element_type=jnp.float32)
        real = mixed[:FOCAL, :FOCAL] - mixed[FOCAL:, FOCAL:]
        imag = mixed[:FOCAL, FOCAL:] + mixed[FOCAL:, :FOCAL]
        power = real * real + imag * imag
        spot = spot_map(info_ref, pair)
        spot_power = total_of(spot * power)
        all_power = total_of(power) + 1e-06
        ratio = spot_power / all_power
        factor = FOCAL * FOCAL / total_of(spot)
        score_ref[pair] = jnp.sum(ratio * factor)
        weight = (factor * 2.0 / all_power) * (spot - ratio)
        real = (weight * real).astype(jnp.bfloat16)
        imag = (weight * imag).astype(jnp.bfloat16)
        stack = jnp.concatenate(
            [jnp.concatenate([real, imag], axis=1), jnp.concatenate([imag, -real], axis=1)], axis=0
        )
        back = jnp.dot(flat_ref[pair], stack, preferred_element_type=jnp.float32)
        back_ref[:, lane : lane + 2 * FOCAL] = back.astype(jnp.bfloat16)


def table_kernel(scale, cols, info_ref, width_ref, after_ref, *refs):
    del after_ref
    *out_refs, base_ref, centre_ref, turned_ref = refs
    pairs = base_ref.shape[0]
    table_refs, slope_refs = out_refs[:pairs], out_refs[pairs:]
    own_cols = width_ref.shape[1]
    period = 256 * cols
    middle = own_cols // 2
    shift = lax.axis_index("wave") * own_cols + middle - cols // 2
    for pair in range(pairs):
        freq = column_freq(info_ref, pair)
        fill_base(freq, shift, period, base_ref.at[pair], centre_ref.at[pair])
        for part in range(2):
            turned_ref[pair, part] = base_ref[pair, part].T
    centres = [[centre_ref[pair, part].T for part in range(2)] for pair in range(pairs)]
    for index in range(own_cols // (2 * BLOCK)):
        left = middle - (index + 1) * BLOCK
        right = middle + index * BLOCK
        for pair in range(pairs):
            cent_r, cent_i = (centre[:, index : index + 1] for centre in centres[pair])
            base_r, base_i = turned_ref[pair, 0], turned_ref[pair, 1]
            rr, ii = base_r * cent_r, base_i * cent_i
            ri, ir = base_r * cent_i, base_i * cent_r
            for start, values in ((left, (rr + ii, ir - ri)), (right, (rr - ii, ir + ri))):
                for part, value in enumerate(values):
                    row = part * FOCAL
                    table_refs[pair][row : row + FOCAL, start : start + BLOCK] = value.astype(jnp.bfloat16)
        for start in (left, right):
            slopes = near_slopes(width_ref[:, start : start + BLOCK], scale, info_ref, pairs)
            for pair in range(pairs):
                slope_refs[pair][0, :, start : start + BLOCK] = slopes[pair][0]
                slope_refs[pair][1, :, start : start + BLOCK] = slopes[pair][1]


def grad_kernel(pairs, back_ref, *refs):
    *in_refs, out_ref = refs
    table_refs, slope_refs, total_ref = in_refs[:pairs], in_refs[pairs : 2 * pairs], in_refs[2 * pairs :]
    rows_dev, own_cols = out_ref.shape
    lefts = []
    for pair in range(pairs):
        lane = 2 * pair * FOCAL
        real, imag = back_ref[:, lane : lane + FOCAL], back_ref[:, lane + FOCAL : lane + 2 * FOCAL]
        lefts.append(
            jnp.concatenate(
                [jnp.concatenate([real, imag], axis=1), jnp.concatenate([imag, -real], axis=1)], axis=0
            )
        )
    size = 2 * BLOCK
    for start in range(0, own_cols, size):
        place = slice(start, start + size)
        total = total_ref[0][:, place] if total_ref else jnp.zeros((rows_dev, size), jnp.float32)
        for pair in range(pairs):
            grad = jnp.dot(lefts[pair], table_refs[pair][:, place], preferred_element_type=jnp.float32)
            total += grad[:rows_dev] * slope_refs[pair][0, :, place]
            total += grad[rows_dev:] * slope_refs[pair][1, :, place]
        out_ref[:, place] = total


VMEM = pl.BlockSpec(memory_space=pltpu.VMEM)
SMEM = pl.BlockSpec(memory_space=pltpu.SMEM)
ANY = pl.BlockSpec(memory_space=pl.ANY)
HBM = pl.BlockSpec(memory_space=pltpu.HBM)


def call(kernel, name, outs, in_specs, out_specs, scratch, flops, moved):
    return pl.pallas_call(
        kernel,
        name=name,
        out_shape=outs,
        in_specs=in_specs,
        out_specs=out_specs,
        scratch_shapes=scratch,
        cost_estimate=pl.CostEstimate(flops=flops, bytes_accessed=moved, transcendentals=0),
        compiler_params=pltpu.CompilerParams(vmem_limit_bytes=VMEM_LIMIT),
    )


def on_device(widths, coef_table, wave_ids, angle_ids, targets):
    rows_dev, cols = widths.shape
    pairs_dev = wave_ids.shape[0]
    peers = lax.axis_size("aperture")
    copies = lax.axis_size("wave")
    rows = rows_dev * peers
    own_cols = cols // copies
    lanes = 2 * pairs_dev * FOCAL
    f32, bf16 = jnp.float32, jnp.bfloat16
    shape = jax.ShapeDtypeStruct

    def in_hbm(value):
        return pltpu.with_memory_space_constraint(value, pltpu.HBM)

    def exchange(value, step):
        return lax.ppermute(value, "aperture", [(index, index ^ step) for index in range(peers)])

    def to_core(value):
        return lax.ppermute(value, "wave", [(index, (index + 1) % copies) for index in range(copies)])

    mine, info, own = call(
        forward_kernel, "forward",
        (
            shape((rows_dev, lanes), bf16),
            shape((pairs_dev, INFO_ROWS, FOCAL), f32), shape((rows_dev, own_cols), f32),
        ),
        [HBM] * 5, (VMEM,) * 3,
        [
            pltpu.SMEM(wave_ids.shape, jnp.int32),
            pltpu.SMEM(angle_ids.shape, jnp.int32),
            pltpu.SMEM(targets.shape, jnp.int32),
            pltpu.VMEM(coef_table.shape[::-1], f32),
            pltpu.VMEM(widths.shape, f32),
            pltpu.VMEM((pairs_dev, 2, BLOCK, FOCAL), f32),
            pltpu.VMEM((pairs_dev, 2, cols // (2 * BLOCK), FOCAL), f32),
            pltpu.VMEM((pairs_dev, 2, 2 * rows_dev, FOCAL), f32),
            pltpu.SemaphoreType.DMA((5,)),
        ],
        10**9, 10**7,
    )(*(in_hbm(value) for value in (wave_ids, angle_ids, targets, coef_table.T, widths)))
    far_info = to_core(info)

    def column_tables(info, after, name):
        outs = [shape((2 * FOCAL, own_cols), bf16)] * pairs_dev
        outs += [shape((2, rows_dev, own_cols), f32)] * pairs_dev
        got = call(
            functools.partial(table_kernel, math.sqrt(rows * cols), cols), name,
            outs, [VMEM, VMEM, ANY], [VMEM] * len(outs),
            [
                pltpu.VMEM((pairs_dev, 2, BLOCK, FOCAL), f32),
                pltpu.VMEM((pairs_dev, 2, own_cols // (2 * BLOCK), FOCAL), f32),
                pltpu.VMEM((pairs_dev, 2, FOCAL, BLOCK), f32),
            ],
            10**9, 10**7,
        )(info, own, after)
        return list(got[:pairs_dev]), list(got[pairs_dev:])

    tables, slopes = column_tables(info, mine, "own_tables")
    if peers <= DIRECT:
        steps = list(range(peers - 2, 0, -2))
        got = [exchange(mine, step) for step in steps]
        near = exchange(mine, 1)
        *got, slopes[0] = lax.optimization_barrier((*got, slopes[0]))
        first = got[0]
        joined = call(join_kernel, "join", shape(((len(steps) - 1) * rows_dev, lanes), bf16),
                      [VMEM] * (len(steps) - 1), VMEM, [], 10**6, 10**6)(*got[1:])
        sections = [mine, near, first, joined, exchange(first, 1), exchange(joined, 1)]
        steps = [0, 1, *steps, *(step ^ 1 for step in steps)]
        after = joined
    else:
        blocks = jnp.tile(mine[None], (peers, 1, 1))
        blocks = lax.all_to_all(blocks, "aperture", 0, 0, tiled=True)
        sections, steps, after = [blocks.reshape(rows, lanes)], None, mine
    tall, flat = call(
        row_kernel, "row_tables",
        (shape((pairs_dev, 2 * FOCAL, rows), bf16), shape((pairs_dev, rows_dev, 2 * FOCAL), bf16)),
        [VMEM, ANY], (VMEM, VMEM), [], 10**8, 10**6,
    )(info, after)
    far_tables, far_slopes = column_tables(far_info, flat, "far_tables")

    back, scores = call(
        functools.partial(focus_kernel, steps), "focus",
        (shape((rows_dev, lanes), bf16), shape((pairs_dev,), f32)),
        [VMEM, VMEM, VMEM, ANY] + [VMEM] * len(sections), (VMEM, SMEM), [pltpu.VMEM((rows, lanes), bf16)],
        10**8, 10**6,
    )(info, tall, flat, far_slopes[0], *sections)

    def add_grad(back, tables, slopes, name, *total):
        ins = [back, *tables, *slopes, *total]
        return call(
            functools.partial(grad_kernel, pairs_dev), name,
            shape((rows_dev, own_cols), f32), [VMEM] * len(ins), VMEM, [], 10**9, 10**7,
        )(*ins)

    far_back = to_core(back)
    grad = add_grad(back, tables, slopes, "gradient_own")
    grad = add_grad(far_back, far_tables, far_slopes, "gradient_far", grad)
    return grad, scores


def solution(mesh):
    in_specs = (
        P(("group", "aperture"), None),
        P(),
        P(("group", "wave")),
        P(("group", "wave")),
        P(("group", "wave"), None),
    )
    out_specs = (P(("group", "aperture"), "wave"), P(("group", "wave")))
    return jax.shard_map(
        on_device, mesh=mesh, in_specs=in_specs, out_specs=out_specs, check_vma=False
    )
```

```python
import functools
import math

import jax
import jax.numpy as jnp
from jax import lax
from jax.experimental import pallas as pl
from jax.experimental.pallas import tpu as pltpu
from jax.sharding import PartitionSpec as P

FOCAL = 256
SPOT = 4
SHIFT = 32
TERMS = 8
BLOCK = 256
GRAIN = 16
VMEM_LIMIT = 16 * 1024 * 1024
WAVE_ROW, ANGLE_ROW, AIM_ROW, INFO_ROWS = 16, 17, 18, 24
DIRECT = 16

COS = (
    1.0, -19.7392088015709, 64.93939395773512, -85.45681453397417, 60.24458621302471,
    -26.425616460281425, 7.8991596631575085, -1.6968741456712442, 0.2437618617467591,
)
SIN = (
    6.2831853071792665, -41.34170224019464, 81.60524925425943, -76.70585885700535,
    42.05867547580699, -15.094428387947755, 3.818490079304055, -0.7122771247541972,
    0.09149844789363434,
)


def horner(terms, u):
    value = terms[-1] * u + terms[-2]
    for term in terms[-3::-1]:
        value = value * u + term
    return value


def unit_waves(counts, period):
    half = period // 2
    centred = ((counts + half) & (period - 1)) - half
    t = centred.astype(jnp.float32) * (1.0 / period)
    u = t * t
    return horner(COS, u), -(t * horner(SIN, u))


def iota(shape, axis):
    return lax.broadcasted_iota(jnp.int32, shape, axis)


def pick_coef(table, wave):
    chosen = jnp.where(iota(table.shape, 1) == wave, table, 0.0)
    return jnp.sum(chosen, axis=1, keepdims=True)


def column_freq(info_ref, pair):
    wave = info_ref[pair, WAVE_ROW : WAVE_ROW + 1, :].astype(jnp.int32)
    angle = info_ref[pair, ANGLE_ROW : ANGLE_ROW + 1, :].astype(jnp.int32)
    return (iota((1, FOCAL), 1) - FOCAL // 2 + SHIFT * angle) * (BLOCK + wave)


def fill_base(freq, shift, period, base_ref, centre_ref):
    low_r, low_i = unit_waves(iota((GRAIN, 1), 0) * freq, period)
    steps = BLOCK // GRAIN
    high_r, high_i = unit_waves((iota((steps, 1), 0) * GRAIN - BLOCK // 2 + shift) * freq, period)
    for step in range(steps):
        one_r, one_i = high_r[step : step + 1], high_i[step : step + 1]
        rows = slice(step * GRAIN, (step + 1) * GRAIN)
        base_ref[0, rows, :] = one_r * low_r - one_i * low_i
        base_ref[1, rows, :] = one_r * low_i + one_i * low_r
    count = centre_ref.shape[1]
    cent_r, cent_i = unit_waves((iota((count, 1), 0) * BLOCK + BLOCK // 2) * freq, period)
    centre_ref[0] = cent_r
    centre_ref[1] = cent_i


def block_pair(base_ref, centre_ref, index):
    cent_r = centre_ref[0, index : index + 1, :]
    cent_i = centre_ref[1, index : index + 1, :]
    base_r, base_i = base_ref[0], base_ref[1]
    rr, ii = base_r * cent_r, base_i * cent_i
    ri, ir = base_r * cent_i, base_i * cent_r
    before = ((rr + ii).astype(jnp.bfloat16), (ir - ri).astype(jnp.bfloat16))
    after = ((rr - ii).astype(jnp.bfloat16), (ir + ri).astype(jnp.bfloat16))
    return before, after


def near_fields(s, info_ref, pairs):
    def coef(pair, row):
        return info_ref[pair, row : row + 1, :]

    outs = [[coef(p, k) + coef(p, k + 1) * s for k in (0, TERMS)] for p in range(pairs)]
    twice = s + s
    before, current = jnp.ones_like(s), s
    for order in range(2, TERMS):
        before, current = current, twice * current - before
        for pair, out in enumerate(outs):
            out[0] = out[0] + coef(pair, order) * current
            out[1] = out[1] + coef(pair, TERMS + order) * current
    return outs


def near_slopes(s, scale, info_ref, pairs):
    def coef(pair, row):
        return info_ref[pair, row : row + 1, :] * (scale * (row % TERMS))

    twice = s + s
    before, current = jnp.ones_like(s), twice
    outs = [[coef(p, k) + coef(p, k + 1) * twice for k in (1, TERMS + 1)] for p in range(pairs)]
    for order in range(3, TERMS):
        before, current = current, twice * current - before
        for pair, out in enumerate(outs):
            out[0] = out[0] + coef(pair, order) * current
            out[1] = out[1] + coef(pair, TERMS + order) * current
    return outs


def forward_kernel(
    wave_hbm, angle_hbm, aim_hbm, coef_hbm, width_hbm, mine_ref, info_ref, own_ref,
    wave_ref, angle_ref, aim_ref, coef_ref, width_ref, base_ref, centre_ref, acc_ref, sems,
):
    rows_dev, cols = width_ref.shape
    pairs = wave_ref.shape[0]
    period = 256 * cols
    moves = [
        pltpu.make_async_copy(source, target, sems.at[index])
        for index, (source, target) in enumerate((
            (wave_hbm, wave_ref), (angle_hbm, angle_ref), (aim_hbm, aim_ref),
            (coef_hbm, coef_ref), (width_hbm, width_ref),
        ))
    ]
    for move in moves:
        move.start()
    for move in moves[:4]:
        move.wait()
    for pair in range(pairs):
        coef = pick_coef(coef_ref[...], wave_ref[pair])
        info_ref[pair, :WAVE_ROW, :] = jnp.broadcast_to(coef, (WAVE_ROW, FOCAL))
        row = iota((INFO_ROWS - WAVE_ROW, FOCAL), 0) + WAVE_ROW
        ids = jnp.where(row == WAVE_ROW, wave_ref[pair], 0)
        ids = jnp.where(row == ANGLE_ROW, angle_ref[pair], ids)
        ids = jnp.where(row == AIM_ROW, aim_ref[pair, 0], ids)
        ids = jnp.where(row == AIM_ROW + 1, aim_ref[pair, 1], ids)
        info_ref[pair, WAVE_ROW:, :] = ids.astype(jnp.float32)
    for pair in range(pairs):
        fill_base(column_freq(info_ref, pair), 0, period, base_ref.at[pair], centre_ref.at[pair])
    acc_ref[...] = jnp.zeros_like(acc_ref)
    moves[4].wait()
    for index in range(cols // (2 * BLOCK)):
        left = cols // 2 - (index + 1) * BLOCK
        right = cols // 2 + index * BLOCK
        nears = []
        for start in (left, right):
            outs = near_fields(width_ref[:, start : start + BLOCK], info_ref, pairs)
            nears.append([jnp.concatenate(out, axis=0).astype(jnp.bfloat16) for out in outs])
        for pair in range(pairs):
            before, after = block_pair(base_ref.at[pair], centre_ref.at[pair], index)
            near = jnp.concatenate([nears[0][pair], nears[1][pair]], axis=1)
            for part in range(2):
                table = jnp.concatenate([before[part], after[part]], axis=0)
                acc_ref[pair, part] += jnp.dot(near, table, preferred_element_type=jnp.float32)
    own_cols = own_ref.shape[1]
    first = pl.multiple_of(lax.axis_index("wave") * own_cols, own_cols)
    own_ref[...] = width_ref[:, pl.ds(first, own_cols)]
    for pair in range(pairs):
        real = acc_ref[pair, 0, :rows_dev] - acc_ref[pair, 1, rows_dev:]
        imag = acc_ref[pair, 1, :rows_dev] + acc_ref[pair, 0, rows_dev:]
        for part, value in enumerate((real, imag)):
            lane = (2 * pair + part) * FOCAL
            mine_ref[:, lane : lane + FOCAL] = value.astype(jnp.bfloat16)


def spot_map(info_ref, pair):
    aims = [info_ref[pair, row : row + 1, :] for row in (AIM_ROW, AIM_ROW + 1)]
    rows_off = iota((FOCAL, FOCAL), 0).astype(jnp.float32) - aims[0]
    cols_off = iota((1, FOCAL), 1).astype(jnp.float32) - aims[1]
    return jnp.exp(-(rows_off * rows_off + cols_off * cols_off) / (2.0 * SPOT * SPOT))


def total_of(value):
    return jnp.sum(jnp.sum(value, axis=0, keepdims=True), axis=1, keepdims=True)


def row_kernel(info_ref, tall_ref, flat_ref, spot_ref, gain_ref):
    pairs, _, rows = tall_ref.shape
    rows_dev = flat_ref.shape[1]
    period = 256 * rows
    size = min(rows, FOCAL)
    for pair in range(pairs):
        wave = info_ref[pair, WAVE_ROW : WAVE_ROW + 1, :].astype(jnp.int32) + BLOCK
        focal = (iota((FOCAL, 1), 0) - FOCAL // 2) * wave

        def step(index, carry):
            start = pl.multiple_of(index * size, size)
            place = iota((1, size), 1) + (start - rows // 2)
            real, imag = unit_waves(focal[:, :size] * place, period)
            tall_ref[pair, :FOCAL, pl.ds(start, size)] = real.astype(jnp.bfloat16)
            tall_ref[pair, FOCAL:, pl.ds(start, size)] = imag.astype(jnp.bfloat16)
            return carry

        if rows == size:
            step(0, 0)
        else:
            lax.fori_loop(0, rows // size, step, 0)
        focal = (iota((1, FOCAL), 1) - FOCAL // 2) * wave
        first = lax.axis_index("aperture") * rows_dev - rows // 2
        real, imag = unit_waves((iota((rows_dev, 1), 0) + first) * focal, period)
        flat_ref[pair, :, :FOCAL] = real.astype(jnp.bfloat16)
        flat_ref[pair, :, FOCAL:] = imag.astype(jnp.bfloat16)
        spot = spot_map(info_ref, pair)
        spot_ref[pair] = spot
        gain_ref[pair] = jnp.broadcast_to(FOCAL * FOCAL / total_of(spot), gain_ref.shape[1:])


def join_kernel(*refs):
    *in_refs, out_ref = refs
    count = in_refs[0].shape[0]
    for index, ref in enumerate(in_refs):
        out_ref[index * count : (index + 1) * count, :] = ref[...]


def focus_kernel(steps, tall_ref, flat_ref, spot_ref, gain_ref, after_ref, *refs):
    del after_ref
    *sect_refs, back_ref, score_ref, rows_ref = refs
    pairs = tall_ref.shape[0]
    rows_dev = back_ref.shape[0]
    if steps is None:
        rows_ref = sect_refs[0]
    else:
        me = lax.axis_index("aperture")
        blocks = [
            ref[index * rows_dev : (index + 1) * rows_dev, :]
            for ref in sect_refs
            for index in range(ref.shape[0] // rows_dev)
        ]
        for step, block in zip(steps, blocks, strict=True):
            start = pl.multiple_of((me ^ step) * rows_dev, rows_dev)
            rows_ref[pl.ds(start, rows_dev), :] = block
    fields, sums = [], []
    for pair in range(pairs):
        lane = 2 * pair * FOCAL
        section = rows_ref[:, lane : lane + 2 * FOCAL]
        mixed = jnp.dot(tall_ref[pair], section, preferred_element_type=jnp.float32)
        real = mixed[:FOCAL, :FOCAL] - mixed[FOCAL:, FOCAL:]
        imag = mixed[:FOCAL, FOCAL:] + mixed[FOCAL:, :FOCAL]
        power = real * real + imag * imag
        fields.append((real, imag))
        sums.append((total_of(spot_ref[pair] * power), total_of(power) + 1e-06))
    for pair, ((real, imag), (spot_power, all_power)) in enumerate(zip(fields, sums)):
        ratio = spot_power / all_power
        gain = gain_ref[pair, :1, :1]
        score_ref[pair] = jnp.sum(ratio * gain)
        weight = (gain * 2.0 / all_power) * (spot_ref[pair] - ratio)
        real = (weight * real).astype(jnp.bfloat16)
        imag = (weight * imag).astype(jnp.bfloat16)
        stack = jnp.concatenate(
            [jnp.concatenate([real, imag], axis=1), jnp.concatenate([imag, -real], axis=1)], axis=0
        )
        back = jnp.dot(flat_ref[pair], stack, preferred_element_type=jnp.float32)
        lane = 2 * pair * FOCAL
        back_ref[:, lane : lane + 2 * FOCAL] = back.astype(jnp.bfloat16)


def table_kernel(scale, cols, info_ref, width_ref, *refs):
    *out_refs, base_ref, centre_ref, turned_ref = refs
    pairs = base_ref.shape[0]
    out_refs = out_refs[-2 * pairs :]
    table_refs, slope_refs = out_refs[:pairs], out_refs[pairs:]
    own_cols = width_ref.shape[1]
    period = 256 * cols
    middle = own_cols // 2
    shift = lax.axis_index("wave") * own_cols + middle - cols // 2
    for pair in range(pairs):
        freq = column_freq(info_ref, pair)
        fill_base(freq, shift, period, base_ref.at[pair], centre_ref.at[pair])
        for part in range(2):
            turned_ref[pair, part] = base_ref[pair, part].T
    centres = [[centre_ref[pair, part].T for part in range(2)] for pair in range(pairs)]
    for index in range(own_cols // (2 * BLOCK)):
        left = middle - (index + 1) * BLOCK
        right = middle + index * BLOCK
        for pair in range(pairs):
            cent_r, cent_i = (centre[:, index : index + 1] for centre in centres[pair])
            base_r, base_i = turned_ref[pair, 0], turned_ref[pair, 1]
            rr, ii = base_r * cent_r, base_i * cent_i
            ri, ir = base_r * cent_i, base_i * cent_r
            for start, values in ((left, (rr + ii, ir - ri)), (right, (rr - ii, ir + ri))):
                for part, value in enumerate(values):
                    row = part * FOCAL
                    table_refs[pair][row : row + FOCAL, start : start + BLOCK] = value.astype(jnp.bfloat16)
        for start in (left, right):
            slopes = near_slopes(width_ref[:, start : start + BLOCK], scale, info_ref, pairs)
            for pair in range(pairs):
                slope_refs[pair][0, :, start : start + BLOCK] = slopes[pair][0]
                slope_refs[pair][1, :, start : start + BLOCK] = slopes[pair][1]


def last_grad_kernel(pairs, *refs):
    *in_refs, out_hbm, out_ref, sems = refs
    size = 2 * BLOCK
    moves = []

    def send(start):
        place = slice(start, start + size)
        index = start // size
        moves.append(pltpu.make_async_copy(out_ref.at[:, place], out_hbm.at[:, place], sems.at[index]))
        moves[-1].start()

    grad_kernel(pairs, *in_refs, out_ref, send=send)
    for move in moves:
        move.wait()


def grad_kernel(pairs, back_ref, *refs, send=None):
    *in_refs, out_ref = refs
    table_refs, slope_refs, total_ref = in_refs[:pairs], in_refs[pairs : 2 * pairs], in_refs[2 * pairs :]
    rows_dev, own_cols = out_ref.shape
    lefts = []
    for pair in range(pairs):
        lane = 2 * pair * FOCAL
        real, imag = back_ref[:, lane : lane + FOCAL], back_ref[:, lane + FOCAL : lane + 2 * FOCAL]
        lefts.append(
            jnp.concatenate(
                [jnp.concatenate([real, imag], axis=1), jnp.concatenate([imag, -real], axis=1)], axis=0
            )
        )
    size = 2 * BLOCK
    for start in range(0, own_cols, size):
        place = slice(start, start + size)
        total = total_ref[0][:, place] if total_ref else jnp.zeros((rows_dev, size), jnp.float32)
        for pair in range(pairs):
            grad = jnp.dot(lefts[pair], table_refs[pair][:, place], preferred_element_type=jnp.float32)
            total += grad[:rows_dev] * slope_refs[pair][0, :, place]
            total += grad[rows_dev:] * slope_refs[pair][1, :, place]
        out_ref[:, place] = total
        if send is not None:
            send(start)


VMEM = pl.BlockSpec(memory_space=pltpu.VMEM)
SMEM = pl.BlockSpec(memory_space=pltpu.SMEM)
ANY = pl.BlockSpec(memory_space=pl.ANY)
HBM = pl.BlockSpec(memory_space=pltpu.HBM)


def call(kernel, name, outs, in_specs, out_specs, scratch, flops, moved):
    return pl.pallas_call(
        kernel,
        name=name,
        out_shape=outs,
        in_specs=in_specs,
        out_specs=out_specs,
        scratch_shapes=scratch,
        cost_estimate=pl.CostEstimate(flops=flops, bytes_accessed=moved, transcendentals=0),
        compiler_params=pltpu.CompilerParams(vmem_limit_bytes=VMEM_LIMIT),
    )


def on_device(widths, coef_table, wave_ids, angle_ids, targets):
    rows_dev, cols = widths.shape
    pairs_dev = wave_ids.shape[0]
    peers = lax.axis_size("aperture")
    copies = lax.axis_size("wave")
    rows = rows_dev * peers
    own_cols = cols // copies
    lanes = 2 * pairs_dev * FOCAL
    f32, bf16 = jnp.float32, jnp.bfloat16
    shape = jax.ShapeDtypeStruct

    def in_hbm(value):
        return pltpu.with_memory_space_constraint(value, pltpu.HBM)

    def exchange(value, step):
        return lax.ppermute(value, "aperture", [(index, index ^ step) for index in range(peers)])

    def to_core(value):
        return lax.ppermute(value, "wave", [(index, (index + 1) % copies) for index in range(copies)])

    mine, info, own = call(
        forward_kernel, "forward",
        (
            shape((rows_dev, lanes), bf16),
            shape((pairs_dev, INFO_ROWS, FOCAL), f32), shape((rows_dev, own_cols), f32),
        ),
        [HBM] * 5, (VMEM,) * 3,
        [
            pltpu.SMEM(wave_ids.shape, jnp.int32),
            pltpu.SMEM(angle_ids.shape, jnp.int32),
            pltpu.SMEM(targets.shape, jnp.int32),
            pltpu.VMEM(coef_table.shape[::-1], f32),
            pltpu.VMEM(widths.shape, f32),
            pltpu.VMEM((pairs_dev, 2, BLOCK, FOCAL), f32),
            pltpu.VMEM((pairs_dev, 2, cols // (2 * BLOCK), FOCAL), f32),
            pltpu.VMEM((pairs_dev, 2, 2 * rows_dev, FOCAL), f32),
            pltpu.SemaphoreType.DMA((5,)),
        ],
        10**9, 10**7,
    )(*(in_hbm(value) for value in (wave_ids, angle_ids, targets, coef_table.T, widths)))
    far_info = to_core(info)

    def column_tables(info, name, *after):
        outs = [shape((2 * FOCAL, own_cols), bf16)] * pairs_dev
        outs += [shape((2, rows_dev, own_cols), f32)] * pairs_dev
        got = call(
            functools.partial(table_kernel, math.sqrt(rows * cols), cols), name,
            outs, [VMEM, VMEM] + [ANY] * len(after), [VMEM] * len(outs),
            [
                pltpu.VMEM((pairs_dev, 2, BLOCK, FOCAL), f32),
                pltpu.VMEM((pairs_dev, 2, own_cols // (2 * BLOCK), FOCAL), f32),
                pltpu.VMEM((pairs_dev, 2, FOCAL, BLOCK), f32),
            ],
            10**9, 10**7,
        )(info, own, *after)
        return list(got[:pairs_dev]), list(got[pairs_dev:])

    tall, flat, spots, gains = call(
        row_kernel, "row_tables",
        (
            shape((pairs_dev, 2 * FOCAL, rows), bf16), shape((pairs_dev, rows_dev, 2 * FOCAL), bf16),
            shape((pairs_dev, FOCAL, FOCAL), f32), shape((pairs_dev, 8, 128), f32),
        ),
        [VMEM], (VMEM,) * 4, [], 10**8, 10**6,
    )(info)
    if peers <= DIRECT:
        steps = list(range(peers - 2, 0, -2))
        got = [exchange(mine, step) for step in steps]
        near = exchange(mine, 1)
        first, flat = lax.optimization_barrier((got[0], flat))
        joined = call(join_kernel, "join", shape(((len(steps) - 1) * rows_dev, lanes), bf16),
                      [VMEM] * (len(steps) - 1), VMEM, [], 10**6, 10**6)(*got[1:])
        sections = [mine, near, first, joined, exchange(first, 1), exchange(joined, 1)]
        steps = [0, 1, *steps, *(step ^ 1 for step in steps)]
        after = [near, joined]
    else:
        blocks = jnp.tile(mine[None], (peers, 1, 1))
        blocks = lax.all_to_all(blocks, "aperture", 0, 0, tiled=True)
        sections, steps, after = [blocks.reshape(rows, lanes)], None, []
    tables, slopes = column_tables(info, "own_tables", *after)
    far_tables, far_slopes = column_tables(far_info, "far_tables", slopes[0])

    back, scores = call(
        functools.partial(focus_kernel, steps), "focus",
        (shape((rows_dev, lanes), bf16), shape((pairs_dev,), f32)),
        [VMEM] * 4 + [ANY] + [VMEM] * len(sections), (VMEM, SMEM), [pltpu.VMEM((rows, lanes), bf16)],
        10**8, 10**6,
    )(tall, flat, spots, gains, far_slopes[0], *sections)

    out = shape((rows_dev, own_cols), f32)
    ins = [back, *tables, *slopes]
    grad = call(
        functools.partial(grad_kernel, pairs_dev), "gradient_own",
        out, [VMEM] * len(ins), VMEM, [], 10**9, 10**7,
    )(*ins)
    ins = [to_core(back), *far_tables, *far_slopes, grad]
    grad = call(
        functools.partial(last_grad_kernel, pairs_dev), "gradient_far",
        out, [VMEM] * len(ins), HBM,
        [pltpu.VMEM(out.shape, f32), pltpu.SemaphoreType.DMA((own_cols // (2 * BLOCK),))], 10**9, 10**7,
    )(*ins)
    return grad, scores


def solution(mesh):
    in_specs = (
        P(("group", "aperture"), None),
        P(),
        P(("group", "wave")),
        P(("group", "wave")),
        P(("group", "wave"), None),
    )
    out_specs = (P(("group", "aperture"), "wave"), P(("group", "wave")))
    return jax.shard_map(
        on_device, mesh=mesh, in_specs=in_specs, out_specs=out_specs, check_vma=False
    )
```

```python
import functools
import math

import jax
import jax.numpy as jnp
from jax import lax
from jax.experimental import pallas as pl
from jax.experimental.pallas import tpu as pltpu
from jax.sharding import PartitionSpec as P

FOCAL = 256
SPOT = 4
SHIFT = 32
TERMS = 8
BLOCK = 256
GRAIN = 16
LANES = 128
VMEM_LIMIT = 16 * 1024 * 1024
WAVE_ROW, ANGLE_ROW, AIM_ROW, INFO_ROWS = 16, 17, 18, 24
DIRECT = 16

COS = (
    1.0, -19.7392088015709, 64.93939395773512, -85.45681453397417, 60.24458621302471,
    -26.425616460281425, 7.8991596631575085, -1.6968741456712442, 0.2437618617467591,
)
SIN = (
    6.2831853071792665, -41.34170224019464, 81.60524925425943, -76.70585885700535,
    42.05867547580699, -15.094428387947755, 3.818490079304055, -0.7122771247541972,
    0.09149844789363434,
)


def horner(terms, u):
    value = terms[-1] * u + terms[-2]
    for term in terms[-3::-1]:
        value = value * u + term
    return value


def unit_waves(counts, period):
    half = period // 2
    centred = ((counts + half) & (period - 1)) - half
    t = centred.astype(jnp.float32) * (1.0 / period)
    u = t * t
    return horner(COS, u), -(t * horner(SIN, u))


def iota(shape, axis):
    return lax.broadcasted_iota(jnp.int32, shape, axis)


def pick_coef(table, wave):
    chosen = jnp.where(iota(table.shape, 1) == wave, table, 0.0)
    return jnp.sum(chosen, axis=1, keepdims=True)


def column_freq(info_ref, pair):
    wave = info_ref[pair, WAVE_ROW : WAVE_ROW + 1, :].astype(jnp.int32)
    angle = info_ref[pair, ANGLE_ROW : ANGLE_ROW + 1, :].astype(jnp.int32)
    return (iota((1, FOCAL), 1) - FOCAL // 2 + SHIFT * angle) * (BLOCK + wave)


def fill_base(freq, shift, period, base_ref, centre_ref):
    low_r, low_i = unit_waves(iota((GRAIN, 1), 0) * freq, period)
    steps = BLOCK // GRAIN
    high_r, high_i = unit_waves((iota((steps, 1), 0) * GRAIN - BLOCK // 2 + shift) * freq, period)
    for step in range(steps):
        one_r, one_i = high_r[step : step + 1], high_i[step : step + 1]
        rows = slice(step * GRAIN, (step + 1) * GRAIN)
        base_ref[0, rows, :] = one_r * low_r - one_i * low_i
        base_ref[1, rows, :] = one_r * low_i + one_i * low_r
    count = centre_ref.shape[1]
    cent_r, cent_i = unit_waves((iota((count, 1), 0) * BLOCK + BLOCK // 2) * freq, period)
    centre_ref[0] = cent_r
    centre_ref[1] = cent_i


def near_fields(s, info_ref, pairs):
    def coef(pair, row):
        return info_ref[pair, row : row + 1, :]

    outs = [[coef(p, k) + coef(p, k + 1) * s for k in (0, TERMS)] for p in range(pairs)]
    twice = s + s
    before, current = jnp.ones_like(s), s
    for order in range(2, TERMS):
        before, current = current, twice * current - before
        for pair, out in enumerate(outs):
            out[0] = out[0] + coef(pair, order) * current
            out[1] = out[1] + coef(pair, TERMS + order) * current
    return outs


def near_slopes(s, scale, info_ref, pairs):
    def coef(pair, row):
        return info_ref[pair, row : row + 1, :] * (scale * (row % TERMS))

    twice = s + s
    before, current = jnp.ones_like(s), twice
    outs = [[coef(p, k) + coef(p, k + 1) * twice for k in (1, TERMS + 1)] for p in range(pairs)]
    for order in range(3, TERMS):
        before, current = current, twice * current - before
        for pair, out in enumerate(outs):
            out[0] = out[0] + coef(pair, order) * current
            out[1] = out[1] + coef(pair, TERMS + order) * current
    return outs


def turn_round(value):
    rows, cols = value.shape
    order = LANES - 1 - iota((rows, LANES), 1)
    parts = [
        jnp.take_along_axis(value[:, start : start + LANES], order, axis=1)
        for start in range(cols - LANES, -1, -LANES)
    ]
    return jnp.concatenate(parts, axis=1)


def write_tables(index, base_ref, centres, table_ref):
    middle = table_ref.shape[1] // 2
    cent_r, cent_i = (centre[:, index : index + 1] for centre in centres)
    base_r, base_i = base_ref[0], base_ref[1]
    rr, ii = base_r * cent_r, base_i * cent_i
    ri, ir = base_r * cent_i, base_i * cent_r
    left, right = middle - (index + 1) * BLOCK, middle + index * BLOCK
    tables = []
    for start, values in ((left, (rr + ii, ir - ri)), (right, (rr - ii, ir + ri))):
        table = jnp.concatenate(values, axis=0).astype(jnp.bfloat16)
        table_ref[:, start : start + BLOCK] = table
        tables.append(table)
    return tables


def turned_waves(info_ref, pair, cols, base_ref, centre_ref, turned_ref):
    shift = cols // 4 + 1 - lax.axis_index("wave")
    fill_base(column_freq(info_ref, pair), shift, 256 * cols, base_ref, centre_ref)
    for part in range(2):
        turned_ref[part] = base_ref[part].T
    return [centre_ref[part].T for part in range(2)]


def forward_kernel(
    wave_hbm, angle_hbm, aim_hbm, coef_hbm, width_hbm, mine_ref, info_ref, own_ref, *refs
):
    pairs = info_ref.shape[0]
    table_refs, refs = refs[:pairs], refs[pairs:]
    (
        wave_ref, angle_ref, aim_ref, coef_ref, width_ref, far_ref, base_ref, centre_ref, turned_ref, acc_ref, sems,
    ) = refs
    rows_dev, cols = width_ref.shape
    half = cols // 2
    moves = [
        pltpu.make_async_copy(source, target, sems.at[index])
        for index, (source, target) in enumerate((
            (wave_hbm, wave_ref), (angle_hbm, angle_ref), (aim_hbm, aim_ref),
            (coef_hbm, coef_ref), (width_hbm, width_ref),
        ))
    ]
    for move in moves:
        move.start()
    for move in moves[:4]:
        move.wait()
    for pair in range(pairs):
        coef = pick_coef(coef_ref[...], wave_ref[pair])
        info_ref[pair, :WAVE_ROW, :] = jnp.broadcast_to(coef, (WAVE_ROW, FOCAL))
        row = iota((INFO_ROWS - WAVE_ROW, FOCAL), 0) + WAVE_ROW
        ids = jnp.where(row == WAVE_ROW, wave_ref[pair], 0)
        ids = jnp.where(row == ANGLE_ROW, angle_ref[pair], ids)
        ids = jnp.where(row == AIM_ROW, aim_ref[pair, 0], ids)
        ids = jnp.where(row == AIM_ROW + 1, aim_ref[pair, 1], ids)
        info_ref[pair, WAVE_ROW:, :] = ids.astype(jnp.float32)
    centres = [
        turned_waves(info_ref, pair, cols, base_ref.at[pair], centre_ref.at[pair], turned_ref.at[pair])
        for pair in range(pairs)
    ]
    acc_ref[...] = jnp.zeros_like(acc_ref)
    moves[4].wait()
    core = lax.axis_index("wave")

    @pl.when(core == 1)
    def _():
        own_ref[...] = width_ref[:, half:]
        far_ref[...] = pltpu.roll(turn_round(width_ref[:, :half]), 1, 1)

    @pl.when(core == 0)
    def _():
        own_ref[...] = turn_round(width_ref[:, :half])
        far_ref[...] = pltpu.roll(width_ref[:, half:], half - 1, 1)

    void = jnp.where(core == 1, 0, half - 1)
    for index in range(half // (2 * BLOCK)):
        nears = [[] for _ in range(pairs)]
        for start in (half // 2 - (index + 1) * BLOCK, half // 2 + index * BLOCK):
            sides = []
            for ref in (own_ref, far_ref):
                sides.append(near_fields(ref[:, start : start + BLOCK], info_ref, pairs))
            if start in (0, half - BLOCK):
                keep = iota((rows_dev, BLOCK), 1) + start != void
                sides[1] = [[jnp.where(keep, part, 0.0) for part in out] for out in sides[1]]
            for pair in range(pairs):
                both = jnp.concatenate([*sides[0][pair], *sides[1][pair]], axis=0)
                nears[pair].append(both.astype(jnp.bfloat16))
        for pair in range(pairs):
            tables = write_tables(index, turned_ref.at[pair], centres[pair], table_refs[pair])
            acc_ref[pair] += lax.dot_general(
                jnp.concatenate(nears[pair], axis=1),
                jnp.concatenate(tables, axis=1),
                (((1,), (1,)), ((), ())),
                preferred_element_type=jnp.float32,
            )
    alone = jnp.where(core == 1, 0, half)
    column = width_ref[:, pl.ds(pl.multiple_of(alone, LANES), LANES)]
    columns = near_fields(jnp.concatenate([column, column], axis=1), info_ref, pairs)
    for pair in range(pairs):
        acc = [acc_ref[pair, part * rows_dev : (part + 1) * rows_dev, :] for part in range(4)]
        (own_rr, own_ri), (own_ir, own_ii), (far_rr, far_ri), (far_ir, far_ii) = (
            (part[:, :FOCAL], part[:, FOCAL:]) for part in acc
        )
        cross_r, cross_i = far_ii - own_ii, own_ri - far_ri
        real = own_rr + far_rr + jnp.where(core == 1, cross_r, -cross_r)
        imag = own_ir + far_ir + jnp.where(core == 1, cross_i, -cross_i)
        near_r, near_i = (part[:, :1].astype(jnp.bfloat16).astype(jnp.float32) for part in columns[pair])
        wave_r, wave_i = (
            part.astype(jnp.bfloat16).astype(jnp.float32)
            for part in unit_waves((alone - half) * column_freq(info_ref, pair), 256 * cols)
        )
        real = real + (near_r * wave_r - near_i * wave_i)
        imag = imag + (near_r * wave_i + near_i * wave_r)
        for part, value in enumerate((real, imag)):
            lane = (2 * pair + part) * FOCAL
            mine_ref[:, lane : lane + FOCAL] = value.astype(jnp.bfloat16)


def spot_map(info_ref, pair):
    aims = [info_ref[pair, row : row + 1, :] for row in (AIM_ROW, AIM_ROW + 1)]
    rows_off = iota((FOCAL, FOCAL), 0).astype(jnp.float32) - aims[0]
    cols_off = iota((1, FOCAL), 1).astype(jnp.float32) - aims[1]
    return jnp.exp(-(rows_off * rows_off + cols_off * cols_off) / (2.0 * SPOT * SPOT))


def total_of(value):
    return jnp.sum(jnp.sum(value, axis=0, keepdims=True), axis=1, keepdims=True)


def row_kernel(info_ref, tall_ref, flat_ref, spot_ref, gain_ref):
    pairs, _, rows = tall_ref.shape
    rows_dev = flat_ref.shape[1]
    period = 256 * rows
    size = min(rows, FOCAL)
    for pair in range(pairs):
        wave = info_ref[pair, WAVE_ROW : WAVE_ROW + 1, :].astype(jnp.int32) + BLOCK
        focal = (iota((FOCAL, 1), 0) - FOCAL // 2) * wave

        def step(index, carry):
            start = pl.multiple_of(index * size, size)
            place = iota((1, size), 1) + (start - rows // 2)
            real, imag = unit_waves(focal[:, :size] * place, period)
            tall_ref[pair, :FOCAL, pl.ds(start, size)] = real.astype(jnp.bfloat16)
            tall_ref[pair, FOCAL:, pl.ds(start, size)] = imag.astype(jnp.bfloat16)
            return carry

        if rows == size:
            step(0, 0)
        else:
            lax.fori_loop(0, rows // size, step, 0)
        focal = (iota((1, FOCAL), 1) - FOCAL // 2) * wave
        first = lax.axis_index("aperture") * rows_dev - rows // 2
        real, imag = unit_waves((iota((rows_dev, 1), 0) + first) * focal, period)
        flat_ref[pair, :, :FOCAL] = real.astype(jnp.bfloat16)
        flat_ref[pair, :, FOCAL:] = imag.astype(jnp.bfloat16)
        spot = spot_map(info_ref, pair)
        spot_ref[pair] = spot
        gain_ref[pair] = jnp.broadcast_to(FOCAL * FOCAL / total_of(spot), gain_ref.shape[1:])


def join_kernel(*refs):
    *in_refs, out_ref = refs
    count = in_refs[0].shape[0]
    for index, ref in enumerate(in_refs):
        out_ref[index * count : (index + 1) * count, :] = ref[...]


def focus_kernel(steps, tall_ref, flat_ref, spot_ref, gain_ref, after_ref, *refs):
    del after_ref
    *sect_refs, back_ref, score_ref, rows_ref = refs
    pairs = tall_ref.shape[0]
    rows_dev = back_ref.shape[0]
    if steps is None:
        rows_ref = sect_refs[0]
    else:
        me = lax.axis_index("aperture")
        blocks = [
            ref[index * rows_dev : (index + 1) * rows_dev, :]
            for ref in sect_refs
            for index in range(ref.shape[0] // rows_dev)
        ]
        for step, block in zip(steps, blocks, strict=True):
            start = pl.multiple_of((me ^ step) * rows_dev, rows_dev)
            rows_ref[pl.ds(start, rows_dev), :] = block
    fields, sums = [], []
    for pair in range(pairs):
        lane = 2 * pair * FOCAL
        section = rows_ref[:, lane : lane + 2 * FOCAL]
        mixed = jnp.dot(tall_ref[pair], section, preferred_element_type=jnp.float32)
        real = mixed[:FOCAL, :FOCAL] - mixed[FOCAL:, FOCAL:]
        imag = mixed[:FOCAL, FOCAL:] + mixed[FOCAL:, :FOCAL]
        power = real * real + imag * imag
        fields.append((real, imag))
        sums.append((total_of(spot_ref[pair] * power), total_of(power) + 1e-06))
    for pair, ((real, imag), (spot_power, all_power)) in enumerate(zip(fields, sums)):
        ratio = spot_power / all_power
        gain = gain_ref[pair, :1, :1]
        score_ref[pair] = jnp.sum(ratio * gain)
        weight = (gain * 2.0 / all_power) * (spot_ref[pair] - ratio)
        real = (weight * real).astype(jnp.bfloat16)
        imag = (weight * imag).astype(jnp.bfloat16)
        stack = jnp.concatenate(
            [jnp.concatenate([real, imag], axis=1), jnp.concatenate([imag, -real], axis=1)], axis=0
        )
        back = jnp.dot(flat_ref[pair], stack, preferred_element_type=jnp.float32)
        lane = 2 * pair * FOCAL
        back_ref[:, lane : lane + 2 * FOCAL] = back.astype(jnp.bfloat16)


def table_kernel(scale, cols, info_ref, far_info_ref, width_ref, *refs):
    *out_refs, base_ref, centre_ref, turned_ref = refs
    pairs = base_ref.shape[0]
    out_refs = out_refs[-3 * pairs :]
    table_refs, slope_refs = out_refs[:pairs], out_refs[pairs:]
    own_cols = width_ref.shape[1]
    centres = [
        turned_waves(far_info_ref, pair, cols, base_ref.at[pair], centre_ref.at[pair], turned_ref.at[pair])
        for pair in range(pairs)
    ]
    for index in range(own_cols // (2 * BLOCK)):
        for pair in range(pairs):
            write_tables(index, turned_ref.at[pair], centres[pair], table_refs[pair])
        for start in (2 * index * BLOCK, (2 * index + 1) * BLOCK):
            place = slice(start, start + BLOCK)
            for core, ref in enumerate((info_ref, far_info_ref)):
                slopes = near_slopes(width_ref[:, place], scale, ref, pairs)
                for pair in range(pairs):
                    slope_refs[core * pairs + pair][0, :, place] = slopes[pair][0]
                    slope_refs[core * pairs + pair][1, :, place] = slopes[pair][1]


def last_grad_kernel(pairs, *refs):
    *in_refs, out_hbm, out_ref, sems = refs
    rows_dev, own_cols = out_ref.shape
    size = 2 * BLOCK
    core = lax.axis_index("wave")
    moves = []

    def send(start, total):
        place = pl.multiple_of(jnp.where(core == 1, start, own_cols - size - start), size)
        place = pl.ds(place, size)
        out_ref[:, place] = jnp.where(core == 1, total, turn_round(total))
        index = start // size
        moves.append(pltpu.make_async_copy(out_ref.at[:, place], out_hbm.at[:, place], sems.at[index]))
        moves[-1].start()

    grad_kernel(pairs, *in_refs, out_ref, send=send)
    for move in moves:
        move.wait()


def grad_kernel(pairs, back_ref, *refs, send=None):
    *in_refs, out_ref = refs
    table_refs, slope_refs, total_ref = in_refs[:pairs], in_refs[pairs : 2 * pairs], in_refs[2 * pairs :]
    rows_dev, own_cols = out_ref.shape
    core = lax.axis_index("wave")
    lefts = []
    for pair in range(pairs):
        lane = 2 * pair * FOCAL
        real, imag = back_ref[:, lane : lane + FOCAL], back_ref[:, lane + FOCAL : lane + 2 * FOCAL]
        above = jnp.where(core == 1, imag, -imag)
        below = jnp.where(core == 1, -real, real)
        lefts.append(
            jnp.concatenate(
                [jnp.concatenate([real, above], axis=1), jnp.concatenate([imag, below], axis=1)], axis=0
            )
        )
    size = 2 * BLOCK
    for start in range(0, own_cols, size):
        place = slice(start, start + size)
        total = total_ref[0][:, place] if total_ref else jnp.zeros((rows_dev, size), jnp.float32)
        for pair in range(pairs):
            grad = jnp.dot(lefts[pair], table_refs[pair][:, place], preferred_element_type=jnp.float32)
            total += grad[:rows_dev] * slope_refs[pair][0, :, place]
            total += grad[rows_dev:] * slope_refs[pair][1, :, place]
        if send is None:
            out_ref[:, place] = total
        else:
            send(start, total)


VMEM = pl.BlockSpec(memory_space=pltpu.VMEM)
SMEM = pl.BlockSpec(memory_space=pltpu.SMEM)
ANY = pl.BlockSpec(memory_space=pl.ANY)
HBM = pl.BlockSpec(memory_space=pltpu.HBM)


def call(kernel, name, outs, in_specs, out_specs, scratch, flops, moved):
    return pl.pallas_call(
        kernel,
        name=name,
        out_shape=outs,
        in_specs=in_specs,
        out_specs=out_specs,
        scratch_shapes=scratch,
        cost_estimate=pl.CostEstimate(flops=flops, bytes_accessed=moved, transcendentals=0),
        compiler_params=pltpu.CompilerParams(vmem_limit_bytes=VMEM_LIMIT),
    )


def on_device(widths, coef_table, wave_ids, angle_ids, targets):
    rows_dev, cols = widths.shape
    pairs_dev = wave_ids.shape[0]
    peers = lax.axis_size("aperture")
    copies = lax.axis_size("wave")
    rows = rows_dev * peers
    own_cols = cols // copies
    lanes = 2 * pairs_dev * FOCAL
    f32, bf16 = jnp.float32, jnp.bfloat16
    shape = jax.ShapeDtypeStruct

    def in_hbm(value):
        return pltpu.with_memory_space_constraint(value, pltpu.HBM)

    def exchange(value, step):
        return lax.ppermute(value, "aperture", [(index, index ^ step) for index in range(peers)])

    def to_core(value):
        return lax.ppermute(value, "wave", [(index, (index + 1) % copies) for index in range(copies)])

    waves = [
        pltpu.VMEM((pairs_dev, 2, BLOCK, FOCAL), f32),
        pltpu.VMEM((pairs_dev, 2, 8, FOCAL), f32),
        pltpu.VMEM((pairs_dev, 2, FOCAL, BLOCK), f32),
    ]
    mine, info, own, *tables = call(
        forward_kernel, "forward",
        (
            shape((rows_dev, lanes), bf16),
            shape((pairs_dev, INFO_ROWS, FOCAL), f32), shape((rows_dev, own_cols), f32),
            *[shape((2 * FOCAL, own_cols), bf16)] * pairs_dev,
        ),
        [HBM] * 5, (VMEM,) * (3 + pairs_dev),
        [
            pltpu.SMEM(wave_ids.shape, jnp.int32),
            pltpu.SMEM(angle_ids.shape, jnp.int32),
            pltpu.SMEM(targets.shape, jnp.int32),
            pltpu.VMEM(coef_table.shape[::-1], f32),
            pltpu.VMEM(widths.shape, f32),
            pltpu.VMEM((rows_dev, own_cols), f32),
            *waves,
            pltpu.VMEM((pairs_dev, 4 * rows_dev, 2 * FOCAL), f32),
            pltpu.SemaphoreType.DMA((5,)),
        ],
        10**9, 10**7,
    )(*(in_hbm(value) for value in (wave_ids, angle_ids, targets, coef_table.T, widths)))
    far_info = to_core(info)

    tall, flat, spots, gains = call(
        row_kernel, "row_tables",
        (
            shape((pairs_dev, 2 * FOCAL, rows), bf16), shape((pairs_dev, rows_dev, 2 * FOCAL), bf16),
            shape((pairs_dev, FOCAL, FOCAL), f32), shape((pairs_dev, 8, 128), f32),
        ),
        [VMEM], (VMEM,) * 4, [], 10**8, 10**6,
    )(info)
    if peers <= DIRECT:
        steps = list(range(peers - 2, 0, -2))
        got = [exchange(mine, step) for step in steps]
        near = exchange(mine, 1)
        first, flat = lax.optimization_barrier((got[0], flat))
        joined = call(join_kernel, "join", shape(((len(steps) - 1) * rows_dev, lanes), bf16),
                      [VMEM] * (len(steps) - 1), VMEM, [], 10**6, 10**6)(*got[1:])
        sections = [mine, near, first, joined, exchange(first, 1), exchange(joined, 1)]
        steps = [0, 1, *steps, *(step ^ 1 for step in steps)]
        after = [near, joined]
    else:
        blocks = jnp.tile(mine[None], (peers, 1, 1))
        blocks = lax.all_to_all(blocks, "aperture", 0, 0, tiled=True)
        sections, steps, after = [blocks.reshape(rows, lanes)], None, []
    outs = [shape((2 * FOCAL, own_cols), bf16)] * pairs_dev + [shape((2, rows_dev, own_cols), f32)] * 2 * pairs_dev
    made = call(
        functools.partial(table_kernel, math.sqrt(rows * cols), cols), "far_tables",
        outs, [VMEM] * 3 + [ANY] * len(after), [VMEM] * len(outs), waves, 10**9, 10**7,
    )(info, far_info, own, *after)
    far_tables, slopes, far_slopes = made[:pairs_dev], made[pairs_dev : 2 * pairs_dev], made[2 * pairs_dev :]

    back, scores = call(
        functools.partial(focus_kernel, steps), "focus",
        (shape((rows_dev, lanes), bf16), shape((pairs_dev,), f32)),
        [VMEM] * 4 + [ANY] + [VMEM] * len(sections), (VMEM, SMEM), [pltpu.VMEM((rows, lanes), bf16)],
        10**8, 10**6,
    )(tall, flat, spots, gains, far_slopes[0], *sections)

    out = shape((rows_dev, own_cols), f32)
    ins = [back, *tables, *slopes]
    grad = call(
        functools.partial(grad_kernel, pairs_dev), "gradient_own",
        out, [VMEM] * len(ins), VMEM, [], 10**9, 10**7,
    )(*ins)
    ins = [to_core(back), *far_tables, *far_slopes, grad]
    grad = call(
        functools.partial(last_grad_kernel, pairs_dev), "gradient_far",
        out, [VMEM] * len(ins), HBM,
        [pltpu.VMEM(out.shape, f32), pltpu.SemaphoreType.DMA((own_cols // (2 * BLOCK),))], 10**9, 10**7,
    )(*ins)
    return grad, scores


def solution(mesh):
    in_specs = (
        P(("group", "aperture"), None),
        P(),
        P(("group", "wave")),
        P(("group", "wave")),
        P(("group", "wave"), None),
    )
    out_specs = (P(("group", "aperture"), "wave"), P(("group", "wave")))
    return jax.shard_map(
        on_device, mesh=mesh, in_specs=in_specs, out_specs=out_specs, check_vma=False
    )
```

```python
import functools
import math

import jax
import jax.numpy as jnp
from jax import lax
from jax.experimental import pallas as pl
from jax.experimental.pallas import tpu as pltpu
from jax.sharding import PartitionSpec as P

FOCAL = 256
SPOT = 4
SHIFT = 32
TERMS = 8
BLOCK = 256
GRAIN = 16
LANES = 128
VMEM_LIMIT = 16 * 1024 * 1024
WAVE_ROW, ANGLE_ROW, AIM_ROW, INFO_ROWS = 16, 17, 18, 24
DIRECT = 16

COS = (
    1.0, -19.7392088015709, 64.93939395773512, -85.45681453397417, 60.24458621302471,
    -26.425616460281425, 7.8991596631575085, -1.6968741456712442, 0.2437618617467591,
)
SIN = (
    6.2831853071792665, -41.34170224019464, 81.60524925425943, -76.70585885700535,
    42.05867547580699, -15.094428387947755, 3.818490079304055, -0.7122771247541972,
    0.09149844789363434,
)


def horner(terms, u):
    value = terms[-1] * u + terms[-2]
    for term in terms[-3::-1]:
        value = value * u + term
    return value


def unit_waves(counts, period):
    half = period // 2
    centred = ((counts + half) & (period - 1)) - half
    t = centred.astype(jnp.float32) * (1.0 / period)
    u = t * t
    return horner(COS, u), -(t * horner(SIN, u))


def iota(shape, axis):
    return lax.broadcasted_iota(jnp.int32, shape, axis)


def pick_coef(table, wave):
    chosen = jnp.where(iota(table.shape, 1) == wave, table, 0.0)
    return jnp.sum(chosen, axis=1, keepdims=True)


def column_freq(info_ref, pair):
    wave = info_ref[pair, WAVE_ROW : WAVE_ROW + 1, :].astype(jnp.int32)
    angle = info_ref[pair, ANGLE_ROW : ANGLE_ROW + 1, :].astype(jnp.int32)
    return (iota((1, FOCAL), 1) - FOCAL // 2 + SHIFT * angle) * (BLOCK + wave)


def fill_base(freq, shift, period, base_ref, centre_ref):
    low_r, low_i = unit_waves(iota((GRAIN, 1), 0) * freq, period)
    steps = BLOCK // GRAIN
    high_r, high_i = unit_waves((iota((steps, 1), 0) * GRAIN - BLOCK // 2 + shift) * freq, period)
    for step in range(steps):
        one_r, one_i = high_r[step : step + 1], high_i[step : step + 1]
        rows = slice(step * GRAIN, (step + 1) * GRAIN)
        base_ref[0, rows, :] = one_r * low_r - one_i * low_i
        base_ref[1, rows, :] = one_r * low_i + one_i * low_r
    count = centre_ref.shape[1]
    cent_r, cent_i = unit_waves((iota((count, 1), 0) * BLOCK + BLOCK // 2) * freq, period)
    centre_ref[0] = cent_r
    centre_ref[1] = cent_i


def near_fields(s, info_ref, pairs):
    def coef(pair, row):
        return info_ref[pair, row : row + 1, :]

    outs = [[coef(p, k) + coef(p, k + 1) * s for k in (0, TERMS)] for p in range(pairs)]
    twice = s + s
    before, current = jnp.ones_like(s), s
    for order in range(2, TERMS):
        before, current = current, twice * current - before
        for pair, out in enumerate(outs):
            out[0] = out[0] + coef(pair, order) * current
            out[1] = out[1] + coef(pair, TERMS + order) * current
    return outs


def near_slopes(s, scale, info_ref, pairs):
    def coef(pair, row):
        return info_ref[pair, row : row + 1, :] * (scale * (row % TERMS))

    twice = s + s
    before, current = jnp.ones_like(s), twice
    outs = [[coef(p, k) + coef(p, k + 1) * twice for k in (1, TERMS + 1)] for p in range(pairs)]
    for order in range(3, TERMS):
        before, current = current, twice * current - before
        for pair, out in enumerate(outs):
            out[0] = out[0] + coef(pair, order) * current
            out[1] = out[1] + coef(pair, TERMS + order) * current
    return outs


def turn_round(value):
    rows, cols = value.shape
    order = LANES - 1 - iota((rows, LANES), 1)
    parts = [
        jnp.take_along_axis(value[:, start : start + LANES], order, axis=1)
        for start in range(cols - LANES, -1, -LANES)
    ]
    return jnp.concatenate(parts, axis=1)


def write_tables(index, base_ref, centres, table_ref):
    middle = table_ref.shape[1] // 2
    cent_r, cent_i = (centre[:, index : index + 1] for centre in centres)
    base_r, base_i = base_ref[0], base_ref[1]
    rr, ii = base_r * cent_r, base_i * cent_i
    ri, ir = base_r * cent_i, base_i * cent_r
    left, right = middle - (index + 1) * BLOCK, middle + index * BLOCK
    tables = []
    for start, values in ((left, (rr + ii, ir - ri)), (right, (rr - ii, ir + ri))):
        table = jnp.concatenate(values, axis=0).astype(jnp.bfloat16)
        table_ref[:, start : start + BLOCK] = table
        tables.append(table)
    return tables


def turned_waves(info_ref, pair, cols, base_ref, centre_ref, turned_ref):
    shift = cols // 4 + 1 - lax.axis_index("wave")
    fill_base(column_freq(info_ref, pair), shift, 256 * cols, base_ref, centre_ref)
    for part in range(2):
        turned_ref[part] = base_ref[part].T
    return [centre_ref[part].T for part in range(2)]


def forward_kernel(
    wave_hbm, angle_hbm, aim_hbm, coef_hbm, width_hbm, mine_ref, info_ref, own_ref, *refs
):
    pairs = info_ref.shape[0]
    table_refs, refs = refs[:pairs], refs[pairs:]
    (
        wave_ref, angle_ref, aim_ref, coef_ref, width_ref, far_ref, base_ref, centre_ref, turned_ref, acc_ref, sems,
    ) = refs
    rows_dev, cols = width_ref.shape
    half = cols // 2
    moves = [
        pltpu.make_async_copy(source, target, sems.at[index])
        for index, (source, target) in enumerate((
            (wave_hbm, wave_ref), (angle_hbm, angle_ref), (aim_hbm, aim_ref),
            (coef_hbm, coef_ref), (width_hbm, width_ref),
        ))
    ]
    for move in moves:
        move.start()
    for move in moves[:4]:
        move.wait()
    for pair in range(pairs):
        coef = pick_coef(coef_ref[...], wave_ref[pair])
        info_ref[pair, :WAVE_ROW, :] = jnp.broadcast_to(coef, (WAVE_ROW, FOCAL))
        row = iota((INFO_ROWS - WAVE_ROW, FOCAL), 0) + WAVE_ROW
        ids = jnp.where(row == WAVE_ROW, wave_ref[pair], 0)
        ids = jnp.where(row == ANGLE_ROW, angle_ref[pair], ids)
        ids = jnp.where(row == AIM_ROW, aim_ref[pair, 0], ids)
        ids = jnp.where(row == AIM_ROW + 1, aim_ref[pair, 1], ids)
        info_ref[pair, WAVE_ROW:, :] = ids.astype(jnp.float32)
    centres = [
        turned_waves(info_ref, pair, cols, base_ref.at[pair], centre_ref.at[pair], turned_ref.at[pair])
        for pair in range(pairs)
    ]
    acc_ref[...] = jnp.zeros_like(acc_ref)
    moves[4].wait()
    core = lax.axis_index("wave")

    @pl.when(core == 1)
    def _():
        own_ref[...] = width_ref[:, half:]
        far_ref[...] = pltpu.roll(turn_round(width_ref[:, :half]), 1, 1)

    @pl.when(core == 0)
    def _():
        own_ref[...] = turn_round(width_ref[:, :half])
        far_ref[...] = pltpu.roll(width_ref[:, half:], half - 1, 1)

    void = jnp.where(core == 1, 0, half - 1)
    for index in range(half // (2 * BLOCK)):
        nears = [[] for _ in range(pairs)]
        for start in (half // 2 - (index + 1) * BLOCK, half // 2 + index * BLOCK):
            sides = []
            for ref in (own_ref, far_ref):
                sides.append(near_fields(ref[:, start : start + BLOCK], info_ref, pairs))
            if start in (0, half - BLOCK):
                keep = iota((rows_dev, BLOCK), 1) + start != void
                sides[1] = [[jnp.where(keep, part, 0.0) for part in out] for out in sides[1]]
            for pair in range(pairs):
                both = jnp.concatenate([*sides[0][pair], *sides[1][pair]], axis=0)
                nears[pair].append(both.astype(jnp.bfloat16))
        for pair in range(pairs):
            tables = write_tables(index, turned_ref.at[pair], centres[pair], table_refs[pair])
            acc_ref[pair] += lax.dot_general(
                jnp.concatenate(nears[pair], axis=1),
                jnp.concatenate(tables, axis=1),
                (((1,), (1,)), ((), ())),
                preferred_element_type=jnp.float32,
            )
    alone = jnp.where(core == 1, 0, half)
    column = width_ref[:, pl.ds(pl.multiple_of(alone, LANES), LANES)]
    columns = near_fields(jnp.concatenate([column, column], axis=1), info_ref, pairs)
    for pair in range(pairs):
        acc = [acc_ref[pair, part * rows_dev : (part + 1) * rows_dev, :] for part in range(4)]
        (own_rr, own_ri), (own_ir, own_ii), (far_rr, far_ri), (far_ir, far_ii) = (
            (part[:, :FOCAL], part[:, FOCAL:]) for part in acc
        )
        cross_r, cross_i = far_ii - own_ii, own_ri - far_ri
        real = own_rr + far_rr + jnp.where(core == 1, cross_r, -cross_r)
        imag = own_ir + far_ir + jnp.where(core == 1, cross_i, -cross_i)
        near_r, near_i = (part[:, :1].astype(jnp.bfloat16).astype(jnp.float32) for part in columns[pair])
        wave_r, wave_i = (
            part.astype(jnp.bfloat16).astype(jnp.float32)
            for part in unit_waves((alone - half) * column_freq(info_ref, pair), 256 * cols)
        )
        real = real + (near_r * wave_r - near_i * wave_i)
        imag = imag + (near_r * wave_i + near_i * wave_r)
        for part, value in enumerate((real, imag)):
            lane = (2 * pair + part) * FOCAL
            mine_ref[:, lane : lane + FOCAL] = value.astype(jnp.bfloat16)


def spot_map(info_ref, pair):
    aims = [info_ref[pair, row : row + 1, :] for row in (AIM_ROW, AIM_ROW + 1)]
    rows_off = iota((FOCAL, FOCAL), 0).astype(jnp.float32) - aims[0]
    cols_off = iota((1, FOCAL), 1).astype(jnp.float32) - aims[1]
    return jnp.exp(-(rows_off * rows_off + cols_off * cols_off) / (2.0 * SPOT * SPOT))


def total_of(value):
    return jnp.sum(jnp.sum(value, axis=0, keepdims=True), axis=1, keepdims=True)


def row_kernel(info_ref, tall_ref, flat_ref, spot_ref, gain_ref):
    pairs, _, rows = tall_ref.shape
    rows_dev = flat_ref.shape[1]
    period = 256 * rows
    size = min(rows, FOCAL)
    for pair in range(pairs):
        wave = info_ref[pair, WAVE_ROW : WAVE_ROW + 1, :].astype(jnp.int32) + BLOCK
        focal = (iota((FOCAL, 1), 0) - FOCAL // 2) * wave

        def step(index, carry):
            start = pl.multiple_of(index * size, size)
            place = iota((1, size), 1) + (start - rows // 2)
            real, imag = unit_waves(focal[:, :size] * place, period)
            tall_ref[pair, :FOCAL, pl.ds(start, size)] = real.astype(jnp.bfloat16)
            tall_ref[pair, FOCAL:, pl.ds(start, size)] = imag.astype(jnp.bfloat16)
            return carry

        if rows == size:
            step(0, 0)
        else:
            lax.fori_loop(0, rows // size, step, 0)
        focal = (iota((1, FOCAL), 1) - FOCAL // 2) * wave
        first = lax.axis_index("aperture") * rows_dev - rows // 2
        real, imag = unit_waves((iota((rows_dev, 1), 0) + first) * focal, period)
        flat_ref[pair, :, :FOCAL] = real.astype(jnp.bfloat16)
        flat_ref[pair, :, FOCAL:] = imag.astype(jnp.bfloat16)
        spot = spot_map(info_ref, pair)
        spot_ref[pair] = spot
        gain_ref[pair] = jnp.broadcast_to(FOCAL * FOCAL / total_of(spot), gain_ref.shape[1:])


def join_kernel(*refs):
    *in_refs, out_ref = refs
    count = in_refs[0].shape[0]
    for index, ref in enumerate(in_refs):
        out_ref[index * count : (index + 1) * count, :] = ref[...]


def focus_kernel(steps, tall_ref, flat_ref, spot_ref, gain_ref, after_ref, *refs):
    del after_ref
    *sect_refs, back_ref, score_ref, rows_ref = refs
    pairs = tall_ref.shape[0]
    rows_dev = back_ref.shape[0]
    if steps is None:
        rows_ref = sect_refs[0]
    else:
        me = lax.axis_index("aperture")
        blocks = [
            ref[index * rows_dev : (index + 1) * rows_dev, :]
            for ref in sect_refs
            for index in range(ref.shape[0] // rows_dev)
        ]
        for step, block in zip(steps, blocks, strict=True):
            start = pl.multiple_of((me ^ step) * rows_dev, rows_dev)
            rows_ref[pl.ds(start, rows_dev), :] = block
    fields, sums = [], []
    for pair in range(pairs):
        lane = 2 * pair * FOCAL
        section = rows_ref[:, lane : lane + 2 * FOCAL]
        mixed = jnp.dot(tall_ref[pair], section, preferred_element_type=jnp.float32)
        real = mixed[:FOCAL, :FOCAL] - mixed[FOCAL:, FOCAL:]
        imag = mixed[:FOCAL, FOCAL:] + mixed[FOCAL:, :FOCAL]
        power = real * real + imag * imag
        fields.append((real, imag))
        sums.append((total_of(spot_ref[pair] * power), total_of(power) + 1e-06))
    for pair, ((real, imag), (spot_power, all_power)) in enumerate(zip(fields, sums)):
        ratio = spot_power / all_power
        gain = gain_ref[pair, :1, :1]
        score_ref[pair] = jnp.sum(ratio * gain)
        weight = (gain * 2.0 / all_power) * (spot_ref[pair] - ratio)
        real = (weight * real).astype(jnp.bfloat16)
        imag = (weight * imag).astype(jnp.bfloat16)
        stack = jnp.concatenate(
            [jnp.concatenate([real, imag], axis=1), jnp.concatenate([imag, -real], axis=1)], axis=0
        )
        back = jnp.dot(flat_ref[pair], stack, preferred_element_type=jnp.float32)
        lane = 2 * pair * FOCAL
        back_ref[:, lane : lane + 2 * FOCAL] = back.astype(jnp.bfloat16)


def table_kernel(scale, cols, info_ref, far_info_ref, width_ref, *refs):
    *out_refs, base_ref, centre_ref, turned_ref = refs
    pairs = base_ref.shape[0]
    out_refs = out_refs[-3 * pairs :]
    table_refs, slope_refs = out_refs[:pairs], out_refs[pairs:]
    own_cols = width_ref.shape[1]
    centres = [
        turned_waves(far_info_ref, pair, cols, base_ref.at[pair], centre_ref.at[pair], turned_ref.at[pair])
        for pair in range(pairs)
    ]
    for index in range(own_cols // (2 * BLOCK)):
        for pair in range(pairs):
            write_tables(index, turned_ref.at[pair], centres[pair], table_refs[pair])
        for start in (2 * index * BLOCK, (2 * index + 1) * BLOCK):
            place = slice(start, start + BLOCK)
            for core, ref in enumerate((info_ref, far_info_ref)):
                slopes = near_slopes(width_ref[:, place], scale, ref, pairs)
                for pair in range(pairs):
                    slope_refs[core * pairs + pair][0, :, place] = slopes[pair][0]
                    slope_refs[core * pairs + pair][1, :, place] = slopes[pair][1]


def last_grad_kernel(pairs, *refs):
    *in_refs, out_hbm, out_ref, sems = refs
    rows_dev, own_cols = out_ref.shape
    size = 2 * BLOCK
    core = lax.axis_index("wave")
    moves = []

    def send(start, total):
        place = pl.multiple_of(jnp.where(core == 1, start, own_cols - size - start), size)
        place = pl.ds(place, size)
        out_ref[:, place] = jnp.where(core == 1, total, turn_round(total))
        index = start // size
        moves.append(pltpu.make_async_copy(out_ref.at[:, place], out_hbm.at[:, place], sems.at[index]))
        moves[-1].start()

    grad_kernel(pairs, *in_refs, out_ref, send=send)
    for move in moves:
        move.wait()


def grad_kernel(pairs, back_ref, *refs, send=None):
    *in_refs, out_ref = refs
    table_refs, slope_refs, total_ref = in_refs[:pairs], in_refs[pairs : 2 * pairs], in_refs[2 * pairs :]
    rows_dev, own_cols = out_ref.shape
    core = lax.axis_index("wave")
    lefts = []
    for pair in range(pairs):
        lane = 2 * pair * FOCAL
        real, imag = back_ref[:, lane : lane + FOCAL], back_ref[:, lane + FOCAL : lane + 2 * FOCAL]
        above = jnp.where(core == 1, imag, -imag)
        below = jnp.where(core == 1, -real, real)
        lefts.append(
            jnp.concatenate(
                [jnp.concatenate([real, above], axis=1), jnp.concatenate([imag, below], axis=1)], axis=0
            )
        )
    size = 2 * BLOCK
    for start in range(0, own_cols, size):
        place = slice(start, start + size)
        total = total_ref[0][:, place] if total_ref else jnp.zeros((rows_dev, size), jnp.float32)
        for pair in range(pairs):
            grad = jnp.dot(lefts[pair], table_refs[pair][:, place], preferred_element_type=jnp.float32)
            total += grad[:rows_dev] * slope_refs[pair][0, :, place]
            total += grad[rows_dev:] * slope_refs[pair][1, :, place]
        if send is None:
            out_ref[:, place] = total
        else:
            send(start, total)


VMEM = pl.BlockSpec(memory_space=pltpu.VMEM)
SMEM = pl.BlockSpec(memory_space=pltpu.SMEM)
ANY = pl.BlockSpec(memory_space=pl.ANY)
HBM = pl.BlockSpec(memory_space=pltpu.HBM)


def call(kernel, name, outs, in_specs, out_specs, scratch, flops, moved):
    return pl.pallas_call(
        kernel,
        name=name,
        out_shape=outs,
        in_specs=in_specs,
        out_specs=out_specs,
        scratch_shapes=scratch,
        cost_estimate=pl.CostEstimate(flops=flops, bytes_accessed=moved, transcendentals=0),
        compiler_params=pltpu.CompilerParams(vmem_limit_bytes=VMEM_LIMIT),
    )


def on_device(widths, coef_table, wave_ids, angle_ids, targets):
    rows_dev, cols = widths.shape
    pairs_dev = wave_ids.shape[0]
    peers = lax.axis_size("aperture")
    copies = lax.axis_size("wave")
    rows = rows_dev * peers
    own_cols = cols // copies
    lanes = 2 * pairs_dev * FOCAL
    f32, bf16 = jnp.float32, jnp.bfloat16
    shape = jax.ShapeDtypeStruct

    def in_hbm(value):
        return pltpu.with_memory_space_constraint(value, pltpu.HBM)

    def exchange(value, step):
        return lax.ppermute(value, "aperture", [(index, index ^ step) for index in range(peers)])

    def to_core(value):
        return lax.ppermute(value, "wave", [(index, (index + 1) % copies) for index in range(copies)])

    waves = [
        pltpu.VMEM((pairs_dev, 2, BLOCK, FOCAL), f32),
        pltpu.VMEM((pairs_dev, 2, 8, FOCAL), f32),
        pltpu.VMEM((pairs_dev, 2, FOCAL, BLOCK), f32),
    ]
    mine, info, own, *tables = call(
        forward_kernel, "forward",
        (
            shape((rows_dev, lanes), bf16),
            shape((pairs_dev, INFO_ROWS, FOCAL), f32), shape((rows_dev, own_cols), f32),
            *[shape((2 * FOCAL, own_cols), bf16)] * pairs_dev,
        ),
        [HBM] * 5, (VMEM,) * (3 + pairs_dev),
        [
            pltpu.SMEM(wave_ids.shape, jnp.int32),
            pltpu.SMEM(angle_ids.shape, jnp.int32),
            pltpu.SMEM(targets.shape, jnp.int32),
            pltpu.VMEM(coef_table.shape[::-1], f32),
            pltpu.VMEM(widths.shape, f32),
            pltpu.VMEM((rows_dev, own_cols), f32),
            *waves,
            pltpu.VMEM((pairs_dev, 4 * rows_dev, 2 * FOCAL), f32),
            pltpu.SemaphoreType.DMA((5,)),
        ],
        10**9, 10**7,
    )(*(in_hbm(value) for value in (wave_ids, angle_ids, targets, coef_table.T, widths)))
    far_info = to_core(info)

    tall, flat, spots, gains = call(
        row_kernel, "row_tables",
        (
            shape((pairs_dev, 2 * FOCAL, rows), bf16), shape((pairs_dev, rows_dev, 2 * FOCAL), bf16),
            shape((pairs_dev, FOCAL, FOCAL), f32), shape((pairs_dev, 8, 128), f32),
        ),
        [VMEM], (VMEM,) * 4, [], 10**8, 10**6,
    )(info)
    if peers <= DIRECT:
        steps = list(range(peers - 2, 0, -2))
        got = [exchange(mine, step) for step in steps]
        near = exchange(mine, 1)
        first, flat = lax.optimization_barrier((got[0], flat))
        joined = call(join_kernel, "join", shape(((len(steps) - 1) * rows_dev, lanes), bf16),
                      [VMEM] * (len(steps) - 1), VMEM, [], 10**6, 10**6)(*got[1:])
        sections = [mine, near, first, joined, exchange(first, 1), exchange(joined, 1)]
        steps = [0, 1, *steps, *(step ^ 1 for step in steps)]
        after = [near, joined]
    else:
        blocks = jnp.tile(mine[None], (peers, 1, 1))
        blocks = lax.all_to_all(blocks, "aperture", 0, 0, tiled=True)
        sections, steps, after = [blocks.reshape(rows, lanes)], None, []
    outs = [shape((2 * FOCAL, own_cols), bf16)] * pairs_dev + [shape((2, rows_dev, own_cols), f32)] * 2 * pairs_dev
    made = call(
        functools.partial(table_kernel, math.sqrt(rows * cols), cols), "far_tables",
        outs, [VMEM] * 3 + [ANY] * len(after), [VMEM] * len(outs), waves, 30 * 10**8, 30 * 10**6,
    )(info, far_info, own, *after)
    far_tables, slopes, far_slopes = made[:pairs_dev], made[pairs_dev : 2 * pairs_dev], made[2 * pairs_dev :]

    back, scores = call(
        functools.partial(focus_kernel, steps), "focus",
        (shape((rows_dev, lanes), bf16), shape((pairs_dev,), f32)),
        [VMEM] * 4 + [ANY] + [VMEM] * len(sections), (VMEM, SMEM), [pltpu.VMEM((rows, lanes), bf16)],
        10**8, 10**6,
    )(tall, flat, spots, gains, far_slopes[0], *sections)

    out = shape((rows_dev, own_cols), f32)
    ins = [back, *tables, *slopes]
    grad = call(
        functools.partial(grad_kernel, pairs_dev), "gradient_own",
        out, [VMEM] * len(ins), VMEM, [], 10**9, 10**7,
    )(*ins)
    ins = [to_core(back), *far_tables, *far_slopes, grad]
    grad = call(
        functools.partial(last_grad_kernel, pairs_dev), "gradient_far",
        out, [VMEM] * len(ins), HBM,
        [pltpu.VMEM(out.shape, f32), pltpu.SemaphoreType.DMA((own_cols // (2 * BLOCK),))], 10**9, 10**7,
    )(*ins)
    return grad, scores


def solution(mesh):
    in_specs = (
        P(("group", "aperture"), None),
        P(),
        P(("group", "wave")),
        P(("group", "wave")),
        P(("group", "wave"), None),
    )
    out_specs = (P(("group", "aperture"), "wave"), P(("group", "wave")))
    return jax.shard_map(
        on_device, mesh=mesh, in_specs=in_specs, out_specs=out_specs, check_vma=False
    )
```

```python
import functools
import itertools
import math

import jax
import jax.numpy as jnp
from jax import lax
from jax.experimental import pallas as pl
from jax.experimental.pallas import tpu as pltpu
from jax.sharding import PartitionSpec as P

FOCAL = 256
SPOT = 4
SHIFT = 32
TERMS = 8
BLOCK = 256
GRAIN = 16
LANES = 128
PIECE = 16
VMEM_LIMIT = 16 * 1024 * 1024
WAVE_ROW, ANGLE_ROW, AIM_ROW, INFO_ROWS = 16, 17, 18, 24
DIRECT = 16

COS = (
    1.0, -19.7392088015709, 64.93939395773512, -85.45681453397417, 60.24458621302471,
    -26.425616460281425, 7.8991596631575085, -1.6968741456712442, 0.2437618617467591,
)
SIN = (
    6.2831853071792665, -41.34170224019464, 81.60524925425943, -76.70585885700535,
    42.05867547580699, -15.094428387947755, 3.818490079304055, -0.7122771247541972,
    0.09149844789363434,
)


def horner(terms, u):
    value = terms[-1] * u + terms[-2]
    for term in terms[-3::-1]:
        value = value * u + term
    return value


def unit_waves(counts, period):
    half = period // 2
    centred = ((counts + half) & (period - 1)) - half
    t = centred.astype(jnp.float32) * (1.0 / period)
    u = t * t
    return horner(COS, u), -(t * horner(SIN, u))


def iota(shape, axis):
    return lax.broadcasted_iota(jnp.int32, shape, axis)


def pick_coef(table, wave):
    chosen = jnp.where(iota(table.shape, 1) == wave, table, 0.0)
    return jnp.sum(chosen, axis=1, keepdims=True)


def column_freq(info_ref, pair):
    wave = info_ref[pair, WAVE_ROW : WAVE_ROW + 1, :].astype(jnp.int32)
    angle = info_ref[pair, ANGLE_ROW : ANGLE_ROW + 1, :].astype(jnp.int32)
    return (iota((1, FOCAL), 1) - FOCAL // 2 + SHIFT * angle) * (BLOCK + wave)


def fill_base(freq, shift, period, base_ref, centre_ref):
    low_r, low_i = unit_waves(iota((GRAIN, 1), 0) * freq, period)
    steps = BLOCK // GRAIN
    high_r, high_i = unit_waves((iota((steps, 1), 0) * GRAIN - BLOCK // 2 + shift) * freq, period)
    for step in range(steps):
        one_r, one_i = high_r[step : step + 1], high_i[step : step + 1]
        rows = slice(step * GRAIN, (step + 1) * GRAIN)
        base_ref[0, rows, :] = one_r * low_r - one_i * low_i
        base_ref[1, rows, :] = one_r * low_i + one_i * low_r
    count = centre_ref.shape[1]
    cent_r, cent_i = unit_waves((iota((count, 1), 0) * BLOCK + BLOCK // 2) * freq, period)
    centre_ref[0] = cent_r
    centre_ref[1] = cent_i


def near_fields(s, info_ref, pairs):
    def coef(pair, row):
        return info_ref[pair, row : row + 1, :LANES]

    outs = [[coef(p, k) + coef(p, k + 1) * s for k in (0, TERMS)] for p in range(pairs)]
    twice = s + s
    before, current = jnp.ones_like(s), s
    for order in range(2, TERMS):
        before, current = current, twice * current - before
        for pair, out in enumerate(outs):
            out[0] = out[0] + coef(pair, order) * current
            out[1] = out[1] + coef(pair, TERMS + order) * current
    return outs


def near_slopes(s, coef_ref, pairs):
    def coef(pair, row):
        return coef_ref[pair, row : row + 1, :]

    twice = s + s
    before, current = jnp.ones_like(s), twice
    outs = [[coef(p, k) + coef(p, k + 1) * twice for k in (1, TERMS + 1)] for p in range(pairs)]
    for order in range(3, TERMS):
        before, current = current, twice * current - before
        for pair, out in enumerate(outs):
            out[0] = out[0] + coef(pair, order) * current
            out[1] = out[1] + coef(pair, TERMS + order) * current
    return outs


def turn_round(value):
    rows, cols = value.shape
    order = LANES - 1 - iota((rows, LANES), 1)
    parts = [
        jnp.take_along_axis(value[:, start : start + LANES], order, axis=1)
        for start in range(cols - LANES, -1, -LANES)
    ]
    return jnp.concatenate(parts, axis=1)


def block_starts(cols, index):
    return cols // 2 - (index + 1) * BLOCK, cols // 2 + index * BLOCK


def both_blocks(base_r, base_i, cent_r, cent_i):
    rr, ii = base_r * cent_r, base_i * cent_i
    ri, ir = base_r * cent_i, base_i * cent_r
    return (rr + ii, ir - ri), (rr - ii, ir + ri)


def own_waves(info_ref, pair, cols, base_ref, centre_ref):
    shift = cols // 4 + 1 - lax.axis_index("wave")
    fill_base(column_freq(info_ref, pair), shift, 256 * cols, base_ref, centre_ref)


def forward_kernel(
    wave_hbm, angle_hbm, aim_hbm, coef_hbm, width_hbm, mine_ref, info_ref, own_ref, *refs
):
    pairs = info_ref.shape[0]
    table_refs, refs = refs[:pairs], refs[pairs:]
    (
        wave_ref, angle_ref, aim_ref, coef_ref, width_ref, far_ref, base_ref, centre_ref, near_ref, acc_ref, sems,
    ) = refs
    rows_dev, cols = width_ref.shape
    half = cols // 2
    moves = [
        pltpu.make_async_copy(source, target, sems.at[index])
        for index, (source, target) in enumerate((
            (wave_hbm, wave_ref), (angle_hbm, angle_ref), (aim_hbm, aim_ref),
            (coef_hbm, coef_ref), (width_hbm, width_ref),
        ))
    ]
    for move in moves:
        move.start()
    for move in moves[:4]:
        move.wait()
    for pair in range(pairs):
        coef = pick_coef(coef_ref[...], wave_ref[pair])
        info_ref[pair, :WAVE_ROW, :] = jnp.broadcast_to(coef, (WAVE_ROW, FOCAL))
        row = iota((INFO_ROWS - WAVE_ROW, FOCAL), 0) + WAVE_ROW
        ids = jnp.where(row == WAVE_ROW, wave_ref[pair], 0)
        ids = jnp.where(row == ANGLE_ROW, angle_ref[pair], ids)
        ids = jnp.where(row == AIM_ROW, aim_ref[pair, 0], ids)
        ids = jnp.where(row == AIM_ROW + 1, aim_ref[pair, 1], ids)
        info_ref[pair, WAVE_ROW:, :] = ids.astype(jnp.float32)
    for pair in range(pairs):
        own_waves(info_ref, pair, cols, base_ref.at[pair], centre_ref.at[pair])
    acc_ref[...] = jnp.zeros_like(acc_ref)
    moves[4].wait()
    core = lax.axis_index("wave")

    @pl.when(core == 1)
    def _():
        own_ref[...] = width_ref[:, half:]
        far_ref[...] = pltpu.roll(turn_round(width_ref[:, :half]), 1, 1)

    @pl.when(core == 0)
    def _():
        own_ref[...] = turn_round(width_ref[:, :half])
        far_ref[...] = pltpu.roll(width_ref[:, half:], half - 1, 1)

    void = jnp.where(core == 1, 0, half - 1)
    for index in range(half // (2 * BLOCK)):
        starts = block_starts(half, index)
        for start in (start + step for start in starts for step in range(0, BLOCK, LANES)):
            for side, ref in enumerate((own_ref, far_ref)):
                outs = near_fields(ref[:, start : start + LANES], info_ref, pairs)
                if side and start in (0, half - LANES):
                    keep = iota((rows_dev, LANES), 1) + start != void
                    outs = [[jnp.where(keep, part, 0.0) for part in out] for out in outs]
                for pair, part in ((pair, part) for pair in range(pairs) for part in range(2)):
                    row = (2 * side + part) * rows_dev
                    near_ref[pair, row : row + rows_dev, start : start + LANES] = outs[pair][part].astype(jnp.bfloat16)
        for pair in range(pairs):
            cent_r, cent_i = (centre_ref[pair, part, index : index + 1, :] for part in range(2))
            for row in range(0, BLOCK, GRAIN):
                base_r, base_i = (base_ref[pair, part, row : row + GRAIN, :] for part in range(2))
                for start, table in zip(starts, both_blocks(base_r, base_i, cent_r, cent_i)):
                    rows = slice(start + row, start + row + GRAIN)
                    table_refs[pair][rows, :FOCAL] = table[0].astype(jnp.bfloat16)
                    table_refs[pair][rows, FOCAL:] = table[1].astype(jnp.bfloat16)
            acc_ref[pair] += jnp.dot(
                jnp.concatenate([near_ref[pair, :, start : start + BLOCK] for start in starts], axis=1),
                jnp.concatenate([table_refs[pair][start : start + BLOCK, :] for start in starts], axis=0),
                preferred_element_type=jnp.float32,
            )
    alone = jnp.where(core == 1, 0, half)
    column = width_ref[:, pl.ds(pl.multiple_of(alone, LANES), LANES)]
    columns = near_fields(column, info_ref, pairs)
    for pair in range(pairs):
        acc = [acc_ref[pair, part * rows_dev : (part + 1) * rows_dev, :] for part in range(4)]
        (own_rr, own_ri), (own_ir, own_ii), (far_rr, far_ri), (far_ir, far_ii) = (
            (part[:, :FOCAL], part[:, FOCAL:]) for part in acc
        )
        cross_r, cross_i = far_ii - own_ii, own_ri - far_ri
        real = own_rr + far_rr + jnp.where(core == 1, cross_r, -cross_r)
        imag = own_ir + far_ir + jnp.where(core == 1, cross_i, -cross_i)
        near_r, near_i = (part[:, :1].astype(jnp.bfloat16).astype(jnp.float32) for part in columns[pair])
        wave_r, wave_i = (
            part.astype(jnp.bfloat16).astype(jnp.float32)
            for part in unit_waves((alone - half) * column_freq(info_ref, pair), 256 * cols)
        )
        real = real + (near_r * wave_r - near_i * wave_i)
        imag = imag + (near_r * wave_i + near_i * wave_r)
        for part, value in enumerate((real, imag)):
            lane = (2 * pair + part) * FOCAL
            mine_ref[:, lane : lane + FOCAL] = value.astype(jnp.bfloat16)


def spot_rows(info_ref, pair, first):
    aims = [info_ref[pair, row : row + 1, :] for row in (AIM_ROW, AIM_ROW + 1)]
    rows_off = (iota((PIECE, FOCAL), 0) + first).astype(jnp.float32) - aims[0]
    cols_off = iota((1, FOCAL), 1).astype(jnp.float32) - aims[1]
    return jnp.exp(-(rows_off * rows_off + cols_off * cols_off) / (2.0 * SPOT * SPOT))


def total_of(value):
    return jnp.sum(jnp.sum(value, axis=0, keepdims=True), axis=1, keepdims=True)


def row_kernel(info_ref, tall_ref, flat_ref, spot_ref, gain_ref):
    pairs, _, rows = tall_ref.shape
    rows_dev = flat_ref.shape[1]
    period = 256 * rows
    size = min(rows, FOCAL)
    for pair in range(pairs):
        wave = info_ref[pair, WAVE_ROW : WAVE_ROW + 1, :].astype(jnp.int32) + BLOCK
        focal = (iota((FOCAL, 1), 0) - FOCAL // 2) * wave

        def step(index, carry):
            start = pl.multiple_of(index * size, size)
            place = iota((1, size), 1) + (start - rows // 2)
            for row in range(0, FOCAL, PIECE):
                real, imag = unit_waves(focal[row : row + PIECE, :size] * place, period)
                tall_ref[pair, row : row + PIECE, pl.ds(start, size)] = real.astype(jnp.bfloat16)
                row += FOCAL
                tall_ref[pair, row : row + PIECE, pl.ds(start, size)] = imag.astype(jnp.bfloat16)
            return carry

        if rows == size:
            step(0, 0)
        else:
            lax.fori_loop(0, rows // size, step, 0)
        focal = (iota((1, FOCAL), 1) - FOCAL // 2) * wave
        first = lax.axis_index("aperture") * rows_dev - rows // 2
        real, imag = unit_waves((iota((rows_dev, 1), 0) + first) * focal, period)
        flat_ref[pair, :, :FOCAL] = real.astype(jnp.bfloat16)
        flat_ref[pair, :, FOCAL:] = imag.astype(jnp.bfloat16)
        total = jnp.zeros((PIECE, FOCAL), jnp.float32)
        for row in range(0, FOCAL, PIECE):
            spot = spot_rows(info_ref, pair, row)
            spot_ref[pair, row : row + PIECE, :] = spot
            total += spot
        gain_ref[pair] = jnp.broadcast_to(FOCAL * FOCAL / total_of(total), gain_ref.shape[1:])


def join_kernel(*refs):
    *in_refs, out_ref = refs
    count = in_refs[0].shape[0]
    for index, ref in enumerate(in_refs):
        out_ref[index * count : (index + 1) * count, :] = ref[...]


def focus_kernel(steps, tall_ref, flat_ref, spot_ref, gain_ref, after_ref, *refs):
    del after_ref
    *sect_refs, back_ref, score_ref, rows_ref, mixed_ref, field_ref, stack_ref = refs
    pairs = tall_ref.shape[0]
    rows_dev = back_ref.shape[0]
    if steps is None:
        rows_ref = sect_refs[0]
    else:
        me = lax.axis_index("aperture")
        blocks = [
            ref[index * rows_dev : (index + 1) * rows_dev, :]
            for ref in sect_refs
            for index in range(ref.shape[0] // rows_dev)
        ]
        for step, block in zip(steps, blocks, strict=True):
            start = pl.multiple_of((me ^ step) * rows_dev, rows_dev)
            rows_ref[pl.ds(start, rows_dev), :] = block
    for pair in range(pairs):
        lane = 2 * pair * FOCAL
        section = rows_ref[:, lane : lane + 2 * FOCAL]
        mixed_ref[pair] = jnp.dot(tall_ref[pair], section, preferred_element_type=jnp.float32)
    pieces = [slice(row, row + PIECE) for row in range(0, FOCAL, PIECE)]
    sums = []
    for pair in range(pairs):
        totals = [jnp.zeros((PIECE, FOCAL), jnp.float32) for _ in range(2)]
        for rows in pieces:
            lower = slice(rows.start + FOCAL, rows.stop + FOCAL)
            real = mixed_ref[pair, rows, :FOCAL] - mixed_ref[pair, lower, FOCAL:]
            imag = mixed_ref[pair, rows, FOCAL:] + mixed_ref[pair, lower, :FOCAL]
            field_ref[pair, 0, rows, :] = real
            field_ref[pair, 1, rows, :] = imag
            power = real * real + imag * imag
            totals = [totals[0] + spot_ref[pair, rows, :] * power, totals[1] + power]
        sums.append((total_of(totals[0]), total_of(totals[1]) + 1e-06))
    for pair, (spot_power, all_power) in enumerate(sums):
        ratio = spot_power / all_power
        gain = gain_ref[pair, :1, :1]
        score_ref[pair] = jnp.sum(ratio * gain)
        scale = gain * 2.0 / all_power
        for rows in pieces:
            lower = slice(rows.start + FOCAL, rows.stop + FOCAL)
            weight = scale * (spot_ref[pair, rows, :] - ratio)
            real = (weight * field_ref[pair, 0, rows, :]).astype(jnp.bfloat16)
            imag = (weight * field_ref[pair, 1, rows, :]).astype(jnp.bfloat16)
            stack_ref[pair, rows, :FOCAL] = real
            stack_ref[pair, rows, FOCAL:] = imag
            stack_ref[pair, lower, :FOCAL] = imag
            stack_ref[pair, lower, FOCAL:] = -real
        back = jnp.dot(flat_ref[pair], stack_ref[pair], preferred_element_type=jnp.float32)
        lane = 2 * pair * FOCAL
        back_ref[:, lane : lane + 2 * FOCAL] = back.astype(jnp.bfloat16)


def table_kernel(scale, cols, info_ref, far_info_ref, width_ref, *refs):
    *out_refs, base_ref, centre_ref, turned_ref, coef_ref = refs
    pairs = base_ref.shape[0]
    out_refs = out_refs[-3 * pairs :]
    table_refs, slope_refs = out_refs[:pairs], out_refs[pairs:]
    own_cols = width_ref.shape[1]
    for core, ref in enumerate((info_ref, far_info_ref)):
        for pair in range(pairs):
            coef = ref[pair, : 2 * TERMS, :LANES]
            coef_ref[core * pairs + pair] = coef * ((iota(coef.shape, 0) % TERMS).astype(jnp.float32) * scale)
    centres = []
    for pair in range(pairs):
        own_waves(far_info_ref, pair, cols, base_ref.at[pair], centre_ref.at[pair])
        for part, row, lane in itertools.product(range(2), range(0, BLOCK, LANES), range(0, FOCAL, LANES)):
            tile = base_ref[pair, part, row : row + LANES, lane : lane + LANES]
            turned_ref[pair, part, lane : lane + LANES, row : row + LANES] = tile.T
        centres.append([centre_ref[pair, part].T for part in range(2)])
    for index in range(own_cols // (2 * BLOCK)):
        starts = block_starts(own_cols, index)
        for pair in range(pairs):
            for row in range(0, FOCAL, GRAIN):
                rows = slice(row, row + GRAIN)
                cent_r, cent_i = (centre[rows, index : index + 1] for centre in centres[pair])
                base_r, base_i = (turned_ref[pair, part, rows, :] for part in range(2))
                for start, table in zip(starts, both_blocks(base_r, base_i, cent_r, cent_i)):
                    for part, value in enumerate(table):
                        place = slice(row + part * FOCAL, row + part * FOCAL + GRAIN)
                        table_refs[pair][place, start : start + BLOCK] = value.astype(jnp.bfloat16)
        for start in (start + step for start in starts for step in range(0, BLOCK, LANES)):
            place = slice(start, start + LANES)
            slopes = near_slopes(width_ref[:, place], coef_ref, 2 * pairs)
            for ref, slope in zip(slope_refs, slopes):
                ref[0, :, place] = slope[0]
                ref[1, :, place] = slope[1]


def last_grad_kernel(pairs, *refs):
    *in_refs, out_hbm, out_ref, sems = refs
    rows_dev, own_cols = out_ref.shape
    size = 2 * BLOCK
    core = lax.axis_index("wave")
    moves = []

    def send(start, total):
        place = pl.multiple_of(jnp.where(core == 1, start, own_cols - size - start), size)
        place = pl.ds(place, size)
        out_ref[:, place] = jnp.where(core == 1, total, turn_round(total))
        index = start // size
        moves.append(pltpu.make_async_copy(out_ref.at[:, place], out_hbm.at[:, place], sems.at[index]))
        moves[-1].start()

    grad_kernel(pairs, *in_refs, out_ref, send=send)
    for move in moves:
        move.wait()


def grad_kernel(pairs, back_ref, *refs, send=None, across=True):
    *in_refs, out_ref = refs
    table_refs, slope_refs, total_ref = in_refs[:pairs], in_refs[pairs : 2 * pairs], in_refs[2 * pairs :]
    rows_dev, own_cols = out_ref.shape
    core = lax.axis_index("wave")
    lefts = []
    for pair in range(pairs):
        lane = 2 * pair * FOCAL
        real, imag = back_ref[:, lane : lane + FOCAL], back_ref[:, lane + FOCAL : lane + 2 * FOCAL]
        above = jnp.where(core == 1, imag, -imag)
        below = jnp.where(core == 1, -real, real)
        lefts.append(
            jnp.concatenate(
                [jnp.concatenate([real, above], axis=1), jnp.concatenate([imag, below], axis=1)], axis=0
            )
        )
    size = 2 * BLOCK
    for start in range(0, own_cols, size):
        place = slice(start, start + size)
        total = total_ref[0][:, place] if total_ref else jnp.zeros((rows_dev, size), jnp.float32)
        for pair in range(pairs):
            if across:
                table, dims = table_refs[pair][:, place], ((1,), (0,))
            else:
                table, dims = table_refs[pair][place, :], ((1,), (1,))
            grad = lax.dot_general(lefts[pair], table, (dims, ((), ())), preferred_element_type=jnp.float32)
            total += grad[:rows_dev] * slope_refs[pair][0, :, place]
            total += grad[rows_dev:] * slope_refs[pair][1, :, place]
        if send is None:
            out_ref[:, place] = total
        else:
            send(start, total)


VMEM = pl.BlockSpec(memory_space=pltpu.VMEM)
SMEM = pl.BlockSpec(memory_space=pltpu.SMEM)
ANY = pl.BlockSpec(memory_space=pl.ANY)
HBM = pl.BlockSpec(memory_space=pltpu.HBM)


def call(kernel, name, outs, in_specs, out_specs, scratch, flops, moved):
    return pl.pallas_call(
        kernel,
        name=name,
        out_shape=outs,
        in_specs=in_specs,
        out_specs=out_specs,
        scratch_shapes=scratch,
        cost_estimate=pl.CostEstimate(flops=flops, bytes_accessed=moved, transcendentals=0),
        compiler_params=pltpu.CompilerParams(vmem_limit_bytes=VMEM_LIMIT),
    )


def on_device(widths, coef_table, wave_ids, angle_ids, targets):
    rows_dev, cols = widths.shape
    pairs_dev = wave_ids.shape[0]
    peers = lax.axis_size("aperture")
    copies = lax.axis_size("wave")
    rows = rows_dev * peers
    own_cols = cols // copies
    lanes = 2 * pairs_dev * FOCAL
    f32, bf16 = jnp.float32, jnp.bfloat16
    shape = jax.ShapeDtypeStruct

    def in_hbm(value):
        return pltpu.with_memory_space_constraint(value, pltpu.HBM)

    def exchange(value, step):
        return lax.ppermute(value, "aperture", [(index, index ^ step) for index in range(peers)])

    def to_core(value):
        return lax.ppermute(value, "wave", [(index, (index + 1) % copies) for index in range(copies)])

    waves = [
        pltpu.VMEM((pairs_dev, 2, BLOCK, FOCAL), f32),
        pltpu.VMEM((pairs_dev, 2, 8, FOCAL), f32),
    ]
    mine, info, own, *tables = call(
        forward_kernel, "forward",
        (
            shape((rows_dev, lanes), bf16),
            shape((pairs_dev, INFO_ROWS, FOCAL), f32), shape((rows_dev, own_cols), f32),
            *[shape((own_cols, 2 * FOCAL), bf16)] * pairs_dev,
        ),
        [HBM] * 5, (VMEM,) * (3 + pairs_dev),
        [
            pltpu.SMEM(wave_ids.shape, jnp.int32),
            pltpu.SMEM(angle_ids.shape, jnp.int32),
            pltpu.SMEM(targets.shape, jnp.int32),
            pltpu.VMEM(coef_table.shape[::-1], f32),
            pltpu.VMEM(widths.shape, f32),
            pltpu.VMEM((rows_dev, own_cols), f32),
            *waves,
            pltpu.VMEM((pairs_dev, 4 * rows_dev, own_cols), bf16),
            pltpu.VMEM((pairs_dev, 4 * rows_dev, 2 * FOCAL), f32),
            pltpu.SemaphoreType.DMA((5,)),
        ],
        10**9, 10**7,
    )(*(in_hbm(value) for value in (wave_ids, angle_ids, targets, coef_table.T, widths)))
    far_info = to_core(info)

    tall, flat, spots, gains = call(
        row_kernel, "row_tables",
        (
            shape((pairs_dev, 2 * FOCAL, rows), bf16), shape((pairs_dev, rows_dev, 2 * FOCAL), bf16),
            shape((pairs_dev, FOCAL, FOCAL), f32), shape((pairs_dev, 8, 128), f32),
        ),
        [VMEM], (VMEM,) * 4, [], 10**8, 10**6,
    )(info)
    if peers <= DIRECT:
        steps = list(range(peers - 2, 0, -2))
        got = [exchange(mine, step) for step in steps]
        near = exchange(mine, 1)
        first, flat = lax.optimization_barrier((got[0], flat))
        joined = call(join_kernel, "join", shape(((len(steps) - 1) * rows_dev, lanes), bf16),
                      [VMEM] * (len(steps) - 1), VMEM, [], 10**6, 10**6)(*got[1:])
        sections = [mine, near, first, joined, exchange(first, 1), exchange(joined, 1)]
        steps = [0, 1, *steps, *(step ^ 1 for step in steps)]
        after = [near, joined]
    else:
        blocks = jnp.tile(mine[None], (peers, 1, 1))
        blocks = lax.all_to_all(blocks, "aperture", 0, 0, tiled=True)
        sections, steps, after = [blocks.reshape(rows, lanes)], None, []
    outs = [shape((2 * FOCAL, own_cols), bf16)] * pairs_dev + [shape((2, rows_dev, own_cols), f32)] * 2 * pairs_dev
    made = call(
        functools.partial(table_kernel, math.sqrt(rows * cols), cols), "far_tables",
        outs, [VMEM] * 3 + [ANY] * len(after), [VMEM] * len(outs),
        [*waves, pltpu.VMEM((pairs_dev, 2, FOCAL, BLOCK), f32), pltpu.VMEM((copies * pairs_dev, 2 * TERMS, LANES), f32)],
        30 * 10**8, 30 * 10**6,
    )(info, far_info, own, *after)
    far_tables, slopes, far_slopes = made[:pairs_dev], made[pairs_dev : 2 * pairs_dev], made[2 * pairs_dev :]

    back, scores = call(
        functools.partial(focus_kernel, steps), "focus",
        (shape((rows_dev, lanes), bf16), shape((pairs_dev,), f32)),
        [VMEM] * 4 + [ANY] + [VMEM] * len(sections), (VMEM, SMEM),
        [
            pltpu.VMEM((rows, lanes), bf16),
            pltpu.VMEM((pairs_dev, 2 * FOCAL, 2 * FOCAL), f32),
            pltpu.VMEM((pairs_dev, 2, FOCAL, FOCAL), f32),
            pltpu.VMEM((pairs_dev, 2 * FOCAL, 2 * FOCAL), bf16),
        ],
        10**8, 10**6,
    )(tall, flat, spots, gains, far_slopes[0], *sections)

    out = shape((rows_dev, own_cols), f32)
    ins = [back, *tables, *slopes]
    grad = call(
        functools.partial(grad_kernel, pairs_dev, across=False), "gradient_own",
        out, [VMEM] * len(ins), VMEM, [], 10**9, 10**7,
    )(*ins)
    ins = [to_core(back), *far_tables, *far_slopes, grad]
    grad = call(
        functools.partial(last_grad_kernel, pairs_dev), "gradient_far",
        out, [VMEM] * len(ins), HBM,
        [pltpu.VMEM(out.shape, f32), pltpu.SemaphoreType.DMA((own_cols // (2 * BLOCK),))], 10**9, 10**7,
    )(*ins)
    return grad, scores


def solution(mesh):
    in_specs = (
        P(("group", "aperture"), None),
        P(),
        P(("group", "wave")),
        P(("group", "wave")),
        P(("group", "wave"), None),
    )
    out_specs = (P(("group", "aperture"), "wave"), P(("group", "wave")))
    return jax.shard_map(
        on_device, mesh=mesh, in_specs=in_specs, out_specs=out_specs, check_vma=False
    )
```

```python
import functools
import itertools
import math

import jax
import jax.numpy as jnp
from jax import lax
from jax.experimental import pallas as pl
from jax.experimental.pallas import tpu as pltpu
from jax.sharding import PartitionSpec as P

FOCAL = 256
SPOT = 4
SHIFT = 32
TERMS = 8
BLOCK = 256
GRAIN = 16
LANES = 128
PIECE = 16
VMEM_LIMIT = 16 * 1024 * 1024
WAVE_ROW, ANGLE_ROW, AIM_ROW, INFO_ROWS = 16, 17, 18, 24
DIRECT = 16

COS = (
    1.0, -19.7392088015709, 64.93939395773512, -85.45681453397417, 60.24458621302471,
    -26.425616460281425, 7.8991596631575085, -1.6968741456712442, 0.2437618617467591,
)
SIN = (
    6.2831853071792665, -41.34170224019464, 81.60524925425943, -76.70585885700535,
    42.05867547580699, -15.094428387947755, 3.818490079304055, -0.7122771247541972,
    0.09149844789363434,
)


def horner(terms, u):
    value = terms[-1] * u + terms[-2]
    for term in terms[-3::-1]:
        value = value * u + term
    return value


def unit_waves(counts, period):
    half = period // 2
    centred = ((counts + half) & (period - 1)) - half
    t = centred.astype(jnp.float32) * (1.0 / period)
    u = t * t
    return horner(COS, u), -(t * horner(SIN, u))


def iota(shape, axis):
    return lax.broadcasted_iota(jnp.int32, shape, axis)


def pick_coef(table, wave):
    chosen = jnp.where(iota(table.shape, 1) == wave, table, 0.0)
    return jnp.sum(chosen, axis=1, keepdims=True)


def column_freq(info_ref, pair):
    wave = info_ref[pair, WAVE_ROW : WAVE_ROW + 1, :].astype(jnp.int32)
    angle = info_ref[pair, ANGLE_ROW : ANGLE_ROW + 1, :].astype(jnp.int32)
    return (iota((1, FOCAL), 1) - FOCAL // 2 + SHIFT * angle) * (BLOCK + wave)


def fill_base(freq, shift, period, base_ref, centre_ref):
    low_r, low_i = unit_waves(iota((GRAIN, 1), 0) * freq, period)
    steps = BLOCK // GRAIN
    high_r, high_i = unit_waves((iota((steps, 1), 0) * GRAIN - BLOCK // 2 + shift) * freq, period)
    for step in range(steps):
        one_r, one_i = high_r[step : step + 1], high_i[step : step + 1]
        rows = slice(step * GRAIN, (step + 1) * GRAIN)
        base_ref[0, rows, :] = one_r * low_r - one_i * low_i
        base_ref[1, rows, :] = one_r * low_i + one_i * low_r
    count = centre_ref.shape[1]
    cent_r, cent_i = unit_waves((iota((count, 1), 0) * BLOCK + BLOCK // 2) * freq, period)
    centre_ref[0] = cent_r
    centre_ref[1] = cent_i


def power_coefs(coef):
    before, current = [1], [0, 1]
    bases = [before, current]
    for _ in range(2, TERMS):
        doubled = [0] + [2 * term for term in current]
        before, current = current, [a - b for a, b in itertools.zip_longest(doubled, before, fillvalue=0)]
        bases.append(current)
    rows = []
    for part, power in itertools.product(range(2), range(TERMS)):
        row = None
        for order in range(power, TERMS, 2):
            place = part * TERMS + order
            term = coef[place : place + 1] * float(bases[order][power])
            row = term if row is None else row + term
        rows.append(row)
    return jnp.concatenate(rows, axis=0)


def near_fields(s, power_ref, pairs):
    outs = []
    for pair, part in itertools.product(range(pairs), range(2)):
        row = (part + 1) * TERMS - 1
        value = power_ref[pair, row : row + 1, :] * s + power_ref[pair, row - 1 : row, :]
        for row in range(row - 2, part * TERMS - 1, -1):
            value = value * s + power_ref[pair, row : row + 1, :]
        outs.append(value)
    return [outs[2 * pair : 2 * pair + 2] for pair in range(pairs)]


def near_slopes(s, coef_ref, pairs):
    def coef(pair, row):
        return coef_ref[pair, row : row + 1, :]

    twice = s + s
    before, current = jnp.ones_like(s), twice
    outs = [[coef(p, k) + coef(p, k + 1) * twice for k in (1, TERMS + 1)] for p in range(pairs)]
    for order in range(3, TERMS):
        before, current = current, twice * current - before
        for pair, out in enumerate(outs):
            out[0] = out[0] + coef(pair, order) * current
            out[1] = out[1] + coef(pair, TERMS + order) * current
    return outs


def turn_round(value):
    rows, cols = value.shape
    order = LANES - 1 - iota((rows, LANES), 1)
    parts = [
        jnp.take_along_axis(value[:, start : start + LANES], order, axis=1)
        for start in range(cols - LANES, -1, -LANES)
    ]
    return jnp.concatenate(parts, axis=1)


def block_starts(cols, index):
    return cols // 2 - (index + 1) * BLOCK, cols // 2 + index * BLOCK


def both_blocks(base_r, base_i, cent_r, cent_i):
    rr, ii = base_r * cent_r, base_i * cent_i
    ri, ir = base_r * cent_i, base_i * cent_r
    return (rr + ii, ir - ri), (rr - ii, ir + ri)


def own_waves(info_ref, pair, cols, base_ref, centre_ref):
    shift = cols // 4 + 1 - lax.axis_index("wave")
    fill_base(column_freq(info_ref, pair), shift, 256 * cols, base_ref, centre_ref)


def forward_kernel(
    wave_hbm, angle_hbm, aim_hbm, coef_hbm, width_hbm, mine_ref, info_ref, own_ref, *refs
):
    pairs = info_ref.shape[0]
    table_refs, refs = refs[:pairs], refs[pairs:]
    (
        wave_ref, angle_ref, aim_ref, coef_ref, width_ref, far_ref, base_ref, centre_ref, power_ref, near_ref, acc_ref,
        sems,
    ) = refs
    rows_dev, cols = width_ref.shape
    half = cols // 2
    moves = [
        pltpu.make_async_copy(source, target, sems.at[index])
        for index, (source, target) in enumerate((
            (wave_hbm, wave_ref), (angle_hbm, angle_ref), (aim_hbm, aim_ref),
            (coef_hbm, coef_ref), (width_hbm, width_ref),
        ))
    ]
    for move in moves:
        move.start()
    for move in moves:
        move.wait()
    for pair in range(pairs):
        coef = pick_coef(coef_ref[...], wave_ref[pair])
        coef = jnp.broadcast_to(coef, (WAVE_ROW, FOCAL))
        info_ref[pair, :WAVE_ROW, :] = coef
        power_ref[pair] = power_coefs(coef[:, :LANES])
        row = iota((INFO_ROWS - WAVE_ROW, FOCAL), 0) + WAVE_ROW
        ids = jnp.where(row == WAVE_ROW, wave_ref[pair], 0)
        ids = jnp.where(row == ANGLE_ROW, angle_ref[pair], ids)
        ids = jnp.where(row == AIM_ROW, aim_ref[pair, 0], ids)
        ids = jnp.where(row == AIM_ROW + 1, aim_ref[pair, 1], ids)
        info_ref[pair, WAVE_ROW:, :] = ids.astype(jnp.float32)
    for pair in range(pairs):
        own_waves(info_ref, pair, cols, base_ref.at[pair], centre_ref.at[pair])
    core = lax.axis_index("wave")
    left, right = turn_round(width_ref[:, :half]), width_ref[:, half:]
    own_ref[...] = jnp.where(core == 1, right, left)
    far_ref[...] = jnp.where(core == 1, pltpu.roll(left, 1, 1), pltpu.roll(right, half - 1, 1))

    void = jnp.where(core == 1, 0, half - 1)
    for index in range(half // (2 * BLOCK)):
        starts = block_starts(half, index)
        for start in (start + step for start in starts for step in range(0, BLOCK, LANES)):
            for side, ref in enumerate((own_ref, far_ref)):
                outs = near_fields(ref[:, start : start + LANES], power_ref, pairs)
                if side and start in (0, half - LANES):
                    keep = iota((rows_dev, LANES), 1) + start != void
                    outs = [[jnp.where(keep, part, 0.0) for part in out] for out in outs]
                for pair, part in ((pair, part) for pair in range(pairs) for part in range(2)):
                    row = (2 * side + part) * rows_dev
                    near_ref[pair, row : row + rows_dev, start : start + LANES] = outs[pair][part].astype(jnp.bfloat16)
        for pair in range(pairs):
            cent_r, cent_i = (centre_ref[pair, part, index : index + 1, :] for part in range(2))
            for row in range(0, BLOCK, GRAIN):
                base_r, base_i = (base_ref[pair, part, row : row + GRAIN, :] for part in range(2))
                for start, table in zip(starts, both_blocks(base_r, base_i, cent_r, cent_i)):
                    rows = slice(start + row, start + row + GRAIN)
                    table_refs[pair][rows, :FOCAL] = table[0].astype(jnp.bfloat16)
                    table_refs[pair][rows, FOCAL:] = table[1].astype(jnp.bfloat16)
            product = jnp.dot(
                jnp.concatenate([near_ref[pair, :, start : start + BLOCK] for start in starts], axis=1),
                jnp.concatenate([table_refs[pair][start : start + BLOCK, :] for start in starts], axis=0),
                preferred_element_type=jnp.float32,
            )
            acc_ref[pair] = product if index == 0 else acc_ref[pair] + product
    alone = jnp.where(core == 1, 0, half)
    column = width_ref[:, pl.ds(pl.multiple_of(alone, LANES), LANES)]
    columns = near_fields(column, power_ref, pairs)
    for pair in range(pairs):
        acc = [acc_ref[pair, part * rows_dev : (part + 1) * rows_dev, :] for part in range(4)]
        (own_rr, own_ri), (own_ir, own_ii), (far_rr, far_ri), (far_ir, far_ii) = (
            (part[:, :FOCAL], part[:, FOCAL:]) for part in acc
        )
        cross_r, cross_i = far_ii - own_ii, own_ri - far_ri
        real = own_rr + far_rr + jnp.where(core == 1, cross_r, -cross_r)
        imag = own_ir + far_ir + jnp.where(core == 1, cross_i, -cross_i)
        near_r, near_i = (part[:, :1].astype(jnp.bfloat16).astype(jnp.float32) for part in columns[pair])
        wave_r, wave_i = (
            part.astype(jnp.bfloat16).astype(jnp.float32)
            for part in unit_waves((alone - half) * column_freq(info_ref, pair), 256 * cols)
        )
        real = real + (near_r * wave_r - near_i * wave_i)
        imag = imag + (near_r * wave_i + near_i * wave_r)
        for part, value in enumerate((real, imag)):
            lane = (2 * pair + part) * FOCAL
            mine_ref[:, lane : lane + FOCAL] = value.astype(jnp.bfloat16)


def spot_rows(info_ref, pair, first):
    aims = [info_ref[pair, row : row + 1, :] for row in (AIM_ROW, AIM_ROW + 1)]
    rows_off = (iota((PIECE, FOCAL), 0) + first).astype(jnp.float32) - aims[0]
    cols_off = iota((1, FOCAL), 1).astype(jnp.float32) - aims[1]
    return jnp.exp(-(rows_off * rows_off + cols_off * cols_off) / (2.0 * SPOT * SPOT))


def total_of(value):
    return jnp.sum(jnp.sum(value, axis=0, keepdims=True), axis=1, keepdims=True)


def row_kernel(info_ref, tall_ref, flat_ref, spot_ref, gain_ref):
    pairs, _, rows = tall_ref.shape
    rows_dev = flat_ref.shape[1]
    period = 256 * rows
    size = min(rows, FOCAL)
    for pair in range(pairs):
        wave = info_ref[pair, WAVE_ROW : WAVE_ROW + 1, :].astype(jnp.int32) + BLOCK
        focal = (iota((FOCAL, 1), 0) - FOCAL // 2) * wave

        def step(index, carry):
            start = pl.multiple_of(index * size, size)
            place = iota((1, size), 1) + (start - rows // 2)
            for row in range(0, FOCAL, PIECE):
                real, imag = unit_waves(focal[row : row + PIECE, :size] * place, period)
                tall_ref[pair, row : row + PIECE, pl.ds(start, size)] = real.astype(jnp.bfloat16)
                row += FOCAL
                tall_ref[pair, row : row + PIECE, pl.ds(start, size)] = imag.astype(jnp.bfloat16)
            return carry

        if rows == size:
            step(0, 0)
        else:
            lax.fori_loop(0, rows // size, step, 0)
        focal = (iota((1, FOCAL), 1) - FOCAL // 2) * wave
        first = lax.axis_index("aperture") * rows_dev - rows // 2
        real, imag = unit_waves((iota((rows_dev, 1), 0) + first) * focal, period)
        flat_ref[pair, :, :FOCAL] = real.astype(jnp.bfloat16)
        flat_ref[pair, :, FOCAL:] = imag.astype(jnp.bfloat16)
        total = jnp.zeros((PIECE, FOCAL), jnp.float32)
        for row in range(0, FOCAL, PIECE):
            spot = spot_rows(info_ref, pair, row)
            spot_ref[pair, row : row + PIECE, :] = spot
            total += spot
        gain_ref[pair] = jnp.broadcast_to(FOCAL * FOCAL / total_of(total), gain_ref.shape[1:])


def join_kernel(*refs):
    *in_refs, out_ref = refs
    count = in_refs[0].shape[0]
    for index, ref in enumerate(in_refs):
        out_ref[index * count : (index + 1) * count, :] = ref[...]


def focus_kernel(steps, tall_ref, flat_ref, spot_ref, gain_ref, after_ref, *refs):
    del after_ref
    *sect_refs, back_ref, score_ref, rows_ref, mixed_ref, field_ref, stack_ref = refs
    pairs = tall_ref.shape[0]
    rows_dev = back_ref.shape[0]
    if steps is None:
        rows_ref = sect_refs[0]
    else:
        me = lax.axis_index("aperture")
        blocks = [
            ref[index * rows_dev : (index + 1) * rows_dev, :]
            for ref in sect_refs
            for index in range(ref.shape[0] // rows_dev)
        ]
        for step, block in zip(steps, blocks, strict=True):
            start = pl.multiple_of((me ^ step) * rows_dev, rows_dev)
            rows_ref[pl.ds(start, rows_dev), :] = block
    for pair in range(pairs):
        lane = 2 * pair * FOCAL
        section = rows_ref[:, lane : lane + 2 * FOCAL]
        mixed_ref[pair] = jnp.dot(tall_ref[pair], section, preferred_element_type=jnp.float32)
    pieces = [slice(row, row + PIECE) for row in range(0, FOCAL, PIECE)]
    sums = []
    for pair in range(pairs):
        totals = [jnp.zeros((PIECE, FOCAL), jnp.float32) for _ in range(2)]
        for rows in pieces:
            lower = slice(rows.start + FOCAL, rows.stop + FOCAL)
            real = mixed_ref[pair, rows, :FOCAL] - mixed_ref[pair, lower, FOCAL:]
            imag = mixed_ref[pair, rows, FOCAL:] + mixed_ref[pair, lower, :FOCAL]
            field_ref[pair, 0, rows, :] = real
            field_ref[pair, 1, rows, :] = imag
            power = real * real + imag * imag
            totals = [totals[0] + spot_ref[pair, rows, :] * power, totals[1] + power]
        sums.append((total_of(totals[0]), total_of(totals[1]) + 1e-06))
    for pair, (spot_power, all_power) in enumerate(sums):
        ratio = spot_power / all_power
        gain = gain_ref[pair, :1, :1]
        score_ref[pair] = jnp.sum(ratio * gain)
        scale = gain * 2.0 / all_power
        for rows in pieces:
            weight = scale * (spot_ref[pair, rows, :] - ratio)
            stack_ref[pair, rows, :FOCAL] = (weight * field_ref[pair, 0, rows, :]).astype(jnp.bfloat16)
            stack_ref[pair, rows, FOCAL:] = (weight * field_ref[pair, 1, rows, :]).astype(jnp.bfloat16)
        flat = jnp.concatenate([flat_ref[pair, :, :FOCAL], flat_ref[pair, :, FOCAL:]], axis=0)
        back = jnp.dot(flat, stack_ref[pair], preferred_element_type=jnp.float32)
        real = back[:rows_dev, :FOCAL] + back[rows_dev:, FOCAL:]
        imag = back[:rows_dev, FOCAL:] - back[rows_dev:, :FOCAL]
        lane = 2 * pair * FOCAL
        back_ref[:, lane : lane + FOCAL] = real.astype(jnp.bfloat16)
        back_ref[:, lane + FOCAL : lane + 2 * FOCAL] = imag.astype(jnp.bfloat16)


def table_kernel(scale, cols, info_ref, far_info_ref, width_ref, *refs):
    *out_refs, base_ref, centre_ref, turned_ref, coef_ref = refs
    pairs = base_ref.shape[0]
    out_refs = out_refs[-3 * pairs :]
    table_refs, slope_refs = out_refs[:pairs], out_refs[pairs:]
    own_cols = width_ref.shape[1]
    for core, ref in enumerate((info_ref, far_info_ref)):
        for pair in range(pairs):
            coef = ref[pair, : 2 * TERMS, :LANES]
            coef_ref[core * pairs + pair] = coef * ((iota(coef.shape, 0) % TERMS).astype(jnp.float32) * scale)
    centres = []
    for pair in range(pairs):
        own_waves(far_info_ref, pair, cols, base_ref.at[pair], centre_ref.at[pair])
        for part, row, lane in itertools.product(range(2), range(0, BLOCK, LANES), range(0, FOCAL, LANES)):
            tile = base_ref[pair, part, row : row + LANES, lane : lane + LANES]
            turned_ref[pair, part, lane : lane + LANES, row : row + LANES] = tile.T
        centres.append([centre_ref[pair, part].T for part in range(2)])
    for index in range(own_cols // (2 * BLOCK)):
        starts = block_starts(own_cols, index)
        for pair in range(pairs):
            for row in range(0, FOCAL, GRAIN):
                rows = slice(row, row + GRAIN)
                cent_r, cent_i = (centre[rows, index : index + 1] for centre in centres[pair])
                base_r, base_i = (turned_ref[pair, part, rows, :] for part in range(2))
                for start, table in zip(starts, both_blocks(base_r, base_i, cent_r, cent_i)):
                    for part, value in enumerate(table):
                        place = slice(row + part * FOCAL, row + part * FOCAL + GRAIN)
                        table_refs[pair][place, start : start + BLOCK] = value.astype(jnp.bfloat16)
        for start in (start + step for start in starts for step in range(0, BLOCK, LANES)):
            place = slice(start, start + LANES)
            slopes = near_slopes(width_ref[:, place], coef_ref, 2 * pairs)
            for ref, slope in zip(slope_refs, slopes):
                ref[0, :, place] = slope[0]
                ref[1, :, place] = slope[1]


def last_grad_kernel(pairs, *refs):
    *in_refs, out_hbm, out_ref, sems = refs
    rows_dev, own_cols = out_ref.shape
    size = 2 * BLOCK
    core = lax.axis_index("wave")
    moves = []

    def send(start, total):
        place = pl.multiple_of(jnp.where(core == 1, start, own_cols - size - start), size)
        place = pl.ds(place, size)
        out_ref[:, place] = jnp.where(core == 1, total, turn_round(total))
        index = start // size
        moves.append(pltpu.make_async_copy(out_ref.at[:, place], out_hbm.at[:, place], sems.at[index]))
        moves[-1].start()

    grad_kernel(pairs, *in_refs, out_ref, send=send)
    for move in moves:
        move.wait()


def grad_kernel(pairs, back_ref, *refs, send=None, across=True):
    *in_refs, out_ref = refs
    table_refs, slope_refs, total_ref = in_refs[:pairs], in_refs[pairs : 2 * pairs], in_refs[2 * pairs :]
    rows_dev, own_cols = out_ref.shape
    core = lax.axis_index("wave")
    lefts = []
    for pair in range(pairs):
        lane = 2 * pair * FOCAL
        real, imag = back_ref[:, lane : lane + FOCAL], back_ref[:, lane + FOCAL : lane + 2 * FOCAL]
        above = jnp.where(core == 1, imag, -imag)
        below = jnp.where(core == 1, -real, real)
        lefts.append(
            jnp.concatenate(
                [jnp.concatenate([real, above], axis=1), jnp.concatenate([imag, below], axis=1)], axis=0
            )
        )
    size = 2 * BLOCK
    for start in range(0, own_cols, size):
        place = slice(start, start + size)
        total = total_ref[0][:, place] if total_ref else jnp.zeros((rows_dev, size), jnp.float32)
        for pair in range(pairs):
            if across:
                table, dims = table_refs[pair][:, place], ((1,), (0,))
            else:
                table, dims = table_refs[pair][place, :], ((1,), (1,))
            grad = lax.dot_general(lefts[pair], table, (dims, ((), ())), preferred_element_type=jnp.float32)
            total += grad[:rows_dev] * slope_refs[pair][0, :, place]
            total += grad[rows_dev:] * slope_refs[pair][1, :, place]
        if send is None:
            out_ref[:, place] = total
        else:
            send(start, total)


VMEM = pl.BlockSpec(memory_space=pltpu.VMEM)
SMEM = pl.BlockSpec(memory_space=pltpu.SMEM)
ANY = pl.BlockSpec(memory_space=pl.ANY)
HBM = pl.BlockSpec(memory_space=pltpu.HBM)


def call(kernel, name, outs, in_specs, out_specs, scratch, flops, moved):
    return pl.pallas_call(
        kernel,
        name=name,
        out_shape=outs,
        in_specs=in_specs,
        out_specs=out_specs,
        scratch_shapes=scratch,
        cost_estimate=pl.CostEstimate(flops=flops, bytes_accessed=moved, transcendentals=0),
        compiler_params=pltpu.CompilerParams(vmem_limit_bytes=VMEM_LIMIT),
    )


def on_device(widths, coef_table, wave_ids, angle_ids, targets):
    rows_dev, cols = widths.shape
    pairs_dev = wave_ids.shape[0]
    peers = lax.axis_size("aperture")
    copies = lax.axis_size("wave")
    rows = rows_dev * peers
    own_cols = cols // copies
    lanes = 2 * pairs_dev * FOCAL
    f32, bf16 = jnp.float32, jnp.bfloat16
    shape = jax.ShapeDtypeStruct

    def in_hbm(value):
        return pltpu.with_memory_space_constraint(value, pltpu.HBM)

    def exchange(value, step):
        return lax.ppermute(value, "aperture", [(index, index ^ step) for index in range(peers)])

    def to_core(value):
        return lax.ppermute(value, "wave", [(index, (index + 1) % copies) for index in range(copies)])

    waves = [
        pltpu.VMEM((pairs_dev, 2, BLOCK, FOCAL), f32),
        pltpu.VMEM((pairs_dev, 2, 8, FOCAL), f32),
    ]
    mine, info, own, *tables = call(
        forward_kernel, "forward",
        (
            shape((rows_dev, lanes), bf16),
            shape((pairs_dev, INFO_ROWS, FOCAL), f32), shape((rows_dev, own_cols), f32),
            *[shape((own_cols, 2 * FOCAL), bf16)] * pairs_dev,
        ),
        [HBM] * 5, (VMEM,) * (3 + pairs_dev),
        [
            pltpu.SMEM(wave_ids.shape, jnp.int32),
            pltpu.SMEM(angle_ids.shape, jnp.int32),
            pltpu.SMEM(targets.shape, jnp.int32),
            pltpu.VMEM(coef_table.shape[::-1], f32),
            pltpu.VMEM(widths.shape, f32),
            pltpu.VMEM((rows_dev, own_cols), f32),
            *waves,
            pltpu.VMEM((pairs_dev, 2 * TERMS, LANES), f32),
            pltpu.VMEM((pairs_dev, 4 * rows_dev, own_cols), bf16),
            pltpu.VMEM((pairs_dev, 4 * rows_dev, 2 * FOCAL), f32),
            pltpu.SemaphoreType.DMA((5,)),
        ],
        10**9, 10**7,
    )(*(in_hbm(value) for value in (wave_ids, angle_ids, targets, coef_table.T, widths)))
    far_info = to_core(info)

    tall, flat, spots, gains = call(
        row_kernel, "row_tables",
        (
            shape((pairs_dev, 2 * FOCAL, rows), bf16), shape((pairs_dev, rows_dev, 2 * FOCAL), bf16),
            shape((pairs_dev, FOCAL, FOCAL), f32), shape((pairs_dev, 8, 128), f32),
        ),
        [VMEM], (VMEM,) * 4, [], 10**8, 10**6,
    )(info)
    if peers <= DIRECT:
        steps = list(range(peers - 2, 0, -2))
        got = [exchange(mine, step) for step in steps]
        near = exchange(mine, 1)
        first, flat = lax.optimization_barrier((got[0], flat))
        joined = call(join_kernel, "join", shape(((len(steps) - 1) * rows_dev, lanes), bf16),
                      [VMEM] * (len(steps) - 1), VMEM, [], 10**6, 10**6)(*got[1:])
        sections = [mine, near, first, joined, exchange(first, 1), exchange(joined, 1)]
        steps = [0, 1, *steps, *(step ^ 1 for step in steps)]
        after = [near, joined]
    else:
        blocks = jnp.tile(mine[None], (peers, 1, 1))
        blocks = lax.all_to_all(blocks, "aperture", 0, 0, tiled=True)
        sections, steps, after = [blocks.reshape(rows, lanes)], None, []
    outs = [shape((2 * FOCAL, own_cols), bf16)] * pairs_dev + [shape((2, rows_dev, own_cols), f32)] * 2 * pairs_dev
    made = call(
        functools.partial(table_kernel, math.sqrt(rows * cols), cols), "far_tables",
        outs, [VMEM] * 3 + [ANY] * len(after), [VMEM] * len(outs),
        [*waves, pltpu.VMEM((pairs_dev, 2, FOCAL, BLOCK), f32), pltpu.VMEM((copies * pairs_dev, 2 * TERMS, LANES), f32)],
        30 * 10**8, 30 * 10**6,
    )(info, far_info, own, *after)
    far_tables, slopes, far_slopes = made[:pairs_dev], made[pairs_dev : 2 * pairs_dev], made[2 * pairs_dev :]

    back, scores = call(
        functools.partial(focus_kernel, steps), "focus",
        (shape((rows_dev, lanes), bf16), shape((pairs_dev,), f32)),
        [VMEM] * 4 + [ANY] + [VMEM] * len(sections), (VMEM, SMEM),
        [
            pltpu.VMEM((rows, lanes), bf16),
            pltpu.VMEM((pairs_dev, 2 * FOCAL, 2 * FOCAL), f32),
            pltpu.VMEM((pairs_dev, 2, FOCAL, FOCAL), f32),
            pltpu.VMEM((pairs_dev, FOCAL, 2 * FOCAL), bf16),
        ],
        10**8, 10**6,
    )(tall, flat, spots, gains, far_slopes[0], *sections)

    out = shape((rows_dev, own_cols), f32)
    ins = [back, *tables, *slopes]
    grad = call(
        functools.partial(grad_kernel, pairs_dev, across=False), "gradient_own",
        out, [VMEM] * len(ins), VMEM, [], 10**9, 10**7,
    )(*ins)
    ins = [to_core(back), *far_tables, *far_slopes, grad]
    grad = call(
        functools.partial(last_grad_kernel, pairs_dev), "gradient_far",
        out, [VMEM] * len(ins), HBM,
        [pltpu.VMEM(out.shape, f32), pltpu.SemaphoreType.DMA((own_cols // (2 * BLOCK),))], 10**9, 10**7,
    )(*ins)
    return grad, scores


def solution(mesh):
    in_specs = (
        P(("group", "aperture"), None),
        P(),
        P(("group", "wave")),
        P(("group", "wave")),
        P(("group", "wave"), None),
    )
    out_specs = (P(("group", "aperture"), "wave"), P(("group", "wave")))
    return jax.shard_map(
        on_device, mesh=mesh, in_specs=in_specs, out_specs=out_specs, check_vma=False
    )
```

```python
import functools
import itertools
import math

import jax
import jax.numpy as jnp
from jax import lax
from jax.experimental import pallas as pl
from jax.experimental.pallas import tpu as pltpu
from jax.sharding import PartitionSpec as P

FOCAL = 256
SPOT = 4
SHIFT = 32
TERMS = 8
BLOCK = 256
GRAIN = 16
LANES = 128
PIECE = 16
SPLITS = 4
VMEM_LIMIT = 16 * 1024 * 1024
WAVE_ROW, ANGLE_ROW, AIM_ROW, INFO_ROWS = 16, 17, 18, 24
DIRECT = 16

COS = (
    1.0, -19.7392088015709, 64.93939395773512, -85.45681453397417, 60.24458621302471,
    -26.425616460281425, 7.8991596631575085, -1.6968741456712442, 0.2437618617467591,
)
SIN = (
    6.2831853071792665, -41.34170224019464, 81.60524925425943, -76.70585885700535,
    42.05867547580699, -15.094428387947755, 3.818490079304055, -0.7122771247541972,
    0.09149844789363434,
)


def horner(terms, u):
    value = terms[-1] * u + terms[-2]
    for term in terms[-3::-1]:
        value = value * u + term
    return value


def unit_waves(counts, period):
    half = period // 2
    centred = ((counts + half) & (period - 1)) - half
    t = centred.astype(jnp.float32) * (1.0 / period)
    u = t * t
    return horner(COS, u), -(t * horner(SIN, u))


def iota(shape, axis):
    return lax.broadcasted_iota(jnp.int32, shape, axis)


def pick_coef(table, wave):
    chosen = jnp.where(iota(table.shape, 1) == wave, table, 0.0)
    return jnp.sum(chosen, axis=1, keepdims=True)


def column_freq(info_ref, pair):
    wave = info_ref[pair, WAVE_ROW : WAVE_ROW + 1, :].astype(jnp.int32)
    angle = info_ref[pair, ANGLE_ROW : ANGLE_ROW + 1, :].astype(jnp.int32)
    return (iota((1, FOCAL), 1) - FOCAL // 2 + SHIFT * angle) * (BLOCK + wave)


def fill_base(freq, shift, period, base_ref, centre_ref):
    low_r, low_i = unit_waves(iota((GRAIN, 1), 0) * freq, period)
    steps = BLOCK // GRAIN
    high_r, high_i = unit_waves((iota((steps, 1), 0) * GRAIN - BLOCK // 2 + shift) * freq, period)
    for step in range(steps):
        one_r, one_i = high_r[step : step + 1], high_i[step : step + 1]
        rows = slice(step * GRAIN, (step + 1) * GRAIN)
        base_ref[0, rows, :] = one_r * low_r - one_i * low_i
        base_ref[1, rows, :] = one_r * low_i + one_i * low_r
    count = centre_ref.shape[1]
    cent_r, cent_i = unit_waves((iota((count, 1), 0) * BLOCK + BLOCK // 2) * freq, period)
    centre_ref[0] = cent_r
    centre_ref[1] = cent_i


def power_coefs(coef):
    before, current = [1], [0, 1]
    bases = [before, current]
    for _ in range(2, TERMS):
        doubled = [0] + [2 * term for term in current]
        before, current = current, [a - b for a, b in itertools.zip_longest(doubled, before, fillvalue=0)]
        bases.append(current)
    rows = []
    for part, power in itertools.product(range(2), range(TERMS)):
        row = None
        for order in range(power, TERMS, 2):
            place = part * TERMS + order
            term = coef[place : place + 1] * float(bases[order][power])
            row = term if row is None else row + term
        rows.append(row)
    return jnp.concatenate(rows, axis=0)


def near_fields(s, power_ref, pairs):
    outs = []
    for pair, part in itertools.product(range(pairs), range(2)):
        row = (part + 1) * TERMS - 1
        value = power_ref[pair, row : row + 1, :] * s + power_ref[pair, row - 1 : row, :]
        for row in range(row - 2, part * TERMS - 1, -1):
            value = value * s + power_ref[pair, row : row + 1, :]
        outs.append(value)
    return [outs[2 * pair : 2 * pair + 2] for pair in range(pairs)]


def near_slopes(s, coef_ref, pairs):
    def coef(pair, row):
        return coef_ref[pair, row : row + 1, :]

    twice = s + s
    before, current = jnp.ones_like(s), twice
    outs = [[coef(p, k) + coef(p, k + 1) * twice for k in (1, TERMS + 1)] for p in range(pairs)]
    for order in range(3, TERMS):
        before, current = current, twice * current - before
        for pair, out in enumerate(outs):
            out[0] = out[0] + coef(pair, order) * current
            out[1] = out[1] + coef(pair, TERMS + order) * current
    return outs


def turn_round(value):
    rows, cols = value.shape
    order = LANES - 1 - iota((rows, LANES), 1)
    parts = [
        jnp.take_along_axis(value[:, start : start + LANES], order, axis=1)
        for start in range(cols - LANES, -1, -LANES)
    ]
    return jnp.concatenate(parts, axis=1)


def both_sides(width_ref, core, start):
    rows, cols = width_ref.shape
    half = cols // 2
    lane = iota((rows, LANES), 1)

    def right(place):
        place = half + place
        return width_ref[:, place : place + LANES]

    def left(place, turn):
        place = half - LANES - place
        return jnp.take_along_axis(width_ref[:, place : place + LANES], turn - lane, axis=1)

    own = jnp.where(core == 1, right(start), left(start, LANES - 1))
    mirrored = jnp.take_along_axis(
        width_ref[:, half - LANES - start : half - start], (LANES - lane) % LANES, axis=1
    )
    edge = width_ref[:, half - start : half - start + 1]
    mirrored = jnp.where(lane == 0, edge, mirrored)
    after = min(start + LANES, half - LANES)
    shifted = jnp.where(lane == LANES - 1, right(after)[:, :1], pltpu.roll(right(start), LANES - 1, 1))
    return own, jnp.where(core == 1, mirrored, shifted)


def block_starts(cols, index):
    return cols // 2 - (index + 1) * BLOCK, cols // 2 + index * BLOCK


def both_blocks(base_r, base_i, cent_r, cent_i):
    rr, ii = base_r * cent_r, base_i * cent_i
    ri, ir = base_r * cent_i, base_i * cent_r
    return (rr + ii, ir - ri), (rr - ii, ir + ri)


def own_waves(info_ref, pair, cols, base_ref, centre_ref):
    shift = cols // 4 + 1 - lax.axis_index("wave")
    fill_base(column_freq(info_ref, pair), shift, 256 * cols, base_ref, centre_ref)


def forward_kernel(
    wave_hbm, angle_hbm, aim_hbm, coef_hbm, width_hbm, mine_ref, info_ref, own_ref, *refs
):
    pairs = info_ref.shape[0]
    table_refs, refs = refs[:pairs], refs[pairs:]
    (
        wave_ref, angle_ref, aim_ref, coef_ref, width_ref, base_ref, centre_ref, power_ref, near_ref, acc_ref,
        sems,
    ) = refs
    rows_dev, cols = width_ref.shape
    half = cols // 2
    copies = [(wave_hbm, wave_ref), (angle_hbm, angle_ref), (aim_hbm, aim_ref), (coef_hbm, coef_ref)]
    for start in range(0, cols, cols // SPLITS):
        place = slice(start, start + cols // SPLITS)
        copies.append((width_hbm.at[:, place], width_ref.at[:, place]))
    moves = [
        pltpu.make_async_copy(source, target, sems.at[index]) for index, (source, target) in enumerate(copies)
    ]
    for move in moves:
        move.start()
    for move in moves:
        move.wait()
    for pair in range(pairs):
        coef = pick_coef(coef_ref[...], wave_ref[pair])
        coef = jnp.broadcast_to(coef, (WAVE_ROW, FOCAL))
        info_ref[pair, :WAVE_ROW, :] = coef
        power_ref[pair] = power_coefs(coef[:, :LANES])
        row = iota((INFO_ROWS - WAVE_ROW, FOCAL), 0) + WAVE_ROW
        ids = jnp.where(row == WAVE_ROW, wave_ref[pair], 0)
        ids = jnp.where(row == ANGLE_ROW, angle_ref[pair], ids)
        ids = jnp.where(row == AIM_ROW, aim_ref[pair, 0], ids)
        ids = jnp.where(row == AIM_ROW + 1, aim_ref[pair, 1], ids)
        info_ref[pair, WAVE_ROW:, :] = ids.astype(jnp.float32)
    for pair in range(pairs):
        own_waves(info_ref, pair, cols, base_ref.at[pair], centre_ref.at[pair])
    core = lax.axis_index("wave")
    void = jnp.where(core == 1, 0, half - 1)
    for index in range(half // (2 * BLOCK)):
        starts = block_starts(half, index)
        for start in (start + step for start in starts for step in range(0, BLOCK, LANES)):
            sides = both_sides(width_ref, core, start)
            own_ref[:, start : start + LANES] = sides[0]
            for side, widths in enumerate(sides):
                outs = near_fields(widths, power_ref, pairs)
                if side and start in (0, half - LANES):
                    keep = iota((rows_dev, LANES), 1) + start != void
                    outs = [[jnp.where(keep, part, 0.0) for part in out] for out in outs]
                for pair, part in ((pair, part) for pair in range(pairs) for part in range(2)):
                    row = (2 * side + part) * rows_dev
                    near_ref[pair, row : row + rows_dev, start : start + LANES] = outs[pair][part].astype(jnp.bfloat16)
        for pair in range(pairs):
            cent_r, cent_i = (centre_ref[pair, part, index : index + 1, :] for part in range(2))
            for row in range(0, BLOCK, GRAIN):
                base_r, base_i = (base_ref[pair, part, row : row + GRAIN, :] for part in range(2))
                for start, table in zip(starts, both_blocks(base_r, base_i, cent_r, cent_i)):
                    rows = slice(start + row, start + row + GRAIN)
                    table_refs[pair][rows, :FOCAL] = table[0].astype(jnp.bfloat16)
                    table_refs[pair][rows, FOCAL:] = table[1].astype(jnp.bfloat16)
            product = jnp.dot(
                jnp.concatenate([near_ref[pair, :, start : start + BLOCK] for start in starts], axis=1),
                jnp.concatenate([table_refs[pair][start : start + BLOCK, :] for start in starts], axis=0),
                preferred_element_type=jnp.float32,
            )
            acc_ref[pair] = product if index == 0 else acc_ref[pair] + product
    alone = jnp.where(core == 1, 0, half)
    column = width_ref[:, pl.ds(pl.multiple_of(alone, LANES), LANES)]
    columns = near_fields(column, power_ref, pairs)
    for pair in range(pairs):
        acc = [acc_ref[pair, part * rows_dev : (part + 1) * rows_dev, :] for part in range(4)]
        (own_rr, own_ri), (own_ir, own_ii), (far_rr, far_ri), (far_ir, far_ii) = (
            (part[:, :FOCAL], part[:, FOCAL:]) for part in acc
        )
        cross_r, cross_i = far_ii - own_ii, own_ri - far_ri
        real = own_rr + far_rr + jnp.where(core == 1, cross_r, -cross_r)
        imag = own_ir + far_ir + jnp.where(core == 1, cross_i, -cross_i)
        near_r, near_i = (part[:, :1].astype(jnp.bfloat16).astype(jnp.float32) for part in columns[pair])
        wave_r, wave_i = (
            part.astype(jnp.bfloat16).astype(jnp.float32)
            for part in unit_waves((alone - half) * column_freq(info_ref, pair), 256 * cols)
        )
        real = real + (near_r * wave_r - near_i * wave_i)
        imag = imag + (near_r * wave_i + near_i * wave_r)
        for part, value in enumerate((real, imag)):
            lane = (2 * pair + part) * FOCAL
            mine_ref[:, lane : lane + FOCAL] = value.astype(jnp.bfloat16)


def spot_rows(info_ref, pair, first):
    aims = [info_ref[pair, row : row + 1, :] for row in (AIM_ROW, AIM_ROW + 1)]
    rows_off = (iota((PIECE, FOCAL), 0) + first).astype(jnp.float32) - aims[0]
    cols_off = iota((1, FOCAL), 1).astype(jnp.float32) - aims[1]
    return jnp.exp(-(rows_off * rows_off + cols_off * cols_off) / (2.0 * SPOT * SPOT))


def total_of(value):
    return jnp.sum(jnp.sum(value, axis=0, keepdims=True), axis=1, keepdims=True)


def row_kernel(info_ref, tall_ref, flat_ref, spot_ref, gain_ref):
    pairs, _, rows = tall_ref.shape
    rows_dev = flat_ref.shape[1]
    period = 256 * rows
    size = min(rows, FOCAL)
    for pair in range(pairs):
        wave = info_ref[pair, WAVE_ROW : WAVE_ROW + 1, :].astype(jnp.int32) + BLOCK
        focal = (iota((FOCAL, 1), 0) - FOCAL // 2) * wave

        def step(index, carry):
            start = pl.multiple_of(index * size, size)
            place = iota((1, size), 1) + (start - rows // 2)
            for row in range(0, FOCAL, PIECE):
                real, imag = unit_waves(focal[row : row + PIECE, :size] * place, period)
                tall_ref[pair, row : row + PIECE, pl.ds(start, size)] = real.astype(jnp.bfloat16)
                row += FOCAL
                tall_ref[pair, row : row + PIECE, pl.ds(start, size)] = imag.astype(jnp.bfloat16)
            return carry

        if rows == size:
            step(0, 0)
        else:
            lax.fori_loop(0, rows // size, step, 0)
        focal = (iota((1, FOCAL), 1) - FOCAL // 2) * wave
        first = lax.axis_index("aperture") * rows_dev - rows // 2
        real, imag = unit_waves((iota((rows_dev, 1), 0) + first) * focal, period)
        flat_ref[pair, :, :FOCAL] = real.astype(jnp.bfloat16)
        flat_ref[pair, :, FOCAL:] = imag.astype(jnp.bfloat16)
        total = jnp.zeros((PIECE, FOCAL), jnp.float32)
        for row in range(0, FOCAL, PIECE):
            spot = spot_rows(info_ref, pair, row)
            spot_ref[pair, row : row + PIECE, :] = spot
            total += spot
        gain_ref[pair] = jnp.broadcast_to(FOCAL * FOCAL / total_of(total), gain_ref.shape[1:])


def focus_kernel(steps, tall_ref, flat_ref, spot_ref, gain_ref, after_ref, *refs):
    del after_ref
    *sect_refs, back_ref, score_ref, rows_ref, mixed_ref, field_ref, stack_ref = refs
    pairs = tall_ref.shape[0]
    rows_dev = back_ref.shape[0]
    if steps is None:
        rows_ref = sect_refs[0]
    else:
        me = lax.axis_index("aperture")
        blocks = [
            ref[index * rows_dev : (index + 1) * rows_dev, :]
            for ref in sect_refs
            for index in range(ref.shape[0] // rows_dev)
        ]
        for step, block in zip(steps, blocks, strict=True):
            start = pl.multiple_of((me ^ step) * rows_dev, rows_dev)
            rows_ref[pl.ds(start, rows_dev), :] = block
    for pair in range(pairs):
        lane = 2 * pair * FOCAL
        section = rows_ref[:, lane : lane + 2 * FOCAL]
        mixed_ref[pair] = jnp.dot(tall_ref[pair], section, preferred_element_type=jnp.float32)
    pieces = [slice(row, row + PIECE) for row in range(0, FOCAL, PIECE)]
    sums = []
    for pair in range(pairs):
        totals = [jnp.zeros((PIECE, FOCAL), jnp.float32) for _ in range(2)]
        for rows in pieces:
            lower = slice(rows.start + FOCAL, rows.stop + FOCAL)
            real = mixed_ref[pair, rows, :FOCAL] - mixed_ref[pair, lower, FOCAL:]
            imag = mixed_ref[pair, rows, FOCAL:] + mixed_ref[pair, lower, :FOCAL]
            field_ref[pair, 0, rows, :] = real
            field_ref[pair, 1, rows, :] = imag
            power = real * real + imag * imag
            totals = [totals[0] + spot_ref[pair, rows, :] * power, totals[1] + power]
        sums.append((total_of(totals[0]), total_of(totals[1]) + 1e-06))
    for pair, (spot_power, all_power) in enumerate(sums):
        ratio = spot_power / all_power
        gain = gain_ref[pair, :1, :1]
        score_ref[pair] = jnp.sum(ratio * gain)
        scale = gain * 2.0 / all_power
        for rows in pieces:
            lower = slice(rows.start + FOCAL, rows.stop + FOCAL)
            weight = scale * (spot_ref[pair, rows, :] - ratio)
            real = (weight * field_ref[pair, 0, rows, :]).astype(jnp.bfloat16)
            imag = (weight * field_ref[pair, 1, rows, :]).astype(jnp.bfloat16)
            stack_ref[pair, rows, :FOCAL] = real
            stack_ref[pair, rows, FOCAL:] = imag
            stack_ref[pair, lower, :FOCAL] = imag
            stack_ref[pair, lower, FOCAL:] = -real
        back = jnp.dot(flat_ref[pair], stack_ref[pair], preferred_element_type=jnp.float32)
        lane = 2 * pair * FOCAL
        back_ref[:, lane : lane + 2 * FOCAL] = back.astype(jnp.bfloat16)


def table_kernel(scale, cols, info_ref, far_info_ref, width_ref, *refs):
    *out_refs, base_ref, centre_ref, turned_ref, coef_ref = refs
    pairs = base_ref.shape[0]
    out_refs = out_refs[-3 * pairs :]
    table_refs, slope_refs = out_refs[:pairs], out_refs[pairs:]
    own_cols = width_ref.shape[1]
    for core, ref in enumerate((info_ref, far_info_ref)):
        for pair in range(pairs):
            coef = ref[pair, : 2 * TERMS, :LANES]
            coef_ref[core * pairs + pair] = coef * ((iota(coef.shape, 0) % TERMS).astype(jnp.float32) * scale)
    centres = []
    for pair in range(pairs):
        own_waves(far_info_ref, pair, cols, base_ref.at[pair], centre_ref.at[pair])
        for part, row, lane in itertools.product(range(2), range(0, BLOCK, LANES), range(0, FOCAL, LANES)):
            tile = base_ref[pair, part, row : row + LANES, lane : lane + LANES]
            turned_ref[pair, part, lane : lane + LANES, row : row + LANES] = tile.T
        centres.append([centre_ref[pair, part].T for part in range(2)])
    for index in range(own_cols // (2 * BLOCK)):
        starts = block_starts(own_cols, index)
        for pair in range(pairs):
            for row in range(0, FOCAL, GRAIN):
                rows = slice(row, row + GRAIN)
                cent_r, cent_i = (centre[rows, index : index + 1] for centre in centres[pair])
                base_r, base_i = (turned_ref[pair, part, rows, :] for part in range(2))
                for start, table in zip(starts, both_blocks(base_r, base_i, cent_r, cent_i)):
                    for part, value in enumerate(table):
                        place = slice(row + part * FOCAL, row + part * FOCAL + GRAIN)
                        table_refs[pair][place, start : start + BLOCK] = value.astype(jnp.bfloat16)
        for start in (start + step for start in starts for step in range(0, BLOCK, LANES)):
            place = slice(start, start + LANES)
            slopes = near_slopes(width_ref[:, place], coef_ref, 2 * pairs)
            for ref, slope in zip(slope_refs, slopes):
                ref[0, :, place] = slope[0]
                ref[1, :, place] = slope[1]


def last_grad_kernel(pairs, *refs):
    *in_refs, out_hbm, out_ref, sems = refs
    rows_dev, own_cols = out_ref.shape
    size = 2 * BLOCK
    core = lax.axis_index("wave")
    moves = []

    def send(start, total):
        place = pl.multiple_of(jnp.where(core == 1, start, own_cols - size - start), size)
        place = pl.ds(place, size)
        out_ref[:, place] = jnp.where(core == 1, total, turn_round(total))
        index = start // size
        moves.append(pltpu.make_async_copy(out_ref.at[:, place], out_hbm.at[:, place], sems.at[index]))
        moves[-1].start()

    grad_kernel(pairs, *in_refs, out_ref, send=send)
    for move in moves:
        move.wait()


def grad_kernel(pairs, back_ref, *refs, send=None, across=True):
    *in_refs, out_ref = refs
    table_refs, slope_refs, total_ref = in_refs[:pairs], in_refs[pairs : 2 * pairs], in_refs[2 * pairs :]
    rows_dev, own_cols = out_ref.shape
    core = lax.axis_index("wave")
    lefts = []
    for pair in range(pairs):
        lane = 2 * pair * FOCAL
        real, imag = back_ref[:, lane : lane + FOCAL], back_ref[:, lane + FOCAL : lane + 2 * FOCAL]
        above = jnp.where(core == 1, imag, -imag)
        below = jnp.where(core == 1, -real, real)
        lefts.append(
            jnp.concatenate(
                [jnp.concatenate([real, above], axis=1), jnp.concatenate([imag, below], axis=1)], axis=0
            )
        )
    size = 2 * BLOCK
    for start in range(0, own_cols, size):
        place = slice(start, start + size)
        total = total_ref[0][:, place] if total_ref else jnp.zeros((rows_dev, size), jnp.float32)
        for pair in range(pairs):
            if across:
                table, dims = table_refs[pair][:, place], ((1,), (0,))
            else:
                table, dims = table_refs[pair][place, :], ((1,), (1,))
            grad = lax.dot_general(lefts[pair], table, (dims, ((), ())), preferred_element_type=jnp.float32)
            total += grad[:rows_dev] * slope_refs[pair][0, :, place]
            total += grad[rows_dev:] * slope_refs[pair][1, :, place]
        if send is None:
            out_ref[:, place] = total
        else:
            send(start, total)


VMEM = pl.BlockSpec(memory_space=pltpu.VMEM)
SMEM = pl.BlockSpec(memory_space=pltpu.SMEM)
ANY = pl.BlockSpec(memory_space=pl.ANY)
HBM = pl.BlockSpec(memory_space=pltpu.HBM)


def call(kernel, name, outs, in_specs, out_specs, scratch, flops, moved):
    return pl.pallas_call(
        kernel,
        name=name,
        out_shape=outs,
        in_specs=in_specs,
        out_specs=out_specs,
        scratch_shapes=scratch,
        cost_estimate=pl.CostEstimate(flops=flops, bytes_accessed=moved, transcendentals=0),
        compiler_params=pltpu.CompilerParams(vmem_limit_bytes=VMEM_LIMIT),
    )


def on_device(widths, coef_table, wave_ids, angle_ids, targets):
    rows_dev, cols = widths.shape
    pairs_dev = wave_ids.shape[0]
    peers = lax.axis_size("aperture")
    copies = lax.axis_size("wave")
    rows = rows_dev * peers
    own_cols = cols // copies
    lanes = 2 * pairs_dev * FOCAL
    f32, bf16 = jnp.float32, jnp.bfloat16
    shape = jax.ShapeDtypeStruct

    def in_hbm(value):
        return pltpu.with_memory_space_constraint(value, pltpu.HBM)

    def exchange(value, step):
        return lax.ppermute(value, "aperture", [(index, index ^ step) for index in range(peers)])

    def to_core(value):
        return lax.ppermute(value, "wave", [(index, (index + 1) % copies) for index in range(copies)])

    waves = [
        pltpu.VMEM((pairs_dev, 2, BLOCK, FOCAL), f32),
        pltpu.VMEM((pairs_dev, 2, 8, FOCAL), f32),
    ]
    mine, info, own, *tables = call(
        forward_kernel, "forward",
        (
            shape((rows_dev, lanes), bf16),
            shape((pairs_dev, INFO_ROWS, FOCAL), f32), shape((rows_dev, own_cols), f32),
            *[shape((own_cols, 2 * FOCAL), bf16)] * pairs_dev,
        ),
        [HBM] * 5, (VMEM,) * (3 + pairs_dev),
        [
            pltpu.SMEM(wave_ids.shape, jnp.int32),
            pltpu.SMEM(angle_ids.shape, jnp.int32),
            pltpu.SMEM(targets.shape, jnp.int32),
            pltpu.VMEM(coef_table.shape[::-1], f32),
            pltpu.VMEM(widths.shape, f32),
            *waves,
            pltpu.VMEM((pairs_dev, 2 * TERMS, LANES), f32),
            pltpu.VMEM((pairs_dev, 4 * rows_dev, own_cols), bf16),
            pltpu.VMEM((pairs_dev, 4 * rows_dev, 2 * FOCAL), f32),
            pltpu.SemaphoreType.DMA((4 + SPLITS,)),
        ],
        10**9, 10**7,
    )(*(in_hbm(value) for value in (wave_ids, angle_ids, targets, coef_table.T, widths)))
    far_info = to_core(info)

    tall, flat, spots, gains = call(
        row_kernel, "row_tables",
        (
            shape((pairs_dev, 2 * FOCAL, rows), bf16), shape((pairs_dev, rows_dev, 2 * FOCAL), bf16),
            shape((pairs_dev, FOCAL, FOCAL), f32), shape((pairs_dev, 8, 128), f32),
        ),
        [VMEM], (VMEM,) * 4, [], 10**8, 10**6,
    )(info)
    if peers <= DIRECT:
        steps = list(range(peers - 2, 0, -2))
        got = [exchange(mine, step) for step in steps]
        near = exchange(mine, 1)
        got[0], flat = lax.optimization_barrier((got[0], flat))
        for index in range(1, len(got) - 1):
            got[index], _ = lax.optimization_barrier((got[index], got[index + 1]))
        sections = [mine, near, *got, *(exchange(block, 1) for block in got)]
        steps = [0, 1, *steps, *(step ^ 1 for step in steps)]
        after = [near, *got]
    else:
        blocks = jnp.tile(mine[None], (peers, 1, 1))
        blocks = lax.all_to_all(blocks, "aperture", 0, 0, tiled=True)
        sections, steps, after = [blocks.reshape(rows, lanes)], None, []
    outs = [shape((2 * FOCAL, own_cols), bf16)] * pairs_dev + [shape((2, rows_dev, own_cols), f32)] * 2 * pairs_dev
    made = call(
        functools.partial(table_kernel, math.sqrt(rows * cols), cols), "far_tables",
        outs, [VMEM] * 3 + [ANY] * len(after), [VMEM] * len(outs),
        [*waves, pltpu.VMEM((pairs_dev, 2, FOCAL, BLOCK), f32), pltpu.VMEM((copies * pairs_dev, 2 * TERMS, LANES), f32)],
        30 * 10**8, 30 * 10**6,
    )(info, far_info, own, *after)
    far_tables, slopes, far_slopes = made[:pairs_dev], made[pairs_dev : 2 * pairs_dev], made[2 * pairs_dev :]

    back, scores = call(
        functools.partial(focus_kernel, steps), "focus",
        (shape((rows_dev, lanes), bf16), shape((pairs_dev,), f32)),
        [VMEM] * 4 + [ANY] + [VMEM] * len(sections), (VMEM, SMEM),
        [
            pltpu.VMEM((rows, lanes), bf16),
            pltpu.VMEM((pairs_dev, 2 * FOCAL, 2 * FOCAL), f32),
            pltpu.VMEM((pairs_dev, 2, FOCAL, FOCAL), f32),
            pltpu.VMEM((pairs_dev, 2 * FOCAL, 2 * FOCAL), bf16),
        ],
        10**8, 10**6,
    )(tall, flat, spots, gains, far_slopes[0], *sections)

    out = shape((rows_dev, own_cols), f32)
    ins = [back, *tables, *slopes]
    grad = call(
        functools.partial(grad_kernel, pairs_dev, across=False), "gradient_own",
        out, [VMEM] * len(ins), VMEM, [], 10**9, 10**7,
    )(*ins)
    ins = [to_core(back), *far_tables, *far_slopes, grad]
    grad = call(
        functools.partial(last_grad_kernel, pairs_dev), "gradient_far",
        out, [VMEM] * len(ins), HBM,
        [pltpu.VMEM(out.shape, f32), pltpu.SemaphoreType.DMA((own_cols // (2 * BLOCK),))], 10**9, 10**7,
    )(*ins)
    return grad, scores


def solution(mesh):
    in_specs = (
        P(("group", "aperture"), None),
        P(),
        P(("group", "wave")),
        P(("group", "wave")),
        P(("group", "wave"), None),
    )
    out_specs = (P(("group", "aperture"), "wave"), P(("group", "wave")))
    return jax.shard_map(
        on_device, mesh=mesh, in_specs=in_specs, out_specs=out_specs, check_vma=False
    )
```

```python
import functools
import itertools
import math

import jax
import jax.numpy as jnp
from jax import lax
from jax.experimental import pallas as pl
from jax.experimental.pallas import tpu as pltpu
from jax.sharding import PartitionSpec as P

FOCAL = 256
SPOT = 4
SHIFT = 32
TERMS = 8
BLOCK = 256
GRAIN = 16
LANES = 128
PIECE = 16
VMEM_LIMIT = 16 * 1024 * 1024
WAVE_ROW, ANGLE_ROW, AIM_ROW, INFO_ROWS = 16, 17, 18, 24
CUBE = 8

COS = (
    1.0, -19.7392088015709, 64.93939395773512, -85.45681453397417, 60.24458621302471,
    -26.425616460281425, 7.8991596631575085, -1.6968741456712442, 0.2437618617467591,
)
SIN = (
    6.2831853071792665, -41.34170224019464, 81.60524925425943, -76.70585885700535,
    42.05867547580699, -15.094428387947755, 3.818490079304055, -0.7122771247541972,
    0.09149844789363434,
)


def horner(terms, u):
    value = terms[-1] * u + terms[-2]
    for term in terms[-3::-1]:
        value = value * u + term
    return value


def unit_waves(counts, period):
    half = period // 2
    centred = ((counts + half) & (period - 1)) - half
    t = centred.astype(jnp.float32) * (1.0 / period)
    u = t * t
    return horner(COS, u), -(t * horner(SIN, u))


def iota(shape, axis):
    return lax.broadcasted_iota(jnp.int32, shape, axis)


def pick_coef(table, wave):
    chosen = jnp.where(iota(table.shape, 1) == wave, table, 0.0)
    return jnp.sum(chosen, axis=1, keepdims=True)


def column_freq(info_ref, pair):
    wave = info_ref[pair, WAVE_ROW : WAVE_ROW + 1, :].astype(jnp.int32)
    angle = info_ref[pair, ANGLE_ROW : ANGLE_ROW + 1, :].astype(jnp.int32)
    return (iota((1, FOCAL), 1) - FOCAL // 2 + SHIFT * angle) * (BLOCK + wave)


def fill_base(freq, shift, period, base_ref, centre_ref):
    low_r, low_i = unit_waves(iota((GRAIN, 1), 0) * freq, period)
    steps = BLOCK // GRAIN
    high_r, high_i = unit_waves((iota((steps, 1), 0) * GRAIN - BLOCK // 2 + shift) * freq, period)
    for step in range(steps):
        one_r, one_i = high_r[step : step + 1], high_i[step : step + 1]
        rows = slice(step * GRAIN, (step + 1) * GRAIN)
        base_ref[0, rows, :] = one_r * low_r - one_i * low_i
        base_ref[1, rows, :] = one_r * low_i + one_i * low_r
    count = centre_ref.shape[1]
    cent_r, cent_i = unit_waves((iota((count, 1), 0) * BLOCK + BLOCK // 2) * freq, period)
    centre_ref[0] = cent_r
    centre_ref[1] = cent_i


def power_coefs(coef):
    before, current = [1], [0, 1]
    bases = [before, current]
    for _ in range(2, TERMS):
        doubled = [0] + [2 * term for term in current]
        before, current = current, [a - b for a, b in itertools.zip_longest(doubled, before, fillvalue=0)]
        bases.append(current)
    rows = []
    for part, power in itertools.product(range(2), range(TERMS)):
        row = None
        for order in range(power, TERMS, 2):
            place = part * TERMS + order
            term = coef[place : place + 1] * float(bases[order][power])
            row = term if row is None else row + term
        rows.append(row)
    return jnp.concatenate(rows, axis=0)


def near_fields(s, power_ref, pairs):
    outs = []
    for pair, part in itertools.product(range(pairs), range(2)):
        row = (part + 1) * TERMS - 1
        value = power_ref[pair, row : row + 1, :] * s + power_ref[pair, row - 1 : row, :]
        for row in range(row - 2, part * TERMS - 1, -1):
            value = value * s + power_ref[pair, row : row + 1, :]
        outs.append(value)
    return [outs[2 * pair : 2 * pair + 2] for pair in range(pairs)]


def near_slopes(s, coef_ref, pairs):
    def coef(pair, row):
        return coef_ref[pair, row : row + 1, :]

    twice = s + s
    before, current = jnp.ones_like(s), twice
    outs = [[coef(p, k) + coef(p, k + 1) * twice for k in (1, TERMS + 1)] for p in range(pairs)]
    for order in range(3, TERMS):
        before, current = current, twice * current - before
        for pair, out in enumerate(outs):
            out[0] = out[0] + coef(pair, order) * current
            out[1] = out[1] + coef(pair, TERMS + order) * current
    return outs


def turn_round(value):
    rows, cols = value.shape
    order = LANES - 1 - iota((rows, LANES), 1)
    parts = [
        jnp.take_along_axis(value[:, start : start + LANES], order, axis=1)
        for start in range(cols - LANES, -1, -LANES)
    ]
    return jnp.concatenate(parts, axis=1)


def block_starts(cols, index):
    return cols // 2 - (index + 1) * BLOCK, cols // 2 + index * BLOCK


def both_blocks(base_r, base_i, cent_r, cent_i):
    rr, ii = base_r * cent_r, base_i * cent_i
    ri, ir = base_r * cent_i, base_i * cent_r
    return (rr + ii, ir - ri), (rr - ii, ir + ri)


def own_waves(info_ref, pair, cols, base_ref, centre_ref):
    shift = cols // 4 + 1 - lax.axis_index("wave")
    fill_base(column_freq(info_ref, pair), shift, 256 * cols, base_ref, centre_ref)


def forward_kernel(
    wave_hbm, angle_hbm, aim_hbm, coef_hbm, width_hbm, mine_ref, info_ref, own_ref, *refs
):
    pairs = info_ref.shape[0]
    table_refs, refs = refs[:pairs], refs[pairs:]
    (
        wave_ref, angle_ref, aim_ref, coef_ref, width_ref, far_ref, base_ref, centre_ref, power_ref, near_ref, acc_ref,
        sems,
    ) = refs
    rows_dev, cols = width_ref.shape
    half = cols // 2
    moves = [
        pltpu.make_async_copy(source, target, sems.at[index])
        for index, (source, target) in enumerate((
            (wave_hbm, wave_ref), (angle_hbm, angle_ref), (aim_hbm, aim_ref),
            (coef_hbm, coef_ref), (width_hbm, width_ref),
        ))
    ]
    for move in moves:
        move.start()
    for move in moves:
        move.wait()
    for pair in range(pairs):
        coef = pick_coef(coef_ref[...], wave_ref[pair])
        coef = jnp.broadcast_to(coef, (WAVE_ROW, FOCAL))
        info_ref[pair, :WAVE_ROW, :] = coef
        power_ref[pair] = power_coefs(coef[:, :LANES])
        row = iota((INFO_ROWS - WAVE_ROW, FOCAL), 0) + WAVE_ROW
        ids = jnp.where(row == WAVE_ROW, wave_ref[pair], 0)
        ids = jnp.where(row == ANGLE_ROW, angle_ref[pair], ids)
        ids = jnp.where(row == AIM_ROW, aim_ref[pair, 0], ids)
        ids = jnp.where(row == AIM_ROW + 1, aim_ref[pair, 1], ids)
        info_ref[pair, WAVE_ROW:, :] = ids.astype(jnp.float32)
    for pair in range(pairs):
        own_waves(info_ref, pair, cols, base_ref.at[pair], centre_ref.at[pair])
    core = lax.axis_index("wave")
    left, right = turn_round(width_ref[:, :half]), width_ref[:, half:]
    own_ref[...] = jnp.where(core == 1, right, left)
    far_ref[...] = jnp.where(core == 1, pltpu.roll(left, 1, 1), pltpu.roll(right, half - 1, 1))

    void = jnp.where(core == 1, 0, half - 1)
    for index in range(half // (2 * BLOCK)):
        starts = block_starts(half, index)
        for start in (start + step for start in starts for step in range(0, BLOCK, LANES)):
            for side, ref in enumerate((own_ref, far_ref)):
                outs = near_fields(ref[:, start : start + LANES], power_ref, pairs)
                if side and start in (0, half - LANES):
                    keep = iota((rows_dev, LANES), 1) + start != void
                    outs = [[jnp.where(keep, part, 0.0) for part in out] for out in outs]
                for pair, part in ((pair, part) for pair in range(pairs) for part in range(2)):
                    row = (2 * side + part) * rows_dev
                    near_ref[pair, row : row + rows_dev, start : start + LANES] = outs[pair][part].astype(jnp.bfloat16)
        for pair in range(pairs):
            cent_r, cent_i = (centre_ref[pair, part, index : index + 1, :] for part in range(2))
            for row in range(0, BLOCK, GRAIN):
                base_r, base_i = (base_ref[pair, part, row : row + GRAIN, :] for part in range(2))
                for start, table in zip(starts, both_blocks(base_r, base_i, cent_r, cent_i)):
                    rows = slice(start + row, start + row + GRAIN)
                    table_refs[pair][rows, :FOCAL] = table[0].astype(jnp.bfloat16)
                    table_refs[pair][rows, FOCAL:] = table[1].astype(jnp.bfloat16)
            product = jnp.dot(
                jnp.concatenate([near_ref[pair, :, start : start + BLOCK] for start in starts], axis=1),
                jnp.concatenate([table_refs[pair][start : start + BLOCK, :] for start in starts], axis=0),
                preferred_element_type=jnp.float32,
            )
            acc_ref[pair] = product if index == 0 else acc_ref[pair] + product
    alone = jnp.where(core == 1, 0, half)
    column = width_ref[:, pl.ds(pl.multiple_of(alone, LANES), LANES)]
    columns = near_fields(column, power_ref, pairs)
    for pair in range(pairs):
        acc = [acc_ref[pair, part * rows_dev : (part + 1) * rows_dev, :] for part in range(4)]
        (own_rr, own_ri), (own_ir, own_ii), (far_rr, far_ri), (far_ir, far_ii) = (
            (part[:, :FOCAL], part[:, FOCAL:]) for part in acc
        )
        cross_r, cross_i = far_ii - own_ii, own_ri - far_ri
        real = own_rr + far_rr + jnp.where(core == 1, cross_r, -cross_r)
        imag = own_ir + far_ir + jnp.where(core == 1, cross_i, -cross_i)
        near_r, near_i = (part[:, :1].astype(jnp.bfloat16).astype(jnp.float32) for part in columns[pair])
        wave_r, wave_i = (
            part.astype(jnp.bfloat16).astype(jnp.float32)
            for part in unit_waves((alone - half) * column_freq(info_ref, pair), 256 * cols)
        )
        real = real + (near_r * wave_r - near_i * wave_i)
        imag = imag + (near_r * wave_i + near_i * wave_r)
        for part, value in enumerate((real, imag)):
            lane = (2 * pair + part) * FOCAL
            mine_ref[:, lane : lane + FOCAL] = value.astype(jnp.bfloat16)


def spot_rows(info_ref, pair, first):
    aims = [info_ref[pair, row : row + 1, :] for row in (AIM_ROW, AIM_ROW + 1)]
    rows_off = (iota((PIECE, FOCAL), 0) + first).astype(jnp.float32) - aims[0]
    cols_off = iota((1, FOCAL), 1).astype(jnp.float32) - aims[1]
    return jnp.exp(-(rows_off * rows_off + cols_off * cols_off) / (2.0 * SPOT * SPOT))


def total_of(value):
    return jnp.sum(jnp.sum(value, axis=0, keepdims=True), axis=1, keepdims=True)


def row_kernel(info_ref, tall_ref, flat_ref, spot_ref, gain_ref):
    pairs, _, rows = tall_ref.shape
    rows_dev = flat_ref.shape[1]
    period = 256 * rows
    size = min(rows, FOCAL)
    for pair in range(pairs):
        wave = info_ref[pair, WAVE_ROW : WAVE_ROW + 1, :].astype(jnp.int32) + BLOCK
        focal = (iota((FOCAL, 1), 0) - FOCAL // 2) * wave

        def step(index, carry):
            start = pl.multiple_of(index * size, size)
            place = iota((1, size), 1) + (start - rows // 2)
            for row in range(0, FOCAL, PIECE):
                real, imag = unit_waves(focal[row : row + PIECE, :size] * place, period)
                tall_ref[pair, row : row + PIECE, pl.ds(start, size)] = real.astype(jnp.bfloat16)
                row += FOCAL
                tall_ref[pair, row : row + PIECE, pl.ds(start, size)] = imag.astype(jnp.bfloat16)
            return carry

        if rows == size:
            step(0, 0)
        else:
            lax.fori_loop(0, rows // size, step, 0)
        focal = (iota((1, FOCAL), 1) - FOCAL // 2) * wave
        first = lax.axis_index("aperture") * rows_dev - rows // 2
        real, imag = unit_waves((iota((rows_dev, 1), 0) + first) * focal, period)
        flat_ref[pair, :, :FOCAL] = real.astype(jnp.bfloat16)
        flat_ref[pair, :, FOCAL:] = imag.astype(jnp.bfloat16)
        total = jnp.zeros((PIECE, FOCAL), jnp.float32)
        for row in range(0, FOCAL, PIECE):
            spot = spot_rows(info_ref, pair, row)
            spot_ref[pair, row : row + PIECE, :] = spot
            total += spot
        gain_ref[pair] = jnp.broadcast_to(FOCAL * FOCAL / total_of(total), gain_ref.shape[1:])


def join_kernel(*refs):
    *in_refs, out_ref = refs
    count = in_refs[0].shape[0]
    for index, ref in enumerate(in_refs):
        out_ref[index * count : (index + 1) * count, :] = ref[...]


def focus_kernel(steps, tall_ref, flat_ref, spot_ref, gain_ref, after_ref, *refs):
    del after_ref
    *sect_refs, back_ref, score_ref, rows_ref, mixed_ref, field_ref, stack_ref = refs
    pairs = tall_ref.shape[0]
    rows_dev = back_ref.shape[0]
    if steps is None:
        rows_ref = sect_refs[0]
    else:
        me = lax.axis_index("aperture")
        blocks = [
            ref[index * rows_dev : (index + 1) * rows_dev, :]
            for ref in sect_refs
            for index in range(ref.shape[0] // rows_dev)
        ]
        for step, block in zip(steps, blocks, strict=True):
            start = pl.multiple_of((me ^ step) * rows_dev, rows_dev)
            rows_ref[pl.ds(start, rows_dev), :] = block
    for pair in range(pairs):
        lane = 2 * pair * FOCAL
        section = rows_ref[:, lane : lane + 2 * FOCAL]
        mixed_ref[pair] = jnp.dot(tall_ref[pair], section, preferred_element_type=jnp.float32)
    pieces = [slice(row, row + PIECE) for row in range(0, FOCAL, PIECE)]
    sums = []
    for pair in range(pairs):
        totals = [jnp.zeros((PIECE, FOCAL), jnp.float32) for _ in range(2)]
        for rows in pieces:
            lower = slice(rows.start + FOCAL, rows.stop + FOCAL)
            real = mixed_ref[pair, rows, :FOCAL] - mixed_ref[pair, lower, FOCAL:]
            imag = mixed_ref[pair, rows, FOCAL:] + mixed_ref[pair, lower, :FOCAL]
            field_ref[pair, 0, rows, :] = real
            field_ref[pair, 1, rows, :] = imag
            power = real * real + imag * imag
            totals = [totals[0] + spot_ref[pair, rows, :] * power, totals[1] + power]
        sums.append((total_of(totals[0]), total_of(totals[1]) + 1e-06))
    for pair, (spot_power, all_power) in enumerate(sums):
        ratio = spot_power / all_power
        gain = gain_ref[pair, :1, :1]
        score_ref[pair] = jnp.sum(ratio * gain)
        scale = gain * 2.0 / all_power
        for rows in pieces:
            lower = slice(rows.start + FOCAL, rows.stop + FOCAL)
            weight = scale * (spot_ref[pair, rows, :] - ratio)
            real = (weight * field_ref[pair, 0, rows, :]).astype(jnp.bfloat16)
            imag = (weight * field_ref[pair, 1, rows, :]).astype(jnp.bfloat16)
            stack_ref[pair, rows, :FOCAL] = real
            stack_ref[pair, rows, FOCAL:] = imag
            stack_ref[pair, lower, :FOCAL] = imag
            stack_ref[pair, lower, FOCAL:] = -real
        back = jnp.dot(flat_ref[pair], stack_ref[pair], preferred_element_type=jnp.float32)
        lane = 2 * pair * FOCAL
        back_ref[:, lane : lane + 2 * FOCAL] = back.astype(jnp.bfloat16)


def table_kernel(scale, cols, info_ref, far_info_ref, width_ref, *refs):
    *out_refs, base_ref, centre_ref, turned_ref, coef_ref = refs
    pairs = base_ref.shape[0]
    out_refs = out_refs[-3 * pairs :]
    table_refs, slope_refs = out_refs[:pairs], out_refs[pairs:]
    own_cols = width_ref.shape[1]
    for core, ref in enumerate((info_ref, far_info_ref)):
        for pair in range(pairs):
            coef = ref[pair, : 2 * TERMS, :LANES]
            coef_ref[core * pairs + pair] = coef * ((iota(coef.shape, 0) % TERMS).astype(jnp.float32) * scale)
    centres = []
    for pair in range(pairs):
        own_waves(far_info_ref, pair, cols, base_ref.at[pair], centre_ref.at[pair])
        for part, row, lane in itertools.product(range(2), range(0, BLOCK, LANES), range(0, FOCAL, LANES)):
            tile = base_ref[pair, part, row : row + LANES, lane : lane + LANES]
            turned_ref[pair, part, lane : lane + LANES, row : row + LANES] = tile.T
        centres.append([centre_ref[pair, part].T for part in range(2)])
    for index in range(own_cols // (2 * BLOCK)):
        starts = block_starts(own_cols, index)
        for pair in range(pairs):
            for row in range(0, FOCAL, GRAIN):
                rows = slice(row, row + GRAIN)
                cent_r, cent_i = (centre[rows, index : index + 1] for centre in centres[pair])
                base_r, base_i = (turned_ref[pair, part, rows, :] for part in range(2))
                for start, table in zip(starts, both_blocks(base_r, base_i, cent_r, cent_i)):
                    for part, value in enumerate(table):
                        place = slice(row + part * FOCAL, row + part * FOCAL + GRAIN)
                        table_refs[pair][place, start : start + BLOCK] = value.astype(jnp.bfloat16)
        for start in (start + step for start in starts for step in range(0, BLOCK, LANES)):
            place = slice(start, start + LANES)
            slopes = near_slopes(width_ref[:, place], coef_ref, 2 * pairs)
            for ref, slope in zip(slope_refs, slopes):
                ref[0, :, place] = slope[0]
                ref[1, :, place] = slope[1]


def last_grad_kernel(pairs, *refs):
    *in_refs, out_hbm, out_ref, sems = refs
    rows_dev, own_cols = out_ref.shape
    size = 2 * BLOCK
    core = lax.axis_index("wave")
    moves = []

    def send(start, total):
        place = pl.multiple_of(jnp.where(core == 1, start, own_cols - size - start), size)
        place = pl.ds(place, size)
        out_ref[:, place] = jnp.where(core == 1, total, turn_round(total))
        index = start // size
        moves.append(pltpu.make_async_copy(out_ref.at[:, place], out_hbm.at[:, place], sems.at[index]))
        moves[-1].start()

    grad_kernel(pairs, *in_refs, out_ref, send=send)
    for move in moves:
        move.wait()


def grad_kernel(pairs, back_ref, *refs, send=None, across=True):
    *in_refs, out_ref = refs
    table_refs, slope_refs, total_ref = in_refs[:pairs], in_refs[pairs : 2 * pairs], in_refs[2 * pairs :]
    rows_dev, own_cols = out_ref.shape
    core = lax.axis_index("wave")
    lefts = []
    for pair in range(pairs):
        lane = 2 * pair * FOCAL
        real, imag = back_ref[:, lane : lane + FOCAL], back_ref[:, lane + FOCAL : lane + 2 * FOCAL]
        above = jnp.where(core == 1, imag, -imag)
        below = jnp.where(core == 1, -real, real)
        lefts.append(
            jnp.concatenate(
                [jnp.concatenate([real, above], axis=1), jnp.concatenate([imag, below], axis=1)], axis=0
            )
        )
    size = 2 * BLOCK
    for start in range(0, own_cols, size):
        place = slice(start, start + size)
        total = total_ref[0][:, place] if total_ref else jnp.zeros((rows_dev, size), jnp.float32)
        for pair in range(pairs):
            if across:
                table, dims = table_refs[pair][:, place], ((1,), (0,))
            else:
                table, dims = table_refs[pair][place, :], ((1,), (1,))
            grad = lax.dot_general(lefts[pair], table, (dims, ((), ())), preferred_element_type=jnp.float32)
            total += grad[:rows_dev] * slope_refs[pair][0, :, place]
            total += grad[rows_dev:] * slope_refs[pair][1, :, place]
        if send is None:
            out_ref[:, place] = total
        else:
            send(start, total)


VMEM = pl.BlockSpec(memory_space=pltpu.VMEM)
SMEM = pl.BlockSpec(memory_space=pltpu.SMEM)
ANY = pl.BlockSpec(memory_space=pl.ANY)
HBM = pl.BlockSpec(memory_space=pltpu.HBM)


def call(kernel, name, outs, in_specs, out_specs, scratch, flops, moved):
    return pl.pallas_call(
        kernel,
        name=name,
        out_shape=outs,
        in_specs=in_specs,
        out_specs=out_specs,
        scratch_shapes=scratch,
        cost_estimate=pl.CostEstimate(flops=flops, bytes_accessed=moved, transcendentals=0),
        compiler_params=pltpu.CompilerParams(vmem_limit_bytes=VMEM_LIMIT),
    )


def on_device(widths, coef_table, wave_ids, angle_ids, targets):
    rows_dev, cols = widths.shape
    pairs_dev = wave_ids.shape[0]
    peers = lax.axis_size("aperture")
    copies = lax.axis_size("wave")
    rows = rows_dev * peers
    own_cols = cols // copies
    lanes = 2 * pairs_dev * FOCAL
    f32, bf16 = jnp.float32, jnp.bfloat16
    shape = jax.ShapeDtypeStruct

    def in_hbm(value):
        return pltpu.with_memory_space_constraint(value, pltpu.HBM)

    def exchange(value, step):
        return lax.ppermute(value, "aperture", [(index, index ^ step) for index in range(peers)])

    def to_core(value):
        return lax.ppermute(value, "wave", [(index, (index + 1) % copies) for index in range(copies)])

    waves = [
        pltpu.VMEM((pairs_dev, 2, BLOCK, FOCAL), f32),
        pltpu.VMEM((pairs_dev, 2, 8, FOCAL), f32),
    ]
    mine, info, own, *tables = call(
        forward_kernel, "forward",
        (
            shape((rows_dev, lanes), bf16),
            shape((pairs_dev, INFO_ROWS, FOCAL), f32), shape((rows_dev, own_cols), f32),
            *[shape((own_cols, 2 * FOCAL), bf16)] * pairs_dev,
        ),
        [HBM] * 5, (VMEM,) * (3 + pairs_dev),
        [
            pltpu.SMEM(wave_ids.shape, jnp.int32),
            pltpu.SMEM(angle_ids.shape, jnp.int32),
            pltpu.SMEM(targets.shape, jnp.int32),
            pltpu.VMEM(coef_table.shape[::-1], f32),
            pltpu.VMEM(widths.shape, f32),
            pltpu.VMEM((rows_dev, own_cols), f32),
            *waves,
            pltpu.VMEM((pairs_dev, 2 * TERMS, LANES), f32),
            pltpu.VMEM((pairs_dev, 4 * rows_dev, own_cols), bf16),
            pltpu.VMEM((pairs_dev, 4 * rows_dev, 2 * FOCAL), f32),
            pltpu.SemaphoreType.DMA((5,)),
        ],
        10**9, 10**7,
    )(*(in_hbm(value) for value in (wave_ids, angle_ids, targets, coef_table.T, widths)))
    far_info = to_core(info)

    tall, flat, spots, gains = call(
        row_kernel, "row_tables",
        (
            shape((pairs_dev, 2 * FOCAL, rows), bf16), shape((pairs_dev, rows_dev, 2 * FOCAL), bf16),
            shape((pairs_dev, FOCAL, FOCAL), f32), shape((pairs_dev, 8, 128), f32),
        ),
        [VMEM], (VMEM,) * 4, [], 10**8, 10**6,
    )(info)
    if peers == CUBE:
        across = exchange(mine, 4)
        beside = exchange(mine, 2)
        near = exchange(mine, 1)
        across, flat = lax.optimization_barrier((across, flat))
        relayed = exchange(across, 2)
        joined = call(
            join_kernel, "join", shape((2 * rows_dev, lanes), bf16), [VMEM] * 2, VMEM, [], 10**6, 10**6
        )(across, beside)
        sections = [mine, near, joined, relayed, exchange(joined, 1), exchange(relayed, 1)]
        steps = [0, 1, 4, 2, 6, 5, 3, 7]
        after = [near, joined, relayed]
    else:
        blocks = jnp.tile(mine[None], (peers, 1, 1))
        blocks = lax.all_to_all(blocks, "aperture", 0, 0, tiled=True)
        sections, steps, after = [blocks.reshape(rows, lanes)], None, []
    outs = [shape((2 * FOCAL, own_cols), bf16)] * pairs_dev + [shape((2, rows_dev, own_cols), f32)] * 2 * pairs_dev
    made = call(
        functools.partial(table_kernel, math.sqrt(rows * cols), cols), "far_tables",
        outs, [VMEM] * 3 + [ANY] * len(after), [VMEM] * len(outs),
        [*waves, pltpu.VMEM((pairs_dev, 2, FOCAL, BLOCK), f32), pltpu.VMEM((copies * pairs_dev, 2 * TERMS, LANES), f32)],
        30 * 10**8, 30 * 10**6,
    )(info, far_info, own, *after)
    far_tables, slopes, far_slopes = made[:pairs_dev], made[pairs_dev : 2 * pairs_dev], made[2 * pairs_dev :]

    back, scores = call(
        functools.partial(focus_kernel, steps), "focus",
        (shape((rows_dev, lanes), bf16), shape((pairs_dev,), f32)),
        [VMEM] * 4 + [ANY] + [VMEM] * len(sections), (VMEM, SMEM),
        [
            pltpu.VMEM((rows, lanes), bf16),
            pltpu.VMEM((pairs_dev, 2 * FOCAL, 2 * FOCAL), f32),
            pltpu.VMEM((pairs_dev, 2, FOCAL, FOCAL), f32),
            pltpu.VMEM((pairs_dev, 2 * FOCAL, 2 * FOCAL), bf16),
        ],
        10**8, 10**6,
    )(tall, flat, spots, gains, far_slopes[0], *sections)

    out = shape((rows_dev, own_cols), f32)
    ins = [back, *tables, *slopes]
    grad = call(
        functools.partial(grad_kernel, pairs_dev, across=False), "gradient_own",
        out, [VMEM] * len(ins), VMEM, [], 10**9, 10**7,
    )(*ins)
    ins = [to_core(back), *far_tables, *far_slopes, grad]
    grad = call(
        functools.partial(last_grad_kernel, pairs_dev), "gradient_far",
        out, [VMEM] * len(ins), HBM,
        [pltpu.VMEM(out.shape, f32), pltpu.SemaphoreType.DMA((own_cols // (2 * BLOCK),))], 10**9, 10**7,
    )(*ins)
    return grad, scores


def solution(mesh):
    in_specs = (
        P(("group", "aperture"), None),
        P(),
        P(("group", "wave")),
        P(("group", "wave")),
        P(("group", "wave"), None),
    )
    out_specs = (P(("group", "aperture"), "wave"), P(("group", "wave")))
    return jax.shard_map(
        on_device, mesh=mesh, in_specs=in_specs, out_specs=out_specs, check_vma=False
    )
```

```python
import functools
import itertools
import math

import jax
import jax.numpy as jnp
from jax import lax
from jax.experimental import pallas as pl
from jax.experimental.pallas import tpu as pltpu
from jax.sharding import PartitionSpec as P

FOCAL = 256
SPOT = 4
SHIFT = 32
TERMS = 8
BLOCK = 256
GRAIN = 16
LANES = 128
PIECE = 16
SUBLANES = 8
VMEM_LIMIT = 16 * 1024 * 1024
WAVE_ROW, ANGLE_ROW, AIM_ROW, INFO_ROWS = 16, 17, 18, 24
DIRECT = 16

COS = (
    1.0, -19.7392088015709, 64.93939395773512, -85.45681453397417, 60.24458621302471,
    -26.425616460281425, 7.8991596631575085, -1.6968741456712442, 0.2437618617467591,
)
SIN = (
    6.2831853071792665, -41.34170224019464, 81.60524925425943, -76.70585885700535,
    42.05867547580699, -15.094428387947755, 3.818490079304055, -0.7122771247541972,
    0.09149844789363434,
)


def horner(terms, u):
    value = terms[-1] * u + terms[-2]
    for term in terms[-3::-1]:
        value = value * u + term
    return value


def unit_waves(counts, period):
    half = period // 2
    centred = ((counts + half) & (period - 1)) - half
    t = centred.astype(jnp.float32) * (1.0 / period)
    u = t * t
    return horner(COS, u), -(t * horner(SIN, u))


def iota(shape, axis):
    return lax.broadcasted_iota(jnp.int32, shape, axis)


def pick_coef(table, wave):
    chosen = jnp.where(iota(table.shape, 1) == wave, table, 0.0)
    return jnp.sum(chosen, axis=1, keepdims=True)


def column_freq(info_ref, pair):
    wave = info_ref[pair, WAVE_ROW : WAVE_ROW + 1, :].astype(jnp.int32)
    angle = info_ref[pair, ANGLE_ROW : ANGLE_ROW + 1, :].astype(jnp.int32)
    return (iota((1, FOCAL), 1) - FOCAL // 2 + SHIFT * angle) * (BLOCK + wave)


def fill_base(freq, shift, period, base_ref, centre_ref):
    low_r, low_i = unit_waves(iota((GRAIN, 1), 0) * freq, period)
    steps = BLOCK // GRAIN
    high_r, high_i = unit_waves((iota((steps, 1), 0) * GRAIN - BLOCK // 2 + shift) * freq, period)
    for step in range(steps):
        one_r, one_i = high_r[step : step + 1], high_i[step : step + 1]
        rows = slice(step * GRAIN, (step + 1) * GRAIN)
        base_ref[0, rows, :] = one_r * low_r - one_i * low_i
        base_ref[1, rows, :] = one_r * low_i + one_i * low_r
    count = centre_ref.shape[1]
    cent_r, cent_i = unit_waves((iota((count, 1), 0) * BLOCK + BLOCK // 2) * freq, period)
    centre_ref[0] = cent_r
    centre_ref[1] = cent_i


def power_coefs(coef):
    before, current = [1], [0, 1]
    bases = [before, current]
    for _ in range(2, TERMS):
        doubled = [0] + [2 * term for term in current]
        before, current = current, [a - b for a, b in itertools.zip_longest(doubled, before, fillvalue=0)]
        bases.append(current)
    rows = []
    for part, power in itertools.product(range(2), range(TERMS)):
        row = None
        for order in range(power, TERMS, 2):
            place = part * TERMS + order
            term = coef[place : place + 1] * float(bases[order][power])
            row = term if row is None else row + term
        rows.append(row)
    return jnp.concatenate(rows, axis=0)


def as_tiles(rows):
    return jnp.broadcast_to(rows[:, None, :], (rows.shape[0], SUBLANES, rows.shape[1]))


def split_rows(value):
    return value.reshape(value.shape[0] // SUBLANES, SUBLANES, value.shape[1])


def join_rows(value):
    return value.reshape(value.shape[0] * SUBLANES, value.shape[2])


def near_fields(s, power_ref, pairs):
    s = split_rows(s)
    outs = []
    for pair, part in itertools.product(range(pairs), range(2)):
        row = (part + 1) * TERMS - 1
        value = power_ref[pair, row] * s + power_ref[pair, row - 1]
        for row in range(row - 2, part * TERMS - 1, -1):
            value = value * s + power_ref[pair, row]
        outs.append(join_rows(value))
    return [outs[2 * pair : 2 * pair + 2] for pair in range(pairs)]


def near_slopes(s, coef_ref, pairs):
    s = split_rows(s)
    twice = s + s
    before, current = jnp.ones_like(s), twice
    outs = [
        [coef_ref[pair, row] + coef_ref[pair, row + 1] * twice for row in (1, TERMS + 1)] for pair in range(pairs)
    ]
    for order in range(3, TERMS):
        before, current = current, twice * current - before
        for pair, out in enumerate(outs):
            out[0] = out[0] + coef_ref[pair, order] * current
            out[1] = out[1] + coef_ref[pair, TERMS + order] * current
    return [[join_rows(part) for part in out] for out in outs]


def turn_round(value):
    rows, cols = value.shape
    order = LANES - 1 - iota((rows, LANES), 1)
    parts = [
        jnp.take_along_axis(value[:, start : start + LANES], order, axis=1)
        for start in range(cols - LANES, -1, -LANES)
    ]
    return jnp.concatenate(parts, axis=1)


def block_starts(cols, index):
    return cols // 2 - (index + 1) * BLOCK, cols // 2 + index * BLOCK


def both_blocks(base_r, base_i, cent_r, cent_i):
    rr, ii = base_r * cent_r, base_i * cent_i
    ri, ir = base_r * cent_i, base_i * cent_r
    return (rr + ii, ir - ri), (rr - ii, ir + ri)


def own_waves(info_ref, pair, cols, base_ref, centre_ref):
    shift = cols // 4 + 1 - lax.axis_index("wave")
    fill_base(column_freq(info_ref, pair), shift, 256 * cols, base_ref, centre_ref)


def forward_kernel(
    wave_hbm, angle_hbm, aim_hbm, coef_hbm, width_hbm, mine_ref, info_ref, own_ref, *refs
):
    pairs = info_ref.shape[0]
    table_refs, refs = refs[:pairs], refs[pairs:]
    (
        wave_ref, angle_ref, aim_ref, coef_ref, width_ref, far_ref, base_ref, centre_ref, power_ref, near_ref, acc_ref,
        sems,
    ) = refs
    rows_dev, cols = width_ref.shape
    half = cols // 2
    moves = [
        pltpu.make_async_copy(source, target, sems.at[index])
        for index, (source, target) in enumerate((
            (wave_hbm, wave_ref), (angle_hbm, angle_ref), (aim_hbm, aim_ref),
            (coef_hbm, coef_ref), (width_hbm, width_ref),
        ))
    ]
    for move in moves:
        move.start()
    for move in moves:
        move.wait()
    for pair in range(pairs):
        coef = pick_coef(coef_ref[...], wave_ref[pair])
        coef = jnp.broadcast_to(coef, (WAVE_ROW, FOCAL))
        info_ref[pair, :WAVE_ROW, :] = coef
        power_ref[pair] = as_tiles(power_coefs(coef[:, :LANES]))
        row = iota((INFO_ROWS - WAVE_ROW, FOCAL), 0) + WAVE_ROW
        ids = jnp.where(row == WAVE_ROW, wave_ref[pair], 0)
        ids = jnp.where(row == ANGLE_ROW, angle_ref[pair], ids)
        ids = jnp.where(row == AIM_ROW, aim_ref[pair, 0], ids)
        ids = jnp.where(row == AIM_ROW + 1, aim_ref[pair, 1], ids)
        info_ref[pair, WAVE_ROW:, :] = ids.astype(jnp.float32)
    for pair in range(pairs):
        own_waves(info_ref, pair, cols, base_ref.at[pair], centre_ref.at[pair])
    core = lax.axis_index("wave")
    left, right = turn_round(width_ref[:, :half]), width_ref[:, half:]
    own_ref[...] = jnp.where(core == 1, right, left)
    far_ref[...] = jnp.where(core == 1, pltpu.roll(left, 1, 1), pltpu.roll(right, half - 1, 1))

    alone = jnp.where(core == 1, 0, half)
    column = width_ref[:, pl.ds(pl.multiple_of(alone, LANES), LANES)]
    columns = near_fields(column, power_ref, pairs)
    void = jnp.where(core == 1, 0, half - 1)
    for index in range(half // (2 * BLOCK)):
        starts = block_starts(half, index)
        for start in (start + step for start in starts for step in range(0, BLOCK, LANES)):
            for side, ref in enumerate((own_ref, far_ref)):
                outs = near_fields(ref[:, start : start + LANES], power_ref, pairs)
                if side and start in (0, half - LANES):
                    keep = iota((rows_dev, LANES), 1) + start != void
                    outs = [[jnp.where(keep, part, 0.0) for part in out] for out in outs]
                for pair, part in ((pair, part) for pair in range(pairs) for part in range(2)):
                    row = (2 * side + part) * rows_dev
                    near_ref[pair, row : row + rows_dev, start : start + LANES] = outs[pair][part].astype(jnp.bfloat16)
        for pair in range(pairs):
            cent_r, cent_i = (centre_ref[pair, part, index : index + 1, :] for part in range(2))
            for row in range(0, BLOCK, GRAIN):
                base_r, base_i = (base_ref[pair, part, row : row + GRAIN, :] for part in range(2))
                for start, table in zip(starts, both_blocks(base_r, base_i, cent_r, cent_i)):
                    rows = slice(start + row, start + row + GRAIN)
                    table_refs[pair][rows, :FOCAL] = table[0].astype(jnp.bfloat16)
                    table_refs[pair][rows, FOCAL:] = table[1].astype(jnp.bfloat16)
            product = jnp.dot(
                jnp.concatenate([near_ref[pair, :, start : start + BLOCK] for start in starts], axis=1),
                jnp.concatenate([table_refs[pair][start : start + BLOCK, :] for start in starts], axis=0),
                preferred_element_type=jnp.float32,
            )
            acc_ref[pair] = product if index == 0 else acc_ref[pair] + product
    for pair in range(pairs):
        acc = [acc_ref[pair, part * rows_dev : (part + 1) * rows_dev, :] for part in range(4)]
        (own_rr, own_ri), (own_ir, own_ii), (far_rr, far_ri), (far_ir, far_ii) = (
            (part[:, :FOCAL], part[:, FOCAL:]) for part in acc
        )
        cross_r, cross_i = far_ii - own_ii, own_ri - far_ri
        real = own_rr + far_rr + jnp.where(core == 1, cross_r, -cross_r)
        imag = own_ir + far_ir + jnp.where(core == 1, cross_i, -cross_i)
        near_r, near_i = (part[:, :1].astype(jnp.bfloat16).astype(jnp.float32) for part in columns[pair])
        wave_r, wave_i = (
            part.astype(jnp.bfloat16).astype(jnp.float32)
            for part in unit_waves((alone - half) * column_freq(info_ref, pair), 256 * cols)
        )
        real = real + (near_r * wave_r - near_i * wave_i)
        imag = imag + (near_r * wave_i + near_i * wave_r)
        for part, value in enumerate((real, imag)):
            lane = (2 * pair + part) * FOCAL
            mine_ref[:, lane : lane + FOCAL] = value.astype(jnp.bfloat16)


def spot_rows(info_ref, pair, first):
    aims = [info_ref[pair, row : row + 1, :] for row in (AIM_ROW, AIM_ROW + 1)]
    rows_off = (iota((PIECE, FOCAL), 0) + first).astype(jnp.float32) - aims[0]
    cols_off = iota((1, FOCAL), 1).astype(jnp.float32) - aims[1]
    return jnp.exp(-(rows_off * rows_off + cols_off * cols_off) / (2.0 * SPOT * SPOT))


def total_of(value):
    return jnp.sum(jnp.sum(value, axis=0, keepdims=True), axis=1, keepdims=True)


def row_kernel(info_ref, tall_ref, flat_ref, spot_ref, gain_ref):
    pairs, _, rows = tall_ref.shape
    rows_dev = flat_ref.shape[1]
    period = 256 * rows
    size = min(rows, FOCAL)
    for pair in range(pairs):
        wave = info_ref[pair, WAVE_ROW : WAVE_ROW + 1, :].astype(jnp.int32) + BLOCK
        focal = (iota((FOCAL, 1), 0) - FOCAL // 2) * wave

        def step(index, carry):
            start = pl.multiple_of(index * size, size)
            place = iota((1, size), 1) + (start - rows // 2)
            for row in range(0, FOCAL, PIECE):
                real, imag = unit_waves(focal[row : row + PIECE, :size] * place, period)
                tall_ref[pair, row : row + PIECE, pl.ds(start, size)] = real.astype(jnp.bfloat16)
                row += FOCAL
                tall_ref[pair, row : row + PIECE, pl.ds(start, size)] = imag.astype(jnp.bfloat16)
            return carry

        if rows == size:
            step(0, 0)
        else:
            lax.fori_loop(0, rows // size, step, 0)
        focal = (iota((1, FOCAL), 1) - FOCAL // 2) * wave
        first = lax.axis_index("aperture") * rows_dev - rows // 2
        real, imag = unit_waves((iota((rows_dev, 1), 0) + first) * focal, period)
        flat_ref[pair, :, :FOCAL] = real.astype(jnp.bfloat16)
        flat_ref[pair, :, FOCAL:] = imag.astype(jnp.bfloat16)
        total = jnp.zeros((PIECE, FOCAL), jnp.float32)
        for row in range(0, FOCAL, PIECE):
            spot = spot_rows(info_ref, pair, row)
            spot_ref[pair, row : row + PIECE, :] = spot
            total += spot
        gain_ref[pair] = jnp.broadcast_to(FOCAL * FOCAL / total_of(total), gain_ref.shape[1:])


def join_kernel(*refs):
    *in_refs, out_ref = refs
    count = in_refs[0].shape[0]
    for index, ref in enumerate(in_refs):
        out_ref[index * count : (index + 1) * count, :] = ref[...]


def focus_kernel(steps, tall_ref, flat_ref, spot_ref, gain_ref, after_ref, *refs):
    del after_ref
    *sect_refs, back_ref, score_ref, rows_ref, mixed_ref, field_ref, stack_ref = refs
    pairs = tall_ref.shape[0]
    rows_dev = back_ref.shape[0]
    if steps is None:
        rows_ref = sect_refs[0]
    else:
        me = lax.axis_index("aperture")
        blocks = [
            ref[index * rows_dev : (index + 1) * rows_dev, :]
            for ref in sect_refs
            for index in range(ref.shape[0] // rows_dev)
        ]
        for step, block in zip(steps, blocks, strict=True):
            start = pl.multiple_of((me ^ step) * rows_dev, rows_dev)
            rows_ref[pl.ds(start, rows_dev), :] = block
    for pair in range(pairs):
        lane = 2 * pair * FOCAL
        section = rows_ref[:, lane : lane + 2 * FOCAL]
        mixed_ref[pair] = jnp.dot(tall_ref[pair], section, preferred_element_type=jnp.float32)
    pieces = [slice(row, row + PIECE) for row in range(0, FOCAL, PIECE)]
    sums = []
    for pair in range(pairs):
        totals = [jnp.zeros((PIECE, FOCAL), jnp.float32) for _ in range(2)]
        for rows in pieces:
            lower = slice(rows.start + FOCAL, rows.stop + FOCAL)
            real = mixed_ref[pair, rows, :FOCAL] - mixed_ref[pair, lower, FOCAL:]
            imag = mixed_ref[pair, rows, FOCAL:] + mixed_ref[pair, lower, :FOCAL]
            field_ref[pair, 0, rows, :] = real
            field_ref[pair, 1, rows, :] = imag
            power = real * real + imag * imag
            totals = [totals[0] + spot_ref[pair, rows, :] * power, totals[1] + power]
        sums.append((total_of(totals[0]), total_of(totals[1]) + 1e-06))
    for pair, (spot_power, all_power) in enumerate(sums):
        ratio = spot_power / all_power
        gain = gain_ref[pair, :1, :1]
        score_ref[pair] = jnp.sum(ratio * gain)
        scale = gain * 2.0 / all_power
        for rows in pieces:
            lower = slice(rows.start + FOCAL, rows.stop + FOCAL)
            weight = scale * (spot_ref[pair, rows, :] - ratio)
            real = (weight * field_ref[pair, 0, rows, :]).astype(jnp.bfloat16)
            imag = (weight * field_ref[pair, 1, rows, :]).astype(jnp.bfloat16)
            stack_ref[pair, rows, :FOCAL] = real
            stack_ref[pair, rows, FOCAL:] = imag
            stack_ref[pair, lower, :FOCAL] = imag
            stack_ref[pair, lower, FOCAL:] = -real
        back = jnp.dot(flat_ref[pair], stack_ref[pair], preferred_element_type=jnp.float32)
        lane = 2 * pair * FOCAL
        back_ref[:, lane : lane + 2 * FOCAL] = back.astype(jnp.bfloat16)


def table_kernel(scale, cols, info_ref, far_info_ref, width_ref, *refs):
    *out_refs, base_ref, centre_ref, turned_ref, coef_ref = refs
    pairs = base_ref.shape[0]
    out_refs = out_refs[-3 * pairs :]
    table_refs, slope_refs = out_refs[:pairs], out_refs[pairs:]
    own_cols = width_ref.shape[1]
    for core, ref in enumerate((info_ref, far_info_ref)):
        for pair in range(pairs):
            coef = ref[pair, : 2 * TERMS, :LANES]
            coef = coef * ((iota(coef.shape, 0) % TERMS).astype(jnp.float32) * scale)
            coef_ref[core * pairs + pair] = as_tiles(coef)
    centres = []
    for pair in range(pairs):
        own_waves(far_info_ref, pair, cols, base_ref.at[pair], centre_ref.at[pair])
        for part, row, lane in itertools.product(range(2), range(0, BLOCK, LANES), range(0, FOCAL, LANES)):
            tile = base_ref[pair, part, row : row + LANES, lane : lane + LANES]
            turned_ref[pair, part, lane : lane + LANES, row : row + LANES] = tile.T
        centres.append([centre_ref[pair, part].T for part in range(2)])
    for index in range(own_cols // (2 * BLOCK)):
        starts = block_starts(own_cols, index)
        for pair in range(pairs):
            for row in range(0, FOCAL, GRAIN):
                rows = slice(row, row + GRAIN)
                cent_r, cent_i = (centre[rows, index : index + 1] for centre in centres[pair])
                base_r, base_i = (turned_ref[pair, part, rows, :] for part in range(2))
                for start, table in zip(starts, both_blocks(base_r, base_i, cent_r, cent_i)):
                    for part, value in enumerate(table):
                        place = slice(row + part * FOCAL, row + part * FOCAL + GRAIN)
                        table_refs[pair][place, start : start + BLOCK] = value.astype(jnp.bfloat16)
        for start in (start + step for start in starts for step in range(0, BLOCK, LANES)):
            place = slice(start, start + LANES)
            slopes = near_slopes(width_ref[:, place], coef_ref, 2 * pairs)
            for ref, slope in zip(slope_refs, slopes):
                ref[0, :, place] = slope[0]
                ref[1, :, place] = slope[1]


def last_grad_kernel(pairs, *refs):
    *in_refs, out_hbm, out_ref, sems = refs
    rows_dev, own_cols = out_ref.shape
    size = 2 * BLOCK
    core = lax.axis_index("wave")
    moves = []

    def send(start, total):
        place = pl.multiple_of(jnp.where(core == 1, start, own_cols - size - start), size)
        place = pl.ds(place, size)
        out_ref[:, place] = jnp.where(core == 1, total, turn_round(total))
        index = start // size
        moves.append(pltpu.make_async_copy(out_ref.at[:, place], out_hbm.at[:, place], sems.at[index]))
        moves[-1].start()

    grad_kernel(pairs, *in_refs, out_ref, send=send)
    for move in moves:
        move.wait()


def grad_kernel(pairs, back_ref, *refs, send=None, across=True):
    *in_refs, out_ref = refs
    table_refs, slope_refs, total_ref = in_refs[:pairs], in_refs[pairs : 2 * pairs], in_refs[2 * pairs :]
    rows_dev, own_cols = out_ref.shape
    core = lax.axis_index("wave")
    lefts = []
    for pair in range(pairs):
        lane = 2 * pair * FOCAL
        real, imag = back_ref[:, lane : lane + FOCAL], back_ref[:, lane + FOCAL : lane + 2 * FOCAL]
        above = jnp.where(core == 1, imag, -imag)
        below = jnp.where(core == 1, -real, real)
        lefts.append(
            jnp.concatenate(
                [jnp.concatenate([real, above], axis=1), jnp.concatenate([imag, below], axis=1)], axis=0
            )
        )
    size = 2 * BLOCK
    for start in range(0, own_cols, size):
        place = slice(start, start + size)
        total = total_ref[0][:, place] if total_ref else jnp.zeros((rows_dev, size), jnp.float32)
        for pair in range(pairs):
            if across:
                table, dims = table_refs[pair][:, place], ((1,), (0,))
            else:
                table, dims = table_refs[pair][place, :], ((1,), (1,))
            grad = lax.dot_general(lefts[pair], table, (dims, ((), ())), preferred_element_type=jnp.float32)
            total += grad[:rows_dev] * slope_refs[pair][0, :, place]
            total += grad[rows_dev:] * slope_refs[pair][1, :, place]
        if send is None:
            out_ref[:, place] = total
        else:
            send(start, total)


VMEM = pl.BlockSpec(memory_space=pltpu.VMEM)
SMEM = pl.BlockSpec(memory_space=pltpu.SMEM)
ANY = pl.BlockSpec(memory_space=pl.ANY)
HBM = pl.BlockSpec(memory_space=pltpu.HBM)


def call(kernel, name, outs, in_specs, out_specs, scratch, flops, moved):
    return pl.pallas_call(
        kernel,
        name=name,
        out_shape=outs,
        in_specs=in_specs,
        out_specs=out_specs,
        scratch_shapes=scratch,
        cost_estimate=pl.CostEstimate(flops=flops, bytes_accessed=moved, transcendentals=0),
        compiler_params=pltpu.CompilerParams(vmem_limit_bytes=VMEM_LIMIT),
    )


def on_device(widths, coef_table, wave_ids, angle_ids, targets):
    rows_dev, cols = widths.shape
    pairs_dev = wave_ids.shape[0]
    peers = lax.axis_size("aperture")
    copies = lax.axis_size("wave")
    rows = rows_dev * peers
    own_cols = cols // copies
    lanes = 2 * pairs_dev * FOCAL
    f32, bf16 = jnp.float32, jnp.bfloat16
    shape = jax.ShapeDtypeStruct

    def in_hbm(value):
        return pltpu.with_memory_space_constraint(value, pltpu.HBM)

    def exchange(value, step):
        return lax.ppermute(value, "aperture", [(index, index ^ step) for index in range(peers)])

    def to_core(value):
        return lax.ppermute(value, "wave", [(index, (index + 1) % copies) for index in range(copies)])

    waves = [
        pltpu.VMEM((pairs_dev, 2, BLOCK, FOCAL), f32),
        pltpu.VMEM((pairs_dev, 2, 8, FOCAL), f32),
    ]
    mine, info, own, *tables = call(
        forward_kernel, "forward",
        (
            shape((rows_dev, lanes), bf16),
            shape((pairs_dev, INFO_ROWS, FOCAL), f32), shape((rows_dev, own_cols), f32),
            *[shape((own_cols, 2 * FOCAL), bf16)] * pairs_dev,
        ),
        [HBM] * 5, (VMEM,) * (3 + pairs_dev),
        [
            pltpu.SMEM(wave_ids.shape, jnp.int32),
            pltpu.SMEM(angle_ids.shape, jnp.int32),
            pltpu.SMEM(targets.shape, jnp.int32),
            pltpu.VMEM(coef_table.shape[::-1], f32),
            pltpu.VMEM(widths.shape, f32),
            pltpu.VMEM((rows_dev, own_cols), f32),
            *waves,
            pltpu.VMEM((pairs_dev, 2 * TERMS, SUBLANES, LANES), f32),
            pltpu.VMEM((pairs_dev, 4 * rows_dev, own_cols), bf16),
            pltpu.VMEM((pairs_dev, 4 * rows_dev, 2 * FOCAL), f32),
            pltpu.SemaphoreType.DMA((5,)),
        ],
        10**9, 10**7,
    )(*(in_hbm(value) for value in (wave_ids, angle_ids, targets, coef_table.T, widths)))
    far_info = to_core(info)

    tall, flat, spots, gains = call(
        row_kernel, "row_tables",
        (
            shape((pairs_dev, 2 * FOCAL, rows), bf16), shape((pairs_dev, rows_dev, 2 * FOCAL), bf16),
            shape((pairs_dev, FOCAL, FOCAL), f32), shape((pairs_dev, 8, 128), f32),
        ),
        [VMEM], (VMEM,) * 4, [], 10**8, 10**6,
    )(info)
    if peers <= DIRECT:
        steps = list(range(peers - 2, 0, -2))
        got = [exchange(mine, step) for step in steps]
        near = exchange(mine, 1)
        first, flat = lax.optimization_barrier((got[0], flat))
        joined = call(join_kernel, "join", shape(((len(steps) - 1) * rows_dev, lanes), bf16),
                      [VMEM] * (len(steps) - 1), VMEM, [], 10**6, 10**6)(*got[1:])
        sections = [mine, near, first, joined, exchange(first, 1), exchange(joined, 1)]
        steps = [0, 1, *steps, *(step ^ 1 for step in steps)]
        after = [near, joined]
    else:
        blocks = jnp.tile(mine[None], (peers, 1, 1))
        blocks = lax.all_to_all(blocks, "aperture", 0, 0, tiled=True)
        sections, steps, after = [blocks.reshape(rows, lanes)], None, []
    outs = [shape((2 * FOCAL, own_cols), bf16)] * pairs_dev + [shape((2, rows_dev, own_cols), f32)] * 2 * pairs_dev
    made = call(
        functools.partial(table_kernel, math.sqrt(rows * cols), cols), "far_tables",
        outs, [VMEM] * 3 + [ANY] * len(after), [VMEM] * len(outs),
        [*waves, pltpu.VMEM((pairs_dev, 2, FOCAL, BLOCK), f32), pltpu.VMEM((copies * pairs_dev, 2 * TERMS, SUBLANES, LANES), f32)],
        30 * 10**8, 30 * 10**6,
    )(info, far_info, own, *after)
    far_tables, slopes, far_slopes = made[:pairs_dev], made[pairs_dev : 2 * pairs_dev], made[2 * pairs_dev :]

    back, scores = call(
        functools.partial(focus_kernel, steps), "focus",
        (shape((rows_dev, lanes), bf16), shape((pairs_dev,), f32)),
        [VMEM] * 4 + [ANY] + [VMEM] * len(sections), (VMEM, SMEM),
        [
            pltpu.VMEM((rows, lanes), bf16),
            pltpu.VMEM((pairs_dev, 2 * FOCAL, 2 * FOCAL), f32),
            pltpu.VMEM((pairs_dev, 2, FOCAL, FOCAL), f32),
            pltpu.VMEM((pairs_dev, 2 * FOCAL, 2 * FOCAL), bf16),
        ],
        10**8, 10**6,
    )(tall, flat, spots, gains, far_slopes[0], *sections)

    out = shape((rows_dev, own_cols), f32)
    ins = [back, *tables, *slopes]
    grad = call(
        functools.partial(grad_kernel, pairs_dev, across=False), "gradient_own",
        out, [VMEM] * len(ins), VMEM, [], 10**9, 10**7,
    )(*ins)
    ins = [to_core(back), *far_tables, *far_slopes, grad]
    grad = call(
        functools.partial(last_grad_kernel, pairs_dev), "gradient_far",
        out, [VMEM] * len(ins), HBM,
        [pltpu.VMEM(out.shape, f32), pltpu.SemaphoreType.DMA((own_cols // (2 * BLOCK),))], 10**9, 10**7,
    )(*ins)
    return grad, scores


def solution(mesh):
    in_specs = (
        P(("group", "aperture"), None),
        P(),
        P(("group", "wave")),
        P(("group", "wave")),
        P(("group", "wave"), None),
    )
    out_specs = (P(("group", "aperture"), "wave"), P(("group", "wave")))
    return jax.shard_map(
        on_device, mesh=mesh, in_specs=in_specs, out_specs=out_specs, check_vma=False
    )
```

```python
import functools
import itertools
import math

import jax
import jax.numpy as jnp
from jax import lax
from jax.experimental import pallas as pl
from jax.experimental.pallas import tpu as pltpu
from jax.sharding import PartitionSpec as P

FOCAL = 256
SPOT = 4
SHIFT = 32
TERMS = 8
BLOCK = 256
GRAIN = 16
LANES = 128
PIECE = 16
SUBLANES = 8
VMEM_LIMIT = 16 * 1024 * 1024
WAVE_ROW, ANGLE_ROW, AIM_ROW, INFO_ROWS = 16, 17, 18, 24
DIRECT = 16

COS = (
    1.0, -19.7392088015709, 64.93939395773512, -85.45681453397417, 60.24458621302471,
    -26.425616460281425, 7.8991596631575085, -1.6968741456712442, 0.2437618617467591,
)
SIN = (
    6.2831853071792665, -41.34170224019464, 81.60524925425943, -76.70585885700535,
    42.05867547580699, -15.094428387947755, 3.818490079304055, -0.7122771247541972,
    0.09149844789363434,
)


def horner(terms, u):
    value = terms[-1] * u + terms[-2]
    for term in terms[-3::-1]:
        value = value * u + term
    return value


def unit_waves(counts, period):
    half = period // 2
    centred = ((counts + half) & (period - 1)) - half
    t = centred.astype(jnp.float32) * (1.0 / period)
    u = t * t
    return horner(COS, u), -(t * horner(SIN, u))


def iota(shape, axis):
    return lax.broadcasted_iota(jnp.int32, shape, axis)


def pick_coef(table, wave):
    chosen = jnp.where(iota(table.shape, 1) == wave, table, 0.0)
    return jnp.sum(chosen, axis=1, keepdims=True)


def column_freq(info_ref, pair):
    wave = info_ref[pair, WAVE_ROW : WAVE_ROW + 1, :].astype(jnp.int32)
    angle = info_ref[pair, ANGLE_ROW : ANGLE_ROW + 1, :].astype(jnp.int32)
    return (iota((1, FOCAL), 1) - FOCAL // 2 + SHIFT * angle) * (BLOCK + wave)


def fill_base(freq, shift, period, base_ref, centre_ref):
    low_r, low_i = unit_waves(iota((GRAIN, 1), 0) * freq, period)
    steps = BLOCK // GRAIN
    high_r, high_i = unit_waves((iota((steps, 1), 0) * GRAIN - BLOCK // 2 + shift) * freq, period)
    for step in range(steps):
        one_r, one_i = high_r[step : step + 1], high_i[step : step + 1]
        rows = slice(step * GRAIN, (step + 1) * GRAIN)
        base_ref[0, rows, :] = one_r * low_r - one_i * low_i
        base_ref[1, rows, :] = one_r * low_i + one_i * low_r
    count = centre_ref.shape[1]
    cent_r, cent_i = unit_waves((iota((count, 1), 0) * BLOCK + BLOCK // 2) * freq, period)
    centre_ref[0] = cent_r
    centre_ref[1] = cent_i


def power_coefs(coef):
    before, current = [1], [0, 1]
    bases = [before, current]
    for _ in range(2, TERMS):
        doubled = [0] + [2 * term for term in current]
        before, current = current, [a - b for a, b in itertools.zip_longest(doubled, before, fillvalue=0)]
        bases.append(current)
    rows = []
    for part, power in itertools.product(range(2), range(TERMS)):
        row = None
        for order in range(power, TERMS, 2):
            place = part * TERMS + order
            term = coef[place : place + 1] * float(bases[order][power])
            row = term if row is None else row + term
        rows.append(row)
    return jnp.concatenate(rows, axis=0)


def as_tiles(rows):
    return jnp.broadcast_to(rows[:, None, :], (rows.shape[0], SUBLANES, rows.shape[1]))


def split_rows(value):
    return value.reshape(value.shape[0] // SUBLANES, SUBLANES, value.shape[1])


def join_rows(value):
    return value.reshape(value.shape[0] * SUBLANES, value.shape[2])


def near_fields(s, power_ref, pairs):
    s = split_rows(s)
    outs = []
    for pair, part in itertools.product(range(pairs), range(2)):
        row = (part + 1) * TERMS - 1
        value = power_ref[pair, row] * s + power_ref[pair, row - 1]
        for row in range(row - 2, part * TERMS - 1, -1):
            value = value * s + power_ref[pair, row]
        outs.append(join_rows(value))
    return [outs[2 * pair : 2 * pair + 2] for pair in range(pairs)]


def near_slopes(s, coef_ref, pairs):
    s = split_rows(s)
    twice = s + s
    before, current = jnp.ones_like(s), twice
    outs = [
        [coef_ref[pair, row] + coef_ref[pair, row + 1] * twice for row in (1, TERMS + 1)] for pair in range(pairs)
    ]
    for order in range(3, TERMS):
        before, current = current, twice * current - before
        for pair, out in enumerate(outs):
            out[0] = out[0] + coef_ref[pair, order] * current
            out[1] = out[1] + coef_ref[pair, TERMS + order] * current
    return [[join_rows(part) for part in out] for out in outs]


def turn_round(value):
    rows, cols = value.shape
    order = LANES - 1 - iota((rows, LANES), 1)
    parts = [
        jnp.take_along_axis(value[:, start : start + LANES], order, axis=1)
        for start in range(cols - LANES, -1, -LANES)
    ]
    return jnp.concatenate(parts, axis=1)


def block_starts(cols, index):
    return cols // 2 - (index + 1) * BLOCK, cols // 2 + index * BLOCK


def both_blocks(base_r, base_i, cent_r, cent_i):
    rr, ii = base_r * cent_r, base_i * cent_i
    ri, ir = base_r * cent_i, base_i * cent_r
    return (rr + ii, ir - ri), (rr - ii, ir + ri)


def own_waves(info_ref, pair, cols, base_ref, centre_ref):
    shift = cols // 4 + 1 - lax.axis_index("wave")
    fill_base(column_freq(info_ref, pair), shift, 256 * cols, base_ref, centre_ref)


def forward_kernel(
    wave_hbm, angle_hbm, aim_hbm, coef_hbm, width_hbm, mine_ref, info_ref, own_ref, *refs
):
    pairs = info_ref.shape[0]
    table_refs, refs = refs[:pairs], refs[pairs:]
    (
        wave_ref, angle_ref, aim_ref, coef_ref, width_ref, far_ref, base_ref, centre_ref, power_ref, near_ref, acc_ref,
        sems,
    ) = refs
    rows_dev, cols = width_ref.shape
    half = cols // 2
    moves = [
        pltpu.make_async_copy(source, target, sems.at[index])
        for index, (source, target) in enumerate((
            (wave_hbm, wave_ref), (angle_hbm, angle_ref), (aim_hbm, aim_ref),
            (coef_hbm, coef_ref), (width_hbm, width_ref),
        ))
    ]
    for move in moves:
        move.start()
    for move in moves:
        move.wait()
    for pair in range(pairs):
        coef = pick_coef(coef_ref[...], wave_ref[pair])
        coef = jnp.broadcast_to(coef, (WAVE_ROW, FOCAL))
        info_ref[pair, :WAVE_ROW, :] = coef
        power_ref[pair] = as_tiles(power_coefs(coef[:, :LANES]))
        row = iota((INFO_ROWS - WAVE_ROW, FOCAL), 0) + WAVE_ROW
        ids = jnp.where(row == WAVE_ROW, wave_ref[pair], 0)
        ids = jnp.where(row == ANGLE_ROW, angle_ref[pair], ids)
        ids = jnp.where(row == AIM_ROW, aim_ref[pair, 0], ids)
        ids = jnp.where(row == AIM_ROW + 1, aim_ref[pair, 1], ids)
        info_ref[pair, WAVE_ROW:, :] = ids.astype(jnp.float32)
    for pair in range(pairs):
        own_waves(info_ref, pair, cols, base_ref.at[pair], centre_ref.at[pair])
    core = lax.axis_index("wave")
    left, right = turn_round(width_ref[:, :half]), width_ref[:, half:]
    own_ref[...] = jnp.where(core == 1, right, left)
    far_ref[...] = jnp.where(core == 1, pltpu.roll(left, 1, 1), pltpu.roll(right, half - 1, 1))

    alone = jnp.where(core == 1, 0, half)
    column = width_ref[:, pl.ds(pl.multiple_of(alone, LANES), LANES)]
    columns = near_fields(column, power_ref, pairs)
    void = jnp.where(core == 1, 0, half - 1)
    for index in range(half // (2 * BLOCK)):
        starts = block_starts(half, index)
        for start in (start + step for start in starts for step in range(0, BLOCK, LANES)):
            for side, ref in enumerate((own_ref, far_ref)):
                outs = near_fields(ref[:, start : start + LANES], power_ref, pairs)
                if side and start in (0, half - LANES):
                    keep = iota((rows_dev, LANES), 1) + start != void
                    outs = [[jnp.where(keep, part, 0.0) for part in out] for out in outs]
                for pair, part in ((pair, part) for pair in range(pairs) for part in range(2)):
                    row = (2 * side + part) * rows_dev
                    near_ref[pair, row : row + rows_dev, start : start + LANES] = outs[pair][part].astype(jnp.bfloat16)
        for pair in range(pairs):
            cent_r, cent_i = (centre_ref[pair, part, index : index + 1, :] for part in range(2))
            for row in range(0, BLOCK, GRAIN):
                base_r, base_i = (base_ref[pair, part, row : row + GRAIN, :] for part in range(2))
                for start, table in zip(starts, both_blocks(base_r, base_i, cent_r, cent_i)):
                    rows = slice(start + row, start + row + GRAIN)
                    table_refs[pair][rows, :FOCAL] = table[0].astype(jnp.bfloat16)
                    table_refs[pair][rows, FOCAL:] = table[1].astype(jnp.bfloat16)
            product = jnp.dot(
                jnp.concatenate([near_ref[pair, :, start : start + BLOCK] for start in starts], axis=1),
                jnp.concatenate([table_refs[pair][start : start + BLOCK, :] for start in starts], axis=0),
                preferred_element_type=jnp.float32,
            )
            acc_ref[pair] = product if index == 0 else acc_ref[pair] + product
    for pair in range(pairs):
        acc = [acc_ref[pair, part * rows_dev : (part + 1) * rows_dev, :] for part in range(4)]
        (own_rr, own_ri), (own_ir, own_ii), (far_rr, far_ri), (far_ir, far_ii) = (
            (part[:, :FOCAL], part[:, FOCAL:]) for part in acc
        )
        cross_r, cross_i = far_ii - own_ii, own_ri - far_ri
        real = own_rr + far_rr + jnp.where(core == 1, cross_r, -cross_r)
        imag = own_ir + far_ir + jnp.where(core == 1, cross_i, -cross_i)
        near_r, near_i = (part[:, :1].astype(jnp.bfloat16).astype(jnp.float32) for part in columns[pair])
        wave_r, wave_i = (
            part.astype(jnp.bfloat16).astype(jnp.float32)
            for part in unit_waves((alone - half) * column_freq(info_ref, pair), 256 * cols)
        )
        real = real + (near_r * wave_r - near_i * wave_i)
        imag = imag + (near_r * wave_i + near_i * wave_r)
        for part, value in enumerate((real, imag)):
            lane = (2 * pair + part) * FOCAL
            mine_ref[:, lane : lane + FOCAL] = value.astype(jnp.bfloat16)


def spot_rows(info_ref, pair, first):
    aims = [info_ref[pair, row : row + 1, :] for row in (AIM_ROW, AIM_ROW + 1)]
    rows_off = (iota((PIECE, FOCAL), 0) + first).astype(jnp.float32) - aims[0]
    cols_off = iota((1, FOCAL), 1).astype(jnp.float32) - aims[1]
    return jnp.exp(-(rows_off * rows_off + cols_off * cols_off) / (2.0 * SPOT * SPOT))


def total_of(value):
    return jnp.sum(jnp.sum(value, axis=0, keepdims=True), axis=1, keepdims=True)


def row_kernel(info_ref, tall_ref, flat_ref, spot_ref, gain_ref):
    pairs, _, rows = tall_ref.shape
    rows_dev = flat_ref.shape[1]
    period = 256 * rows
    size = min(rows, FOCAL)
    for pair in range(pairs):
        wave = info_ref[pair, WAVE_ROW : WAVE_ROW + 1, :].astype(jnp.int32) + BLOCK
        focal = (iota((FOCAL, 1), 0) - FOCAL // 2) * wave

        def step(index, carry):
            start = pl.multiple_of(index * size, size)
            place = iota((1, size), 1) + (start - rows // 2)
            for row in range(0, FOCAL, PIECE):
                real, imag = unit_waves(focal[row : row + PIECE, :size] * place, period)
                tall_ref[pair, row : row + PIECE, pl.ds(start, size)] = real.astype(jnp.bfloat16)
                row += FOCAL
                tall_ref[pair, row : row + PIECE, pl.ds(start, size)] = imag.astype(jnp.bfloat16)
            return carry

        if rows == size:
            step(0, 0)
        else:
            lax.fori_loop(0, rows // size, step, 0)
        focal = (iota((1, FOCAL), 1) - FOCAL // 2) * wave
        first = lax.axis_index("aperture") * rows_dev - rows // 2
        real, imag = unit_waves((iota((rows_dev, 1), 0) + first) * focal, period)
        flat_ref[pair, :, :FOCAL] = real.astype(jnp.bfloat16)
        flat_ref[pair, :, FOCAL:] = imag.astype(jnp.bfloat16)
        total = jnp.zeros((PIECE, FOCAL), jnp.float32)
        for row in range(0, FOCAL, PIECE):
            spot = spot_rows(info_ref, pair, row)
            spot_ref[pair, row : row + PIECE, :] = spot
            total += spot
        gain_ref[pair] = jnp.broadcast_to(FOCAL * FOCAL / total_of(total), gain_ref.shape[1:])


def join_kernel(*refs):
    *in_refs, out_ref = refs
    count = in_refs[0].shape[0]
    for index, ref in enumerate(in_refs):
        out_ref[index * count : (index + 1) * count, :] = ref[...]


def focus_kernel(steps, tall_ref, flat_ref, spot_ref, gain_ref, after_ref, *refs):
    del after_ref
    *sect_refs, back_ref, score_ref, rows_ref, mixed_ref, field_ref, stack_ref = refs
    pairs = tall_ref.shape[0]
    rows_dev = back_ref.shape[0]
    if steps is None:
        rows_ref = sect_refs[0]
    else:
        me = lax.axis_index("aperture")
        blocks = [
            ref[index * rows_dev : (index + 1) * rows_dev, :]
            for ref in sect_refs
            for index in range(ref.shape[0] // rows_dev)
        ]
        for step, block in zip(steps, blocks, strict=True):
            start = pl.multiple_of((me ^ step) * rows_dev, rows_dev)
            rows_ref[pl.ds(start, rows_dev), :] = block
    for pair in range(pairs):
        lane = 2 * pair * FOCAL
        section = rows_ref[:, lane : lane + 2 * FOCAL]
        mixed_ref[pair] = jnp.dot(tall_ref[pair], section, preferred_element_type=jnp.float32)
    pieces = [slice(row, row + PIECE) for row in range(0, FOCAL, PIECE)]
    sums = []
    for pair in range(pairs):
        totals = [jnp.zeros((PIECE, FOCAL), jnp.float32) for _ in range(2)]
        for rows in pieces:
            lower = slice(rows.start + FOCAL, rows.stop + FOCAL)
            real = mixed_ref[pair, rows, :FOCAL] - mixed_ref[pair, lower, FOCAL:]
            imag = mixed_ref[pair, rows, FOCAL:] + mixed_ref[pair, lower, :FOCAL]
            field_ref[pair, 0, rows, :] = real
            field_ref[pair, 1, rows, :] = imag
            power = real * real + imag * imag
            totals = [totals[0] + spot_ref[pair, rows, :] * power, totals[1] + power]
        sums.append((total_of(totals[0]), total_of(totals[1]) + 1e-06))
    for pair, (spot_power, all_power) in enumerate(sums):
        ratio = spot_power / all_power
        gain = gain_ref[pair, :1, :1]
        score_ref[pair] = jnp.sum(ratio * gain)
        scale = gain * 2.0 / all_power
        for rows in pieces:
            lower = slice(rows.start + FOCAL, rows.stop + FOCAL)
            weight = scale * (spot_ref[pair, rows, :] - ratio)
            real = (weight * field_ref[pair, 0, rows, :]).astype(jnp.bfloat16)
            imag = (weight * field_ref[pair, 1, rows, :]).astype(jnp.bfloat16)
            stack_ref[pair, rows, :FOCAL] = real
            stack_ref[pair, rows, FOCAL:] = imag
            stack_ref[pair, lower, :FOCAL] = imag
            stack_ref[pair, lower, FOCAL:] = -real
        back = jnp.dot(flat_ref[pair], stack_ref[pair], preferred_element_type=jnp.float32)
        lane = 2 * pair * FOCAL
        back_ref[:, lane : lane + 2 * FOCAL] = back.astype(jnp.bfloat16)


def table_kernel(scale, cols, info_ref, far_info_ref, width_ref, *refs):
    *out_refs, base_ref, centre_ref, turned_ref, coef_ref = refs
    pairs = base_ref.shape[0]
    out_refs = out_refs[-3 * pairs :]
    table_refs, slope_refs = out_refs[:pairs], out_refs[pairs:]
    own_cols = width_ref.shape[1]
    for core, ref in enumerate((info_ref, far_info_ref)):
        for pair in range(pairs):
            coef = ref[pair, : 2 * TERMS, :LANES]
            coef = coef * ((iota(coef.shape, 0) % TERMS).astype(jnp.float32) * scale)
            coef_ref[core * pairs + pair] = as_tiles(coef)
    centres = []
    for pair in range(pairs):
        own_waves(far_info_ref, pair, cols, base_ref.at[pair], centre_ref.at[pair])
        for part, row, lane in itertools.product(range(2), range(0, BLOCK, LANES), range(0, FOCAL, LANES)):
            tile = base_ref[pair, part, row : row + LANES, lane : lane + LANES]
            turned_ref[pair, part, lane : lane + LANES, row : row + LANES] = tile.T
        centres.append([centre_ref[pair, part].T for part in range(2)])
    for index in range(own_cols // (2 * BLOCK)):
        starts = block_starts(own_cols, index)
        for pair in range(pairs):
            for row in range(0, FOCAL, GRAIN):
                rows = slice(row, row + GRAIN)
                cent_r, cent_i = (centre[rows, index : index + 1] for centre in centres[pair])
                base_r, base_i = (turned_ref[pair, part, rows, :] for part in range(2))
                for start, table in zip(starts, both_blocks(base_r, base_i, cent_r, cent_i)):
                    for part, value in enumerate(table):
                        place = slice(row + part * FOCAL, row + part * FOCAL + GRAIN)
                        table_refs[pair][place, start : start + BLOCK] = value.astype(jnp.bfloat16)
        for start in (start + step for start in starts for step in range(0, BLOCK, LANES)):
            place = slice(start, start + LANES)
            slopes = near_slopes(width_ref[:, place], coef_ref, 2 * pairs)
            for ref, slope in zip(slope_refs, slopes):
                ref[0, :, place] = slope[0]
                ref[1, :, place] = slope[1]


def last_grad_kernel(pairs, *refs):
    *in_refs, out_hbm, out_ref, sems = refs
    rows_dev, own_cols = out_ref.shape
    size = 2 * BLOCK
    core = lax.axis_index("wave")
    moves = []

    def send(start, total):
        place = pl.multiple_of(jnp.where(core == 1, start, own_cols - size - start), size)
        place = pl.ds(place, size)
        out_ref[:, place] = jnp.where(core == 1, total, turn_round(total))
        index = start // size
        moves.append(pltpu.make_async_copy(out_ref.at[:, place], out_hbm.at[:, place], sems.at[index]))
        moves[-1].start()

    grad_kernel(pairs, *in_refs, out_ref, send=send)
    for move in moves:
        move.wait()


def grad_kernel(pairs, back_ref, *refs, send=None, across=True):
    *in_refs, out_ref = refs
    table_refs, slope_refs, total_ref = in_refs[:pairs], in_refs[pairs : 2 * pairs], in_refs[2 * pairs :]
    rows_dev, own_cols = out_ref.shape
    core = lax.axis_index("wave")
    lefts = []
    for pair in range(pairs):
        lane = 2 * pair * FOCAL
        real, imag = back_ref[:, lane : lane + FOCAL], back_ref[:, lane + FOCAL : lane + 2 * FOCAL]
        above = jnp.where(core == 1, imag, -imag)
        below = jnp.where(core == 1, -real, real)
        lefts.append(
            jnp.concatenate(
                [jnp.concatenate([real, above], axis=1), jnp.concatenate([imag, below], axis=1)], axis=0
            )
        )
    size = 2 * BLOCK
    for start in range(0, own_cols, size):
        place = slice(start, start + size)
        total = total_ref[0][:, place] if total_ref else jnp.zeros((rows_dev, size), jnp.float32)
        for pair in range(pairs):
            if across:
                table, dims = table_refs[pair][:, place], ((1,), (0,))
            else:
                table, dims = table_refs[pair][place, :], ((1,), (1,))
            grad = lax.dot_general(lefts[pair], table, (dims, ((), ())), preferred_element_type=jnp.float32)
            total += grad[:rows_dev] * slope_refs[pair][0, :, place]
            total += grad[rows_dev:] * slope_refs[pair][1, :, place]
        if send is None:
            out_ref[:, place] = total
        else:
            send(start, total)


VMEM = pl.BlockSpec(memory_space=pltpu.VMEM)
SMEM = pl.BlockSpec(memory_space=pltpu.SMEM)
ANY = pl.BlockSpec(memory_space=pl.ANY)
HBM = pl.BlockSpec(memory_space=pltpu.HBM)


def call(kernel, name, outs, in_specs, out_specs, scratch, flops, moved):
    return pl.pallas_call(
        kernel,
        name=name,
        out_shape=outs,
        in_specs=in_specs,
        out_specs=out_specs,
        scratch_shapes=scratch,
        cost_estimate=pl.CostEstimate(flops=flops, bytes_accessed=moved, transcendentals=0),
        compiler_params=pltpu.CompilerParams(vmem_limit_bytes=VMEM_LIMIT),
    )


def on_device(widths, coef_table, wave_ids, angle_ids, targets):
    rows_dev, cols = widths.shape
    pairs_dev = wave_ids.shape[0]
    peers = lax.axis_size("aperture")
    copies = lax.axis_size("wave")
    rows = rows_dev * peers
    own_cols = cols // copies
    lanes = 2 * pairs_dev * FOCAL
    f32, bf16 = jnp.float32, jnp.bfloat16
    shape = jax.ShapeDtypeStruct

    def in_hbm(value):
        return pltpu.with_memory_space_constraint(value, pltpu.HBM)

    def exchange(value, step):
        return lax.ppermute(value, "aperture", [(index, index ^ step) for index in range(peers)])

    def to_core(value):
        return lax.ppermute(value, "wave", [(index, (index + 1) % copies) for index in range(copies)])

    waves = [
        pltpu.VMEM((pairs_dev, 2, BLOCK, FOCAL), f32),
        pltpu.VMEM((pairs_dev, 2, 8, FOCAL), f32),
    ]
    mine, info, own, *tables = call(
        forward_kernel, "forward",
        (
            shape((rows_dev, lanes), bf16),
            shape((pairs_dev, INFO_ROWS, FOCAL), f32), shape((rows_dev, own_cols), f32),
            *[shape((own_cols, 2 * FOCAL), bf16)] * pairs_dev,
        ),
        [HBM] * 5, (VMEM,) * (3 + pairs_dev),
        [
            pltpu.SMEM(wave_ids.shape, jnp.int32),
            pltpu.SMEM(angle_ids.shape, jnp.int32),
            pltpu.SMEM(targets.shape, jnp.int32),
            pltpu.VMEM(coef_table.shape[::-1], f32),
            pltpu.VMEM(widths.shape, f32),
            pltpu.VMEM((rows_dev, own_cols), f32),
            *waves,
            pltpu.VMEM((pairs_dev, 2 * TERMS, SUBLANES, LANES), f32),
            pltpu.VMEM((pairs_dev, 4 * rows_dev, own_cols), bf16),
            pltpu.VMEM((pairs_dev, 4 * rows_dev, 2 * FOCAL), f32),
            pltpu.SemaphoreType.DMA((5,)),
        ],
        10**9, 10**7,
    )(*(in_hbm(value) for value in (wave_ids, angle_ids, targets, coef_table.T, widths)))
    far_info = to_core(info)

    tall, flat, spots, gains = call(
        row_kernel, "row_tables",
        (
            shape((pairs_dev, 2 * FOCAL, rows), bf16), shape((pairs_dev, rows_dev, 2 * FOCAL), bf16),
            shape((pairs_dev, FOCAL, FOCAL), f32), shape((pairs_dev, 8, 128), f32),
        ),
        [VMEM], (VMEM,) * 4, [], 10**8, 10**6,
    )(info)
    gathered = lax.all_gather(mine, "aperture", axis=0, tiled=True)
    sections, steps, after = [gathered], None, []
    outs = [shape((2 * FOCAL, own_cols), bf16)] * pairs_dev + [shape((2, rows_dev, own_cols), f32)] * 2 * pairs_dev
    made = call(
        functools.partial(table_kernel, math.sqrt(rows * cols), cols), "far_tables",
        outs, [VMEM] * 3 + [ANY] * len(after), [VMEM] * len(outs),
        [*waves, pltpu.VMEM((pairs_dev, 2, FOCAL, BLOCK), f32), pltpu.VMEM((copies * pairs_dev, 2 * TERMS, SUBLANES, LANES), f32)],
        30 * 10**8, 30 * 10**6,
    )(info, far_info, own, *after)
    far_tables, slopes, far_slopes = made[:pairs_dev], made[pairs_dev : 2 * pairs_dev], made[2 * pairs_dev :]

    back, scores = call(
        functools.partial(focus_kernel, steps), "focus",
        (shape((rows_dev, lanes), bf16), shape((pairs_dev,), f32)),
        [VMEM] * 4 + [ANY] + [VMEM] * len(sections), (VMEM, SMEM),
        [
            pltpu.VMEM((rows, lanes), bf16),
            pltpu.VMEM((pairs_dev, 2 * FOCAL, 2 * FOCAL), f32),
            pltpu.VMEM((pairs_dev, 2, FOCAL, FOCAL), f32),
            pltpu.VMEM((pairs_dev, 2 * FOCAL, 2 * FOCAL), bf16),
        ],
        10**8, 10**6,
    )(tall, flat, spots, gains, far_slopes[0], *sections)

    out = shape((rows_dev, own_cols), f32)
    ins = [back, *tables, *slopes]
    grad = call(
        functools.partial(grad_kernel, pairs_dev, across=False), "gradient_own",
        out, [VMEM] * len(ins), VMEM, [], 10**9, 10**7,
    )(*ins)
    ins = [to_core(back), *far_tables, *far_slopes, grad]
    grad = call(
        functools.partial(last_grad_kernel, pairs_dev), "gradient_far",
        out, [VMEM] * len(ins), HBM,
        [pltpu.VMEM(out.shape, f32), pltpu.SemaphoreType.DMA((own_cols // (2 * BLOCK),))], 10**9, 10**7,
    )(*ins)
    return grad, scores


def solution(mesh):
    in_specs = (
        P(("group", "aperture"), None),
        P(),
        P(("group", "wave")),
        P(("group", "wave")),
        P(("group", "wave"), None),
    )
    out_specs = (P(("group", "aperture"), "wave"), P(("group", "wave")))
    return jax.shard_map(
        on_device, mesh=mesh, in_specs=in_specs, out_specs=out_specs, check_vma=False
    )
```

```python
import functools
import itertools
import math

import jax
import jax.numpy as jnp
from jax import lax
from jax.experimental import pallas as pl
from jax.experimental.pallas import tpu as pltpu
from jax.sharding import PartitionSpec as P

FOCAL = 256
SPOT = 4
SHIFT = 32
TERMS = 8
BLOCK = 256
GRAIN = 16
LANES = 128
PIECE = 16
SUBLANES = 8
VMEM_LIMIT = 16 * 1024 * 1024
WAVE_ROW, ANGLE_ROW, AIM_ROW, INFO_ROWS = 16, 17, 18, 24
DIRECT = 16

COS = (
    1.0, -19.7392088015709, 64.93939395773512, -85.45681453397417, 60.24458621302471,
    -26.425616460281425, 7.8991596631575085, -1.6968741456712442, 0.2437618617467591,
)
SIN = (
    6.2831853071792665, -41.34170224019464, 81.60524925425943, -76.70585885700535,
    42.05867547580699, -15.094428387947755, 3.818490079304055, -0.7122771247541972,
    0.09149844789363434,
)


def horner(terms, u):
    value = terms[-1] * u + terms[-2]
    for term in terms[-3::-1]:
        value = value * u + term
    return value


def unit_waves(counts, period):
    half = period // 2
    centred = ((counts + half) & (period - 1)) - half
    t = centred.astype(jnp.float32) * (1.0 / period)
    u = t * t
    return horner(COS, u), -(t * horner(SIN, u))


def iota(shape, axis):
    return lax.broadcasted_iota(jnp.int32, shape, axis)


def pick_coef(table, wave):
    chosen = jnp.where(iota(table.shape, 1) == wave, table, 0.0)
    return jnp.sum(chosen, axis=1, keepdims=True)


def column_freq(info_ref, pair):
    wave = info_ref[pair, WAVE_ROW : WAVE_ROW + 1, :].astype(jnp.int32)
    angle = info_ref[pair, ANGLE_ROW : ANGLE_ROW + 1, :].astype(jnp.int32)
    return (iota((1, FOCAL), 1) - FOCAL // 2 + SHIFT * angle) * (BLOCK + wave)


def fill_base(freq, shift, period, base_ref, centre_ref):
    low_r, low_i = unit_waves(iota((GRAIN, 1), 0) * freq, period)
    steps = BLOCK // GRAIN
    high_r, high_i = unit_waves((iota((steps, 1), 0) * GRAIN - BLOCK // 2 + shift) * freq, period)
    for step in range(steps):
        one_r, one_i = high_r[step : step + 1], high_i[step : step + 1]
        rows = slice(step * GRAIN, (step + 1) * GRAIN)
        base_ref[0, rows, :] = one_r * low_r - one_i * low_i
        base_ref[1, rows, :] = one_r * low_i + one_i * low_r
    count = centre_ref.shape[1]
    cent_r, cent_i = unit_waves((iota((count, 1), 0) * BLOCK + BLOCK // 2) * freq, period)
    centre_ref[0] = cent_r
    centre_ref[1] = cent_i


def power_coefs(coef):
    before, current = [1], [0, 1]
    bases = [before, current]
    for _ in range(2, TERMS):
        doubled = [0] + [2 * term for term in current]
        before, current = current, [a - b for a, b in itertools.zip_longest(doubled, before, fillvalue=0)]
        bases.append(current)
    rows = []
    for part, power in itertools.product(range(2), range(TERMS)):
        row = None
        for order in range(power, TERMS, 2):
            place = part * TERMS + order
            term = coef[place : place + 1] * float(bases[order][power])
            row = term if row is None else row + term
        rows.append(row)
    return jnp.concatenate(rows, axis=0)


def as_tiles(rows):
    return jnp.broadcast_to(rows[:, None, :], (rows.shape[0], SUBLANES, rows.shape[1]))


def split_rows(value):
    return value.reshape(value.shape[0] // SUBLANES, SUBLANES, value.shape[1])


def join_rows(value):
    return value.reshape(value.shape[0] * SUBLANES, value.shape[2])


def near_fields(s, power_ref, pairs):
    s = split_rows(s)
    outs = []
    for pair, part in itertools.product(range(pairs), range(2)):
        row = (part + 1) * TERMS - 1
        value = power_ref[pair, row] * s + power_ref[pair, row - 1]
        for row in range(row - 2, part * TERMS - 1, -1):
            value = value * s + power_ref[pair, row]
        outs.append(join_rows(value))
    return [outs[2 * pair : 2 * pair + 2] for pair in range(pairs)]


def near_slopes(s, power_ref, pairs):
    s = split_rows(s)
    outs = []
    for pair, part in itertools.product(range(pairs), range(2)):
        row = (part + 1) * TERMS - 1
        value = power_ref[pair, row] * s + power_ref[pair, row - 1]
        for row in range(row - 2, part * TERMS, -1):
            value = value * s + power_ref[pair, row]
        outs.append(join_rows(value))
    return [outs[2 * pair : 2 * pair + 2] for pair in range(pairs)]


def turn_round(value):
    rows, cols = value.shape
    order = LANES - 1 - iota((rows, LANES), 1)
    parts = [
        jnp.take_along_axis(value[:, start : start + LANES], order, axis=1)
        for start in range(cols - LANES, -1, -LANES)
    ]
    return jnp.concatenate(parts, axis=1)


def block_starts(cols, index):
    return cols // 2 - (index + 1) * BLOCK, cols // 2 + index * BLOCK


def both_blocks(base_r, base_i, cent_r, cent_i):
    rr, ii = base_r * cent_r, base_i * cent_i
    ri, ir = base_r * cent_i, base_i * cent_r
    return (rr + ii, ir - ri), (rr - ii, ir + ri)


def own_waves(info_ref, pair, cols, base_ref, centre_ref):
    shift = cols // 4 + 1 - lax.axis_index("wave")
    fill_base(column_freq(info_ref, pair), shift, 256 * cols, base_ref, centre_ref)


def forward_kernel(
    wave_hbm, angle_hbm, aim_hbm, coef_hbm, width_hbm, mine_ref, info_ref, own_ref, *refs
):
    pairs = info_ref.shape[0]
    (
        wave_ref, angle_ref, aim_ref, coef_ref, width_ref, far_ref, base_ref, centre_ref, power_ref, near_ref, table_ref,
        acc_ref, sems,
    ) = refs
    rows_dev, cols = width_ref.shape
    half = cols // 2
    moves = [
        pltpu.make_async_copy(source, target, sems.at[index])
        for index, (source, target) in enumerate((
            (wave_hbm, wave_ref), (angle_hbm, angle_ref), (aim_hbm, aim_ref),
            (coef_hbm, coef_ref), (width_hbm, width_ref),
        ))
    ]
    for move in moves:
        move.start()
    for move in moves:
        move.wait()
    for pair in range(pairs):
        coef = pick_coef(coef_ref[...], wave_ref[pair])
        coef = jnp.broadcast_to(coef, (WAVE_ROW, FOCAL))
        info_ref[pair, :WAVE_ROW, :] = coef
        power_ref[pair] = as_tiles(power_coefs(coef[:, :LANES]))
        row = iota((INFO_ROWS - WAVE_ROW, FOCAL), 0) + WAVE_ROW
        ids = jnp.where(row == WAVE_ROW, wave_ref[pair], 0)
        ids = jnp.where(row == ANGLE_ROW, angle_ref[pair], ids)
        ids = jnp.where(row == AIM_ROW, aim_ref[pair, 0], ids)
        ids = jnp.where(row == AIM_ROW + 1, aim_ref[pair, 1], ids)
        info_ref[pair, WAVE_ROW:, :] = ids.astype(jnp.float32)
    for pair in range(pairs):
        own_waves(info_ref, pair, cols, base_ref.at[pair], centre_ref.at[pair])
    core = lax.axis_index("wave")
    left, right = turn_round(width_ref[:, :half]), width_ref[:, half:]
    own_ref[...] = jnp.where(core == 1, right, left)
    far_ref[...] = jnp.where(core == 1, pltpu.roll(left, 1, 1), pltpu.roll(right, half - 1, 1))

    alone = jnp.where(core == 1, 0, half)
    column = width_ref[:, pl.ds(pl.multiple_of(alone, LANES), LANES)]
    columns = near_fields(column, power_ref, pairs)
    void = jnp.where(core == 1, 0, half - 1)
    for index in range(half // (2 * BLOCK)):
        starts = block_starts(half, index)
        for start in (start + step for start in starts for step in range(0, BLOCK, LANES)):
            for side, ref in enumerate((own_ref, far_ref)):
                outs = near_fields(ref[:, start : start + LANES], power_ref, pairs)
                if side and start in (0, half - LANES):
                    keep = iota((rows_dev, LANES), 1) + start != void
                    outs = [[jnp.where(keep, part, 0.0) for part in out] for out in outs]
                for pair, part in ((pair, part) for pair in range(pairs) for part in range(2)):
                    row = (2 * side + part) * rows_dev
                    near_ref[pair, row : row + rows_dev, start : start + LANES] = outs[pair][part].astype(jnp.bfloat16)
        for pair in range(pairs):
            cent_r, cent_i = (centre_ref[pair, part, index : index + 1, :] for part in range(2))
            for row in range(0, BLOCK, GRAIN):
                base_r, base_i = (base_ref[pair, part, row : row + GRAIN, :] for part in range(2))
                for start, table in zip(starts, both_blocks(base_r, base_i, cent_r, cent_i)):
                    rows = slice(start + row, start + row + GRAIN)
                    table_ref[pair, rows, :FOCAL] = table[0].astype(jnp.bfloat16)
                    table_ref[pair, rows, FOCAL:] = table[1].astype(jnp.bfloat16)
            product = jnp.dot(
                jnp.concatenate([near_ref[pair, :, start : start + BLOCK] for start in starts], axis=1),
                jnp.concatenate([table_ref[pair, start : start + BLOCK, :] for start in starts], axis=0),
                preferred_element_type=jnp.float32,
            )
            acc_ref[pair] = product if index == 0 else acc_ref[pair] + product
    for pair in range(pairs):
        acc = [acc_ref[pair, part * rows_dev : (part + 1) * rows_dev, :] for part in range(4)]
        (own_rr, own_ri), (own_ir, own_ii), (far_rr, far_ri), (far_ir, far_ii) = (
            (part[:, :FOCAL], part[:, FOCAL:]) for part in acc
        )
        cross_r, cross_i = far_ii - own_ii, own_ri - far_ri
        real = own_rr + far_rr + jnp.where(core == 1, cross_r, -cross_r)
        imag = own_ir + far_ir + jnp.where(core == 1, cross_i, -cross_i)
        near_r, near_i = (part[:, :1].astype(jnp.bfloat16).astype(jnp.float32) for part in columns[pair])
        wave_r, wave_i = (
            part.astype(jnp.bfloat16).astype(jnp.float32)
            for part in unit_waves((alone - half) * column_freq(info_ref, pair), 256 * cols)
        )
        real = real + (near_r * wave_r - near_i * wave_i)
        imag = imag + (near_r * wave_i + near_i * wave_r)
        for part, value in enumerate((real, imag)):
            lane = (2 * pair + part) * FOCAL
            mine_ref[:, lane : lane + FOCAL] = value.astype(jnp.bfloat16)


def spot_rows(info_ref, pair, first):
    aims = [info_ref[pair, row : row + 1, :] for row in (AIM_ROW, AIM_ROW + 1)]
    rows_off = (iota((PIECE, FOCAL), 0) + first).astype(jnp.float32) - aims[0]
    cols_off = iota((1, FOCAL), 1).astype(jnp.float32) - aims[1]
    return jnp.exp(-(rows_off * rows_off + cols_off * cols_off) / (2.0 * SPOT * SPOT))


def total_of(value):
    return jnp.sum(jnp.sum(value, axis=0, keepdims=True), axis=1, keepdims=True)


def row_kernel(info_ref, tall_ref, flat_ref, spot_ref, gain_ref):
    pairs, _, rows = tall_ref.shape
    rows_dev = flat_ref.shape[1]
    period = 256 * rows
    size = min(rows, FOCAL)
    for pair in range(pairs):
        wave = info_ref[pair, WAVE_ROW : WAVE_ROW + 1, :].astype(jnp.int32) + BLOCK
        focal = (iota((FOCAL, 1), 0) - FOCAL // 2) * wave

        def step(index, carry):
            start = pl.multiple_of(index * size, size)
            place = iota((1, size), 1) + (start - rows // 2)
            for row in range(0, FOCAL, PIECE):
                real, imag = unit_waves(focal[row : row + PIECE, :size] * place, period)
                tall_ref[pair, row : row + PIECE, pl.ds(start, size)] = real.astype(jnp.bfloat16)
                row += FOCAL
                tall_ref[pair, row : row + PIECE, pl.ds(start, size)] = imag.astype(jnp.bfloat16)
            return carry

        if rows == size:
            step(0, 0)
        else:
            lax.fori_loop(0, rows // size, step, 0)
        focal = (iota((1, FOCAL), 1) - FOCAL // 2) * wave
        first = lax.axis_index("aperture") * rows_dev - rows // 2
        real, imag = unit_waves((iota((rows_dev, 1), 0) + first) * focal, period)
        flat_ref[pair, :, :FOCAL] = real.astype(jnp.bfloat16)
        flat_ref[pair, :, FOCAL:] = imag.astype(jnp.bfloat16)
        total = jnp.zeros((PIECE, FOCAL), jnp.float32)
        for row in range(0, FOCAL, PIECE):
            spot = spot_rows(info_ref, pair, row)
            spot_ref[pair, row : row + PIECE, :] = spot
            total += spot
        gain_ref[pair] = jnp.broadcast_to(FOCAL * FOCAL / total_of(total), gain_ref.shape[1:])


def join_kernel(*refs):
    *in_refs, out_ref = refs
    count = in_refs[0].shape[0]
    for index, ref in enumerate(in_refs):
        out_ref[index * count : (index + 1) * count, :] = ref[...]


def focus_kernel(pair, steps, tall_ref, flat_ref, spot_ref, gain_ref, after_ref, *refs):
    del after_ref
    last = pair == tall_ref.shape[0] - 1
    *in_refs, back_ref, score_ref, rows_ref, mixed_ref, field_ref, stack_ref = refs
    before_refs, sect_refs = in_refs[:pair], in_refs[pair:]
    rows_dev = back_ref.shape[0]
    lanes = slice(2 * pair * FOCAL, 2 * (pair + 1) * FOCAL)
    if steps is None:
        section = sect_refs[0][:, lanes]
    else:
        me = lax.axis_index("aperture")
        blocks = [
            ref[index * rows_dev : (index + 1) * rows_dev, lanes]
            for ref in sect_refs
            for index in range(ref.shape[0] // rows_dev)
        ]
        for step, block in zip(steps, blocks, strict=True):
            start = pl.multiple_of((me ^ step) * rows_dev, rows_dev)
            rows_ref[pl.ds(start, rows_dev), :] = block
        section = rows_ref[...]
    mixed_ref[...] = jnp.dot(tall_ref[pair], section, preferred_element_type=jnp.float32)
    pieces = [slice(row, row + PIECE) for row in range(0, FOCAL, PIECE)]
    totals = [jnp.zeros((PIECE, FOCAL), jnp.float32) for _ in range(2)]
    for rows in pieces:
        lower = slice(rows.start + FOCAL, rows.stop + FOCAL)
        real = mixed_ref[rows, :FOCAL] - mixed_ref[lower, FOCAL:]
        imag = mixed_ref[rows, FOCAL:] + mixed_ref[lower, :FOCAL]
        field_ref[0, rows, :] = real
        field_ref[1, rows, :] = imag
        power = real * real + imag * imag
        totals = [totals[0] + spot_ref[pair, rows, :] * power, totals[1] + power]
    spot_power, all_power = total_of(totals[0]), total_of(totals[1]) + 1e-06
    ratio = spot_power / all_power
    gain = gain_ref[pair, :1, :1]
    if last:
        for index, ref in enumerate(before_refs):
            score_ref[index] = jnp.sum(ref[:1, :1])
        score_ref[pair] = jnp.sum(ratio * gain)
    else:
        score_ref[...] = jnp.broadcast_to(ratio * gain, score_ref.shape)
    scale = gain * 2.0 / all_power
    for rows in pieces:
        lower = slice(rows.start + FOCAL, rows.stop + FOCAL)
        weight = scale * (spot_ref[pair, rows, :] - ratio)
        real = (weight * field_ref[0, rows, :]).astype(jnp.bfloat16)
        imag = (weight * field_ref[1, rows, :]).astype(jnp.bfloat16)
        stack_ref[rows, :FOCAL] = real
        stack_ref[rows, FOCAL:] = imag
        stack_ref[lower, :FOCAL] = imag
        stack_ref[lower, FOCAL:] = -real
    back = jnp.dot(flat_ref[pair], stack_ref[...], preferred_element_type=jnp.float32)
    back_ref[...] = back.astype(jnp.bfloat16)


def table_kernel(scale, cols, info_ref, far_info_ref, width_ref, *refs):
    *out_refs, base_ref, centre_ref, turned_ref, power_ref = refs
    pairs = power_ref.shape[0]
    out_refs = out_refs[-2 * pairs :]
    table_refs, slope_refs = out_refs[:pairs], out_refs[pairs:]
    own_cols = width_ref.shape[1]
    sources = [(ref, pair) for ref in (info_ref, far_info_ref) for pair in range(pairs // 2)]
    centres = []
    for pair, (ref, source) in enumerate(sources):
        power = power_coefs(ref[source, : 2 * TERMS, :LANES])
        power_ref[pair] = as_tiles(power * ((iota(power.shape, 0) % TERMS).astype(jnp.float32) * scale))
        own_waves(ref, source, cols, base_ref.at[pair], centre_ref.at[pair])
        for part, row, lane in itertools.product(range(2), range(0, BLOCK, LANES), range(0, FOCAL, LANES)):
            tile = base_ref[pair, part, row : row + LANES, lane : lane + LANES]
            turned_ref[pair, part, lane : lane + LANES, row : row + LANES] = tile.T
        centres.append([centre_ref[pair, part].T for part in range(2)])
    for index in range(own_cols // (2 * BLOCK)):
        starts = block_starts(own_cols, index)
        for pair in range(pairs):
            for row in range(0, FOCAL, GRAIN):
                rows = slice(row, row + GRAIN)
                cent_r, cent_i = (centre[rows, index : index + 1] for centre in centres[pair])
                base_r, base_i = (turned_ref[pair, part, rows, :] for part in range(2))
                for start, table in zip(starts, both_blocks(base_r, base_i, cent_r, cent_i)):
                    for part, value in enumerate(table):
                        place = slice(row + part * FOCAL, row + part * FOCAL + GRAIN)
                        table_refs[pair][place, start : start + BLOCK] = value.astype(jnp.bfloat16)
        for start in (start + step for start in starts for step in range(0, BLOCK, LANES)):
            place = slice(start, start + LANES)
            slopes = near_slopes(width_ref[:, place], power_ref, pairs)
            for ref, slope in zip(slope_refs, slopes):
                ref[0, :, place] = slope[0]
                ref[1, :, place] = slope[1]


def last_grad_kernel(pairs, *refs):
    *in_refs, out_hbm, out_ref, sems = refs
    rows_dev, own_cols = out_ref.shape
    size = 2 * BLOCK
    core = lax.axis_index("wave")
    moves = []

    def send(start, total):
        place = pl.multiple_of(jnp.where(core == 1, start, own_cols - size - start), size)
        place = pl.ds(place, size)
        out_ref[:, place] = jnp.where(core == 1, total, turn_round(total))
        index = start // size
        moves.append(pltpu.make_async_copy(out_ref.at[:, place], out_hbm.at[:, place], sems.at[index]))
        moves[-1].start()

    grad_kernel(pairs, *in_refs, out_ref, send=send)
    for move in moves:
        move.wait()


def grad_kernel(pairs, *refs, send=None):
    *in_refs, out_ref = refs
    back_refs, table_refs, slope_refs = (in_refs[first * pairs : (first + 1) * pairs] for first in range(3))
    total_ref = in_refs[3 * pairs :]
    rows_dev, own_cols = out_ref.shape
    core = lax.axis_index("wave")
    lefts = []
    for ref in back_refs:
        real, imag = ref[:, :FOCAL], ref[:, FOCAL:]
        above = jnp.where(core == 1, imag, -imag)
        below = jnp.where(core == 1, -real, real)
        lefts.append(
            jnp.concatenate(
                [jnp.concatenate([real, above], axis=1), jnp.concatenate([imag, below], axis=1)], axis=0
            )
        )
    size = 2 * BLOCK
    for start in range(0, own_cols, size):
        place = slice(start, start + size)
        total = total_ref[0][:, place] if total_ref else jnp.zeros((rows_dev, size), jnp.float32)
        for left, table_ref, slope_ref in zip(lefts, table_refs, slope_refs):
            grad = jnp.dot(left, table_ref[:, place], preferred_element_type=jnp.float32)
            total += grad[:rows_dev] * slope_ref[0, :, place]
            total += grad[rows_dev:] * slope_ref[1, :, place]
        if send is None:
            out_ref[:, place] = total
        else:
            send(start, total)


VMEM = pl.BlockSpec(memory_space=pltpu.VMEM)
SMEM = pl.BlockSpec(memory_space=pltpu.SMEM)
ANY = pl.BlockSpec(memory_space=pl.ANY)
HBM = pl.BlockSpec(memory_space=pltpu.HBM)


def call(kernel, name, outs, in_specs, out_specs, scratch, flops, moved):
    return pl.pallas_call(
        kernel,
        name=name,
        out_shape=outs,
        in_specs=in_specs,
        out_specs=out_specs,
        scratch_shapes=scratch,
        cost_estimate=pl.CostEstimate(flops=flops, bytes_accessed=moved, transcendentals=0),
        compiler_params=pltpu.CompilerParams(vmem_limit_bytes=VMEM_LIMIT),
    )


def on_device(widths, coef_table, wave_ids, angle_ids, targets):
    rows_dev, cols = widths.shape
    pairs_dev = wave_ids.shape[0]
    peers = lax.axis_size("aperture")
    copies = lax.axis_size("wave")
    rows = rows_dev * peers
    pairs = pairs_dev * copies
    own_cols = cols // copies
    lanes = 2 * pairs_dev * FOCAL
    f32, bf16 = jnp.float32, jnp.bfloat16
    shape = jax.ShapeDtypeStruct

    def in_hbm(value):
        return pltpu.with_memory_space_constraint(value, pltpu.HBM)

    def exchange(value, step):
        return lax.ppermute(value, "aperture", [(index, index ^ step) for index in range(peers)])

    def to_core(value):
        return lax.ppermute(value, "wave", [(index, (index + 1) % copies) for index in range(copies)])

    waves = [
        pltpu.VMEM((pairs_dev, 2, BLOCK, FOCAL), f32),
        pltpu.VMEM((pairs_dev, 2, 8, FOCAL), f32),
    ]
    mine, info, own = call(
        forward_kernel, "forward",
        (
            shape((rows_dev, lanes), bf16),
            shape((pairs_dev, INFO_ROWS, FOCAL), f32), shape((rows_dev, own_cols), f32),
        ),
        [HBM] * 5, (VMEM,) * 3,
        [
            pltpu.SMEM(wave_ids.shape, jnp.int32),
            pltpu.SMEM(angle_ids.shape, jnp.int32),
            pltpu.SMEM(targets.shape, jnp.int32),
            pltpu.VMEM(coef_table.shape[::-1], f32),
            pltpu.VMEM(widths.shape, f32),
            pltpu.VMEM((rows_dev, own_cols), f32),
            *waves,
            pltpu.VMEM((pairs_dev, 2 * TERMS, SUBLANES, LANES), f32),
            pltpu.VMEM((pairs_dev, 4 * rows_dev, own_cols), bf16),
            pltpu.VMEM((pairs_dev, own_cols, 2 * FOCAL), bf16),
            pltpu.VMEM((pairs_dev, 4 * rows_dev, 2 * FOCAL), f32),
            pltpu.SemaphoreType.DMA((5,)),
        ],
        10**9, 10**7,
    )(*(in_hbm(value) for value in (wave_ids, angle_ids, targets, coef_table.T, widths)))
    far_info = to_core(info)

    tall, flat, spots, gains = call(
        row_kernel, "row_tables",
        (
            shape((pairs_dev, 2 * FOCAL, rows), bf16), shape((pairs_dev, rows_dev, 2 * FOCAL), bf16),
            shape((pairs_dev, FOCAL, FOCAL), f32), shape((pairs_dev, 8, 128), f32),
        ),
        [VMEM], (VMEM,) * 4, [], 10**8, 10**6,
    )(info)
    if peers <= DIRECT:
        steps = list(range(peers - 2, 0, -2))
        got = [exchange(mine, step) for step in steps]
        near = exchange(mine, 1)
        first, flat = lax.optimization_barrier((got[0], flat))
        joined = call(join_kernel, "join", shape(((len(steps) - 1) * rows_dev, lanes), bf16),
                      [VMEM] * (len(steps) - 1), VMEM, [], 10**6, 10**6)(*got[1:])
        sections = [mine, near, first, joined, exchange(first, 1), exchange(joined, 1)]
        steps = [0, 1, *steps, *(step ^ 1 for step in steps)]
        after = [near, joined]
    else:
        blocks = jnp.tile(mine[None], (peers, 1, 1))
        blocks = lax.all_to_all(blocks, "aperture", 0, 0, tiled=True)
        sections, steps, after = [blocks.reshape(rows, lanes)], None, []
    outs = [shape((2 * FOCAL, own_cols), bf16)] * pairs + [shape((2, rows_dev, own_cols), f32)] * pairs
    made = call(
        functools.partial(table_kernel, math.sqrt(rows * cols), cols), "column_tables",
        outs, [VMEM] * 3 + [ANY] * len(after), [VMEM] * len(outs),
        [
            pltpu.VMEM((pairs, 2, BLOCK, FOCAL), f32),
            pltpu.VMEM((pairs, 2, 8, FOCAL), f32),
            pltpu.VMEM((pairs, 2, FOCAL, BLOCK), f32),
            pltpu.VMEM((pairs, 2 * TERMS, SUBLANES, LANES), f32),
        ],
        30 * 10**8, 30 * 10**6,
    )(info, far_info, own, *after)
    tables, slopes = made[:pairs], made[pairs:]

    backs, scores, last = [], [], slopes[0]
    for pair in range(pairs_dev):
        final = pair == pairs_dev - 1
        score = shape((pairs_dev,), f32) if final else shape((SUBLANES, LANES), f32)
        last, score = call(
            functools.partial(focus_kernel, pair, steps), f"focus_{pair}",
            (shape((rows_dev, 2 * FOCAL), bf16), score),
            [VMEM] * 4 + [ANY] + [VMEM] * (pair + len(sections)), (VMEM, SMEM if final else VMEM),
            [
                pltpu.VMEM((rows, 2 * FOCAL), bf16),
                pltpu.VMEM((2 * FOCAL, 2 * FOCAL), f32),
                pltpu.VMEM((2, FOCAL, FOCAL), f32),
                pltpu.VMEM((2 * FOCAL, 2 * FOCAL), bf16),
            ],
            10**8, 10**6,
        )(tall, flat, spots, gains, last, *scores, *sections)
        backs.append(last)
        scores.append(score)
    backs = backs + [to_core(back) for back in backs]

    out = shape((rows_dev, own_cols), f32)
    grad = ()
    for first, count in ((0, pairs_dev), *((pair, 1) for pair in range(pairs_dev, pairs))):
        some = slice(first, first + count)
        ins = [*backs[some], *tables[some], *slopes[some], *grad]
        final = first + count == pairs
        result = call(
            functools.partial(last_grad_kernel if final else grad_kernel, count), f"gradient_{first}",
            out, [VMEM] * len(ins), HBM if final else VMEM,
            [pltpu.VMEM(out.shape, f32), pltpu.SemaphoreType.DMA((own_cols // (2 * BLOCK),))] if final else [],
            10**9, 10**7,
        )(*ins)
        grad = (result,)
    return result, scores[-1]


def solution(mesh):
    in_specs = (
        P(("group", "aperture"), None),
        P(),
        P(("group", "wave")),
        P(("group", "wave")),
        P(("group", "wave"), None),
    )
    out_specs = (P(("group", "aperture"), "wave"), P(("group", "wave")))
    return jax.shard_map(
        on_device, mesh=mesh, in_specs=in_specs, out_specs=out_specs, check_vma=False
    )
```

```python
import functools
import itertools
import math

import jax
import jax.numpy as jnp
from jax import lax
from jax.experimental import pallas as pl
from jax.experimental.pallas import tpu as pltpu
from jax.sharding import PartitionSpec as P

FOCAL = 256
SPOT = 4
SHIFT = 32
TERMS = 8
BLOCK = 256
GRAIN = 16
LANES = 128
PIECE = 16
SUBLANES = 8
VMEM_LIMIT = 16 * 1024 * 1024
WAVE_ROW, ANGLE_ROW, AIM_ROW, INFO_ROWS = 16, 17, 18, 24
DIRECT = 16

COS = (
    1.0, -19.7392088015709, 64.93939395773512, -85.45681453397417, 60.24458621302471,
    -26.425616460281425, 7.8991596631575085, -1.6968741456712442, 0.2437618617467591,
)
SIN = (
    6.2831853071792665, -41.34170224019464, 81.60524925425943, -76.70585885700535,
    42.05867547580699, -15.094428387947755, 3.818490079304055, -0.7122771247541972,
    0.09149844789363434,
)


def horner(terms, u):
    value = terms[-1] * u + terms[-2]
    for term in terms[-3::-1]:
        value = value * u + term
    return value


def unit_waves(counts, period):
    half = period // 2
    centred = ((counts + half) & (period - 1)) - half
    t = centred.astype(jnp.float32) * (1.0 / period)
    u = t * t
    return horner(COS, u), -(t * horner(SIN, u))


def iota(shape, axis):
    return lax.broadcasted_iota(jnp.int32, shape, axis)


def pick_coef(table, wave):
    chosen = jnp.where(iota(table.shape, 1) == wave, table, 0.0)
    return jnp.sum(chosen, axis=1, keepdims=True)


def column_freq(info_ref, pair):
    wave = info_ref[pair, WAVE_ROW : WAVE_ROW + 1, :].astype(jnp.int32)
    angle = info_ref[pair, ANGLE_ROW : ANGLE_ROW + 1, :].astype(jnp.int32)
    return (iota((1, FOCAL), 1) - FOCAL // 2 + SHIFT * angle) * (BLOCK + wave)


def fill_base(freq, shift, period, base_ref, centre_ref):
    low_r, low_i = unit_waves(iota((GRAIN, 1), 0) * freq, period)
    steps = BLOCK // GRAIN
    high_r, high_i = unit_waves((iota((steps, 1), 0) * GRAIN - BLOCK // 2 + shift) * freq, period)
    for step in range(steps):
        one_r, one_i = high_r[step : step + 1], high_i[step : step + 1]
        rows = slice(step * GRAIN, (step + 1) * GRAIN)
        base_ref[0, rows, :] = one_r * low_r - one_i * low_i
        base_ref[1, rows, :] = one_r * low_i + one_i * low_r
    count = centre_ref.shape[1]
    cent_r, cent_i = unit_waves((iota((count, 1), 0) * BLOCK + BLOCK // 2) * freq, period)
    centre_ref[0] = cent_r
    centre_ref[1] = cent_i


def power_coefs(coef):
    before, current = [1], [0, 1]
    bases = [before, current]
    for _ in range(2, TERMS):
        doubled = [0] + [2 * term for term in current]
        before, current = current, [a - b for a, b in itertools.zip_longest(doubled, before, fillvalue=0)]
        bases.append(current)
    rows = []
    for part, power in itertools.product(range(2), range(TERMS)):
        row = None
        for order in range(power, TERMS, 2):
            place = part * TERMS + order
            term = coef[place : place + 1] * float(bases[order][power])
            row = term if row is None else row + term
        rows.append(row)
    return jnp.concatenate(rows, axis=0)


def as_tiles(rows):
    return jnp.broadcast_to(rows[:, None, :], (rows.shape[0], SUBLANES, rows.shape[1]))


def split_rows(value):
    return value.reshape(value.shape[0] // SUBLANES, SUBLANES, value.shape[1])


def join_rows(value):
    return value.reshape(value.shape[0] * SUBLANES, value.shape[2])


def near_fields(s, power_ref, pairs):
    s = split_rows(s)
    outs = []
    for pair, part in itertools.product(range(pairs), range(2)):
        row = (part + 1) * TERMS - 1
        value = power_ref[pair, row] * s + power_ref[pair, row - 1]
        for row in range(row - 2, part * TERMS - 1, -1):
            value = value * s + power_ref[pair, row]
        outs.append(join_rows(value))
    return [outs[2 * pair : 2 * pair + 2] for pair in range(pairs)]


def near_slopes(s, power_ref, pairs):
    s = split_rows(s)
    outs = []
    for pair, part in itertools.product(range(pairs), range(2)):
        row = (part + 1) * TERMS - 1
        value = power_ref[pair, row] * s + power_ref[pair, row - 1]
        for row in range(row - 2, part * TERMS, -1):
            value = value * s + power_ref[pair, row]
        outs.append(join_rows(value))
    return [outs[2 * pair : 2 * pair + 2] for pair in range(pairs)]


def turn_round(value):
    rows, cols = value.shape
    order = LANES - 1 - iota((rows, LANES), 1)
    parts = [
        jnp.take_along_axis(value[:, start : start + LANES], order, axis=1)
        for start in range(cols - LANES, -1, -LANES)
    ]
    return jnp.concatenate(parts, axis=1)


def block_starts(cols, index):
    return cols // 2 - (index + 1) * BLOCK, cols // 2 + index * BLOCK


def both_blocks(base_r, base_i, cent_r, cent_i):
    rr, ii = base_r * cent_r, base_i * cent_i
    ri, ir = base_r * cent_i, base_i * cent_r
    return (rr + ii, ir - ri), (rr - ii, ir + ri)


def own_waves(info_ref, pair, cols, base_ref, centre_ref):
    shift = cols // 4 + 1 - lax.axis_index("wave")
    fill_base(column_freq(info_ref, pair), shift, 256 * cols, base_ref, centre_ref)


def forward_kernel(
    wave_hbm, angle_hbm, aim_hbm, coef_hbm, width_hbm, mine_ref, info_ref, own_ref, *refs
):
    pairs = info_ref.shape[0]
    (
        wave_ref, angle_ref, aim_ref, coef_ref, width_ref, far_ref, base_ref, centre_ref, power_ref, near_ref, table_ref,
        acc_ref, sems,
    ) = refs
    rows_dev, cols = width_ref.shape
    half = cols // 2
    moves = [
        pltpu.make_async_copy(source, target, sems.at[index])
        for index, (source, target) in enumerate((
            (wave_hbm, wave_ref), (angle_hbm, angle_ref), (aim_hbm, aim_ref),
            (coef_hbm, coef_ref), (width_hbm, width_ref),
        ))
    ]
    for move in moves:
        move.start()
    for move in moves:
        move.wait()
    for pair in range(pairs):
        coef = pick_coef(coef_ref[...], wave_ref[pair])
        coef = jnp.broadcast_to(coef, (WAVE_ROW, FOCAL))
        info_ref[pair, :WAVE_ROW, :] = coef
        power_ref[pair] = as_tiles(power_coefs(coef[:, :LANES]))
        row = iota((INFO_ROWS - WAVE_ROW, FOCAL), 0) + WAVE_ROW
        ids = jnp.where(row == WAVE_ROW, wave_ref[pair], 0)
        ids = jnp.where(row == ANGLE_ROW, angle_ref[pair], ids)
        ids = jnp.where(row == AIM_ROW, aim_ref[pair, 0], ids)
        ids = jnp.where(row == AIM_ROW + 1, aim_ref[pair, 1], ids)
        info_ref[pair, WAVE_ROW:, :] = ids.astype(jnp.float32)
    for pair in range(pairs):
        own_waves(info_ref, pair, cols, base_ref.at[pair], centre_ref.at[pair])
    core = lax.axis_index("wave")
    left, right = turn_round(width_ref[:, :half]), width_ref[:, half:]
    own_ref[...] = jnp.where(core == 1, right, left)
    far_ref[...] = jnp.where(core == 1, pltpu.roll(left, 1, 1), pltpu.roll(right, half - 1, 1))

    alone = jnp.where(core == 1, 0, half)
    column = width_ref[:, pl.ds(pl.multiple_of(alone, LANES), LANES)]
    columns = near_fields(column, power_ref, pairs)
    void = jnp.where(core == 1, 0, half - 1)
    for index in range(half // (2 * BLOCK)):
        starts = block_starts(half, index)
        for start in (start + step for start in starts for step in range(0, BLOCK, LANES)):
            for side, ref in enumerate((own_ref, far_ref)):
                outs = near_fields(ref[:, start : start + LANES], power_ref, pairs)
                if side and start in (0, half - LANES):
                    keep = iota((rows_dev, LANES), 1) + start != void
                    outs = [[jnp.where(keep, part, 0.0) for part in out] for out in outs]
                for pair, part in ((pair, part) for pair in range(pairs) for part in range(2)):
                    row = (2 * side + part) * rows_dev
                    near_ref[pair, row : row + rows_dev, start : start + LANES] = outs[pair][part].astype(jnp.bfloat16)
        for pair in range(pairs):
            cent_r, cent_i = (centre_ref[pair, part, index : index + 1, :] for part in range(2))
            for row in range(0, BLOCK, GRAIN):
                base_r, base_i = (base_ref[pair, part, row : row + GRAIN, :] for part in range(2))
                for start, table in zip(starts, both_blocks(base_r, base_i, cent_r, cent_i)):
                    rows = slice(start + row, start + row + GRAIN)
                    table_ref[pair, rows, :FOCAL] = table[0].astype(jnp.bfloat16)
                    table_ref[pair, rows, FOCAL:] = table[1].astype(jnp.bfloat16)
            product = jnp.dot(
                jnp.concatenate([near_ref[pair, :, start : start + BLOCK] for start in starts], axis=1),
                jnp.concatenate([table_ref[pair, start : start + BLOCK, :] for start in starts], axis=0),
                preferred_element_type=jnp.float32,
            )
            acc_ref[pair] = product if index == 0 else acc_ref[pair] + product
    for pair in range(pairs):
        acc = [acc_ref[pair, part * rows_dev : (part + 1) * rows_dev, :] for part in range(4)]
        (own_rr, own_ri), (own_ir, own_ii), (far_rr, far_ri), (far_ir, far_ii) = (
            (part[:, :FOCAL], part[:, FOCAL:]) for part in acc
        )
        cross_r, cross_i = far_ii - own_ii, own_ri - far_ri
        real = own_rr + far_rr + jnp.where(core == 1, cross_r, -cross_r)
        imag = own_ir + far_ir + jnp.where(core == 1, cross_i, -cross_i)
        near_r, near_i = (part[:, :1].astype(jnp.bfloat16).astype(jnp.float32) for part in columns[pair])
        wave_r, wave_i = (
            part.astype(jnp.bfloat16).astype(jnp.float32)
            for part in unit_waves((alone - half) * column_freq(info_ref, pair), 256 * cols)
        )
        real = real + (near_r * wave_r - near_i * wave_i)
        imag = imag + (near_r * wave_i + near_i * wave_r)
        for part, value in enumerate((real, imag)):
            lane = (2 * pair + part) * FOCAL
            mine_ref[:, lane : lane + FOCAL] = value.astype(jnp.bfloat16)


def spot_rows(info_ref, pair, first):
    aims = [info_ref[pair, row : row + 1, :] for row in (AIM_ROW, AIM_ROW + 1)]
    rows_off = (iota((PIECE, FOCAL), 0) + first).astype(jnp.float32) - aims[0]
    cols_off = iota((1, FOCAL), 1).astype(jnp.float32) - aims[1]
    return jnp.exp(-(rows_off * rows_off + cols_off * cols_off) / (2.0 * SPOT * SPOT))


def total_of(value):
    return jnp.sum(jnp.sum(value, axis=0, keepdims=True), axis=1, keepdims=True)


def row_kernel(info_ref, tall_ref, flat_ref, spot_ref, gain_ref):
    pairs, _, rows = tall_ref.shape
    rows_dev = flat_ref.shape[1]
    period = 256 * rows
    size = min(rows, FOCAL)
    for pair in range(pairs):
        wave = info_ref[pair, WAVE_ROW : WAVE_ROW + 1, :].astype(jnp.int32) + BLOCK
        focal = (iota((FOCAL, 1), 0) - FOCAL // 2) * wave

        def step(index, carry):
            start = pl.multiple_of(index * size, size)
            place = iota((1, size), 1) + (start - rows // 2)
            for row in range(0, FOCAL, PIECE):
                real, imag = unit_waves(focal[row : row + PIECE, :size] * place, period)
                tall_ref[pair, row : row + PIECE, pl.ds(start, size)] = real.astype(jnp.bfloat16)
                row += FOCAL
                tall_ref[pair, row : row + PIECE, pl.ds(start, size)] = imag.astype(jnp.bfloat16)
            return carry

        if rows == size:
            step(0, 0)
        else:
            lax.fori_loop(0, rows // size, step, 0)
        focal = (iota((1, FOCAL), 1) - FOCAL // 2) * wave
        first = lax.axis_index("aperture") * rows_dev - rows // 2
        real, imag = unit_waves((iota((rows_dev, 1), 0) + first) * focal, period)
        flat_ref[pair, :, :FOCAL] = real.astype(jnp.bfloat16)
        flat_ref[pair, :, FOCAL:] = imag.astype(jnp.bfloat16)
        total = jnp.zeros((PIECE, FOCAL), jnp.float32)
        for row in range(0, FOCAL, PIECE):
            spot = spot_rows(info_ref, pair, row)
            spot_ref[pair, row : row + PIECE, :] = spot
            total += spot
        gain_ref[pair] = jnp.broadcast_to(FOCAL * FOCAL / total_of(total), gain_ref.shape[1:])


def join_kernel(*refs):
    *in_refs, out_ref = refs
    count = in_refs[0].shape[0]
    for index, ref in enumerate(in_refs):
        out_ref[index * count : (index + 1) * count, :] = ref[...]


def focus_kernel(steps, tall_ref, flat_ref, spot_ref, gain_ref, after_ref, *refs):
    del after_ref
    *sect_refs, back_ref, score_ref, rows_ref, mixed_ref, field_ref, stack_ref = refs
    pairs = tall_ref.shape[0]
    rows_dev = back_ref.shape[0]
    if steps is None:
        rows_ref = sect_refs[0]
    else:
        me = lax.axis_index("aperture")
        blocks = [
            ref[index * rows_dev : (index + 1) * rows_dev, :]
            for ref in sect_refs
            for index in range(ref.shape[0] // rows_dev)
        ]
        for step, block in zip(steps, blocks, strict=True):
            start = pl.multiple_of((me ^ step) * rows_dev, rows_dev)
            rows_ref[pl.ds(start, rows_dev), :] = block
    for pair in range(pairs):
        lane = 2 * pair * FOCAL
        section = rows_ref[:, lane : lane + 2 * FOCAL]
        mixed_ref[pair] = jnp.dot(tall_ref[pair], section, preferred_element_type=jnp.float32)
    pieces = [slice(row, row + PIECE) for row in range(0, FOCAL, PIECE)]
    sums = []
    for pair in range(pairs):
        totals = [jnp.zeros((PIECE, FOCAL), jnp.float32) for _ in range(2)]
        for rows in pieces:
            lower = slice(rows.start + FOCAL, rows.stop + FOCAL)
            real = mixed_ref[pair, rows, :FOCAL] - mixed_ref[pair, lower, FOCAL:]
            imag = mixed_ref[pair, rows, FOCAL:] + mixed_ref[pair, lower, :FOCAL]
            field_ref[pair, 0, rows, :] = real
            field_ref[pair, 1, rows, :] = imag
            power = real * real + imag * imag
            totals = [totals[0] + spot_ref[pair, rows, :] * power, totals[1] + power]
        sums.append((total_of(totals[0]), total_of(totals[1]) + 1e-06))
    for pair, (spot_power, all_power) in enumerate(sums):
        ratio = spot_power / all_power
        gain = gain_ref[pair, :1, :1]
        score_ref[pair] = jnp.broadcast_to(ratio * gain, score_ref.shape[1:])
        scale = gain * 2.0 / all_power
        for rows in pieces:
            lower = slice(rows.start + FOCAL, rows.stop + FOCAL)
            weight = scale * (spot_ref[pair, rows, :] - ratio)
            real = (weight * field_ref[pair, 0, rows, :]).astype(jnp.bfloat16)
            imag = (weight * field_ref[pair, 1, rows, :]).astype(jnp.bfloat16)
            stack_ref[pair, rows, :FOCAL] = real
            stack_ref[pair, rows, FOCAL:] = imag
            stack_ref[pair, lower, :FOCAL] = imag
            stack_ref[pair, lower, FOCAL:] = -real
        back = jnp.dot(flat_ref[pair], stack_ref[pair], preferred_element_type=jnp.float32)
        lane = 2 * pair * FOCAL
        back_ref[:, lane : lane + 2 * FOCAL] = back.astype(jnp.bfloat16)


def table_kernel(scale, cols, info_ref, far_info_ref, width_ref, *refs):
    *out_refs, base_ref, centre_ref, turned_ref, power_ref = refs
    pairs = power_ref.shape[0]
    out_refs = out_refs[-2 * pairs :]
    table_refs, slope_refs = out_refs[:pairs], out_refs[pairs:]
    own_cols = width_ref.shape[1]
    sources = [(ref, pair) for ref in (info_ref, far_info_ref) for pair in range(pairs // 2)]
    centres = []
    for pair, (ref, source) in enumerate(sources):
        power = power_coefs(ref[source, : 2 * TERMS, :LANES])
        power_ref[pair] = as_tiles(power * ((iota(power.shape, 0) % TERMS).astype(jnp.float32) * scale))
        own_waves(ref, source, cols, base_ref.at[pair], centre_ref.at[pair])
        for part, row, lane in itertools.product(range(2), range(0, BLOCK, LANES), range(0, FOCAL, LANES)):
            tile = base_ref[pair, part, row : row + LANES, lane : lane + LANES]
            turned_ref[pair, part, lane : lane + LANES, row : row + LANES] = tile.T
        centres.append([centre_ref[pair, part].T for part in range(2)])
    for index in range(own_cols // (2 * BLOCK)):
        starts = block_starts(own_cols, index)
        for pair in range(pairs):
            for row in range(0, FOCAL, GRAIN):
                rows = slice(row, row + GRAIN)
                cent_r, cent_i = (centre[rows, index : index + 1] for centre in centres[pair])
                base_r, base_i = (turned_ref[pair, part, rows, :] for part in range(2))
                for start, table in zip(starts, both_blocks(base_r, base_i, cent_r, cent_i)):
                    for part, value in enumerate(table):
                        place = slice(row + part * FOCAL, row + part * FOCAL + GRAIN)
                        table_refs[pair][place, start : start + BLOCK] = value.astype(jnp.bfloat16)
        for start in (start + step for start in starts for step in range(0, BLOCK, LANES)):
            place = slice(start, start + LANES)
            slopes = near_slopes(width_ref[:, place], power_ref, pairs)
            for ref, slope in zip(slope_refs, slopes):
                ref[0, :, place] = slope[0]
                ref[1, :, place] = slope[1]


def own_grad_kernel(*refs):
    *in_refs, tile_ref, out_ref, score_ref = refs
    for pair in range(score_ref.shape[0]):
        score_ref[pair] = jnp.sum(tile_ref[pair, :1, :1])
    add_grads(in_refs, None, out_ref, 2 * BLOCK)


def last_grad_kernel(*refs):
    *in_refs, total_ref, out_hbm, out_ref, sems = refs
    own_cols = out_ref.shape[1]
    core = lax.axis_index("wave")
    moves = []

    def send(start, total):
        size = total.shape[1]
        place = pl.multiple_of(jnp.where(core == 1, start, own_cols - size - start), size)
        place = pl.ds(place, size)
        out_ref[:, place] = jnp.where(core == 1, total, turn_round(total))
        index = start // size
        moves.append(pltpu.make_async_copy(out_ref.at[:, place], out_hbm.at[:, place], sems.at[index]))
        moves[-1].start()

    add_grads(in_refs, total_ref, out_ref, BLOCK, send)
    for move in moves:
        move.wait()


def add_grads(in_refs, total_ref, out_ref, size, send=None):
    back_ref, *in_refs = in_refs
    pairs = len(in_refs) // 2
    table_refs, slope_refs = in_refs[:pairs], in_refs[pairs:]
    rows_dev, own_cols = out_ref.shape
    core = lax.axis_index("wave")
    lefts = []
    for pair in range(pairs):
        lane = 2 * pair * FOCAL
        real, imag = back_ref[:, lane : lane + FOCAL], back_ref[:, lane + FOCAL : lane + 2 * FOCAL]
        above = jnp.where(core == 1, imag, -imag)
        below = jnp.where(core == 1, -real, real)
        lefts.append(
            jnp.concatenate(
                [jnp.concatenate([real, above], axis=1), jnp.concatenate([imag, below], axis=1)], axis=0
            )
        )
    for start in range(0, own_cols, size):
        place = slice(start, start + size)
        total = jnp.zeros((rows_dev, size), jnp.float32) if total_ref is None else total_ref[:, place]
        for left, table_ref, slope_ref in zip(lefts, table_refs, slope_refs):
            grad = jnp.dot(left, table_ref[:, place], preferred_element_type=jnp.float32)
            total += grad[:rows_dev] * slope_ref[0, :, place]
            total += grad[rows_dev:] * slope_ref[1, :, place]
        if send is None:
            out_ref[:, place] = total
        else:
            send(start, total)


VMEM = pl.BlockSpec(memory_space=pltpu.VMEM)
SMEM = pl.BlockSpec(memory_space=pltpu.SMEM)
ANY = pl.BlockSpec(memory_space=pl.ANY)
HBM = pl.BlockSpec(memory_space=pltpu.HBM)


def call(kernel, name, outs, in_specs, out_specs, scratch, flops, moved):
    return pl.pallas_call(
        kernel,
        name=name,
        out_shape=outs,
        in_specs=in_specs,
        out_specs=out_specs,
        scratch_shapes=scratch,
        cost_estimate=pl.CostEstimate(flops=flops, bytes_accessed=moved, transcendentals=0),
        compiler_params=pltpu.CompilerParams(vmem_limit_bytes=VMEM_LIMIT),
    )


def on_device(widths, coef_table, wave_ids, angle_ids, targets):
    rows_dev, cols = widths.shape
    pairs_dev = wave_ids.shape[0]
    peers = lax.axis_size("aperture")
    copies = lax.axis_size("wave")
    rows = rows_dev * peers
    pairs = pairs_dev * copies
    own_cols = cols // copies
    lanes = 2 * pairs_dev * FOCAL
    f32, bf16 = jnp.float32, jnp.bfloat16
    shape = jax.ShapeDtypeStruct

    def in_hbm(value):
        return pltpu.with_memory_space_constraint(value, pltpu.HBM)

    def exchange(value, step):
        return lax.ppermute(value, "aperture", [(index, index ^ step) for index in range(peers)])

    def to_core(value):
        return lax.ppermute(value, "wave", [(index, (index + 1) % copies) for index in range(copies)])

    waves = [
        pltpu.VMEM((pairs_dev, 2, BLOCK, FOCAL), f32),
        pltpu.VMEM((pairs_dev, 2, 8, FOCAL), f32),
    ]
    mine, info, own = call(
        forward_kernel, "forward",
        (
            shape((rows_dev, lanes), bf16),
            shape((pairs_dev, INFO_ROWS, FOCAL), f32), shape((rows_dev, own_cols), f32),
        ),
        [HBM] * 5, (VMEM,) * 3,
        [
            pltpu.SMEM(wave_ids.shape, jnp.int32),
            pltpu.SMEM(angle_ids.shape, jnp.int32),
            pltpu.SMEM(targets.shape, jnp.int32),
            pltpu.VMEM(coef_table.shape[::-1], f32),
            pltpu.VMEM(widths.shape, f32),
            pltpu.VMEM((rows_dev, own_cols), f32),
            *waves,
            pltpu.VMEM((pairs_dev, 2 * TERMS, SUBLANES, LANES), f32),
            pltpu.VMEM((pairs_dev, 4 * rows_dev, own_cols), bf16),
            pltpu.VMEM((pairs_dev, own_cols, 2 * FOCAL), bf16),
            pltpu.VMEM((pairs_dev, 4 * rows_dev, 2 * FOCAL), f32),
            pltpu.SemaphoreType.DMA((5,)),
        ],
        10**9, 10**7,
    )(*(in_hbm(value) for value in (wave_ids, angle_ids, targets, coef_table.T, widths)))
    far_info = to_core(info)

    tall, flat, spots, gains = call(
        row_kernel, "row_tables",
        (
            shape((pairs_dev, 2 * FOCAL, rows), bf16), shape((pairs_dev, rows_dev, 2 * FOCAL), bf16),
            shape((pairs_dev, FOCAL, FOCAL), f32), shape((pairs_dev, 8, 128), f32),
        ),
        [VMEM], (VMEM,) * 4, [], 10**8, 10**6,
    )(info)
    if peers <= DIRECT:
        steps = list(range(peers - 2, 0, -2))
        got = [exchange(mine, step) for step in steps]
        near = exchange(mine, 1)
        first, flat = lax.optimization_barrier((got[0], flat))
        joined = call(join_kernel, "join", shape(((len(steps) - 1) * rows_dev, lanes), bf16),
                      [VMEM] * (len(steps) - 1), VMEM, [], 10**6, 10**6)(*got[1:])
        sections = [mine, near, first, joined, exchange(first, 1), exchange(joined, 1)]
        steps = [0, 1, *steps, *(step ^ 1 for step in steps)]
        after = [near, joined]
    else:
        blocks = jnp.tile(mine[None], (peers, 1, 1))
        blocks = lax.all_to_all(blocks, "aperture", 0, 0, tiled=True)
        sections, steps, after = [blocks.reshape(rows, lanes)], None, []
    outs = [shape((2 * FOCAL, own_cols), bf16)] * pairs + [shape((2, rows_dev, own_cols), f32)] * pairs
    made = call(
        functools.partial(table_kernel, math.sqrt(rows * cols), cols), "column_tables",
        outs, [VMEM] * 3 + [ANY] * len(after), [VMEM] * len(outs),
        [
            pltpu.VMEM((pairs, 2, BLOCK, FOCAL), f32),
            pltpu.VMEM((pairs, 2, 8, FOCAL), f32),
            pltpu.VMEM((pairs, 2, FOCAL, BLOCK), f32),
            pltpu.VMEM((pairs, 2 * TERMS, SUBLANES, LANES), f32),
        ],
        30 * 10**8, 30 * 10**6,
    )(info, far_info, own, *after)
    tables, slopes = made[:pairs], made[pairs:]

    back, scores = call(
        functools.partial(focus_kernel, steps), "focus",
        (shape((rows_dev, lanes), bf16), shape((pairs_dev, SUBLANES, LANES), f32)),
        [VMEM] * 4 + [ANY] + [VMEM] * len(sections), (VMEM, VMEM),
        [
            pltpu.VMEM((rows, lanes), bf16),
            pltpu.VMEM((pairs_dev, 2 * FOCAL, 2 * FOCAL), f32),
            pltpu.VMEM((pairs_dev, 2, FOCAL, FOCAL), f32),
            pltpu.VMEM((pairs_dev, 2 * FOCAL, 2 * FOCAL), bf16),
        ],
        10**8, 10**6,
    )(tall, flat, spots, gains, slopes[0], *sections)

    out = shape((rows_dev, own_cols), f32)
    ins = [back, *tables[:pairs_dev], *slopes[:pairs_dev], scores]
    grad, scores = call(
        own_grad_kernel, "gradient_own", (out, shape((pairs_dev,), f32)),
        [VMEM] * len(ins), (VMEM, SMEM), [], 10**9, 10**7,
    )(*ins)
    ins = [to_core(back), *tables[pairs_dev:], *slopes[pairs_dev:], grad]
    grad = call(
        last_grad_kernel, "gradient_far", out, [VMEM] * len(ins), HBM,
        [pltpu.VMEM(out.shape, f32), pltpu.SemaphoreType.DMA((own_cols // BLOCK,))], 10**9, 10**7,
    )(*ins)
    return grad, scores


def solution(mesh):
    in_specs = (
        P(("group", "aperture"), None),
        P(),
        P(("group", "wave")),
        P(("group", "wave")),
        P(("group", "wave"), None),
    )
    out_specs = (P(("group", "aperture"), "wave"), P(("group", "wave")))
    return jax.shard_map(
        on_device, mesh=mesh, in_specs=in_specs, out_specs=out_specs, check_vma=False
    )
```

```python
import functools
import itertools
import math

import jax
import jax.numpy as jnp
from jax import lax
from jax.experimental import pallas as pl
from jax.experimental.pallas import tpu as pltpu
from jax.sharding import PartitionSpec as P

FOCAL = 256
SPOT = 4
SHIFT = 32
TERMS = 8
BLOCK = 256
GRAIN = 16
LANES = 128
PIECE = 16
SUBLANES = 8
VMEM_LIMIT = 16 * 1024 * 1024
WAVE_ROW, ANGLE_ROW, AIM_ROW, INFO_ROWS = 16, 17, 18, 24
DIRECT = 16

COS = (
    1.0, -19.7392088015709, 64.93939395773512, -85.45681453397417, 60.24458621302471,
    -26.425616460281425, 7.8991596631575085, -1.6968741456712442, 0.2437618617467591,
)
SIN = (
    6.2831853071792665, -41.34170224019464, 81.60524925425943, -76.70585885700535,
    42.05867547580699, -15.094428387947755, 3.818490079304055, -0.7122771247541972,
    0.09149844789363434,
)


def horner(terms, u):
    value = terms[-1] * u + terms[-2]
    for term in terms[-3::-1]:
        value = value * u + term
    return value


def unit_waves(counts, period):
    half = period // 2
    centred = ((counts + half) & (period - 1)) - half
    t = centred.astype(jnp.float32) * (1.0 / period)
    u = t * t
    return horner(COS, u), -(t * horner(SIN, u))


def iota(shape, axis):
    return lax.broadcasted_iota(jnp.int32, shape, axis)


def pick_coef(table, wave):
    chosen = jnp.where(iota(table.shape, 1) == wave, table, 0.0)
    return jnp.sum(chosen, axis=1, keepdims=True)


def column_freq(info_ref, pair):
    wave = info_ref[pair, WAVE_ROW : WAVE_ROW + 1, :].astype(jnp.int32)
    angle = info_ref[pair, ANGLE_ROW : ANGLE_ROW + 1, :].astype(jnp.int32)
    return (iota((1, FOCAL), 1) - FOCAL // 2 + SHIFT * angle) * (BLOCK + wave)


def fill_base(freq, shift, period, base_ref, centre_ref):
    low_r, low_i = unit_waves(iota((GRAIN, 1), 0) * freq, period)
    steps = BLOCK // GRAIN
    high_r, high_i = unit_waves((iota((steps, 1), 0) * GRAIN - BLOCK // 2 + shift) * freq, period)
    for step in range(steps):
        one_r, one_i = high_r[step : step + 1], high_i[step : step + 1]
        rows = slice(step * GRAIN, (step + 1) * GRAIN)
        base_ref[0, rows, :] = one_r * low_r - one_i * low_i
        base_ref[1, rows, :] = one_r * low_i + one_i * low_r
    count = centre_ref.shape[1]
    cent_r, cent_i = unit_waves((iota((count, 1), 0) * BLOCK + BLOCK // 2) * freq, period)
    centre_ref[0] = cent_r
    centre_ref[1] = cent_i


def power_coefs(coef):
    before, current = [1], [0, 1]
    bases = [before, current]
    for _ in range(2, TERMS):
        doubled = [0] + [2 * term for term in current]
        before, current = current, [a - b for a, b in itertools.zip_longest(doubled, before, fillvalue=0)]
        bases.append(current)
    rows = []
    for part, power in itertools.product(range(2), range(TERMS)):
        row = None
        for order in range(power, TERMS, 2):
            place = part * TERMS + order
            term = coef[place : place + 1] * float(bases[order][power])
            row = term if row is None else row + term
        rows.append(row)
    return jnp.concatenate(rows, axis=0)


def as_tiles(rows):
    return jnp.broadcast_to(rows[:, None, :], (rows.shape[0], SUBLANES, rows.shape[1]))


def split_rows(value):
    return value.reshape(value.shape[0] // SUBLANES, SUBLANES, value.shape[1])


def join_rows(value):
    return value.reshape(value.shape[0] * SUBLANES, value.shape[2])


def near_fields(s, power_ref, pairs):
    s = split_rows(s)
    outs = []
    for pair, part in itertools.product(range(pairs), range(2)):
        row = (part + 1) * TERMS - 1
        value = power_ref[pair, row] * s + power_ref[pair, row - 1]
        for row in range(row - 2, part * TERMS - 1, -1):
            value = value * s + power_ref[pair, row]
        outs.append(join_rows(value))
    return [outs[2 * pair : 2 * pair + 2] for pair in range(pairs)]


def near_slopes(s, power_ref, pairs):
    s = split_rows(s)
    outs = []
    for pair, part in itertools.product(range(pairs), range(2)):
        row = (part + 1) * TERMS - 1
        value = power_ref[pair, row] * s + power_ref[pair, row - 1]
        for row in range(row - 2, part * TERMS, -1):
            value = value * s + power_ref[pair, row]
        outs.append(join_rows(value))
    return [outs[2 * pair : 2 * pair + 2] for pair in range(pairs)]


def turn_round(value):
    rows, cols = value.shape
    order = LANES - 1 - iota((rows, LANES), 1)
    parts = [
        jnp.take_along_axis(value[:, start : start + LANES], order, axis=1)
        for start in range(cols - LANES, -1, -LANES)
    ]
    return jnp.concatenate(parts, axis=1)


def block_starts(cols, index):
    return cols // 2 - (index + 1) * BLOCK, cols // 2 + index * BLOCK


def both_blocks(base_r, base_i, cent_r, cent_i):
    rr, ii = base_r * cent_r, base_i * cent_i
    ri, ir = base_r * cent_i, base_i * cent_r
    return (rr + ii, ir - ri), (rr - ii, ir + ri)


def own_waves(info_ref, pair, cols, base_ref, centre_ref):
    shift = cols // 4 + 1 - lax.axis_index("wave")
    fill_base(column_freq(info_ref, pair), shift, 256 * cols, base_ref, centre_ref)


def forward_kernel(
    wave_hbm, angle_hbm, aim_hbm, coef_hbm, width_hbm, mine_ref, info_ref, own_ref, *refs
):
    pairs = info_ref.shape[0]
    (
        wave_ref, angle_ref, aim_ref, coef_ref, width_ref, far_ref, base_ref, centre_ref, power_ref, near_ref, table_ref,
        acc_ref, sems,
    ) = refs
    rows_dev, cols = width_ref.shape
    half = cols // 2
    copies = [(wave_hbm, wave_ref), (angle_hbm, angle_ref), (aim_hbm, aim_ref), (coef_hbm, coef_ref)]
    for row in range(0, rows_dev, SUBLANES):
        place = slice(row, row + SUBLANES)
        copies.append((width_hbm.at[place, :], width_ref.at[place, :]))
    moves = [
        pltpu.make_async_copy(source, target, sems.at[index]) for index, (source, target) in enumerate(copies)
    ]
    for move in moves:
        move.start()
    for move in moves:
        move.wait()
    for pair in range(pairs):
        coef = pick_coef(coef_ref[...], wave_ref[pair])
        coef = jnp.broadcast_to(coef, (WAVE_ROW, FOCAL))
        info_ref[pair, :WAVE_ROW, :] = coef
        power_ref[pair] = as_tiles(power_coefs(coef[:, :LANES]))
        row = iota((INFO_ROWS - WAVE_ROW, FOCAL), 0) + WAVE_ROW
        ids = jnp.where(row == WAVE_ROW, wave_ref[pair], 0)
        ids = jnp.where(row == ANGLE_ROW, angle_ref[pair], ids)
        ids = jnp.where(row == AIM_ROW, aim_ref[pair, 0], ids)
        ids = jnp.where(row == AIM_ROW + 1, aim_ref[pair, 1], ids)
        info_ref[pair, WAVE_ROW:, :] = ids.astype(jnp.float32)
    for pair in range(pairs):
        own_waves(info_ref, pair, cols, base_ref.at[pair], centre_ref.at[pair])
    core = lax.axis_index("wave")
    left, right = turn_round(width_ref[:, :half]), width_ref[:, half:]
    own_ref[...] = jnp.where(core == 1, right, left)
    far_ref[...] = jnp.where(core == 1, pltpu.roll(left, 1, 1), pltpu.roll(right, half - 1, 1))

    alone = jnp.where(core == 1, 0, half)
    column = width_ref[:, pl.ds(pl.multiple_of(alone, LANES), LANES)]
    columns = near_fields(column, power_ref, pairs)
    void = jnp.where(core == 1, 0, half - 1)
    for index in range(half // (2 * BLOCK)):
        starts = block_starts(half, index)
        for start in (start + step for start in starts for step in range(0, BLOCK, LANES)):
            for side, ref in enumerate((own_ref, far_ref)):
                outs = near_fields(ref[:, start : start + LANES], power_ref, pairs)
                if side and start in (0, half - LANES):
                    keep = iota((rows_dev, LANES), 1) + start != void
                    outs = [[jnp.where(keep, part, 0.0) for part in out] for out in outs]
                for pair, part in ((pair, part) for pair in range(pairs) for part in range(2)):
                    row = (2 * side + part) * rows_dev
                    near_ref[pair, row : row + rows_dev, start : start + LANES] = outs[pair][part].astype(jnp.bfloat16)
        for pair in range(pairs):
            cent_r, cent_i = (centre_ref[pair, part, index : index + 1, :] for part in range(2))
            for row in range(0, BLOCK, GRAIN):
                base_r, base_i = (base_ref[pair, part, row : row + GRAIN, :] for part in range(2))
                for start, table in zip(starts, both_blocks(base_r, base_i, cent_r, cent_i)):
                    rows = slice(start + row, start + row + GRAIN)
                    table_ref[pair, rows, :FOCAL] = table[0].astype(jnp.bfloat16)
                    table_ref[pair, rows, FOCAL:] = table[1].astype(jnp.bfloat16)
            product = jnp.dot(
                jnp.concatenate([near_ref[pair, :, start : start + BLOCK] for start in starts], axis=1),
                jnp.concatenate([table_ref[pair, start : start + BLOCK, :] for start in starts], axis=0),
                preferred_element_type=jnp.float32,
            )
            acc_ref[pair] = product if index == 0 else acc_ref[pair] + product
    for pair in range(pairs):
        acc = [acc_ref[pair, part * rows_dev : (part + 1) * rows_dev, :] for part in range(4)]
        (own_rr, own_ri), (own_ir, own_ii), (far_rr, far_ri), (far_ir, far_ii) = (
            (part[:, :FOCAL], part[:, FOCAL:]) for part in acc
        )
        cross_r, cross_i = far_ii - own_ii, own_ri - far_ri
        real = own_rr + far_rr + jnp.where(core == 1, cross_r, -cross_r)
        imag = own_ir + far_ir + jnp.where(core == 1, cross_i, -cross_i)
        near_r, near_i = (part[:, :1].astype(jnp.bfloat16).astype(jnp.float32) for part in columns[pair])
        wave_r, wave_i = (
            part.astype(jnp.bfloat16).astype(jnp.float32)
            for part in unit_waves((alone - half) * column_freq(info_ref, pair), 256 * cols)
        )
        real = real + (near_r * wave_r - near_i * wave_i)
        imag = imag + (near_r * wave_i + near_i * wave_r)
        for part, value in enumerate((real, imag)):
            lane = (2 * pair + part) * FOCAL
            mine_ref[:, lane : lane + FOCAL] = value.astype(jnp.bfloat16)


def spot_rows(info_ref, pair, first):
    aims = [info_ref[pair, row : row + 1, :] for row in (AIM_ROW, AIM_ROW + 1)]
    rows_off = (iota((PIECE, FOCAL), 0) + first).astype(jnp.float32) - aims[0]
    cols_off = iota((1, FOCAL), 1).astype(jnp.float32) - aims[1]
    return jnp.exp(-(rows_off * rows_off + cols_off * cols_off) / (2.0 * SPOT * SPOT))


def total_of(value):
    return jnp.sum(jnp.sum(value, axis=0, keepdims=True), axis=1, keepdims=True)


def row_kernel(info_ref, tall_ref, flat_ref, spot_ref, gain_ref):
    pairs, _, rows = tall_ref.shape
    rows_dev = flat_ref.shape[1]
    period = 256 * rows
    size = min(rows, FOCAL)
    for pair in range(pairs):
        wave = info_ref[pair, WAVE_ROW : WAVE_ROW + 1, :].astype(jnp.int32) + BLOCK
        focal = (iota((FOCAL, 1), 0) - FOCAL // 2) * wave

        def step(index, carry):
            start = pl.multiple_of(index * size, size)
            place = iota((1, size), 1) + (start - rows // 2)
            for row in range(0, FOCAL, PIECE):
                real, imag = unit_waves(focal[row : row + PIECE, :size] * place, period)
                tall_ref[pair, row : row + PIECE, pl.ds(start, size)] = real.astype(jnp.bfloat16)
                row += FOCAL
                tall_ref[pair, row : row + PIECE, pl.ds(start, size)] = imag.astype(jnp.bfloat16)
            return carry

        if rows == size:
            step(0, 0)
        else:
            lax.fori_loop(0, rows // size, step, 0)
        focal = (iota((1, FOCAL), 1) - FOCAL // 2) * wave
        first = lax.axis_index("aperture") * rows_dev - rows // 2
        real, imag = unit_waves((iota((rows_dev, 1), 0) + first) * focal, period)
        flat_ref[pair, :, :FOCAL] = real.astype(jnp.bfloat16)
        flat_ref[pair, :, FOCAL:] = imag.astype(jnp.bfloat16)
        total = jnp.zeros((PIECE, FOCAL), jnp.float32)
        for row in range(0, FOCAL, PIECE):
            spot = spot_rows(info_ref, pair, row)
            spot_ref[pair, row : row + PIECE, :] = spot
            total += spot
        gain_ref[pair] = jnp.broadcast_to(FOCAL * FOCAL / total_of(total), gain_ref.shape[1:])


def join_kernel(*refs):
    *in_refs, out_ref = refs
    count = in_refs[0].shape[0]
    for index, ref in enumerate(in_refs):
        out_ref[index * count : (index + 1) * count, :] = ref[...]


def focus_kernel(steps, tall_ref, flat_ref, spot_ref, gain_ref, after_ref, *refs):
    del after_ref
    *sect_refs, back_ref, score_ref, rows_ref, mixed_ref, field_ref, stack_ref = refs
    pairs = tall_ref.shape[0]
    rows_dev = back_ref.shape[0]
    if steps is None:
        rows_ref = sect_refs[0]
    else:
        me = lax.axis_index("aperture")
        blocks = [
            ref[index * rows_dev : (index + 1) * rows_dev, :]
            for ref in sect_refs
            for index in range(ref.shape[0] // rows_dev)
        ]
        for step, block in zip(steps, blocks, strict=True):
            start = pl.multiple_of((me ^ step) * rows_dev, rows_dev)
            rows_ref[pl.ds(start, rows_dev), :] = block
    for pair in range(pairs):
        lane = 2 * pair * FOCAL
        section = rows_ref[:, lane : lane + 2 * FOCAL]
        mixed_ref[pair] = jnp.dot(tall_ref[pair], section, preferred_element_type=jnp.float32)
    pieces = [slice(row, row + PIECE) for row in range(0, FOCAL, PIECE)]
    sums = []
    for pair in range(pairs):
        totals = [jnp.zeros((PIECE, FOCAL), jnp.float32) for _ in range(2)]
        for rows in pieces:
            lower = slice(rows.start + FOCAL, rows.stop + FOCAL)
            real = mixed_ref[pair, rows, :FOCAL] - mixed_ref[pair, lower, FOCAL:]
            imag = mixed_ref[pair, rows, FOCAL:] + mixed_ref[pair, lower, :FOCAL]
            field_ref[pair, 0, rows, :] = real
            field_ref[pair, 1, rows, :] = imag
            power = real * real + imag * imag
            totals = [totals[0] + spot_ref[pair, rows, :] * power, totals[1] + power]
        sums.append((total_of(totals[0]), total_of(totals[1]) + 1e-06))
    for pair, (spot_power, all_power) in enumerate(sums):
        ratio = spot_power / all_power
        gain = gain_ref[pair, :1, :1]
        score_ref[pair] = jnp.broadcast_to(ratio * gain, score_ref.shape[1:])
        scale = gain * 2.0 / all_power
        for rows in pieces:
            lower = slice(rows.start + FOCAL, rows.stop + FOCAL)
            weight = scale * (spot_ref[pair, rows, :] - ratio)
            real = (weight * field_ref[pair, 0, rows, :]).astype(jnp.bfloat16)
            imag = (weight * field_ref[pair, 1, rows, :]).astype(jnp.bfloat16)
            stack_ref[pair, rows, :FOCAL] = real
            stack_ref[pair, rows, FOCAL:] = imag
            stack_ref[pair, lower, :FOCAL] = imag
            stack_ref[pair, lower, FOCAL:] = -real
        back = jnp.dot(flat_ref[pair], stack_ref[pair], preferred_element_type=jnp.float32)
        lane = 2 * pair * FOCAL
        back_ref[:, lane : lane + 2 * FOCAL] = back.astype(jnp.bfloat16)


def table_kernel(scale, cols, info_ref, far_info_ref, width_ref, *refs):
    *out_refs, base_ref, centre_ref, turned_ref, power_ref = refs
    pairs = power_ref.shape[0]
    out_refs = out_refs[-2 * pairs :]
    table_refs, slope_refs = out_refs[:pairs], out_refs[pairs:]
    own_cols = width_ref.shape[1]
    sources = [(ref, pair) for ref in (info_ref, far_info_ref) for pair in range(pairs // 2)]
    centres = []
    for pair, (ref, source) in enumerate(sources):
        power = power_coefs(ref[source, : 2 * TERMS, :LANES])
        power_ref[pair] = as_tiles(power * ((iota(power.shape, 0) % TERMS).astype(jnp.float32) * scale))
        own_waves(ref, source, cols, base_ref.at[pair], centre_ref.at[pair])
        for part, row, lane in itertools.product(range(2), range(0, BLOCK, LANES), range(0, FOCAL, LANES)):
            tile = base_ref[pair, part, row : row + LANES, lane : lane + LANES]
            turned_ref[pair, part, lane : lane + LANES, row : row + LANES] = tile.T
        centres.append([centre_ref[pair, part].T for part in range(2)])
    for index in range(own_cols // (2 * BLOCK)):
        starts = block_starts(own_cols, index)
        for pair in range(pairs):
            for row in range(0, FOCAL, GRAIN):
                rows = slice(row, row + GRAIN)
                cent_r, cent_i = (centre[rows, index : index + 1] for centre in centres[pair])
                base_r, base_i = (turned_ref[pair, part, rows, :] for part in range(2))
                for start, table in zip(starts, both_blocks(base_r, base_i, cent_r, cent_i)):
                    for part, value in enumerate(table):
                        place = slice(row + part * FOCAL, row + part * FOCAL + GRAIN)
                        table_refs[pair][place, start : start + BLOCK] = value.astype(jnp.bfloat16)
        for start in (start + step for start in starts for step in range(0, BLOCK, LANES)):
            place = slice(start, start + LANES)
            slopes = near_slopes(width_ref[:, place], power_ref, pairs)
            for ref, slope in zip(slope_refs, slopes):
                ref[0, :, place] = slope[0]
                ref[1, :, place] = slope[1]


def own_grad_kernel(*refs):
    *in_refs, tile_ref, out_ref, score_hbm, score_ref, sem = refs
    for pair in range(score_ref.shape[0]):
        score_ref[pair] = jnp.sum(tile_ref[pair, :1, :1])
    move = pltpu.make_async_copy(score_ref, score_hbm, sem)
    move.start()
    add_grads(in_refs, None, out_ref, 2 * BLOCK)
    move.wait()


def last_grad_kernel(*refs):
    *in_refs, total_ref, out_hbm, out_ref, sems = refs
    own_cols = out_ref.shape[1]
    core = lax.axis_index("wave")
    moves = []

    def send(start, total):
        size = total.shape[1]
        place = pl.multiple_of(jnp.where(core == 1, start, own_cols - size - start), size)
        place = pl.ds(place, size)
        out_ref[:, place] = jnp.where(core == 1, total, turn_round(total))
        index = start // size
        moves.append(pltpu.make_async_copy(out_ref.at[:, place], out_hbm.at[:, place], sems.at[index]))
        moves[-1].start()

    add_grads(in_refs, total_ref, out_ref, 2 * BLOCK, send)
    for move in moves:
        move.wait()


def add_grads(in_refs, total_ref, out_ref, size, send=None):
    back_ref, *in_refs = in_refs
    pairs = len(in_refs) // 2
    table_refs, slope_refs = in_refs[:pairs], in_refs[pairs:]
    rows_dev, own_cols = out_ref.shape
    core = lax.axis_index("wave")
    lefts = []
    for pair in range(pairs):
        lane = 2 * pair * FOCAL
        real, imag = back_ref[:, lane : lane + FOCAL], back_ref[:, lane + FOCAL : lane + 2 * FOCAL]
        above = jnp.where(core == 1, imag, -imag)
        below = jnp.where(core == 1, -real, real)
        lefts.append(
            jnp.concatenate(
                [jnp.concatenate([real, above], axis=1), jnp.concatenate([imag, below], axis=1)], axis=0
            )
        )
    for start in range(0, own_cols, size):
        place = slice(start, start + size)
        total = jnp.zeros((rows_dev, size), jnp.float32) if total_ref is None else total_ref[:, place]
        for left, table_ref, slope_ref in zip(lefts, table_refs, slope_refs):
            grad = jnp.dot(left, table_ref[:, place], preferred_element_type=jnp.float32)
            total += grad[:rows_dev] * slope_ref[0, :, place]
            total += grad[rows_dev:] * slope_ref[1, :, place]
        if send is None:
            out_ref[:, place] = total
        else:
            send(start, total)


VMEM = pl.BlockSpec(memory_space=pltpu.VMEM)
SMEM = pl.BlockSpec(memory_space=pltpu.SMEM)
ANY = pl.BlockSpec(memory_space=pl.ANY)
HBM = pl.BlockSpec(memory_space=pltpu.HBM)


def call(kernel, name, outs, in_specs, out_specs, scratch, flops, moved):
    return pl.pallas_call(
        kernel,
        name=name,
        out_shape=outs,
        in_specs=in_specs,
        out_specs=out_specs,
        scratch_shapes=scratch,
        cost_estimate=pl.CostEstimate(flops=flops, bytes_accessed=moved, transcendentals=0),
        compiler_params=pltpu.CompilerParams(vmem_limit_bytes=VMEM_LIMIT),
    )


def on_device(widths, coef_table, wave_ids, angle_ids, targets):
    rows_dev, cols = widths.shape
    pairs_dev = wave_ids.shape[0]
    peers = lax.axis_size("aperture")
    copies = lax.axis_size("wave")
    rows = rows_dev * peers
    pairs = pairs_dev * copies
    own_cols = cols // copies
    lanes = 2 * pairs_dev * FOCAL
    f32, bf16 = jnp.float32, jnp.bfloat16
    shape = jax.ShapeDtypeStruct

    def in_hbm(value):
        return pltpu.with_memory_space_constraint(value, pltpu.HBM)

    def exchange(value, step):
        return lax.ppermute(value, "aperture", [(index, index ^ step) for index in range(peers)])

    def to_core(value):
        return lax.ppermute(value, "wave", [(index, (index + 1) % copies) for index in range(copies)])

    waves = [
        pltpu.VMEM((pairs_dev, 2, BLOCK, FOCAL), f32),
        pltpu.VMEM((pairs_dev, 2, 8, FOCAL), f32),
    ]
    mine, info, own = call(
        forward_kernel, "forward",
        (
            shape((rows_dev, lanes), bf16),
            shape((pairs_dev, INFO_ROWS, FOCAL), f32), shape((rows_dev, own_cols), f32),
        ),
        [HBM] * 5, (VMEM,) * 3,
        [
            pltpu.SMEM(wave_ids.shape, jnp.int32),
            pltpu.SMEM(angle_ids.shape, jnp.int32),
            pltpu.SMEM(targets.shape, jnp.int32),
            pltpu.VMEM(coef_table.shape[::-1], f32),
            pltpu.VMEM(widths.shape, f32),
            pltpu.VMEM((rows_dev, own_cols), f32),
            *waves,
            pltpu.VMEM((pairs_dev, 2 * TERMS, SUBLANES, LANES), f32),
            pltpu.VMEM((pairs_dev, 4 * rows_dev, own_cols), bf16),
            pltpu.VMEM((pairs_dev, own_cols, 2 * FOCAL), bf16),
            pltpu.VMEM((pairs_dev, 4 * rows_dev, 2 * FOCAL), f32),
            pltpu.SemaphoreType.DMA((4 + rows_dev // SUBLANES,)),
        ],
        10**9, 10**7,
    )(*(in_hbm(value) for value in (wave_ids, angle_ids, targets, coef_table.T, widths)))
    far_info = to_core(info)

    tall, flat, spots, gains = call(
        row_kernel, "row_tables",
        (
            shape((pairs_dev, 2 * FOCAL, rows), bf16), shape((pairs_dev, rows_dev, 2 * FOCAL), bf16),
            shape((pairs_dev, FOCAL, FOCAL), f32), shape((pairs_dev, 8, 128), f32),
        ),
        [VMEM], (VMEM,) * 4, [], 10**8, 10**6,
    )(info)
    if peers <= DIRECT:
        steps = list(range(peers - 2, 0, -2))
        got = [exchange(mine, step) for step in steps]
        near = exchange(mine, 1)
        first, flat = lax.optimization_barrier((got[0], flat))
        joined = call(join_kernel, "join", shape(((len(steps) - 1) * rows_dev, lanes), bf16),
                      [VMEM] * (len(steps) - 1), VMEM, [], 10**6, 10**6)(*got[1:])
        sections = [mine, near, first, joined, exchange(first, 1), exchange(joined, 1)]
        steps = [0, 1, *steps, *(step ^ 1 for step in steps)]
        after = [near, joined]
    else:
        blocks = jnp.tile(mine[None], (peers, 1, 1))
        blocks = lax.all_to_all(blocks, "aperture", 0, 0, tiled=True)
        sections, steps, after = [blocks.reshape(rows, lanes)], None, []
    outs = [shape((2 * FOCAL, own_cols), bf16)] * pairs + [shape((2, rows_dev, own_cols), f32)] * pairs
    made = call(
        functools.partial(table_kernel, math.sqrt(rows * cols), cols), "column_tables",
        outs, [VMEM] * 3 + [ANY] * len(after), [VMEM] * len(outs),
        [
            pltpu.VMEM((pairs, 2, BLOCK, FOCAL), f32),
            pltpu.VMEM((pairs, 2, 8, FOCAL), f32),
            pltpu.VMEM((pairs, 2, FOCAL, BLOCK), f32),
            pltpu.VMEM((pairs, 2 * TERMS, SUBLANES, LANES), f32),
        ],
        30 * 10**8, 30 * 10**6,
    )(info, far_info, own, *after)
    tables, slopes = made[:pairs], made[pairs:]

    back, scores = call(
        functools.partial(focus_kernel, steps), "focus",
        (shape((rows_dev, lanes), bf16), shape((pairs_dev, SUBLANES, LANES), f32)),
        [VMEM] * 4 + [ANY] + [VMEM] * len(sections), (VMEM, VMEM),
        [
            pltpu.VMEM((rows, lanes), bf16),
            pltpu.VMEM((pairs_dev, 2 * FOCAL, 2 * FOCAL), f32),
            pltpu.VMEM((pairs_dev, 2, FOCAL, FOCAL), f32),
            pltpu.VMEM((pairs_dev, 2 * FOCAL, 2 * FOCAL), bf16),
        ],
        10**8, 10**6,
    )(tall, flat, spots, gains, slopes[0], *sections)

    out = shape((rows_dev, own_cols), f32)
    ins = [back, *tables[:pairs_dev], *slopes[:pairs_dev], scores]
    grad, scores = call(
        own_grad_kernel, "gradient_own", (out, shape((pairs_dev,), f32)),
        [VMEM] * len(ins), (VMEM, HBM),
        [pltpu.SMEM((pairs_dev,), f32), pltpu.SemaphoreType.DMA], 10**9, 10**7,
    )(*ins)
    ins = [to_core(back), *tables[pairs_dev:], *slopes[pairs_dev:], grad]
    grad = call(
        last_grad_kernel, "gradient_far", out, [VMEM] * len(ins), HBM,
        [pltpu.VMEM(out.shape, f32), pltpu.SemaphoreType.DMA((own_cols // (2 * BLOCK),))], 10**9, 10**7,
    )(*ins)
    return grad, scores


def solution(mesh):
    in_specs = (
        P(("group", "aperture"), None),
        P(),
        P(("group", "wave")),
        P(("group", "wave")),
        P(("group", "wave"), None),
    )
    out_specs = (P(("group", "aperture"), "wave"), P(("group", "wave")))
    return jax.shard_map(
        on_device, mesh=mesh, in_specs=in_specs, out_specs=out_specs, check_vma=False
    )
```

```python
import functools
import itertools
import math

import jax
import jax.numpy as jnp
from jax import lax
from jax.experimental import pallas as pl
from jax.experimental.pallas import tpu as pltpu
from jax.sharding import PartitionSpec as P

FOCAL = 256
SPOT = 4
SHIFT = 32
TERMS = 8
BLOCK = 256
GRAIN = 16
LANES = 128
PIECE = 16
SUBLANES = 8
VMEM_LIMIT = 16 * 1024 * 1024
WAVE_ROW, ANGLE_ROW, AIM_ROW, INFO_ROWS = 16, 17, 18, 24
DIRECT = 16

COS = (
    1.0, -19.7392088015709, 64.93939395773512, -85.45681453397417, 60.24458621302471,
    -26.425616460281425, 7.8991596631575085, -1.6968741456712442, 0.2437618617467591,
)
SIN = (
    6.2831853071792665, -41.34170224019464, 81.60524925425943, -76.70585885700535,
    42.05867547580699, -15.094428387947755, 3.818490079304055, -0.7122771247541972,
    0.09149844789363434,
)


def horner(terms, u):
    value = terms[-1] * u + terms[-2]
    for term in terms[-3::-1]:
        value = value * u + term
    return value


def unit_waves(counts, period):
    half = period // 2
    centred = ((counts + half) & (period - 1)) - half
    t = centred.astype(jnp.float32) * (1.0 / period)
    u = t * t
    return horner(COS, u), -(t * horner(SIN, u))


def iota(shape, axis):
    return lax.broadcasted_iota(jnp.int32, shape, axis)


def pick_coef(table, wave):
    chosen = jnp.where(iota(table.shape, 1) == wave, table, 0.0)
    return jnp.sum(chosen, axis=1, keepdims=True)


def column_freq(info_ref, pair):
    wave = info_ref[pair, WAVE_ROW : WAVE_ROW + 1, :].astype(jnp.int32)
    angle = info_ref[pair, ANGLE_ROW : ANGLE_ROW + 1, :].astype(jnp.int32)
    return (iota((1, FOCAL), 1) - FOCAL // 2 + SHIFT * angle) * (BLOCK + wave)


def fill_base(freq, shift, period, base_ref, centre_ref):
    low_r, low_i = unit_waves(iota((GRAIN, 1), 0) * freq, period)
    steps = BLOCK // GRAIN
    high_r, high_i = unit_waves((iota((steps, 1), 0) * GRAIN - BLOCK // 2 + shift) * freq, period)
    for step in range(steps):
        one_r, one_i = high_r[step : step + 1], high_i[step : step + 1]
        rows = slice(step * GRAIN, (step + 1) * GRAIN)
        base_ref[0, rows, :] = one_r * low_r - one_i * low_i
        base_ref[1, rows, :] = one_r * low_i + one_i * low_r
    count = centre_ref.shape[1]
    cent_r, cent_i = unit_waves((iota((count, 1), 0) * BLOCK + BLOCK // 2) * freq, period)
    centre_ref[0] = cent_r
    centre_ref[1] = cent_i


def power_coefs(coef):
    before, current = [1], [0, 1]
    bases = [before, current]
    for _ in range(2, TERMS):
        doubled = [0] + [2 * term for term in current]
        before, current = current, [a - b for a, b in itertools.zip_longest(doubled, before, fillvalue=0)]
        bases.append(current)
    rows = []
    for part, power in itertools.product(range(2), range(TERMS)):
        row = None
        for order in range(power, TERMS, 2):
            place = part * TERMS + order
            term = coef[place : place + 1] * float(bases[order][power])
            row = term if row is None else row + term
        rows.append(row)
    return jnp.concatenate(rows, axis=0)


def as_tiles(rows):
    return jnp.broadcast_to(rows[:, None, :], (rows.shape[0], SUBLANES, rows.shape[1]))


def split_rows(value):
    return value.reshape(value.shape[0] // SUBLANES, SUBLANES, value.shape[1])


def join_rows(value):
    return value.reshape(value.shape[0] * SUBLANES, value.shape[2])


def near_fields(s, power_ref, pairs):
    s = split_rows(s)
    outs = []
    for pair, part in itertools.product(range(pairs), range(2)):
        row = (part + 1) * TERMS - 1
        value = power_ref[pair, row] * s + power_ref[pair, row - 1]
        for row in range(row - 2, part * TERMS - 1, -1):
            value = value * s + power_ref[pair, row]
        outs.append(join_rows(value))
    return [outs[2 * pair : 2 * pair + 2] for pair in range(pairs)]


def near_slopes(s, power_ref, pairs):
    s = split_rows(s)
    outs = []
    for pair, part in itertools.product(range(pairs), range(2)):
        row = (part + 1) * TERMS - 1
        value = power_ref[pair, row] * s + power_ref[pair, row - 1]
        for row in range(row - 2, part * TERMS, -1):
            value = value * s + power_ref[pair, row]
        outs.append(join_rows(value))
    return [outs[2 * pair : 2 * pair + 2] for pair in range(pairs)]


def turn_round(value):
    rows, cols = value.shape
    order = LANES - 1 - iota((rows, LANES), 1)
    parts = [
        jnp.take_along_axis(value[:, start : start + LANES], order, axis=1)
        for start in range(cols - LANES, -1, -LANES)
    ]
    return jnp.concatenate(parts, axis=1)


def block_starts(cols, index):
    return cols // 2 - (index + 1) * BLOCK, cols // 2 + index * BLOCK


def both_blocks(base_r, base_i, cent_r, cent_i):
    rr, ii = base_r * cent_r, base_i * cent_i
    ri, ir = base_r * cent_i, base_i * cent_r
    return (rr + ii, ir - ri), (rr - ii, ir + ri)


def own_waves(info_ref, pair, cols, base_ref, centre_ref):
    shift = cols // 4 + 1 - lax.axis_index("wave")
    fill_base(column_freq(info_ref, pair), shift, 256 * cols, base_ref, centre_ref)


def forward_kernel(
    wave_hbm, angle_hbm, aim_hbm, coef_hbm, width_hbm, mine_ref, info_ref, own_ref, *refs
):
    pairs = info_ref.shape[0]
    (
        wave_ref, angle_ref, aim_ref, coef_ref, width_ref, far_ref, base_ref, centre_ref, power_ref, near_ref, table_ref,
        acc_ref, sems,
    ) = refs
    rows_dev, cols = width_ref.shape
    half = cols // 2
    moves = [
        pltpu.make_async_copy(source, target, sems.at[index])
        for index, (source, target) in enumerate((
            (wave_hbm, wave_ref), (angle_hbm, angle_ref), (aim_hbm, aim_ref),
            (coef_hbm, coef_ref), (width_hbm, width_ref),
        ))
    ]
    for move in moves:
        move.start()
    for move in moves:
        move.wait()
    for pair in range(pairs):
        wave = wave_ref[:, pair : pair + 1]
        coef = pick_coef(coef_ref[...], wave)
        coef = jnp.broadcast_to(coef, (WAVE_ROW, FOCAL))
        info_ref[pair, :WAVE_ROW, :] = coef
        power_ref[pair] = as_tiles(power_coefs(coef[:, :LANES]))
        row = iota((INFO_ROWS - WAVE_ROW, FOCAL), 0) + WAVE_ROW
        ids = jnp.where(row == WAVE_ROW, wave, 0)
        ids = jnp.where(row == ANGLE_ROW, angle_ref[:, pair : pair + 1], ids)
        for axis in range(2):
            ids = jnp.where(row == AIM_ROW + axis, aim_ref[pair : pair + 1, axis : axis + 1], ids)
        info_ref[pair, WAVE_ROW:, :] = ids.astype(jnp.float32)
    for pair in range(pairs):
        own_waves(info_ref, pair, cols, base_ref.at[pair], centre_ref.at[pair])
    core = lax.axis_index("wave")
    left, right = turn_round(width_ref[:, :half]), width_ref[:, half:]
    own_ref[...] = jnp.where(core == 1, right, left)
    far_ref[...] = jnp.where(core == 1, pltpu.roll(left, 1, 1), pltpu.roll(right, half - 1, 1))

    alone = jnp.where(core == 1, 0, half)
    column = width_ref[:, pl.ds(pl.multiple_of(alone, LANES), LANES)]
    columns = near_fields(column, power_ref, pairs)
    void = jnp.where(core == 1, 0, half - 1)
    for index in range(half // (2 * BLOCK)):
        starts = block_starts(half, index)
        for start in (start + step for start in starts for step in range(0, BLOCK, LANES)):
            for side, ref in enumerate((own_ref, far_ref)):
                outs = near_fields(ref[:, start : start + LANES], power_ref, pairs)
                if side and start in (0, half - LANES):
                    keep = iota((rows_dev, LANES), 1) + start != void
                    outs = [[jnp.where(keep, part, 0.0) for part in out] for out in outs]
                for pair, part in ((pair, part) for pair in range(pairs) for part in range(2)):
                    row = (2 * side + part) * rows_dev
                    near_ref[pair, row : row + rows_dev, start : start + LANES] = outs[pair][part].astype(jnp.bfloat16)
        for pair in range(pairs):
            cent_r, cent_i = (centre_ref[pair, part, index : index + 1, :] for part in range(2))
            for row in range(0, BLOCK, GRAIN):
                base_r, base_i = (base_ref[pair, part, row : row + GRAIN, :] for part in range(2))
                for start, table in zip(starts, both_blocks(base_r, base_i, cent_r, cent_i)):
                    rows = slice(start + row, start + row + GRAIN)
                    table_ref[pair, rows, :FOCAL] = table[0].astype(jnp.bfloat16)
                    table_ref[pair, rows, FOCAL:] = table[1].astype(jnp.bfloat16)
            product = jnp.dot(
                jnp.concatenate([near_ref[pair, :, start : start + BLOCK] for start in starts], axis=1),
                jnp.concatenate([table_ref[pair, start : start + BLOCK, :] for start in starts], axis=0),
                preferred_element_type=jnp.float32,
            )
            acc_ref[pair] = product if index == 0 else acc_ref[pair] + product
    for pair in range(pairs):
        acc = [acc_ref[pair, part * rows_dev : (part + 1) * rows_dev, :] for part in range(4)]
        (own_rr, own_ri), (own_ir, own_ii), (far_rr, far_ri), (far_ir, far_ii) = (
            (part[:, :FOCAL], part[:, FOCAL:]) for part in acc
        )
        cross_r, cross_i = far_ii - own_ii, own_ri - far_ri
        real = own_rr + far_rr + jnp.where(core == 1, cross_r, -cross_r)
        imag = own_ir + far_ir + jnp.where(core == 1, cross_i, -cross_i)
        near_r, near_i = (part[:, :1].astype(jnp.bfloat16).astype(jnp.float32) for part in columns[pair])
        wave_r, wave_i = (
            part.astype(jnp.bfloat16).astype(jnp.float32)
            for part in unit_waves((alone - half) * column_freq(info_ref, pair), 256 * cols)
        )
        real = real + (near_r * wave_r - near_i * wave_i)
        imag = imag + (near_r * wave_i + near_i * wave_r)
        for part, value in enumerate((real, imag)):
            lane = (2 * pair + part) * FOCAL
            mine_ref[:, lane : lane + FOCAL] = value.astype(jnp.bfloat16)


def spot_rows(info_ref, pair, first):
    aims = [info_ref[pair, row : row + 1, :] for row in (AIM_ROW, AIM_ROW + 1)]
    rows_off = (iota((PIECE, FOCAL), 0) + first).astype(jnp.float32) - aims[0]
    cols_off = iota((1, FOCAL), 1).astype(jnp.float32) - aims[1]
    return jnp.exp(-(rows_off * rows_off + cols_off * cols_off) / (2.0 * SPOT * SPOT))


def total_of(value):
    return jnp.sum(jnp.sum(value, axis=0, keepdims=True), axis=1, keepdims=True)


def row_kernel(info_ref, tall_ref, flat_ref, spot_ref, gain_ref):
    pairs, _, rows = tall_ref.shape
    rows_dev = flat_ref.shape[1]
    period = 256 * rows
    size = min(rows, FOCAL)
    for pair in range(pairs):
        wave = info_ref[pair, WAVE_ROW : WAVE_ROW + 1, :].astype(jnp.int32) + BLOCK
        focal = (iota((FOCAL, 1), 0) - FOCAL // 2) * wave

        def step(index, carry):
            start = pl.multiple_of(index * size, size)
            place = iota((1, size), 1) + (start - rows // 2)
            for row in range(0, FOCAL, PIECE):
                real, imag = unit_waves(focal[row : row + PIECE, :size] * place, period)
                tall_ref[pair, row : row + PIECE, pl.ds(start, size)] = real.astype(jnp.bfloat16)
                row += FOCAL
                tall_ref[pair, row : row + PIECE, pl.ds(start, size)] = imag.astype(jnp.bfloat16)
            return carry

        if rows == size:
            step(0, 0)
        else:
            lax.fori_loop(0, rows // size, step, 0)
        focal = (iota((1, FOCAL), 1) - FOCAL // 2) * wave
        first = lax.axis_index("aperture") * rows_dev - rows // 2
        real, imag = unit_waves((iota((rows_dev, 1), 0) + first) * focal, period)
        flat_ref[pair, :, :FOCAL] = real.astype(jnp.bfloat16)
        flat_ref[pair, :, FOCAL:] = imag.astype(jnp.bfloat16)
        total = jnp.zeros((PIECE, FOCAL), jnp.float32)
        for row in range(0, FOCAL, PIECE):
            spot = spot_rows(info_ref, pair, row)
            spot_ref[pair, row : row + PIECE, :] = spot
            total += spot
        gain_ref[pair] = jnp.broadcast_to(FOCAL * FOCAL / total_of(total), gain_ref.shape[1:])


def join_kernel(*refs):
    *in_refs, out_ref = refs
    count = in_refs[0].shape[0]
    for index, ref in enumerate(in_refs):
        out_ref[index * count : (index + 1) * count, :] = ref[...]


def focus_kernel(steps, tall_ref, flat_ref, spot_ref, gain_ref, after_ref, *refs):
    del after_ref
    *sect_refs, back_ref, score_ref, rows_ref, mixed_ref, field_ref, stack_ref = refs
    pairs = tall_ref.shape[0]
    rows_dev = back_ref.shape[0]
    if steps is None:
        rows_ref = sect_refs[0]
    else:
        me = lax.axis_index("aperture")
        blocks = [
            ref[index * rows_dev : (index + 1) * rows_dev, :]
            for ref in sect_refs
            for index in range(ref.shape[0] // rows_dev)
        ]
        for step, block in zip(steps, blocks, strict=True):
            start = pl.multiple_of((me ^ step) * rows_dev, rows_dev)
            rows_ref[pl.ds(start, rows_dev), :] = block
    for pair in range(pairs):
        lane = 2 * pair * FOCAL
        section = rows_ref[:, lane : lane + 2 * FOCAL]
        mixed_ref[pair] = jnp.dot(tall_ref[pair], section, preferred_element_type=jnp.float32)
    pieces = [slice(row, row + PIECE) for row in range(0, FOCAL, PIECE)]
    sums = []
    for pair in range(pairs):
        totals = [jnp.zeros((PIECE, FOCAL), jnp.float32) for _ in range(2)]
        for rows in pieces:
            lower = slice(rows.start + FOCAL, rows.stop + FOCAL)
            real = mixed_ref[pair, rows, :FOCAL] - mixed_ref[pair, lower, FOCAL:]
            imag = mixed_ref[pair, rows, FOCAL:] + mixed_ref[pair, lower, :FOCAL]
            field_ref[pair, 0, rows, :] = real
            field_ref[pair, 1, rows, :] = imag
            power = real * real + imag * imag
            totals = [totals[0] + spot_ref[pair, rows, :] * power, totals[1] + power]
        sums.append((total_of(totals[0]), total_of(totals[1]) + 1e-06))
    for pair, (spot_power, all_power) in enumerate(sums):
        ratio = spot_power / all_power
        gain = gain_ref[pair, :1, :1]
        score_ref[pair] = jnp.broadcast_to(ratio * gain, score_ref.shape[1:])
        scale = gain * 2.0 / all_power
        for rows in pieces:
            lower = slice(rows.start + FOCAL, rows.stop + FOCAL)
            weight = scale * (spot_ref[pair, rows, :] - ratio)
            real = (weight * field_ref[pair, 0, rows, :]).astype(jnp.bfloat16)
            imag = (weight * field_ref[pair, 1, rows, :]).astype(jnp.bfloat16)
            stack_ref[pair, rows, :FOCAL] = real
            stack_ref[pair, rows, FOCAL:] = imag
            stack_ref[pair, lower, :FOCAL] = imag
            stack_ref[pair, lower, FOCAL:] = -real
        back = jnp.dot(flat_ref[pair], stack_ref[pair], preferred_element_type=jnp.float32)
        lane = 2 * pair * FOCAL
        back_ref[:, lane : lane + 2 * FOCAL] = back.astype(jnp.bfloat16)


def table_kernel(scale, cols, info_ref, far_info_ref, width_ref, *refs):
    *out_refs, base_ref, centre_ref, turned_ref, power_ref = refs
    pairs = power_ref.shape[0]
    out_refs = out_refs[-2 * pairs :]
    table_refs, slope_refs = out_refs[:pairs], out_refs[pairs:]
    own_cols = width_ref.shape[1]
    sources = [(ref, pair) for ref in (info_ref, far_info_ref) for pair in range(pairs // 2)]
    centres = []
    for pair, (ref, source) in enumerate(sources):
        power = power_coefs(ref[source, : 2 * TERMS, :LANES])
        power_ref[pair] = as_tiles(power * ((iota(power.shape, 0) % TERMS).astype(jnp.float32) * scale))
        own_waves(ref, source, cols, base_ref.at[pair], centre_ref.at[pair])
        for part, row, lane in itertools.product(range(2), range(0, BLOCK, LANES), range(0, FOCAL, LANES)):
            tile = base_ref[pair, part, row : row + LANES, lane : lane + LANES]
            turned_ref[pair, part, lane : lane + LANES, row : row + LANES] = tile.T
        centres.append([centre_ref[pair, part].T for part in range(2)])
    for index in range(own_cols // (2 * BLOCK)):
        starts = block_starts(own_cols, index)
        for pair in range(pairs):
            for row in range(0, FOCAL, GRAIN):
                rows = slice(row, row + GRAIN)
                cent_r, cent_i = (centre[rows, index : index + 1] for centre in centres[pair])
                base_r, base_i = (turned_ref[pair, part, rows, :] for part in range(2))
                for start, table in zip(starts, both_blocks(base_r, base_i, cent_r, cent_i)):
                    for part, value in enumerate(table):
                        place = slice(row + part * FOCAL, row + part * FOCAL + GRAIN)
                        table_refs[pair][place, start : start + BLOCK] = value.astype(jnp.bfloat16)
        for start in (start + step for start in starts for step in range(0, BLOCK, LANES)):
            place = slice(start, start + LANES)
            slopes = near_slopes(width_ref[:, place], power_ref, pairs)
            for ref, slope in zip(slope_refs, slopes):
                ref[0, :, place] = slope[0]
                ref[1, :, place] = slope[1]


def own_grad_kernel(*refs):
    *in_refs, tile_ref, out_ref, score_hbm, score_ref, sem = refs
    score_ref[...] = jnp.concatenate([tile_ref[pair, :1, :1] for pair in range(tile_ref.shape[0])], axis=1)
    move = pltpu.make_async_copy(score_ref, score_hbm, sem)
    move.start()
    add_grads(in_refs, None, out_ref, 2 * BLOCK)
    move.wait()


def last_grad_kernel(*refs):
    *in_refs, total_ref, out_hbm, out_ref, sems = refs
    own_cols = out_ref.shape[1]
    core = lax.axis_index("wave")
    moves = []

    def send(start, total):
        size = total.shape[1]
        place = pl.multiple_of(jnp.where(core == 1, start, own_cols - size - start), size)
        place = pl.ds(place, size)
        out_ref[:, place] = jnp.where(core == 1, total, turn_round(total))
        index = start // size
        moves.append(pltpu.make_async_copy(out_ref.at[:, place], out_hbm.at[:, place], sems.at[index]))
        moves[-1].start()

    add_grads(in_refs, total_ref, out_ref, 2 * BLOCK, send)
    for move in moves:
        move.wait()


def add_grads(in_refs, total_ref, out_ref, size, send=None):
    back_ref, *in_refs = in_refs
    pairs = len(in_refs) // 2
    table_refs, slope_refs = in_refs[:pairs], in_refs[pairs:]
    rows_dev, own_cols = out_ref.shape
    core = lax.axis_index("wave")
    lefts = []
    for pair in range(pairs):
        lane = 2 * pair * FOCAL
        real, imag = back_ref[:, lane : lane + FOCAL], back_ref[:, lane + FOCAL : lane + 2 * FOCAL]
        above = jnp.where(core == 1, imag, -imag)
        below = jnp.where(core == 1, -real, real)
        lefts.append(
            jnp.concatenate(
                [jnp.concatenate([real, above], axis=1), jnp.concatenate([imag, below], axis=1)], axis=0
            )
        )
    for start in range(0, own_cols, size):
        place = slice(start, start + size)
        total = jnp.zeros((rows_dev, size), jnp.float32) if total_ref is None else total_ref[:, place]
        for left, table_ref, slope_ref in zip(lefts, table_refs, slope_refs):
            grad = jnp.dot(left, table_ref[:, place], preferred_element_type=jnp.float32)
            total += grad[:rows_dev] * slope_ref[0, :, place]
            total += grad[rows_dev:] * slope_ref[1, :, place]
        if send is None:
            out_ref[:, place] = total
        else:
            send(start, total)


VMEM = pl.BlockSpec(memory_space=pltpu.VMEM)
SMEM = pl.BlockSpec(memory_space=pltpu.SMEM)
ANY = pl.BlockSpec(memory_space=pl.ANY)
HBM = pl.BlockSpec(memory_space=pltpu.HBM)


def call(kernel, name, outs, in_specs, out_specs, scratch, flops, moved):
    return pl.pallas_call(
        kernel,
        name=name,
        out_shape=outs,
        in_specs=in_specs,
        out_specs=out_specs,
        scratch_shapes=scratch,
        cost_estimate=pl.CostEstimate(flops=flops, bytes_accessed=moved, transcendentals=0),
        compiler_params=pltpu.CompilerParams(vmem_limit_bytes=VMEM_LIMIT),
    )


def on_device(widths, coef_table, wave_ids, angle_ids, targets):
    rows_dev, cols = widths.shape
    pairs_dev = wave_ids.shape[0]
    peers = lax.axis_size("aperture")
    copies = lax.axis_size("wave")
    rows = rows_dev * peers
    pairs = pairs_dev * copies
    own_cols = cols // copies
    lanes = 2 * pairs_dev * FOCAL
    f32, bf16 = jnp.float32, jnp.bfloat16
    shape = jax.ShapeDtypeStruct

    def in_hbm(value):
        return pltpu.with_memory_space_constraint(value, pltpu.HBM)

    def exchange(value, step):
        return lax.ppermute(value, "aperture", [(index, index ^ step) for index in range(peers)])

    def to_core(value):
        return lax.ppermute(value, "wave", [(index, (index + 1) % copies) for index in range(copies)])

    waves = [
        pltpu.VMEM((pairs_dev, 2, BLOCK, FOCAL), f32),
        pltpu.VMEM((pairs_dev, 2, 8, FOCAL), f32),
    ]
    mine, info, own = call(
        forward_kernel, "forward",
        (
            shape((rows_dev, lanes), bf16),
            shape((pairs_dev, INFO_ROWS, FOCAL), f32), shape((rows_dev, own_cols), f32),
        ),
        [HBM] * 5, (VMEM,) * 3,
        [
            pltpu.VMEM((1, pairs_dev), jnp.int32),
            pltpu.VMEM((1, pairs_dev), jnp.int32),
            pltpu.VMEM(targets.shape, jnp.int32),
            pltpu.VMEM(coef_table.shape[::-1], f32),
            pltpu.VMEM(widths.shape, f32),
            pltpu.VMEM((rows_dev, own_cols), f32),
            *waves,
            pltpu.VMEM((pairs_dev, 2 * TERMS, SUBLANES, LANES), f32),
            pltpu.VMEM((pairs_dev, 4 * rows_dev, own_cols), bf16),
            pltpu.VMEM((pairs_dev, own_cols, 2 * FOCAL), bf16),
            pltpu.VMEM((pairs_dev, 4 * rows_dev, 2 * FOCAL), f32),
            pltpu.SemaphoreType.DMA((5,)),
        ],
        10**9, 10**7,
    )(*(in_hbm(value) for value in (wave_ids[None], angle_ids[None], targets, coef_table.T, widths)))
    far_info = to_core(info)

    tall, flat, spots, gains = call(
        row_kernel, "row_tables",
        (
            shape((pairs_dev, 2 * FOCAL, rows), bf16), shape((pairs_dev, rows_dev, 2 * FOCAL), bf16),
            shape((pairs_dev, FOCAL, FOCAL), f32), shape((pairs_dev, 8, 128), f32),
        ),
        [VMEM], (VMEM,) * 4, [], 10**8, 10**6,
    )(info)
    if peers <= DIRECT:
        steps = list(range(peers - 2, 0, -2))
        got = [exchange(mine, step) for step in steps]
        near = exchange(mine, 1)
        first, flat = lax.optimization_barrier((got[0], flat))
        joined = call(join_kernel, "join", shape(((len(steps) - 1) * rows_dev, lanes), bf16),
                      [VMEM] * (len(steps) - 1), VMEM, [], 10**6, 10**6)(*got[1:])
        sections = [mine, near, first, joined, exchange(first, 1), exchange(joined, 1)]
        steps = [0, 1, *steps, *(step ^ 1 for step in steps)]
        after = [near, joined]
    else:
        blocks = jnp.tile(mine[None], (peers, 1, 1))
        blocks = lax.all_to_all(blocks, "aperture", 0, 0, tiled=True)
        sections, steps, after = [blocks.reshape(rows, lanes)], None, []
    outs = [shape((2 * FOCAL, own_cols), bf16)] * pairs + [shape((2, rows_dev, own_cols), f32)] * pairs
    made = call(
        functools.partial(table_kernel, math.sqrt(rows * cols), cols), "column_tables",
        outs, [VMEM] * 3 + [ANY] * len(after), [VMEM] * len(outs),
        [
            pltpu.VMEM((pairs, 2, BLOCK, FOCAL), f32),
            pltpu.VMEM((pairs, 2, 8, FOCAL), f32),
            pltpu.VMEM((pairs, 2, FOCAL, BLOCK), f32),
            pltpu.VMEM((pairs, 2 * TERMS, SUBLANES, LANES), f32),
        ],
        30 * 10**8, 30 * 10**6,
    )(info, far_info, own, *after)
    tables, slopes = made[:pairs], made[pairs:]

    back, scores = call(
        functools.partial(focus_kernel, steps), "focus",
        (shape((rows_dev, lanes), bf16), shape((pairs_dev, SUBLANES, LANES), f32)),
        [VMEM] * 4 + [ANY] + [VMEM] * len(sections), (VMEM, VMEM),
        [
            pltpu.VMEM((rows, lanes), bf16),
            pltpu.VMEM((pairs_dev, 2 * FOCAL, 2 * FOCAL), f32),
            pltpu.VMEM((pairs_dev, 2, FOCAL, FOCAL), f32),
            pltpu.VMEM((pairs_dev, 2 * FOCAL, 2 * FOCAL), bf16),
        ],
        10**8, 10**6,
    )(tall, flat, spots, gains, slopes[0], *sections)

    out = shape((rows_dev, own_cols), f32)
    ins = [back, *tables[:pairs_dev], *slopes[:pairs_dev], scores]
    grad, scores = call(
        own_grad_kernel, "gradient_own", (out, shape((1, pairs_dev), f32)),
        [VMEM] * len(ins), (VMEM, HBM),
        [pltpu.VMEM((1, pairs_dev), f32), pltpu.SemaphoreType.DMA], 10**9, 10**7,
    )(*ins)
    ins = [to_core(back), *tables[pairs_dev:], *slopes[pairs_dev:], grad]
    grad = call(
        last_grad_kernel, "gradient_far", out, [VMEM] * len(ins), HBM,
        [pltpu.VMEM(out.shape, f32), pltpu.SemaphoreType.DMA((own_cols // (2 * BLOCK),))], 10**9, 10**7,
    )(*ins)
    return grad, scores[0]


def solution(mesh):
    in_specs = (
        P(("group", "aperture"), None),
        P(),
        P(("group", "wave")),
        P(("group", "wave")),
        P(("group", "wave"), None),
    )
    out_specs = (P(("group", "aperture"), "wave"), P(("group", "wave")))
    return jax.shard_map(
        on_device, mesh=mesh, in_specs=in_specs, out_specs=out_specs, check_vma=False
    )
```

```python
import functools
import itertools
import math

import jax
import jax.numpy as jnp
from jax import lax
from jax.experimental import pallas as pl
from jax.experimental.pallas import tpu as pltpu
from jax.sharding import PartitionSpec as P

FOCAL = 256
SPOT = 4
SHIFT = 32
TERMS = 8
BLOCK = 256
GRAIN = 16
LANES = 128
PIECE = 16
SUBLANES = 8
VMEM_LIMIT = 16 * 1024 * 1024
WAVE_ROW, ANGLE_ROW, AIM_ROW, INFO_ROWS = 16, 17, 18, 24
DIRECT = 16

COS = (
    1.0, -19.7392088015709, 64.93939395773512, -85.45681453397417, 60.24458621302471,
    -26.425616460281425, 7.8991596631575085, -1.6968741456712442, 0.2437618617467591,
)
SIN = (
    6.2831853071792665, -41.34170224019464, 81.60524925425943, -76.70585885700535,
    42.05867547580699, -15.094428387947755, 3.818490079304055, -0.7122771247541972,
    0.09149844789363434,
)


def horner(terms, u):
    value = terms[-1] * u + terms[-2]
    for term in terms[-3::-1]:
        value = value * u + term
    return value


def unit_waves(counts, period):
    half = period // 2
    centred = ((counts + half) & (period - 1)) - half
    t = centred.astype(jnp.float32) * (1.0 / period)
    u = t * t
    return horner(COS, u), -(t * horner(SIN, u))


def iota(shape, axis):
    return lax.broadcasted_iota(jnp.int32, shape, axis)


def pick_coef(table, wave):
    chosen = jnp.where(iota(table.shape, 1) == wave, table, 0.0)
    return jnp.sum(chosen, axis=1, keepdims=True)


def column_freq(info_ref, pair):
    wave = info_ref[pair, WAVE_ROW : WAVE_ROW + 1, :].astype(jnp.int32)
    angle = info_ref[pair, ANGLE_ROW : ANGLE_ROW + 1, :].astype(jnp.int32)
    return (iota((1, FOCAL), 1) - FOCAL // 2 + SHIFT * angle) * (BLOCK + wave)


def fill_base(freq, shift, period, base_ref, centre_ref):
    low_r, low_i = unit_waves(iota((GRAIN, 1), 0) * freq, period)
    steps = BLOCK // GRAIN
    high_r, high_i = unit_waves((iota((steps, 1), 0) * GRAIN - BLOCK // 2 + shift) * freq, period)
    for step in range(steps):
        one_r, one_i = high_r[step : step + 1], high_i[step : step + 1]
        rows = slice(step * GRAIN, (step + 1) * GRAIN)
        base_ref[0, rows, :] = one_r * low_r - one_i * low_i
        base_ref[1, rows, :] = one_r * low_i + one_i * low_r
    count = centre_ref.shape[1]
    cent_r, cent_i = unit_waves((iota((count, 1), 0) * BLOCK + BLOCK // 2) * freq, period)
    centre_ref[0] = cent_r
    centre_ref[1] = cent_i


def power_coefs(coef):
    before, current = [1], [0, 1]
    bases = [before, current]
    for _ in range(2, TERMS):
        doubled = [0] + [2 * term for term in current]
        before, current = current, [a - b for a, b in itertools.zip_longest(doubled, before, fillvalue=0)]
        bases.append(current)
    rows = []
    for part, power in itertools.product(range(2), range(TERMS)):
        row = None
        for order in range(power, TERMS, 2):
            place = part * TERMS + order
            term = coef[place : place + 1] * float(bases[order][power])
            row = term if row is None else row + term
        rows.append(row)
    return jnp.concatenate(rows, axis=0)


def as_tiles(rows):
    return jnp.broadcast_to(rows[:, None, :], (rows.shape[0], SUBLANES, rows.shape[1]))


def split_rows(value):
    return value.reshape(value.shape[0] // SUBLANES, SUBLANES, value.shape[1])


def join_rows(value):
    return value.reshape(value.shape[0] * SUBLANES, value.shape[2])


def near_fields(s, power_ref, pairs):
    s = split_rows(s)
    outs = []
    for pair, part in itertools.product(range(pairs), range(2)):
        row = (part + 1) * TERMS - 1
        value = power_ref[pair, row] * s + power_ref[pair, row - 1]
        for row in range(row - 2, part * TERMS - 1, -1):
            value = value * s + power_ref[pair, row]
        outs.append(join_rows(value))
    return [outs[2 * pair : 2 * pair + 2] for pair in range(pairs)]


def near_slopes(s, power_ref, pairs):
    s = split_rows(s)
    outs = []
    for pair, part in itertools.product(range(pairs), range(2)):
        row = (part + 1) * TERMS - 1
        value = power_ref[pair, row] * s + power_ref[pair, row - 1]
        for row in range(row - 2, part * TERMS, -1):
            value = value * s + power_ref[pair, row]
        outs.append(join_rows(value))
    return [outs[2 * pair : 2 * pair + 2] for pair in range(pairs)]


def turn_round(value):
    rows, cols = value.shape
    order = LANES - 1 - iota((rows, LANES), 1)
    parts = [
        jnp.take_along_axis(value[:, start : start + LANES], order, axis=1)
        for start in range(cols - LANES, -1, -LANES)
    ]
    return jnp.concatenate(parts, axis=1)


def side_pieces(width_ref, core):
    rows, cols = width_ref.shape
    half = cols // 2
    count = half // LANES
    lane = iota((rows, LANES), 1)
    shift = jnp.where(core == 1, 1, LANES - 1)
    edge = jnp.where(core == 1, 0, LANES - 1)

    @functools.cache
    def turned(piece):
        right = width_ref[:, half + piece * LANES : half + (piece + 1) * LANES]
        left = turn_round(width_ref[:, half - (piece + 1) * LANES : half - piece * LANES])
        other = pltpu.roll(jnp.where(core == 1, left, right), shift, 1)
        return jnp.where(core == 1, right, left), other

    def sides(piece):
        own, other = turned(piece)
        beside = jnp.where(core == 1, turned(max(piece - 1, 0))[1], turned(min(piece + 1, count - 1))[1])
        return own, jnp.where(lane == edge, beside, other)

    return sides


def block_starts(cols, index):
    return cols // 2 - (index + 1) * BLOCK, cols // 2 + index * BLOCK


def both_blocks(base_r, base_i, cent_r, cent_i):
    rr, ii = base_r * cent_r, base_i * cent_i
    ri, ir = base_r * cent_i, base_i * cent_r
    return (rr + ii, ir - ri), (rr - ii, ir + ri)


def own_waves(info_ref, pair, cols, base_ref, centre_ref):
    shift = cols // 4 + 1 - lax.axis_index("wave")
    fill_base(column_freq(info_ref, pair), shift, 256 * cols, base_ref, centre_ref)


def forward_kernel(
    wave_hbm, angle_hbm, aim_hbm, coef_hbm, width_hbm, mine_ref, info_ref, own_ref, *refs
):
    pairs = info_ref.shape[0]
    (
        wave_ref, angle_ref, aim_ref, coef_ref, width_ref, base_ref, centre_ref, power_ref, near_ref, table_ref,
        acc_ref, sems,
    ) = refs
    rows_dev, cols = width_ref.shape
    half = cols // 2
    moves = [
        pltpu.make_async_copy(source, target, sems.at[index])
        for index, (source, target) in enumerate((
            (wave_hbm, wave_ref), (angle_hbm, angle_ref), (aim_hbm, aim_ref),
            (coef_hbm, coef_ref), (width_hbm, width_ref),
        ))
    ]
    for move in moves:
        move.start()
    for move in moves:
        move.wait()
    for pair in range(pairs):
        coef = pick_coef(coef_ref[...], wave_ref[pair])
        coef = jnp.broadcast_to(coef, (WAVE_ROW, FOCAL))
        info_ref[pair, :WAVE_ROW, :] = coef
        power_ref[pair] = as_tiles(power_coefs(coef[:, :LANES]))
        row = iota((INFO_ROWS - WAVE_ROW, FOCAL), 0) + WAVE_ROW
        ids = jnp.where(row == WAVE_ROW, wave_ref[pair], 0)
        ids = jnp.where(row == ANGLE_ROW, angle_ref[pair], ids)
        ids = jnp.where(row == AIM_ROW, aim_ref[pair, 0], ids)
        ids = jnp.where(row == AIM_ROW + 1, aim_ref[pair, 1], ids)
        info_ref[pair, WAVE_ROW:, :] = ids.astype(jnp.float32)
    for pair in range(pairs):
        own_waves(info_ref, pair, cols, base_ref.at[pair], centre_ref.at[pair])
    core = lax.axis_index("wave")
    sides = side_pieces(width_ref, core)
    alone = jnp.where(core == 1, 0, half)
    column = width_ref[:, pl.ds(pl.multiple_of(alone, LANES), LANES)]
    columns = near_fields(column, power_ref, pairs)
    void = jnp.where(core == 1, 0, half - 1)
    for index in range(half // (2 * BLOCK)):
        starts = block_starts(half, index)
        for start in (start + step for start in starts for step in range(0, BLOCK, LANES)):
            both = sides(start // LANES)
            own_ref[:, start : start + LANES] = both[0]
            for side, widths in enumerate(both):
                outs = near_fields(widths, power_ref, pairs)
                if side and start in (0, half - LANES):
                    keep = iota((rows_dev, LANES), 1) + start != void
                    outs = [[jnp.where(keep, part, 0.0) for part in out] for out in outs]
                for pair, part in ((pair, part) for pair in range(pairs) for part in range(2)):
                    row = (2 * side + part) * rows_dev
                    near_ref[pair, row : row + rows_dev, start : start + LANES] = outs[pair][part].astype(jnp.bfloat16)
        for pair in range(pairs):
            cent_r, cent_i = (centre_ref[pair, part, index : index + 1, :] for part in range(2))
            for row in range(0, BLOCK, GRAIN):
                base_r, base_i = (base_ref[pair, part, row : row + GRAIN, :] for part in range(2))
                for start, table in zip(starts, both_blocks(base_r, base_i, cent_r, cent_i)):
                    rows = slice(start + row, start + row + GRAIN)
                    table_ref[pair, rows, :FOCAL] = table[0].astype(jnp.bfloat16)
                    table_ref[pair, rows, FOCAL:] = table[1].astype(jnp.bfloat16)
            product = jnp.dot(
                jnp.concatenate([near_ref[pair, :, start : start + BLOCK] for start in starts], axis=1),
                jnp.concatenate([table_ref[pair, start : start + BLOCK, :] for start in starts], axis=0),
                preferred_element_type=jnp.float32,
            )
            acc_ref[pair] = product if index == 0 else acc_ref[pair] + product
    for pair in range(pairs):
        acc = [acc_ref[pair, part * rows_dev : (part + 1) * rows_dev, :] for part in range(4)]
        (own_rr, own_ri), (own_ir, own_ii), (far_rr, far_ri), (far_ir, far_ii) = (
            (part[:, :FOCAL], part[:, FOCAL:]) for part in acc
        )
        cross_r, cross_i = far_ii - own_ii, own_ri - far_ri
        real = own_rr + far_rr + jnp.where(core == 1, cross_r, -cross_r)
        imag = own_ir + far_ir + jnp.where(core == 1, cross_i, -cross_i)
        near_r, near_i = (part[:, :1].astype(jnp.bfloat16).astype(jnp.float32) for part in columns[pair])
        wave_r, wave_i = (
            part.astype(jnp.bfloat16).astype(jnp.float32)
            for part in unit_waves((alone - half) * column_freq(info_ref, pair), 256 * cols)
        )
        real = real + (near_r * wave_r - near_i * wave_i)
        imag = imag + (near_r * wave_i + near_i * wave_r)
        for part, value in enumerate((real, imag)):
            lane = (2 * pair + part) * FOCAL
            mine_ref[:, lane : lane + FOCAL] = value.astype(jnp.bfloat16)


def spot_rows(info_ref, pair, first):
    aims = [info_ref[pair, row : row + 1, :] for row in (AIM_ROW, AIM_ROW + 1)]
    rows_off = (iota((PIECE, FOCAL), 0) + first).astype(jnp.float32) - aims[0]
    cols_off = iota((1, FOCAL), 1).astype(jnp.float32) - aims[1]
    return jnp.exp(-(rows_off * rows_off + cols_off * cols_off) / (2.0 * SPOT * SPOT))


def total_of(value):
    return jnp.sum(jnp.sum(value, axis=0, keepdims=True), axis=1, keepdims=True)


def row_kernel(info_ref, tall_ref, flat_ref, spot_ref, gain_ref):
    pairs, _, rows = tall_ref.shape
    rows_dev = flat_ref.shape[1]
    period = 256 * rows
    size = min(rows, FOCAL)
    for pair in range(pairs):
        wave = info_ref[pair, WAVE_ROW : WAVE_ROW + 1, :].astype(jnp.int32) + BLOCK
        focal = (iota((FOCAL, 1), 0) - FOCAL // 2) * wave

        def step(index, carry):
            start = pl.multiple_of(index * size, size)
            place = iota((1, size), 1) + (start - rows // 2)
            for row in range(0, FOCAL, PIECE):
                real, imag = unit_waves(focal[row : row + PIECE, :size] * place, period)
                tall_ref[pair, row : row + PIECE, pl.ds(start, size)] = real.astype(jnp.bfloat16)
                row += FOCAL
                tall_ref[pair, row : row + PIECE, pl.ds(start, size)] = imag.astype(jnp.bfloat16)
            return carry

        if rows == size:
            step(0, 0)
        else:
            lax.fori_loop(0, rows // size, step, 0)
        focal = (iota((1, FOCAL), 1) - FOCAL // 2) * wave
        first = lax.axis_index("aperture") * rows_dev - rows // 2
        real, imag = unit_waves((iota((rows_dev, 1), 0) + first) * focal, period)
        flat_ref[pair, :, :FOCAL] = real.astype(jnp.bfloat16)
        flat_ref[pair, :, FOCAL:] = imag.astype(jnp.bfloat16)
        total = jnp.zeros((PIECE, FOCAL), jnp.float32)
        for row in range(0, FOCAL, PIECE):
            spot = spot_rows(info_ref, pair, row)
            spot_ref[pair, row : row + PIECE, :] = spot
            total += spot
        gain_ref[pair] = jnp.broadcast_to(FOCAL * FOCAL / total_of(total), gain_ref.shape[1:])


def join_kernel(*refs):
    *in_refs, out_ref = refs
    count = in_refs[0].shape[0]
    for index, ref in enumerate(in_refs):
        out_ref[index * count : (index + 1) * count, :] = ref[...]


def focus_kernel(steps, tall_ref, flat_ref, spot_ref, gain_ref, after_ref, *refs):
    del after_ref
    *sect_refs, back_ref, score_ref, rows_ref, mixed_ref, field_ref, stack_ref = refs
    pairs = tall_ref.shape[0]
    rows_dev = back_ref.shape[0]
    if steps is None:
        rows_ref = sect_refs[0]
    else:
        me = lax.axis_index("aperture")
        blocks = [
            ref[index * rows_dev : (index + 1) * rows_dev, :]
            for ref in sect_refs
            for index in range(ref.shape[0] // rows_dev)
        ]
        for step, block in zip(steps, blocks, strict=True):
            start = pl.multiple_of((me ^ step) * rows_dev, rows_dev)
            rows_ref[pl.ds(start, rows_dev), :] = block
    for pair in range(pairs):
        lane = 2 * pair * FOCAL
        section = rows_ref[:, lane : lane + 2 * FOCAL]
        mixed_ref[pair] = jnp.dot(tall_ref[pair], section, preferred_element_type=jnp.float32)
    pieces = [slice(row, row + PIECE) for row in range(0, FOCAL, PIECE)]
    sums = []
    for pair in range(pairs):
        totals = [jnp.zeros((PIECE, FOCAL), jnp.float32) for _ in range(2)]
        for rows in pieces:
            lower = slice(rows.start + FOCAL, rows.stop + FOCAL)
            real = mixed_ref[pair, rows, :FOCAL] - mixed_ref[pair, lower, FOCAL:]
            imag = mixed_ref[pair, rows, FOCAL:] + mixed_ref[pair, lower, :FOCAL]
            field_ref[pair, 0, rows, :] = real
            field_ref[pair, 1, rows, :] = imag
            power = real * real + imag * imag
            totals = [totals[0] + spot_ref[pair, rows, :] * power, totals[1] + power]
        sums.append((total_of(totals[0]), total_of(totals[1]) + 1e-06))
    for pair, (spot_power, all_power) in enumerate(sums):
        ratio = spot_power / all_power
        gain = gain_ref[pair, :1, :1]
        score_ref[pair] = jnp.broadcast_to(ratio * gain, score_ref.shape[1:])
        scale = gain * 2.0 / all_power
        for rows in pieces:
            lower = slice(rows.start + FOCAL, rows.stop + FOCAL)
            weight = scale * (spot_ref[pair, rows, :] - ratio)
            real = (weight * field_ref[pair, 0, rows, :]).astype(jnp.bfloat16)
            imag = (weight * field_ref[pair, 1, rows, :]).astype(jnp.bfloat16)
            stack_ref[pair, rows, :FOCAL] = real
            stack_ref[pair, rows, FOCAL:] = imag
            stack_ref[pair, lower, :FOCAL] = imag
            stack_ref[pair, lower, FOCAL:] = -real
        back = jnp.dot(flat_ref[pair], stack_ref[pair], preferred_element_type=jnp.float32)
        lane = 2 * pair * FOCAL
        back_ref[:, lane : lane + 2 * FOCAL] = back.astype(jnp.bfloat16)


def table_kernel(scale, cols, info_ref, far_info_ref, width_ref, *refs):
    *out_refs, base_ref, centre_ref, turned_ref, power_ref = refs
    pairs = power_ref.shape[0]
    out_refs = out_refs[-2 * pairs :]
    table_refs, slope_refs = out_refs[:pairs], out_refs[pairs:]
    own_cols = width_ref.shape[1]
    sources = [(ref, pair) for ref in (info_ref, far_info_ref) for pair in range(pairs // 2)]
    centres = []
    for pair, (ref, source) in enumerate(sources):
        power = power_coefs(ref[source, : 2 * TERMS, :LANES])
        power_ref[pair] = as_tiles(power * ((iota(power.shape, 0) % TERMS).astype(jnp.float32) * scale))
        own_waves(ref, source, cols, base_ref.at[pair], centre_ref.at[pair])
        for part, row, lane in itertools.product(range(2), range(0, BLOCK, LANES), range(0, FOCAL, LANES)):
            tile = base_ref[pair, part, row : row + LANES, lane : lane + LANES]
            turned_ref[pair, part, lane : lane + LANES, row : row + LANES] = tile.T
        centres.append([centre_ref[pair, part].T for part in range(2)])
    for index in range(own_cols // (2 * BLOCK)):
        starts = block_starts(own_cols, index)
        for pair in range(pairs):
            for row in range(0, FOCAL, GRAIN):
                rows = slice(row, row + GRAIN)
                cent_r, cent_i = (centre[rows, index : index + 1] for centre in centres[pair])
                base_r, base_i = (turned_ref[pair, part, rows, :] for part in range(2))
                for start, table in zip(starts, both_blocks(base_r, base_i, cent_r, cent_i)):
                    for part, value in enumerate(table):
                        place = slice(row + part * FOCAL, row + part * FOCAL + GRAIN)
                        table_refs[pair][place, start : start + BLOCK] = value.astype(jnp.bfloat16)
        for start in (start + step for start in starts for step in range(0, BLOCK, LANES)):
            place = slice(start, start + LANES)
            slopes = near_slopes(width_ref[:, place], power_ref, pairs)
            for ref, slope in zip(slope_refs, slopes):
                ref[0, :, place] = slope[0]
                ref[1, :, place] = slope[1]


def own_grad_kernel(*refs):
    *in_refs, out_ref = refs
    add_grads(in_refs, None, out_ref, 2 * BLOCK)


def last_grad_kernel(*refs):
    *in_refs, total_ref, tile_ref, out_hbm, score_hbm, out_ref, score_ref, sems = refs
    own_cols = out_ref.shape[1]
    core = lax.axis_index("wave")
    for pair in range(score_ref.shape[0]):
        score_ref[pair] = jnp.sum(tile_ref[pair, :1, :1])
    moves = [pltpu.make_async_copy(score_ref, score_hbm, sems.at[own_cols // (2 * BLOCK)])]
    moves[0].start()

    def send(start, total):
        size = total.shape[1]
        place = pl.multiple_of(jnp.where(core == 1, start, own_cols - size - start), size)
        place = pl.ds(place, size)
        out_ref[:, place] = jnp.where(core == 1, total, turn_round(total))
        index = start // size
        moves.append(pltpu.make_async_copy(out_ref.at[:, place], out_hbm.at[:, place], sems.at[index]))
        moves[-1].start()

    add_grads(in_refs, total_ref, out_ref, 2 * BLOCK, send)
    for move in moves:
        move.wait()


def add_grads(in_refs, total_ref, out_ref, size, send=None):
    back_ref, *in_refs = in_refs
    pairs = len(in_refs) // 2
    table_refs, slope_refs = in_refs[:pairs], in_refs[pairs:]
    rows_dev, own_cols = out_ref.shape
    core = lax.axis_index("wave")
    lefts = []
    for pair in range(pairs):
        lane = 2 * pair * FOCAL
        real, imag = back_ref[:, lane : lane + FOCAL], back_ref[:, lane + FOCAL : lane + 2 * FOCAL]
        above = jnp.where(core == 1, imag, -imag)
        below = jnp.where(core == 1, -real, real)
        lefts.append(
            jnp.concatenate(
                [jnp.concatenate([real, above], axis=1), jnp.concatenate([imag, below], axis=1)], axis=0
            )
        )
    for start in range(0, own_cols, size):
        place = slice(start, start + size)
        total = jnp.zeros((rows_dev, size), jnp.float32) if total_ref is None else total_ref[:, place]
        for left, table_ref, slope_ref in zip(lefts, table_refs, slope_refs):
            grad = jnp.dot(left, table_ref[:, place], preferred_element_type=jnp.float32)
            total += grad[:rows_dev] * slope_ref[0, :, place]
            total += grad[rows_dev:] * slope_ref[1, :, place]
        if send is None:
            out_ref[:, place] = total
        else:
            send(start, total)


VMEM = pl.BlockSpec(memory_space=pltpu.VMEM)
SMEM = pl.BlockSpec(memory_space=pltpu.SMEM)
ANY = pl.BlockSpec(memory_space=pl.ANY)
HBM = pl.BlockSpec(memory_space=pltpu.HBM)


def call(kernel, name, outs, in_specs, out_specs, scratch, flops, moved):
    return pl.pallas_call(
        kernel,
        name=name,
        out_shape=outs,
        in_specs=in_specs,
        out_specs=out_specs,
        scratch_shapes=scratch,
        cost_estimate=pl.CostEstimate(flops=flops, bytes_accessed=moved, transcendentals=0),
        compiler_params=pltpu.CompilerParams(vmem_limit_bytes=VMEM_LIMIT),
    )


def on_device(widths, coef_table, wave_ids, angle_ids, targets):
    rows_dev, cols = widths.shape
    pairs_dev = wave_ids.shape[0]
    peers = lax.axis_size("aperture")
    copies = lax.axis_size("wave")
    rows = rows_dev * peers
    pairs = pairs_dev * copies
    own_cols = cols // copies
    lanes = 2 * pairs_dev * FOCAL
    f32, bf16 = jnp.float32, jnp.bfloat16
    shape = jax.ShapeDtypeStruct

    def in_hbm(value):
        return pltpu.with_memory_space_constraint(value, pltpu.HBM)

    def exchange(value, step):
        return lax.ppermute(value, "aperture", [(index, index ^ step) for index in range(peers)])

    def to_core(value):
        return lax.ppermute(value, "wave", [(index, (index + 1) % copies) for index in range(copies)])

    waves = [
        pltpu.VMEM((pairs_dev, 2, BLOCK, FOCAL), f32),
        pltpu.VMEM((pairs_dev, 2, 8, FOCAL), f32),
    ]
    mine, info, own = call(
        forward_kernel, "forward",
        (
            shape((rows_dev, lanes), bf16),
            shape((pairs_dev, INFO_ROWS, FOCAL), f32), shape((rows_dev, own_cols), f32),
        ),
        [HBM] * 5, (VMEM,) * 3,
        [
            pltpu.SMEM(wave_ids.shape, jnp.int32),
            pltpu.SMEM(angle_ids.shape, jnp.int32),
            pltpu.SMEM(targets.shape, jnp.int32),
            pltpu.VMEM(coef_table.shape[::-1], f32),
            pltpu.VMEM(widths.shape, f32),
            *waves,
            pltpu.VMEM((pairs_dev, 2 * TERMS, SUBLANES, LANES), f32),
            pltpu.VMEM((pairs_dev, 4 * rows_dev, own_cols), bf16),
            pltpu.VMEM((pairs_dev, own_cols, 2 * FOCAL), bf16),
            pltpu.VMEM((pairs_dev, 4 * rows_dev, 2 * FOCAL), f32),
            pltpu.SemaphoreType.DMA((5,)),
        ],
        10**9, 10**7,
    )(*(in_hbm(value) for value in (wave_ids, angle_ids, targets, coef_table.T, widths)))
    far_info = to_core(info)

    tall, flat, spots, gains = call(
        row_kernel, "row_tables",
        (
            shape((pairs_dev, 2 * FOCAL, rows), bf16), shape((pairs_dev, rows_dev, 2 * FOCAL), bf16),
            shape((pairs_dev, FOCAL, FOCAL), f32), shape((pairs_dev, 8, 128), f32),
        ),
        [VMEM], (VMEM,) * 4, [], 10**8, 10**6,
    )(info)
    if peers <= DIRECT:
        steps = list(range(peers - 2, 0, -2))
        got = [exchange(mine, step) for step in steps]
        near = exchange(mine, 1)
        first, flat = lax.optimization_barrier((got[0], flat))
        joined = call(join_kernel, "join", shape(((len(steps) - 1) * rows_dev, lanes), bf16),
                      [VMEM] * (len(steps) - 1), VMEM, [], 10**6, 10**6)(*got[1:])
        sections = [mine, near, first, joined, exchange(first, 1), exchange(joined, 1)]
        steps = [0, 1, *steps, *(step ^ 1 for step in steps)]
        after = [near, joined]
    else:
        blocks = jnp.tile(mine[None], (peers, 1, 1))
        blocks = lax.all_to_all(blocks, "aperture", 0, 0, tiled=True)
        sections, steps, after = [blocks.reshape(rows, lanes)], None, []
    outs = [shape((2 * FOCAL, own_cols), bf16)] * pairs + [shape((2, rows_dev, own_cols), f32)] * pairs
    made = call(
        functools.partial(table_kernel, math.sqrt(rows * cols), cols), "column_tables",
        outs, [VMEM] * 3 + [ANY] * len(after), [VMEM] * len(outs),
        [
            pltpu.VMEM((pairs, 2, BLOCK, FOCAL), f32),
            pltpu.VMEM((pairs, 2, 8, FOCAL), f32),
            pltpu.VMEM((pairs, 2, FOCAL, BLOCK), f32),
            pltpu.VMEM((pairs, 2 * TERMS, SUBLANES, LANES), f32),
        ],
        30 * 10**8, 30 * 10**6,
    )(info, far_info, own, *after)
    tables, slopes = made[:pairs], made[pairs:]

    back, scores = call(
        functools.partial(focus_kernel, steps), "focus",
        (shape((rows_dev, lanes), bf16), shape((pairs_dev, SUBLANES, LANES), f32)),
        [VMEM] * 4 + [ANY] + [VMEM] * len(sections), (VMEM, VMEM),
        [
            pltpu.VMEM((rows, lanes), bf16),
            pltpu.VMEM((pairs_dev, 2 * FOCAL, 2 * FOCAL), f32),
            pltpu.VMEM((pairs_dev, 2, FOCAL, FOCAL), f32),
            pltpu.VMEM((pairs_dev, 2 * FOCAL, 2 * FOCAL), bf16),
        ],
        10**8, 10**6,
    )(tall, flat, spots, gains, slopes[0], *sections)

    out = shape((rows_dev, own_cols), f32)
    ins = [back, *tables[:pairs_dev], *slopes[:pairs_dev]]
    grad = call(
        own_grad_kernel, "gradient_own", out, [VMEM] * len(ins), VMEM, [], 10**9, 10**7,
    )(*ins)
    ins = [to_core(back), *tables[pairs_dev:], *slopes[pairs_dev:], grad, scores]
    grad, scores = call(
        last_grad_kernel, "gradient_far", (out, shape((pairs_dev,), f32)), [VMEM] * len(ins), (HBM, HBM),
        [
            pltpu.VMEM(out.shape, f32),
            pltpu.SMEM((pairs_dev,), f32),
            pltpu.SemaphoreType.DMA((own_cols // (2 * BLOCK) + 1,)),
        ],
        10**9, 10**7,
    )(*ins)
    return grad, scores


def solution(mesh):
    in_specs = (
        P(("group", "aperture"), None),
        P(),
        P(("group", "wave")),
        P(("group", "wave")),
        P(("group", "wave"), None),
    )
    out_specs = (P(("group", "aperture"), "wave"), P(("group", "wave")))
    return jax.shard_map(
        on_device, mesh=mesh, in_specs=in_specs, out_specs=out_specs, check_vma=False
    )
```

```python
import functools
import itertools
import math

import jax
import jax.numpy as jnp
from jax import lax
from jax.experimental import pallas as pl
from jax.experimental.pallas import tpu as pltpu
from jax.sharding import PartitionSpec as P

FOCAL = 256
SPOT = 4
SHIFT = 32
TERMS = 8
BLOCK = 256
GRAIN = 16
LANES = 128
PIECE = 16
SUBLANES = 8
VMEM_LIMIT = 16 * 1024 * 1024
WAVE_ROW, ANGLE_ROW, AIM_ROW, INFO_ROWS = 16, 17, 18, 24
DIRECT = 16

COS = (
    1.0, -19.7392088015709, 64.93939395773512, -85.45681453397417, 60.24458621302471,
    -26.425616460281425, 7.8991596631575085, -1.6968741456712442, 0.2437618617467591,
)
SIN = (
    6.2831853071792665, -41.34170224019464, 81.60524925425943, -76.70585885700535,
    42.05867547580699, -15.094428387947755, 3.818490079304055, -0.7122771247541972,
    0.09149844789363434,
)


def horner(terms, u):
    value = terms[-1] * u + terms[-2]
    for term in terms[-3::-1]:
        value = value * u + term
    return value


def unit_waves(counts, period):
    half = period // 2
    centred = ((counts + half) & (period - 1)) - half
    t = centred.astype(jnp.float32) * (1.0 / period)
    u = t * t
    return horner(COS, u), -(t * horner(SIN, u))


def iota(shape, axis):
    return lax.broadcasted_iota(jnp.int32, shape, axis)


def pick_coef(table, wave):
    chosen = jnp.where(iota(table.shape, 1) == wave, table, 0.0)
    return jnp.sum(chosen, axis=1, keepdims=True)


def column_freq(info_ref, pair):
    wave = info_ref[pair, WAVE_ROW : WAVE_ROW + 1, :].astype(jnp.int32)
    angle = info_ref[pair, ANGLE_ROW : ANGLE_ROW + 1, :].astype(jnp.int32)
    return (iota((1, FOCAL), 1) - FOCAL // 2 + SHIFT * angle) * (BLOCK + wave)


def fill_base(freq, shift, period, base_ref, centre_ref):
    low_r, low_i = unit_waves(iota((GRAIN, 1), 0) * freq, period)
    steps = BLOCK // GRAIN
    high_r, high_i = unit_waves((iota((steps, 1), 0) * GRAIN - BLOCK // 2 + shift) * freq, period)
    for step in range(steps):
        one_r, one_i = high_r[step : step + 1], high_i[step : step + 1]
        rows = slice(step * GRAIN, (step + 1) * GRAIN)
        base_ref[0, rows, :] = one_r * low_r - one_i * low_i
        base_ref[1, rows, :] = one_r * low_i + one_i * low_r
    count = centre_ref.shape[1]
    cent_r, cent_i = unit_waves((iota((count, 1), 0) * BLOCK + BLOCK // 2) * freq, period)
    centre_ref[0] = cent_r
    centre_ref[1] = cent_i


def power_coefs(coef):
    before, current = [1], [0, 1]
    bases = [before, current]
    for _ in range(2, TERMS):
        doubled = [0] + [2 * term for term in current]
        before, current = current, [a - b for a, b in itertools.zip_longest(doubled, before, fillvalue=0)]
        bases.append(current)
    rows = []
    for part, power in itertools.product(range(2), range(TERMS)):
        row = None
        for order in range(power, TERMS, 2):
            place = part * TERMS + order
            term = coef[place : place + 1] * float(bases[order][power])
            row = term if row is None else row + term
        rows.append(row)
    return jnp.concatenate(rows, axis=0)


def as_tiles(rows):
    return jnp.broadcast_to(rows[:, None, :], (rows.shape[0], SUBLANES, rows.shape[1]))


def split_rows(value):
    return value.reshape(value.shape[0] // SUBLANES, SUBLANES, value.shape[1])


def join_rows(value):
    return value.reshape(value.shape[0] * SUBLANES, value.shape[2])


def near_fields(s, power_ref, pairs):
    s = split_rows(s)
    outs = []
    for pair, part in itertools.product(range(pairs), range(2)):
        row = (part + 1) * TERMS - 1
        value = power_ref[pair, row] * s + power_ref[pair, row - 1]
        for row in range(row - 2, part * TERMS - 1, -1):
            value = value * s + power_ref[pair, row]
        outs.append(join_rows(value))
    return [outs[2 * pair : 2 * pair + 2] for pair in range(pairs)]


def near_slopes(s, power_ref, pairs):
    s = split_rows(s)
    outs = []
    for pair, part in itertools.product(range(pairs), range(2)):
        row = (part + 1) * TERMS - 1
        value = power_ref[pair, row] * s + power_ref[pair, row - 1]
        for row in range(row - 2, part * TERMS, -1):
            value = value * s + power_ref[pair, row]
        outs.append(join_rows(value))
    return [outs[2 * pair : 2 * pair + 2] for pair in range(pairs)]


def turn_round(value):
    rows, cols = value.shape
    order = LANES - 1 - iota((rows, LANES), 1)
    parts = [
        jnp.take_along_axis(value[:, start : start + LANES], order, axis=1)
        for start in range(cols - LANES, -1, -LANES)
    ]
    return jnp.concatenate(parts, axis=1)


def side_pieces(width_ref, core):
    rows, cols = width_ref.shape
    half = cols // 2
    count = half // LANES
    lane = iota((rows, LANES), 1)
    shift = jnp.where(core == 1, 1, LANES - 1)
    edge = jnp.where(core == 1, 0, LANES - 1)

    @functools.cache
    def turned(piece):
        right = width_ref[:, half + piece * LANES : half + (piece + 1) * LANES]
        left = turn_round(width_ref[:, half - (piece + 1) * LANES : half - piece * LANES])
        other = pltpu.roll(jnp.where(core == 1, left, right), shift, 1)
        return jnp.where(core == 1, right, left), other

    def sides(piece):
        own, other = turned(piece)
        beside = jnp.where(core == 1, turned(max(piece - 1, 0))[1], turned(min(piece + 1, count - 1))[1])
        return own, jnp.where(lane == edge, beside, other)

    return sides


def block_starts(cols, index):
    return cols // 2 - (index + 1) * BLOCK, cols // 2 + index * BLOCK


def both_blocks(base_r, base_i, cent_r, cent_i):
    rr, ii = base_r * cent_r, base_i * cent_i
    ri, ir = base_r * cent_i, base_i * cent_r
    return (rr + ii, ir - ri), (rr - ii, ir + ri)


def own_waves(info_ref, pair, cols, base_ref, centre_ref):
    shift = cols // 4 + 1 - lax.axis_index("wave")
    fill_base(column_freq(info_ref, pair), shift, 256 * cols, base_ref, centre_ref)


def forward_kernel(
    wave_hbm, angle_hbm, aim_hbm, coef_hbm, width_hbm, mine_ref, info_ref, own_ref, *refs
):
    pairs = info_ref.shape[0]
    (
        wave_ref, angle_ref, aim_ref, coef_ref, width_ref, base_ref, centre_ref, power_ref, near_ref, table_ref,
        acc_ref, sems,
    ) = refs
    rows_dev, cols = width_ref.shape
    half = cols // 2
    moves = [
        pltpu.make_async_copy(source, target, sems.at[index])
        for index, (source, target) in enumerate((
            (wave_hbm, wave_ref), (angle_hbm, angle_ref), (aim_hbm, aim_ref),
            (coef_hbm, coef_ref), (width_hbm, width_ref),
        ))
    ]
    for move in moves:
        move.start()
    for move in moves:
        move.wait()
    for pair in range(pairs):
        coef = pick_coef(coef_ref[...], wave_ref[pair])
        coef = jnp.broadcast_to(coef, (WAVE_ROW, FOCAL))
        info_ref[pair, :WAVE_ROW, :] = coef
        power_ref[pair] = as_tiles(power_coefs(coef[:, :LANES]))
        row = iota((INFO_ROWS - WAVE_ROW, FOCAL), 0) + WAVE_ROW
        ids = jnp.where(row == WAVE_ROW, wave_ref[pair], 0)
        ids = jnp.where(row == ANGLE_ROW, angle_ref[pair], ids)
        ids = jnp.where(row == AIM_ROW, aim_ref[pair, 0], ids)
        ids = jnp.where(row == AIM_ROW + 1, aim_ref[pair, 1], ids)
        info_ref[pair, WAVE_ROW:, :] = ids.astype(jnp.float32)
    for pair in range(pairs):
        own_waves(info_ref, pair, cols, base_ref.at[pair], centre_ref.at[pair])
    core = lax.axis_index("wave")
    sides = side_pieces(width_ref, core)
    alone = jnp.where(core == 1, 0, half)
    column = width_ref[:, pl.ds(pl.multiple_of(alone, LANES), LANES)]
    columns = near_fields(column, power_ref, pairs)
    void = jnp.where(core == 1, 0, half - 1)
    for index in range(half // (2 * BLOCK)):
        starts = block_starts(half, index)
        for start in (start + step for start in starts for step in range(0, BLOCK, LANES)):
            both = sides(start // LANES)
            own_ref[:, start : start + LANES] = both[0]
            for side, widths in enumerate(both):
                outs = near_fields(widths, power_ref, pairs)
                if side and start in (0, half - LANES):
                    keep = iota((rows_dev, LANES), 1) + start != void
                    outs = [[jnp.where(keep, part, 0.0) for part in out] for out in outs]
                for pair, part in ((pair, part) for pair in range(pairs) for part in range(2)):
                    row = (2 * side + part) * rows_dev
                    near_ref[pair, row : row + rows_dev, start : start + LANES] = outs[pair][part].astype(jnp.bfloat16)
        for pair in range(pairs):
            cent_r, cent_i = (centre_ref[pair, part, index : index + 1, :] for part in range(2))
            for row in range(0, BLOCK, GRAIN):
                base_r, base_i = (base_ref[pair, part, row : row + GRAIN, :] for part in range(2))
                for start, table in zip(starts, both_blocks(base_r, base_i, cent_r, cent_i)):
                    rows = slice(start + row, start + row + GRAIN)
                    table_ref[pair, rows, :FOCAL] = table[0].astype(jnp.bfloat16)
                    table_ref[pair, rows, FOCAL:] = table[1].astype(jnp.bfloat16)
            product = jnp.dot(
                jnp.concatenate([near_ref[pair, :, start : start + BLOCK] for start in starts], axis=1),
                jnp.concatenate([table_ref[pair, start : start + BLOCK, :] for start in starts], axis=0),
                preferred_element_type=jnp.float32,
            )
            acc_ref[pair] = product if index == 0 else acc_ref[pair] + product
    for pair in range(pairs):
        acc = [acc_ref[pair, part * rows_dev : (part + 1) * rows_dev, :] for part in range(4)]
        (own_rr, own_ri), (own_ir, own_ii), (far_rr, far_ri), (far_ir, far_ii) = (
            (part[:, :FOCAL], part[:, FOCAL:]) for part in acc
        )
        cross_r, cross_i = far_ii - own_ii, own_ri - far_ri
        real = own_rr + far_rr + jnp.where(core == 1, cross_r, -cross_r)
        imag = own_ir + far_ir + jnp.where(core == 1, cross_i, -cross_i)
        near_r, near_i = (part[:, :1].astype(jnp.bfloat16).astype(jnp.float32) for part in columns[pair])
        wave_r, wave_i = (
            part.astype(jnp.bfloat16).astype(jnp.float32)
            for part in unit_waves((alone - half) * column_freq(info_ref, pair), 256 * cols)
        )
        real = real + (near_r * wave_r - near_i * wave_i)
        imag = imag + (near_r * wave_i + near_i * wave_r)
        for part, value in enumerate((real, imag)):
            lane = (2 * pair + part) * FOCAL
            mine_ref[:, lane : lane + FOCAL] = value.astype(jnp.bfloat16)


def spot_rows(info_ref, pair, first):
    aims = [info_ref[pair, row : row + 1, :] for row in (AIM_ROW, AIM_ROW + 1)]
    rows_off = (iota((PIECE, FOCAL), 0) + first).astype(jnp.float32) - aims[0]
    cols_off = iota((1, FOCAL), 1).astype(jnp.float32) - aims[1]
    return jnp.exp(-(rows_off * rows_off + cols_off * cols_off) / (2.0 * SPOT * SPOT))


def total_of(value):
    return jnp.sum(jnp.sum(value, axis=0, keepdims=True), axis=1, keepdims=True)


def row_kernel(info_ref, tall_ref, flat_ref, spot_ref, gain_ref):
    pairs, _, rows = tall_ref.shape
    rows_dev = flat_ref.shape[1]
    period = 256 * rows
    size = min(rows, FOCAL)
    for pair in range(pairs):
        wave = info_ref[pair, WAVE_ROW : WAVE_ROW + 1, :].astype(jnp.int32) + BLOCK
        focal = (iota((FOCAL, 1), 0) - FOCAL // 2) * wave

        def step(index, carry):
            start = pl.multiple_of(index * size, size)
            place = iota((1, size), 1) + (start - rows // 2)
            for row in range(0, FOCAL, PIECE):
                real, imag = unit_waves(focal[row : row + PIECE, :size] * place, period)
                tall_ref[pair, row : row + PIECE, pl.ds(start, size)] = real.astype(jnp.bfloat16)
                row += FOCAL
                tall_ref[pair, row : row + PIECE, pl.ds(start, size)] = imag.astype(jnp.bfloat16)
            return carry

        if rows == size:
            step(0, 0)
        else:
            lax.fori_loop(0, rows // size, step, 0)
        focal = (iota((1, FOCAL), 1) - FOCAL // 2) * wave
        first = lax.axis_index("aperture") * rows_dev - rows // 2
        real, imag = unit_waves((iota((rows_dev, 1), 0) + first) * focal, period)
        flat_ref[pair, :, :FOCAL] = real.astype(jnp.bfloat16)
        flat_ref[pair, :, FOCAL:] = imag.astype(jnp.bfloat16)
        total = jnp.zeros((PIECE, FOCAL), jnp.float32)
        for row in range(0, FOCAL, PIECE):
            spot = spot_rows(info_ref, pair, row)
            spot_ref[pair, row : row + PIECE, :] = spot
            total += spot
        gain_ref[pair] = jnp.broadcast_to(FOCAL * FOCAL / total_of(total), gain_ref.shape[1:])


def join_kernel(*refs):
    *in_refs, out_ref = refs
    count = in_refs[0].shape[0]
    for index, ref in enumerate(in_refs):
        out_ref[index * count : (index + 1) * count, :] = ref[...]


def focus_kernel(steps, tall_ref, flat_ref, spot_ref, gain_ref, after_ref, *refs):
    del after_ref
    *sect_refs, back_ref, score_ref, rows_ref, mixed_ref, field_ref, stack_ref = refs
    pairs = tall_ref.shape[0]
    rows_dev = back_ref.shape[0]
    if steps is None:
        rows_ref = sect_refs[0]
    else:
        me = lax.axis_index("aperture")
        blocks = [
            ref[index * rows_dev : (index + 1) * rows_dev, :]
            for ref in sect_refs
            for index in range(ref.shape[0] // rows_dev)
        ]
        length = rows_ref.shape[0] // rows_dev // 2
        for (turn, flip), block in zip(steps, blocks, strict=True):
            source = 2 * ((me // 2 + (length - turn)) % length) + ((me % 2) ^ flip)
            start = pl.multiple_of(source * rows_dev, rows_dev)
            rows_ref[pl.ds(start, rows_dev), :] = block
    for pair in range(pairs):
        lane = 2 * pair * FOCAL
        section = rows_ref[:, lane : lane + 2 * FOCAL]
        mixed_ref[pair] = jnp.dot(tall_ref[pair], section, preferred_element_type=jnp.float32)
    pieces = [slice(row, row + PIECE) for row in range(0, FOCAL, PIECE)]
    sums = []
    for pair in range(pairs):
        totals = [jnp.zeros((PIECE, FOCAL), jnp.float32) for _ in range(2)]
        for rows in pieces:
            lower = slice(rows.start + FOCAL, rows.stop + FOCAL)
            real = mixed_ref[pair, rows, :FOCAL] - mixed_ref[pair, lower, FOCAL:]
            imag = mixed_ref[pair, rows, FOCAL:] + mixed_ref[pair, lower, :FOCAL]
            field_ref[pair, 0, rows, :] = real
            field_ref[pair, 1, rows, :] = imag
            power = real * real + imag * imag
            totals = [totals[0] + spot_ref[pair, rows, :] * power, totals[1] + power]
        sums.append((total_of(totals[0]), total_of(totals[1]) + 1e-06))
    for pair, (spot_power, all_power) in enumerate(sums):
        ratio = spot_power / all_power
        gain = gain_ref[pair, :1, :1]
        score_ref[pair] = jnp.broadcast_to(ratio * gain, score_ref.shape[1:])
        scale = gain * 2.0 / all_power
        for rows in pieces:
            lower = slice(rows.start + FOCAL, rows.stop + FOCAL)
            weight = scale * (spot_ref[pair, rows, :] - ratio)
            real = (weight * field_ref[pair, 0, rows, :]).astype(jnp.bfloat16)
            imag = (weight * field_ref[pair, 1, rows, :]).astype(jnp.bfloat16)
            stack_ref[pair, rows, :FOCAL] = real
            stack_ref[pair, rows, FOCAL:] = imag
            stack_ref[pair, lower, :FOCAL] = imag
            stack_ref[pair, lower, FOCAL:] = -real
        back = jnp.dot(flat_ref[pair], stack_ref[pair], preferred_element_type=jnp.float32)
        lane = 2 * pair * FOCAL
        back_ref[:, lane : lane + 2 * FOCAL] = back.astype(jnp.bfloat16)


def table_kernel(scale, cols, info_ref, far_info_ref, width_ref, *refs):
    *out_refs, base_ref, centre_ref, turned_ref, power_ref = refs
    pairs = power_ref.shape[0]
    out_refs = out_refs[-2 * pairs :]
    table_refs, slope_refs = out_refs[:pairs], out_refs[pairs:]
    own_cols = width_ref.shape[1]
    sources = [(ref, pair) for ref in (info_ref, far_info_ref) for pair in range(pairs // 2)]
    centres = []
    for pair, (ref, source) in enumerate(sources):
        power = power_coefs(ref[source, : 2 * TERMS, :LANES])
        power_ref[pair] = as_tiles(power * ((iota(power.shape, 0) % TERMS).astype(jnp.float32) * scale))
        own_waves(ref, source, cols, base_ref.at[pair], centre_ref.at[pair])
        for part, row, lane in itertools.product(range(2), range(0, BLOCK, LANES), range(0, FOCAL, LANES)):
            tile = base_ref[pair, part, row : row + LANES, lane : lane + LANES]
            turned_ref[pair, part, lane : lane + LANES, row : row + LANES] = tile.T
        centres.append([centre_ref[pair, part].T for part in range(2)])
    for index in range(own_cols // (2 * BLOCK)):
        starts = block_starts(own_cols, index)
        for pair in range(pairs):
            for row in range(0, FOCAL, GRAIN):
                rows = slice(row, row + GRAIN)
                cent_r, cent_i = (centre[rows, index : index + 1] for centre in centres[pair])
                base_r, base_i = (turned_ref[pair, part, rows, :] for part in range(2))
                for start, table in zip(starts, both_blocks(base_r, base_i, cent_r, cent_i)):
                    for part, value in enumerate(table):
                        place = slice(row + part * FOCAL, row + part * FOCAL + GRAIN)
                        table_refs[pair][place, start : start + BLOCK] = value.astype(jnp.bfloat16)
        for start in (start + step for start in starts for step in range(0, BLOCK, LANES)):
            place = slice(start, start + LANES)
            slopes = near_slopes(width_ref[:, place], power_ref, pairs)
            for ref, slope in zip(slope_refs, slopes):
                ref[0, :, place] = slope[0]
                ref[1, :, place] = slope[1]


def own_grad_kernel(*refs):
    *in_refs, out_ref = refs
    add_grads(in_refs, None, out_ref, 2 * BLOCK)


def last_grad_kernel(*refs):
    *in_refs, total_ref, tile_ref, out_hbm, score_hbm, out_ref, score_ref, sems = refs
    own_cols = out_ref.shape[1]
    core = lax.axis_index("wave")
    for pair in range(score_ref.shape[0]):
        score_ref[pair] = jnp.sum(tile_ref[pair, :1, :1])
    moves = [pltpu.make_async_copy(score_ref, score_hbm, sems.at[own_cols // (2 * BLOCK)])]
    moves[0].start()

    def send(start, total):
        size = total.shape[1]
        place = pl.multiple_of(jnp.where(core == 1, start, own_cols - size - start), size)
        place = pl.ds(place, size)
        out_ref[:, place] = jnp.where(core == 1, total, turn_round(total))
        index = start // size
        moves.append(pltpu.make_async_copy(out_ref.at[:, place], out_hbm.at[:, place], sems.at[index]))
        moves[-1].start()

    add_grads(in_refs, total_ref, out_ref, 2 * BLOCK, send)
    for move in moves:
        move.wait()


def add_grads(in_refs, total_ref, out_ref, size, send=None):
    back_ref, *in_refs = in_refs
    pairs = len(in_refs) // 2
    table_refs, slope_refs = in_refs[:pairs], in_refs[pairs:]
    rows_dev, own_cols = out_ref.shape
    core = lax.axis_index("wave")
    lefts = []
    for pair in range(pairs):
        lane = 2 * pair * FOCAL
        real, imag = back_ref[:, lane : lane + FOCAL], back_ref[:, lane + FOCAL : lane + 2 * FOCAL]
        above = jnp.where(core == 1, imag, -imag)
        below = jnp.where(core == 1, -real, real)
        lefts.append(
            jnp.concatenate(
                [jnp.concatenate([real, above], axis=1), jnp.concatenate([imag, below], axis=1)], axis=0
            )
        )
    for start in range(0, own_cols, size):
        place = slice(start, start + size)
        total = jnp.zeros((rows_dev, size), jnp.float32) if total_ref is None else total_ref[:, place]
        for left, table_ref, slope_ref in zip(lefts, table_refs, slope_refs):
            grad = jnp.dot(left, table_ref[:, place], preferred_element_type=jnp.float32)
            total += grad[:rows_dev] * slope_ref[0, :, place]
            total += grad[rows_dev:] * slope_ref[1, :, place]
        if send is None:
            out_ref[:, place] = total
        else:
            send(start, total)


VMEM = pl.BlockSpec(memory_space=pltpu.VMEM)
SMEM = pl.BlockSpec(memory_space=pltpu.SMEM)
ANY = pl.BlockSpec(memory_space=pl.ANY)
HBM = pl.BlockSpec(memory_space=pltpu.HBM)


def call(kernel, name, outs, in_specs, out_specs, scratch, flops, moved):
    return pl.pallas_call(
        kernel,
        name=name,
        out_shape=outs,
        in_specs=in_specs,
        out_specs=out_specs,
        scratch_shapes=scratch,
        cost_estimate=pl.CostEstimate(flops=flops, bytes_accessed=moved, transcendentals=0),
        compiler_params=pltpu.CompilerParams(vmem_limit_bytes=VMEM_LIMIT),
    )


def on_device(widths, coef_table, wave_ids, angle_ids, targets):
    rows_dev, cols = widths.shape
    pairs_dev = wave_ids.shape[0]
    peers = lax.axis_size("aperture")
    copies = lax.axis_size("wave")
    rows = rows_dev * peers
    pairs = pairs_dev * copies
    own_cols = cols // copies
    lanes = 2 * pairs_dev * FOCAL
    f32, bf16 = jnp.float32, jnp.bfloat16
    shape = jax.ShapeDtypeStruct

    def in_hbm(value):
        return pltpu.with_memory_space_constraint(value, pltpu.HBM)

    def exchange(value, step):
        return lax.ppermute(value, "aperture", [(index, index ^ step) for index in range(peers)])

    def to_core(value):
        return lax.ppermute(value, "wave", [(index, (index + 1) % copies) for index in range(copies)])

    waves = [
        pltpu.VMEM((pairs_dev, 2, BLOCK, FOCAL), f32),
        pltpu.VMEM((pairs_dev, 2, 8, FOCAL), f32),
    ]
    mine, info, own = call(
        forward_kernel, "forward",
        (
            shape((rows_dev, lanes), bf16),
            shape((pairs_dev, INFO_ROWS, FOCAL), f32), shape((rows_dev, own_cols), f32),
        ),
        [HBM] * 5, (VMEM,) * 3,
        [
            pltpu.SMEM(wave_ids.shape, jnp.int32),
            pltpu.SMEM(angle_ids.shape, jnp.int32),
            pltpu.SMEM(targets.shape, jnp.int32),
            pltpu.VMEM(coef_table.shape[::-1], f32),
            pltpu.VMEM(widths.shape, f32),
            *waves,
            pltpu.VMEM((pairs_dev, 2 * TERMS, SUBLANES, LANES), f32),
            pltpu.VMEM((pairs_dev, 4 * rows_dev, own_cols), bf16),
            pltpu.VMEM((pairs_dev, own_cols, 2 * FOCAL), bf16),
            pltpu.VMEM((pairs_dev, 4 * rows_dev, 2 * FOCAL), f32),
            pltpu.SemaphoreType.DMA((5,)),
        ],
        10**9, 10**7,
    )(*(in_hbm(value) for value in (wave_ids, angle_ids, targets, coef_table.T, widths)))
    far_info = to_core(info)

    tall, flat, spots, gains = call(
        row_kernel, "row_tables",
        (
            shape((pairs_dev, 2 * FOCAL, rows), bf16), shape((pairs_dev, rows_dev, 2 * FOCAL), bf16),
            shape((pairs_dev, FOCAL, FOCAL), f32), shape((pairs_dev, 8, 128), f32),
        ),
        [VMEM], (VMEM,) * 4, [], 10**8, 10**6,
    )(info)
    if peers <= DIRECT:
        length = peers // 2

        def rotate(value, turn):
            return lax.ppermute(
                value, "aperture", [(2 * z + x, 2 * ((z + turn) % length) + x) for z in range(length) for x in range(2)]
            )

        got = [rotate(mine, turn) for turn in range(1, length)]
        near = exchange(mine, 1)
        got[0], flat = lax.optimization_barrier((got[0], flat))
        joined = call(join_kernel, "join", shape(((length - 2) * rows_dev, lanes), bf16),
                      [VMEM] * (length - 2), VMEM, [], 10**6, 10**6)(*got[:-1])
        sections = [mine, near, joined, got[-1], exchange(joined, 1), exchange(got[-1], 1)]
        turns = list(range(1, length))
        steps = [(0, 0), (0, 1), *((turn, 0) for turn in turns), *((turn, 1) for turn in turns)]
        after = [near, joined, got[-1]]
    else:
        blocks = jnp.tile(mine[None], (peers, 1, 1))
        blocks = lax.all_to_all(blocks, "aperture", 0, 0, tiled=True)
        sections, steps, after = [blocks.reshape(rows, lanes)], None, []
    outs = [shape((2 * FOCAL, own_cols), bf16)] * pairs + [shape((2, rows_dev, own_cols), f32)] * pairs
    made = call(
        functools.partial(table_kernel, math.sqrt(rows * cols), cols), "column_tables",
        outs, [VMEM] * 3 + [ANY] * len(after), [VMEM] * len(outs),
        [
            pltpu.VMEM((pairs, 2, BLOCK, FOCAL), f32),
            pltpu.VMEM((pairs, 2, 8, FOCAL), f32),
            pltpu.VMEM((pairs, 2, FOCAL, BLOCK), f32),
            pltpu.VMEM((pairs, 2 * TERMS, SUBLANES, LANES), f32),
        ],
        30 * 10**8, 30 * 10**6,
    )(info, far_info, own, *after)
    tables, slopes = made[:pairs], made[pairs:]

    back, scores = call(
        functools.partial(focus_kernel, steps), "focus",
        (shape((rows_dev, lanes), bf16), shape((pairs_dev, SUBLANES, LANES), f32)),
        [VMEM] * 4 + [ANY] + [VMEM] * len(sections), (VMEM, VMEM),
        [
            pltpu.VMEM((rows, lanes), bf16),
            pltpu.VMEM((pairs_dev, 2 * FOCAL, 2 * FOCAL), f32),
            pltpu.VMEM((pairs_dev, 2, FOCAL, FOCAL), f32),
            pltpu.VMEM((pairs_dev, 2 * FOCAL, 2 * FOCAL), bf16),
        ],
        10**8, 10**6,
    )(tall, flat, spots, gains, slopes[0], *sections)

    out = shape((rows_dev, own_cols), f32)
    ins = [back, *tables[:pairs_dev], *slopes[:pairs_dev]]
    grad = call(
        own_grad_kernel, "gradient_own", out, [VMEM] * len(ins), VMEM, [], 10**9, 10**7,
    )(*ins)
    ins = [to_core(back), *tables[pairs_dev:], *slopes[pairs_dev:], grad, scores]
    grad, scores = call(
        last_grad_kernel, "gradient_far", (out, shape((pairs_dev,), f32)), [VMEM] * len(ins), (HBM, HBM),
        [
            pltpu.VMEM(out.shape, f32),
            pltpu.SMEM((pairs_dev,), f32),
            pltpu.SemaphoreType.DMA((own_cols // (2 * BLOCK) + 1,)),
        ],
        10**9, 10**7,
    )(*ins)
    return grad, scores


def solution(mesh):
    in_specs = (
        P(("group", "aperture"), None),
        P(),
        P(("group", "wave")),
        P(("group", "wave")),
        P(("group", "wave"), None),
    )
    out_specs = (P(("group", "aperture"), "wave"), P(("group", "wave")))
    return jax.shard_map(
        on_device, mesh=mesh, in_specs=in_specs, out_specs=out_specs, check_vma=False
    )
```

```python
import functools
import itertools
import math

import jax
import jax.numpy as jnp
from jax import lax
from jax.experimental import pallas as pl
from jax.experimental.pallas import tpu as pltpu
from jax.sharding import PartitionSpec as P

FOCAL = 256
SPOT = 4
SHIFT = 32
TERMS = 8
BLOCK = 256
GRAIN = 16
LANES = 128
PIECE = 16
SUBLANES = 8
VMEM_LIMIT = 16 * 1024 * 1024
WAVE_ROW, ANGLE_ROW, AIM_ROW, INFO_ROWS = 16, 17, 18, 24
DIRECT = 16

COS = (
    1.0, -19.7392088015709, 64.93939395773512, -85.45681453397417, 60.24458621302471,
    -26.425616460281425, 7.8991596631575085, -1.6968741456712442, 0.2437618617467591,
)
SIN = (
    6.2831853071792665, -41.34170224019464, 81.60524925425943, -76.70585885700535,
    42.05867547580699, -15.094428387947755, 3.818490079304055, -0.7122771247541972,
    0.09149844789363434,
)


def horner(terms, u):
    value = terms[-1] * u + terms[-2]
    for term in terms[-3::-1]:
        value = value * u + term
    return value


def unit_waves(counts, period):
    half = period // 2
    centred = ((counts + half) & (period - 1)) - half
    t = centred.astype(jnp.float32) * (1.0 / period)
    u = t * t
    return horner(COS, u), -(t * horner(SIN, u))


def iota(shape, axis):
    return lax.broadcasted_iota(jnp.int32, shape, axis)


def pick_coef(table, wave):
    chosen = jnp.where(iota(table.shape, 1) == wave, table, 0.0)
    return jnp.sum(chosen, axis=1, keepdims=True)


def column_freq(info_ref, pair):
    wave = info_ref[pair, WAVE_ROW : WAVE_ROW + 1, :].astype(jnp.int32)
    angle = info_ref[pair, ANGLE_ROW : ANGLE_ROW + 1, :].astype(jnp.int32)
    return (iota((1, FOCAL), 1) - FOCAL // 2 + SHIFT * angle) * (BLOCK + wave)


def fill_base(freq, shift, period, base_ref, centre_ref):
    low_r, low_i = unit_waves(iota((GRAIN, 1), 0) * freq, period)
    steps = BLOCK // GRAIN
    high_r, high_i = unit_waves((iota((steps, 1), 0) * GRAIN - BLOCK // 2 + shift) * freq, period)
    for step in range(steps):
        one_r, one_i = high_r[step : step + 1], high_i[step : step + 1]
        rows = slice(step * GRAIN, (step + 1) * GRAIN)
        base_ref[0, rows, :] = one_r * low_r - one_i * low_i
        base_ref[1, rows, :] = one_r * low_i + one_i * low_r
    count = centre_ref.shape[1]
    cent_r, cent_i = unit_waves((iota((count, 1), 0) * BLOCK + BLOCK // 2) * freq, period)
    centre_ref[0] = cent_r
    centre_ref[1] = cent_i


def power_coefs(coef):
    before, current = [1], [0, 1]
    bases = [before, current]
    for _ in range(2, TERMS):
        doubled = [0] + [2 * term for term in current]
        before, current = current, [a - b for a, b in itertools.zip_longest(doubled, before, fillvalue=0)]
        bases.append(current)
    rows = []
    for part, power in itertools.product(range(2), range(TERMS)):
        row = None
        for order in range(power, TERMS, 2):
            place = part * TERMS + order
            term = coef[place : place + 1] * float(bases[order][power])
            row = term if row is None else row + term
        rows.append(row)
    return jnp.concatenate(rows, axis=0)


def as_tiles(rows):
    return jnp.broadcast_to(rows[:, None, :], (rows.shape[0], SUBLANES, rows.shape[1]))


def split_rows(value):
    return value.reshape(value.shape[0] // SUBLANES, SUBLANES, value.shape[1])


def join_rows(value):
    return value.reshape(value.shape[0] * SUBLANES, value.shape[2])


def near_fields(s, power_ref, pairs):
    s = split_rows(s)
    outs = []
    for pair, part in itertools.product(range(pairs), range(2)):
        row = (part + 1) * TERMS - 1
        value = power_ref[pair, row] * s + power_ref[pair, row - 1]
        for row in range(row - 2, part * TERMS - 1, -1):
            value = value * s + power_ref[pair, row]
        outs.append(join_rows(value))
    return [outs[2 * pair : 2 * pair + 2] for pair in range(pairs)]


def near_slopes(s, power_ref, pairs):
    s = split_rows(s)
    outs = []
    for pair, part in itertools.product(range(pairs), range(2)):
        row = (part + 1) * TERMS - 1
        value = power_ref[pair, row] * s + power_ref[pair, row - 1]
        for row in range(row - 2, part * TERMS, -1):
            value = value * s + power_ref[pair, row]
        outs.append(join_rows(value))
    return [outs[2 * pair : 2 * pair + 2] for pair in range(pairs)]


def turn_round(value):
    rows, cols = value.shape
    order = LANES - 1 - iota((rows, LANES), 1)
    parts = [
        jnp.take_along_axis(value[:, start : start + LANES], order, axis=1)
        for start in range(cols - LANES, -1, -LANES)
    ]
    return jnp.concatenate(parts, axis=1)


def side_pieces(width_ref, core):
    rows, cols = width_ref.shape
    half = cols // 2
    count = half // LANES
    lane = iota((rows, LANES), 1)
    shift = jnp.where(core == 1, 1, LANES - 1)
    edge = jnp.where(core == 1, 0, LANES - 1)

    @functools.cache
    def turned(piece):
        right = width_ref[:, half + piece * LANES : half + (piece + 1) * LANES]
        left = turn_round(width_ref[:, half - (piece + 1) * LANES : half - piece * LANES])
        other = pltpu.roll(jnp.where(core == 1, left, right), shift, 1)
        return jnp.where(core == 1, right, left), other

    def sides(piece):
        own, other = turned(piece)
        beside = jnp.where(core == 1, turned(max(piece - 1, 0))[1], turned(min(piece + 1, count - 1))[1])
        return own, jnp.where(lane == edge, beside, other)

    return sides


def block_starts(cols, index):
    return cols // 2 - (index + 1) * BLOCK, cols // 2 + index * BLOCK


def both_blocks(base_r, base_i, cent_r, cent_i):
    rr, ii = base_r * cent_r, base_i * cent_i
    ri, ir = base_r * cent_i, base_i * cent_r
    return (rr + ii, ir - ri), (rr - ii, ir + ri)


def own_waves(info_ref, pair, cols, base_ref, centre_ref):
    shift = cols // 4 + 1 - lax.axis_index("wave")
    fill_base(column_freq(info_ref, pair), shift, 256 * cols, base_ref, centre_ref)


def forward_kernel(
    wave_hbm, angle_hbm, aim_hbm, coef_hbm, width_hbm, mine_ref, info_ref, own_ref, *refs
):
    pairs = info_ref.shape[0]
    (
        wave_ref, angle_ref, aim_ref, coef_ref, width_ref, base_ref, centre_ref, power_ref, near_ref, table_ref,
        acc_ref, sems,
    ) = refs
    rows_dev, cols = width_ref.shape
    half = cols // 2
    moves = [
        pltpu.make_async_copy(source, target, sems.at[index])
        for index, (source, target) in enumerate((
            (width_hbm, width_ref), (wave_hbm, wave_ref), (angle_hbm, angle_ref),
            (coef_hbm, coef_ref), (aim_hbm, aim_ref),
        ))
    ]
    for move in moves:
        move.start()
    for move in moves[1:]:
        move.wait()
    for pair in range(pairs):
        coef = pick_coef(coef_ref[...], wave_ref[pair])
        coef = jnp.broadcast_to(coef, (WAVE_ROW, FOCAL))
        info_ref[pair, :WAVE_ROW, :] = coef
        power_ref[pair] = as_tiles(power_coefs(coef[:, :LANES]))
        row = iota((INFO_ROWS - WAVE_ROW, FOCAL), 0) + WAVE_ROW
        ids = jnp.where(row == WAVE_ROW, wave_ref[pair], 0)
        ids = jnp.where(row == ANGLE_ROW, angle_ref[pair], ids)
        ids = jnp.where(row == AIM_ROW, aim_ref[pair, 0], ids)
        ids = jnp.where(row == AIM_ROW + 1, aim_ref[pair, 1], ids)
        info_ref[pair, WAVE_ROW:, :] = ids.astype(jnp.float32)
    for pair in range(pairs):
        own_waves(info_ref, pair, cols, base_ref.at[pair], centre_ref.at[pair])
    core = lax.axis_index("wave")
    moves[0].wait()
    sides = side_pieces(width_ref, core)
    alone = jnp.where(core == 1, 0, half)
    column = width_ref[:, pl.ds(pl.multiple_of(alone, LANES), LANES)]
    columns = near_fields(column, power_ref, pairs)
    void = jnp.where(core == 1, 0, half - 1)
    for index in range(half // (2 * BLOCK)):
        starts = block_starts(half, index)
        for start in (start + step for start in starts for step in range(0, BLOCK, LANES)):
            both = sides(start // LANES)
            own_ref[:, start : start + LANES] = both[0]
            for side, widths in enumerate(both):
                outs = near_fields(widths, power_ref, pairs)
                if side and start in (0, half - LANES):
                    keep = iota((rows_dev, LANES), 1) + start != void
                    outs = [[jnp.where(keep, part, 0.0) for part in out] for out in outs]
                for pair, part in ((pair, part) for pair in range(pairs) for part in range(2)):
                    row = (2 * side + part) * rows_dev
                    near_ref[pair, row : row + rows_dev, start : start + LANES] = outs[pair][part].astype(jnp.bfloat16)
        for pair in range(pairs):
            cent_r, cent_i = (centre_ref[pair, part, index : index + 1, :] for part in range(2))
            for row in range(0, BLOCK, GRAIN):
                base_r, base_i = (base_ref[pair, part, row : row + GRAIN, :] for part in range(2))
                for start, table in zip(starts, both_blocks(base_r, base_i, cent_r, cent_i)):
                    rows = slice(start + row, start + row + GRAIN)
                    table_ref[pair, rows, :FOCAL] = table[0].astype(jnp.bfloat16)
                    table_ref[pair, rows, FOCAL:] = table[1].astype(jnp.bfloat16)
            product = jnp.dot(
                jnp.concatenate([near_ref[pair, :, start : start + BLOCK] for start in starts], axis=1),
                jnp.concatenate([table_ref[pair, start : start + BLOCK, :] for start in starts], axis=0),
                preferred_element_type=jnp.float32,
            )
            acc_ref[pair] = product if index == 0 else acc_ref[pair] + product
    for pair in range(pairs):
        acc = [acc_ref[pair, part * rows_dev : (part + 1) * rows_dev, :] for part in range(4)]
        (own_rr, own_ri), (own_ir, own_ii), (far_rr, far_ri), (far_ir, far_ii) = (
            (part[:, :FOCAL], part[:, FOCAL:]) for part in acc
        )
        cross_r, cross_i = far_ii - own_ii, own_ri - far_ri
        real = own_rr + far_rr + jnp.where(core == 1, cross_r, -cross_r)
        imag = own_ir + far_ir + jnp.where(core == 1, cross_i, -cross_i)
        near_r, near_i = (part[:, :1].astype(jnp.bfloat16).astype(jnp.float32) for part in columns[pair])
        wave_r, wave_i = (
            part.astype(jnp.bfloat16).astype(jnp.float32)
            for part in unit_waves((alone - half) * column_freq(info_ref, pair), 256 * cols)
        )
        real = real + (near_r * wave_r - near_i * wave_i)
        imag = imag + (near_r * wave_i + near_i * wave_r)
        for part, value in enumerate((real, imag)):
            lane = (2 * pair + part) * FOCAL
            mine_ref[:, lane : lane + FOCAL] = value.astype(jnp.bfloat16)


def spot_rows(info_ref, pair, first):
    aims = [info_ref[pair, row : row + 1, :] for row in (AIM_ROW, AIM_ROW + 1)]
    rows_off = (iota((PIECE, FOCAL), 0) + first).astype(jnp.float32) - aims[0]
    cols_off = iota((1, FOCAL), 1).astype(jnp.float32) - aims[1]
    return jnp.exp(-(rows_off * rows_off + cols_off * cols_off) / (2.0 * SPOT * SPOT))


def total_of(value):
    return jnp.sum(jnp.sum(value, axis=0, keepdims=True), axis=1, keepdims=True)


def row_kernel(info_ref, tall_ref, flat_ref, spot_ref, gain_ref):
    pairs, _, rows = tall_ref.shape
    rows_dev = flat_ref.shape[1]
    period = 256 * rows
    size = min(rows, FOCAL)
    for pair in range(pairs):
        wave = info_ref[pair, WAVE_ROW : WAVE_ROW + 1, :].astype(jnp.int32) + BLOCK
        focal = (iota((FOCAL, 1), 0) - FOCAL // 2) * wave

        def step(index, carry):
            start = pl.multiple_of(index * size, size)
            place = iota((1, size), 1) + (start - rows // 2)
            for row in range(0, FOCAL, PIECE):
                real, imag = unit_waves(focal[row : row + PIECE, :size] * place, period)
                tall_ref[pair, row : row + PIECE, pl.ds(start, size)] = real.astype(jnp.bfloat16)
                row += FOCAL
                tall_ref[pair, row : row + PIECE, pl.ds(start, size)] = imag.astype(jnp.bfloat16)
            return carry

        if rows == size:
            step(0, 0)
        else:
            lax.fori_loop(0, rows // size, step, 0)
        focal = (iota((1, FOCAL), 1) - FOCAL // 2) * wave
        first = lax.axis_index("aperture") * rows_dev - rows // 2
        real, imag = unit_waves((iota((rows_dev, 1), 0) + first) * focal, period)
        flat_ref[pair, :, :FOCAL] = real.astype(jnp.bfloat16)
        flat_ref[pair, :, FOCAL:] = imag.astype(jnp.bfloat16)
        total = jnp.zeros((PIECE, FOCAL), jnp.float32)
        for row in range(0, FOCAL, PIECE):
            spot = spot_rows(info_ref, pair, row)
            spot_ref[pair, row : row + PIECE, :] = spot
            total += spot
        gain_ref[pair] = jnp.broadcast_to(FOCAL * FOCAL / total_of(total), gain_ref.shape[1:])


def join_kernel(*refs):
    *in_refs, out_ref = refs
    count = in_refs[0].shape[0]
    for index, ref in enumerate(in_refs):
        out_ref[index * count : (index + 1) * count, :] = ref[...]


def focus_kernel(steps, tall_ref, flat_ref, spot_ref, gain_ref, after_ref, *refs):
    del after_ref
    *sect_refs, back_ref, score_ref, rows_ref, mixed_ref, field_ref, stack_ref = refs
    pairs = tall_ref.shape[0]
    rows_dev = back_ref.shape[0]
    if steps is None:
        rows_ref = sect_refs[0]
    else:
        me = lax.axis_index("aperture")
        blocks = [
            ref[index * rows_dev : (index + 1) * rows_dev, :]
            for ref in sect_refs
            for index in range(ref.shape[0] // rows_dev)
        ]
        for step, block in zip(steps, blocks, strict=True):
            start = pl.multiple_of((me ^ step) * rows_dev, rows_dev)
            rows_ref[pl.ds(start, rows_dev), :] = block
    for pair in range(pairs):
        lane = 2 * pair * FOCAL
        section = rows_ref[:, lane : lane + 2 * FOCAL]
        mixed_ref[pair] = jnp.dot(tall_ref[pair], section, preferred_element_type=jnp.float32)
    pieces = [slice(row, row + PIECE) for row in range(0, FOCAL, PIECE)]
    sums = []
    for pair in range(pairs):
        totals = [jnp.zeros((PIECE, FOCAL), jnp.float32) for _ in range(2)]
        for rows in pieces:
            lower = slice(rows.start + FOCAL, rows.stop + FOCAL)
            real = mixed_ref[pair, rows, :FOCAL] - mixed_ref[pair, lower, FOCAL:]
            imag = mixed_ref[pair, rows, FOCAL:] + mixed_ref[pair, lower, :FOCAL]
            field_ref[pair, 0, rows, :] = real
            field_ref[pair, 1, rows, :] = imag
            power = real * real + imag * imag
            totals = [totals[0] + spot_ref[pair, rows, :] * power, totals[1] + power]
        sums.append((total_of(totals[0]), total_of(totals[1]) + 1e-06))
    for pair, (spot_power, all_power) in enumerate(sums):
        ratio = spot_power / all_power
        gain = gain_ref[pair, :1, :1]
        score_ref[pair] = jnp.broadcast_to(ratio * gain, score_ref.shape[1:])
        scale = gain * 2.0 / all_power
        for rows in pieces:
            lower = slice(rows.start + FOCAL, rows.stop + FOCAL)
            weight = scale * (spot_ref[pair, rows, :] - ratio)
            real = (weight * field_ref[pair, 0, rows, :]).astype(jnp.bfloat16)
            imag = (weight * field_ref[pair, 1, rows, :]).astype(jnp.bfloat16)
            stack_ref[pair, rows, :FOCAL] = real
            stack_ref[pair, rows, FOCAL:] = imag
            stack_ref[pair, lower, :FOCAL] = imag
            stack_ref[pair, lower, FOCAL:] = -real
        back = jnp.dot(flat_ref[pair], stack_ref[pair], preferred_element_type=jnp.float32)
        lane = 2 * pair * FOCAL
        back_ref[:, lane : lane + 2 * FOCAL] = back.astype(jnp.bfloat16)


def table_kernel(scale, cols, info_ref, far_info_ref, width_ref, *refs):
    *out_refs, base_ref, centre_ref, turned_ref, power_ref = refs
    pairs = power_ref.shape[0]
    out_refs = out_refs[-2 * pairs :]
    table_refs, slope_refs = out_refs[:pairs], out_refs[pairs:]
    own_cols = width_ref.shape[1]
    sources = [(ref, pair) for ref in (info_ref, far_info_ref) for pair in range(pairs // 2)]
    centres = []
    for pair, (ref, source) in enumerate(sources):
        power = power_coefs(ref[source, : 2 * TERMS, :LANES])
        power_ref[pair] = as_tiles(power * ((iota(power.shape, 0) % TERMS).astype(jnp.float32) * scale))
        own_waves(ref, source, cols, base_ref.at[pair], centre_ref.at[pair])
        for part, row, lane in itertools.product(range(2), range(0, BLOCK, LANES), range(0, FOCAL, LANES)):
            tile = base_ref[pair, part, row : row + LANES, lane : lane + LANES]
            turned_ref[pair, part, lane : lane + LANES, row : row + LANES] = tile.T
        centres.append([centre_ref[pair, part].T for part in range(2)])
    for index in range(own_cols // (2 * BLOCK)):
        starts = block_starts(own_cols, index)
        for pair in range(pairs):
            for row in range(0, FOCAL, GRAIN):
                rows = slice(row, row + GRAIN)
                cent_r, cent_i = (centre[rows, index : index + 1] for centre in centres[pair])
                base_r, base_i = (turned_ref[pair, part, rows, :] for part in range(2))
                for start, table in zip(starts, both_blocks(base_r, base_i, cent_r, cent_i)):
                    for part, value in enumerate(table):
                        place = slice(row + part * FOCAL, row + part * FOCAL + GRAIN)
                        table_refs[pair][place, start : start + BLOCK] = value.astype(jnp.bfloat16)
        for start in (start + step for start in starts for step in range(0, BLOCK, LANES)):
            place = slice(start, start + LANES)
            slopes = near_slopes(width_ref[:, place], power_ref, pairs)
            for ref, slope in zip(slope_refs, slopes):
                ref[0, :, place] = slope[0]
                ref[1, :, place] = slope[1]


def own_grad_kernel(*refs):
    *in_refs, out_ref = refs
    add_grads(in_refs, None, out_ref, 2 * BLOCK)


def last_grad_kernel(*refs):
    *in_refs, total_ref, tile_ref, out_hbm, score_hbm, out_ref, score_ref, sems = refs
    own_cols = out_ref.shape[1]
    core = lax.axis_index("wave")
    for pair in range(score_ref.shape[0]):
        score_ref[pair] = jnp.sum(tile_ref[pair, :1, :1])
    moves = [pltpu.make_async_copy(score_ref, score_hbm, sems.at[own_cols // (2 * BLOCK)])]
    moves[0].start()

    def send(start, total):
        size = total.shape[1]
        place = pl.multiple_of(jnp.where(core == 1, start, own_cols - size - start), size)
        place = pl.ds(place, size)
        out_ref[:, place] = jnp.where(core == 1, total, turn_round(total))
        index = start // size
        moves.append(pltpu.make_async_copy(out_ref.at[:, place], out_hbm.at[:, place], sems.at[index]))
        moves[-1].start()

    add_grads(in_refs, total_ref, out_ref, 2 * BLOCK, send)
    for move in moves:
        move.wait()


def add_grads(in_refs, total_ref, out_ref, size, send=None):
    back_ref, *in_refs = in_refs
    pairs = len(in_refs) // 2
    table_refs, slope_refs = in_refs[:pairs], in_refs[pairs:]
    rows_dev, own_cols = out_ref.shape
    core = lax.axis_index("wave")
    lefts = []
    for pair in range(pairs):
        lane = 2 * pair * FOCAL
        real, imag = back_ref[:, lane : lane + FOCAL], back_ref[:, lane + FOCAL : lane + 2 * FOCAL]
        above = jnp.where(core == 1, imag, -imag)
        below = jnp.where(core == 1, -real, real)
        lefts.append(
            jnp.concatenate(
                [jnp.concatenate([real, above], axis=1), jnp.concatenate([imag, below], axis=1)], axis=0
            )
        )
    for start in range(0, own_cols, size):
        place = slice(start, start + size)
        total = jnp.zeros((rows_dev, size), jnp.float32) if total_ref is None else total_ref[:, place]
        for left, table_ref, slope_ref in zip(lefts, table_refs, slope_refs):
            grad = jnp.dot(left, table_ref[:, place], preferred_element_type=jnp.float32)
            total += grad[:rows_dev] * slope_ref[0, :, place]
            total += grad[rows_dev:] * slope_ref[1, :, place]
        if send is None:
            out_ref[:, place] = total
        else:
            send(start, total)


VMEM = pl.BlockSpec(memory_space=pltpu.VMEM)
SMEM = pl.BlockSpec(memory_space=pltpu.SMEM)
ANY = pl.BlockSpec(memory_space=pl.ANY)
HBM = pl.BlockSpec(memory_space=pltpu.HBM)


def call(kernel, name, outs, in_specs, out_specs, scratch, flops, moved):
    return pl.pallas_call(
        kernel,
        name=name,
        out_shape=outs,
        in_specs=in_specs,
        out_specs=out_specs,
        scratch_shapes=scratch,
        cost_estimate=pl.CostEstimate(flops=flops, bytes_accessed=moved, transcendentals=0),
        compiler_params=pltpu.CompilerParams(vmem_limit_bytes=VMEM_LIMIT),
    )


def on_device(widths, coef_table, wave_ids, angle_ids, targets):
    rows_dev, cols = widths.shape
    pairs_dev = wave_ids.shape[0]
    peers = lax.axis_size("aperture")
    copies = lax.axis_size("wave")
    rows = rows_dev * peers
    pairs = pairs_dev * copies
    own_cols = cols // copies
    lanes = 2 * pairs_dev * FOCAL
    f32, bf16 = jnp.float32, jnp.bfloat16
    shape = jax.ShapeDtypeStruct

    def in_hbm(value):
        return pltpu.with_memory_space_constraint(value, pltpu.HBM)

    def exchange(value, step):
        return lax.ppermute(value, "aperture", [(index, index ^ step) for index in range(peers)])

    def to_core(value):
        return lax.ppermute(value, "wave", [(index, (index + 1) % copies) for index in range(copies)])

    waves = [
        pltpu.VMEM((pairs_dev, 2, BLOCK, FOCAL), f32),
        pltpu.VMEM((pairs_dev, 2, 8, FOCAL), f32),
    ]
    mine, info, own = call(
        forward_kernel, "forward",
        (
            shape((rows_dev, lanes), bf16),
            shape((pairs_dev, INFO_ROWS, FOCAL), f32), shape((rows_dev, own_cols), f32),
        ),
        [HBM] * 5, (VMEM,) * 3,
        [
            pltpu.SMEM(wave_ids.shape, jnp.int32),
            pltpu.SMEM(angle_ids.shape, jnp.int32),
            pltpu.SMEM(targets.shape, jnp.int32),
            pltpu.VMEM(coef_table.shape[::-1], f32),
            pltpu.VMEM(widths.shape, f32),
            *waves,
            pltpu.VMEM((pairs_dev, 2 * TERMS, SUBLANES, LANES), f32),
            pltpu.VMEM((pairs_dev, 4 * rows_dev, own_cols), bf16),
            pltpu.VMEM((pairs_dev, own_cols, 2 * FOCAL), bf16),
            pltpu.VMEM((pairs_dev, 4 * rows_dev, 2 * FOCAL), f32),
            pltpu.SemaphoreType.DMA((5,)),
        ],
        10**9, 10**7,
    )(*(in_hbm(value) for value in (wave_ids, angle_ids, targets, coef_table.T, widths)))
    far_info = to_core(info)

    tall, flat, spots, gains = call(
        row_kernel, "row_tables",
        (
            shape((pairs_dev, 2 * FOCAL, rows), bf16), shape((pairs_dev, rows_dev, 2 * FOCAL), bf16),
            shape((pairs_dev, FOCAL, FOCAL), f32), shape((pairs_dev, 8, 128), f32),
        ),
        [VMEM], (VMEM,) * 4, [], 10**8, 10**6,
    )(info)
    if peers <= DIRECT:
        steps = list(range(peers - 2, 0, -2))
        got = [exchange(mine, step) for step in steps]
        near = exchange(mine, 1)
        first, flat = lax.optimization_barrier((got[0], flat))
        joined = call(join_kernel, "join", shape(((len(steps) - 1) * rows_dev, lanes), bf16),
                      [VMEM] * (len(steps) - 1), VMEM, [], 10**6, 10**6)(*got[1:])
        sections = [mine, near, first, joined, exchange(first, 1), exchange(joined, 1)]
        steps = [0, 1, *steps, *(step ^ 1 for step in steps)]
        after = [near, joined]
    else:
        blocks = jnp.tile(mine[None], (peers, 1, 1))
        blocks = lax.all_to_all(blocks, "aperture", 0, 0, tiled=True)
        sections, steps, after = [blocks.reshape(rows, lanes)], None, []
    outs = [shape((2 * FOCAL, own_cols), bf16)] * pairs + [shape((2, rows_dev, own_cols), f32)] * pairs
    made = call(
        functools.partial(table_kernel, math.sqrt(rows * cols), cols), "column_tables",
        outs, [VMEM] * 3 + [ANY] * len(after), [VMEM] * len(outs),
        [
            pltpu.VMEM((pairs, 2, BLOCK, FOCAL), f32),
            pltpu.VMEM((pairs, 2, 8, FOCAL), f32),
            pltpu.VMEM((pairs, 2, FOCAL, BLOCK), f32),
            pltpu.VMEM((pairs, 2 * TERMS, SUBLANES, LANES), f32),
        ],
        30 * 10**8, 30 * 10**6,
    )(info, far_info, own, *after)
    tables, slopes = made[:pairs], made[pairs:]

    back, scores = call(
        functools.partial(focus_kernel, steps), "focus",
        (shape((rows_dev, lanes), bf16), shape((pairs_dev, SUBLANES, LANES), f32)),
        [VMEM] * 4 + [ANY] + [VMEM] * len(sections), (VMEM, VMEM),
        [
            pltpu.VMEM((rows, lanes), bf16),
            pltpu.VMEM((pairs_dev, 2 * FOCAL, 2 * FOCAL), f32),
            pltpu.VMEM((pairs_dev, 2, FOCAL, FOCAL), f32),
            pltpu.VMEM((pairs_dev, 2 * FOCAL, 2 * FOCAL), bf16),
        ],
        10**8, 10**6,
    )(tall, flat, spots, gains, slopes[0], *sections)

    out = shape((rows_dev, own_cols), f32)
    ins = [back, *tables[:pairs_dev], *slopes[:pairs_dev]]
    grad = call(
        own_grad_kernel, "gradient_own", out, [VMEM] * len(ins), VMEM, [], 10**9, 10**7,
    )(*ins)
    ins = [to_core(back), *tables[pairs_dev:], *slopes[pairs_dev:], grad, scores]
    grad, scores = call(
        last_grad_kernel, "gradient_far", (out, shape((pairs_dev,), f32)), [VMEM] * len(ins), (HBM, HBM),
        [
            pltpu.VMEM(out.shape, f32),
            pltpu.SMEM((pairs_dev,), f32),
            pltpu.SemaphoreType.DMA((own_cols // (2 * BLOCK) + 1,)),
        ],
        10**9, 10**7,
    )(*ins)
    return grad, scores


def solution(mesh):
    in_specs = (
        P(("group", "aperture"), None),
        P(),
        P(("group", "wave")),
        P(("group", "wave")),
        P(("group", "wave"), None),
    )
    out_specs = (P(("group", "aperture"), "wave"), P(("group", "wave")))
    return jax.shard_map(
        on_device, mesh=mesh, in_specs=in_specs, out_specs=out_specs, check_vma=False
    )
```

```python
import functools
import itertools
import math

import jax
import jax.numpy as jnp
from jax import lax
from jax.experimental import pallas as pl
from jax.experimental.pallas import tpu as pltpu
from jax.sharding import PartitionSpec as P

FOCAL = 256
SPOT = 4
SHIFT = 32
TERMS = 8
BLOCK = 256
GRAIN = 16
LANES = 128
PIECE = 16
SUBLANES = 8
VMEM_LIMIT = 16 * 1024 * 1024
WAVE_ROW, ANGLE_ROW, AIM_ROW, INFO_ROWS = 16, 17, 18, 24
DIRECT = 16

COS = (
    1.0, -19.7392088015709, 64.93939395773512, -85.45681453397417, 60.24458621302471,
    -26.425616460281425, 7.8991596631575085, -1.6968741456712442, 0.2437618617467591,
)
SIN = (
    6.2831853071792665, -41.34170224019464, 81.60524925425943, -76.70585885700535,
    42.05867547580699, -15.094428387947755, 3.818490079304055, -0.7122771247541972,
    0.09149844789363434,
)


def horner(terms, u):
    value = terms[-1] * u + terms[-2]
    for term in terms[-3::-1]:
        value = value * u + term
    return value


def unit_waves(counts, period):
    half = period // 2
    centred = ((counts + half) & (period - 1)) - half
    t = centred.astype(jnp.float32) * (1.0 / period)
    u = t * t
    return horner(COS, u), -(t * horner(SIN, u))


def iota(shape, axis):
    return lax.broadcasted_iota(jnp.int32, shape, axis)


def pick_coef(table, wave):
    chosen = jnp.where(iota(table.shape, 1) == wave, table, 0.0)
    return jnp.sum(chosen, axis=1, keepdims=True)


def column_freq(info_ref, pair):
    wave = info_ref[pair, WAVE_ROW : WAVE_ROW + 1, :].astype(jnp.int32)
    angle = info_ref[pair, ANGLE_ROW : ANGLE_ROW + 1, :].astype(jnp.int32)
    return (iota((1, FOCAL), 1) - FOCAL // 2 + SHIFT * angle) * (BLOCK + wave)


def fill_base(freq, shift, period, base_ref, centre_ref):
    low_r, low_i = unit_waves(iota((GRAIN, 1), 0) * freq, period)
    steps = BLOCK // GRAIN
    high_r, high_i = unit_waves((iota((steps, 1), 0) * GRAIN - BLOCK // 2 + shift) * freq, period)
    for step in range(steps):
        one_r, one_i = high_r[step : step + 1], high_i[step : step + 1]
        rows = slice(step * GRAIN, (step + 1) * GRAIN)
        base_ref[0, rows, :] = one_r * low_r - one_i * low_i
        base_ref[1, rows, :] = one_r * low_i + one_i * low_r
    count = centre_ref.shape[1]
    cent_r, cent_i = unit_waves((iota((count, 1), 0) * BLOCK + BLOCK // 2) * freq, period)
    centre_ref[0] = cent_r
    centre_ref[1] = cent_i


def power_coefs(coef):
    before, current = [1], [0, 1]
    bases = [before, current]
    for _ in range(2, TERMS):
        doubled = [0] + [2 * term for term in current]
        before, current = current, [a - b for a, b in itertools.zip_longest(doubled, before, fillvalue=0)]
        bases.append(current)
    rows = []
    for part, power in itertools.product(range(2), range(TERMS)):
        row = None
        for order in range(power, TERMS, 2):
            place = part * TERMS + order
            term = coef[place : place + 1] * float(bases[order][power])
            row = term if row is None else row + term
        rows.append(row)
    return jnp.concatenate(rows, axis=0)


def as_tiles(rows):
    return jnp.broadcast_to(rows[:, None, :], (rows.shape[0], SUBLANES, rows.shape[1]))


def split_rows(value):
    return value.reshape(value.shape[0] // SUBLANES, SUBLANES, value.shape[1])


def join_rows(value):
    return value.reshape(value.shape[0] * SUBLANES, value.shape[2])


def side_by_side(s, power_ref, pairs, lowest):
    s = split_rows(s)
    firsts = [(pair, part * TERMS) for pair, part in itertools.product(range(pairs), range(2))]
    values = [power_ref[pair, first + TERMS - 1] * s for pair, first in firsts]
    for power in range(TERMS - 2, lowest - 1, -1):
        values = [value + power_ref[pair, first + power] for value, (pair, first) in zip(values, firsts)]
        if power > lowest:
            values = [value * s for value in values]
    values = [join_rows(value) for value in values]
    return [values[2 * pair : 2 * pair + 2] for pair in range(pairs)]


def near_fields(s, power_ref, pairs):
    return side_by_side(s, power_ref, pairs, 0)


def near_slopes(s, power_ref, pairs):
    return side_by_side(s, power_ref, pairs, 1)


def turn_round(value):
    rows, cols = value.shape
    order = LANES - 1 - iota((rows, LANES), 1)
    parts = [
        jnp.take_along_axis(value[:, start : start + LANES], order, axis=1)
        for start in range(cols - LANES, -1, -LANES)
    ]
    return jnp.concatenate(parts, axis=1)


def side_pieces(width_ref, core):
    rows, cols = width_ref.shape
    half = cols // 2
    count = half // LANES
    lane = iota((rows, LANES), 1)
    shift = jnp.where(core == 1, 1, LANES - 1)
    edge = jnp.where(core == 1, 0, LANES - 1)

    @functools.cache
    def turned(piece):
        right = width_ref[:, half + piece * LANES : half + (piece + 1) * LANES]
        left = turn_round(width_ref[:, half - (piece + 1) * LANES : half - piece * LANES])
        other = pltpu.roll(jnp.where(core == 1, left, right), shift, 1)
        return jnp.where(core == 1, right, left), other

    def sides(piece):
        own, other = turned(piece)
        beside = jnp.where(core == 1, turned(max(piece - 1, 0))[1], turned(min(piece + 1, count - 1))[1])
        return own, jnp.where(lane == edge, beside, other)

    return sides


def block_starts(cols, index):
    return cols // 2 - (index + 1) * BLOCK, cols // 2 + index * BLOCK


def both_blocks(base_r, base_i, cent_r, cent_i):
    rr, ii = base_r * cent_r, base_i * cent_i
    ri, ir = base_r * cent_i, base_i * cent_r
    return (rr + ii, ir - ri), (rr - ii, ir + ri)


def own_waves(info_ref, pair, cols, base_ref, centre_ref):
    shift = cols // 4 + 1 - lax.axis_index("wave")
    fill_base(column_freq(info_ref, pair), shift, 256 * cols, base_ref, centre_ref)


def forward_kernel(
    wave_hbm, angle_hbm, aim_hbm, coef_hbm, width_hbm, mine_ref, info_ref, own_ref, *refs
):
    pairs = info_ref.shape[0]
    (
        wave_ref, angle_ref, aim_ref, coef_ref, width_ref, base_ref, centre_ref, power_ref, near_ref, table_ref,
        acc_ref, sems,
    ) = refs
    rows_dev, cols = width_ref.shape
    half = cols // 2
    moves = [
        pltpu.make_async_copy(source, target, sems.at[index])
        for index, (source, target) in enumerate((
            (width_hbm, width_ref), (wave_hbm, wave_ref), (angle_hbm, angle_ref),
            (coef_hbm, coef_ref), (aim_hbm, aim_ref),
        ))
    ]
    for move in moves:
        move.start()
    for move in moves[1:]:
        move.wait()
    for pair in range(pairs):
        coef = pick_coef(coef_ref[...], wave_ref[pair])
        coef = jnp.broadcast_to(coef, (WAVE_ROW, FOCAL))
        info_ref[pair, :WAVE_ROW, :] = coef
        power_ref[pair] = as_tiles(power_coefs(coef[:, :LANES]))
        row = iota((INFO_ROWS - WAVE_ROW, FOCAL), 0) + WAVE_ROW
        ids = jnp.where(row == WAVE_ROW, wave_ref[pair], 0)
        ids = jnp.where(row == ANGLE_ROW, angle_ref[pair], ids)
        ids = jnp.where(row == AIM_ROW, aim_ref[pair, 0], ids)
        ids = jnp.where(row == AIM_ROW + 1, aim_ref[pair, 1], ids)
        info_ref[pair, WAVE_ROW:, :] = ids.astype(jnp.float32)
    for pair in range(pairs):
        own_waves(info_ref, pair, cols, base_ref.at[pair], centre_ref.at[pair])
    core = lax.axis_index("wave")
    moves[0].wait()
    sides = side_pieces(width_ref, core)
    alone = jnp.where(core == 1, 0, half)
    column = width_ref[:, pl.ds(pl.multiple_of(alone, LANES), LANES)]
    columns = near_fields(column, power_ref, pairs)
    void = jnp.where(core == 1, 0, half - 1)
    for index in range(half // (2 * BLOCK)):
        starts = block_starts(half, index)
        for start in (start + step for start in starts for step in range(0, BLOCK, LANES)):
            both = sides(start // LANES)
            own_ref[:, start : start + LANES] = both[0]
            for side, widths in enumerate(both):
                outs = near_fields(widths, power_ref, pairs)
                if side and start in (0, half - LANES):
                    keep = iota((rows_dev, LANES), 1) + start != void
                    outs = [[jnp.where(keep, part, 0.0) for part in out] for out in outs]
                for pair, part in ((pair, part) for pair in range(pairs) for part in range(2)):
                    row = (2 * side + part) * rows_dev
                    near_ref[pair, row : row + rows_dev, start : start + LANES] = outs[pair][part].astype(jnp.bfloat16)
        for pair in range(pairs):
            cent_r, cent_i = (centre_ref[pair, part, index : index + 1, :] for part in range(2))
            for row in range(0, BLOCK, GRAIN):
                base_r, base_i = (base_ref[pair, part, row : row + GRAIN, :] for part in range(2))
                for start, table in zip(starts, both_blocks(base_r, base_i, cent_r, cent_i)):
                    rows = slice(start + row, start + row + GRAIN)
                    table_ref[pair, rows, :FOCAL] = table[0].astype(jnp.bfloat16)
                    table_ref[pair, rows, FOCAL:] = table[1].astype(jnp.bfloat16)
            product = jnp.dot(
                jnp.concatenate([near_ref[pair, :, start : start + BLOCK] for start in starts], axis=1),
                jnp.concatenate([table_ref[pair, start : start + BLOCK, :] for start in starts], axis=0),
                preferred_element_type=jnp.float32,
            )
            acc_ref[pair] = product if index == 0 else acc_ref[pair] + product
    for pair in range(pairs):
        acc = [acc_ref[pair, part * rows_dev : (part + 1) * rows_dev, :] for part in range(4)]
        (own_rr, own_ri), (own_ir, own_ii), (far_rr, far_ri), (far_ir, far_ii) = (
            (part[:, :FOCAL], part[:, FOCAL:]) for part in acc
        )
        cross_r, cross_i = far_ii - own_ii, own_ri - far_ri
        real = own_rr + far_rr + jnp.where(core == 1, cross_r, -cross_r)
        imag = own_ir + far_ir + jnp.where(core == 1, cross_i, -cross_i)
        near_r, near_i = (part[:, :1].astype(jnp.bfloat16).astype(jnp.float32) for part in columns[pair])
        wave_r, wave_i = (
            part.astype(jnp.bfloat16).astype(jnp.float32)
            for part in unit_waves((alone - half) * column_freq(info_ref, pair), 256 * cols)
        )
        real = real + (near_r * wave_r - near_i * wave_i)
        imag = imag + (near_r * wave_i + near_i * wave_r)
        for part, value in enumerate((real, imag)):
            lane = (2 * pair + part) * FOCAL
            mine_ref[:, lane : lane + FOCAL] = value.astype(jnp.bfloat16)


def spot_rows(info_ref, pair, first):
    aims = [info_ref[pair, row : row + 1, :] for row in (AIM_ROW, AIM_ROW + 1)]
    rows_off = (iota((PIECE, FOCAL), 0) + first).astype(jnp.float32) - aims[0]
    cols_off = iota((1, FOCAL), 1).astype(jnp.float32) - aims[1]
    return jnp.exp(-(rows_off * rows_off + cols_off * cols_off) / (2.0 * SPOT * SPOT))


def total_of(value):
    return jnp.sum(jnp.sum(value, axis=0, keepdims=True), axis=1, keepdims=True)


def row_kernel(info_ref, tall_ref, flat_ref, spot_ref, gain_ref):
    pairs, _, rows = tall_ref.shape
    rows_dev = flat_ref.shape[1]
    period = 256 * rows
    size = min(rows, FOCAL)
    for pair in range(pairs):
        wave = info_ref[pair, WAVE_ROW : WAVE_ROW + 1, :].astype(jnp.int32) + BLOCK
        focal = (iota((FOCAL, 1), 0) - FOCAL // 2) * wave

        def step(index, carry):
            start = pl.multiple_of(index * size, size)
            place = iota((1, size), 1) + (start - rows // 2)
            for row in range(0, FOCAL, PIECE):
                real, imag = unit_waves(focal[row : row + PIECE, :size] * place, period)
                tall_ref[pair, row : row + PIECE, pl.ds(start, size)] = real.astype(jnp.bfloat16)
                row += FOCAL
                tall_ref[pair, row : row + PIECE, pl.ds(start, size)] = imag.astype(jnp.bfloat16)
            return carry

        if rows == size:
            step(0, 0)
        else:
            lax.fori_loop(0, rows // size, step, 0)
        focal = (iota((1, FOCAL), 1) - FOCAL // 2) * wave
        first = lax.axis_index("aperture") * rows_dev - rows // 2
        real, imag = unit_waves((iota((rows_dev, 1), 0) + first) * focal, period)
        flat_ref[pair, :, :FOCAL] = real.astype(jnp.bfloat16)
        flat_ref[pair, :, FOCAL:] = imag.astype(jnp.bfloat16)
        total = jnp.zeros((PIECE, FOCAL), jnp.float32)
        for row in range(0, FOCAL, PIECE):
            spot = spot_rows(info_ref, pair, row)
            spot_ref[pair, row : row + PIECE, :] = spot
            total += spot
        gain_ref[pair] = jnp.broadcast_to(FOCAL * FOCAL / total_of(total), gain_ref.shape[1:])


def join_kernel(*refs):
    *in_refs, out_ref = refs
    count = in_refs[0].shape[0]
    for index, ref in enumerate(in_refs):
        out_ref[index * count : (index + 1) * count, :] = ref[...]


def focus_kernel(steps, tall_ref, flat_ref, spot_ref, gain_ref, after_ref, *refs):
    del after_ref
    *sect_refs, back_ref, score_ref, rows_ref, mixed_ref, field_ref, stack_ref = refs
    pairs = tall_ref.shape[0]
    rows_dev = back_ref.shape[0]
    if steps is None:
        rows_ref = sect_refs[0]
    else:
        me = lax.axis_index("aperture")
        blocks = [
            ref[index * rows_dev : (index + 1) * rows_dev, :]
            for ref in sect_refs
            for index in range(ref.shape[0] // rows_dev)
        ]
        for step, block in zip(steps, blocks, strict=True):
            start = pl.multiple_of((me ^ step) * rows_dev, rows_dev)
            rows_ref[pl.ds(start, rows_dev), :] = block
    for pair in range(pairs):
        lane = 2 * pair * FOCAL
        section = rows_ref[:, lane : lane + 2 * FOCAL]
        mixed_ref[pair] = jnp.dot(tall_ref[pair], section, preferred_element_type=jnp.float32)
    pieces = [slice(row, row + PIECE) for row in range(0, FOCAL, PIECE)]
    sums = []
    for pair in range(pairs):
        totals = [jnp.zeros((PIECE, FOCAL), jnp.float32) for _ in range(2)]
        for rows in pieces:
            lower = slice(rows.start + FOCAL, rows.stop + FOCAL)
            real = mixed_ref[pair, rows, :FOCAL] - mixed_ref[pair, lower, FOCAL:]
            imag = mixed_ref[pair, rows, FOCAL:] + mixed_ref[pair, lower, :FOCAL]
            field_ref[pair, 0, rows, :] = real
            field_ref[pair, 1, rows, :] = imag
            power = real * real + imag * imag
            totals = [totals[0] + spot_ref[pair, rows, :] * power, totals[1] + power]
        sums.append((total_of(totals[0]), total_of(totals[1]) + 1e-06))
    for pair, (spot_power, all_power) in enumerate(sums):
        ratio = spot_power / all_power
        gain = gain_ref[pair, :1, :1]
        score_ref[pair] = jnp.broadcast_to(ratio * gain, score_ref.shape[1:])
        scale = gain * 2.0 / all_power
        for rows in pieces:
            lower = slice(rows.start + FOCAL, rows.stop + FOCAL)
            weight = scale * (spot_ref[pair, rows, :] - ratio)
            real = (weight * field_ref[pair, 0, rows, :]).astype(jnp.bfloat16)
            imag = (weight * field_ref[pair, 1, rows, :]).astype(jnp.bfloat16)
            stack_ref[pair, rows, :FOCAL] = real
            stack_ref[pair, rows, FOCAL:] = imag
            stack_ref[pair, lower, :FOCAL] = imag
            stack_ref[pair, lower, FOCAL:] = -real
        back = jnp.dot(flat_ref[pair], stack_ref[pair], preferred_element_type=jnp.float32)
        lane = 2 * pair * FOCAL
        back_ref[:, lane : lane + 2 * FOCAL] = back.astype(jnp.bfloat16)


def table_kernel(scale, cols, info_ref, far_info_ref, width_ref, *refs):
    *out_refs, base_ref, centre_ref, turned_ref, power_ref = refs
    pairs = power_ref.shape[0]
    out_refs = out_refs[-2 * pairs :]
    table_refs, slope_refs = out_refs[:pairs], out_refs[pairs:]
    own_cols = width_ref.shape[1]
    sources = [(ref, pair) for ref in (info_ref, far_info_ref) for pair in range(pairs // 2)]
    centres = []
    for pair, (ref, source) in enumerate(sources):
        power = power_coefs(ref[source, : 2 * TERMS, :LANES])
        power_ref[pair] = as_tiles(power * ((iota(power.shape, 0) % TERMS).astype(jnp.float32) * scale))
        own_waves(ref, source, cols, base_ref.at[pair], centre_ref.at[pair])
        for part, row, lane in itertools.product(range(2), range(0, BLOCK, LANES), range(0, FOCAL, LANES)):
            tile = base_ref[pair, part, row : row + LANES, lane : lane + LANES]
            turned_ref[pair, part, lane : lane + LANES, row : row + LANES] = tile.T
        centres.append([centre_ref[pair, part].T for part in range(2)])
    for index in range(own_cols // (2 * BLOCK)):
        starts = block_starts(own_cols, index)
        for pair in range(pairs):
            for row in range(0, FOCAL, GRAIN):
                rows = slice(row, row + GRAIN)
                cent_r, cent_i = (centre[rows, index : index + 1] for centre in centres[pair])
                base_r, base_i = (turned_ref[pair, part, rows, :] for part in range(2))
                for start, table in zip(starts, both_blocks(base_r, base_i, cent_r, cent_i)):
                    for part, value in enumerate(table):
                        place = slice(row + part * FOCAL, row + part * FOCAL + GRAIN)
                        table_refs[pair][place, start : start + BLOCK] = value.astype(jnp.bfloat16)
        for start in (start + step for start in starts for step in range(0, BLOCK, LANES)):
            place = slice(start, start + LANES)
            slopes = near_slopes(width_ref[:, place], power_ref, pairs)
            for ref, slope in zip(slope_refs, slopes):
                ref[0, :, place] = slope[0]
                ref[1, :, place] = slope[1]


def own_grad_kernel(*refs):
    *in_refs, out_ref = refs
    add_grads(in_refs, None, out_ref, 2 * BLOCK)


def last_grad_kernel(*refs):
    *in_refs, total_ref, tile_ref, out_hbm, score_hbm, out_ref, score_ref, sems = refs
    own_cols = out_ref.shape[1]
    core = lax.axis_index("wave")
    for pair in range(score_ref.shape[0]):
        score_ref[pair] = jnp.sum(tile_ref[pair, :1, :1])
    moves = [pltpu.make_async_copy(score_ref, score_hbm, sems.at[own_cols // (2 * BLOCK)])]
    moves[0].start()

    def send(start, total):
        size = total.shape[1]
        place = pl.multiple_of(jnp.where(core == 1, start, own_cols - size - start), size)
        place = pl.ds(place, size)
        out_ref[:, place] = jnp.where(core == 1, total, turn_round(total))
        index = start // size
        moves.append(pltpu.make_async_copy(out_ref.at[:, place], out_hbm.at[:, place], sems.at[index]))
        moves[-1].start()

    add_grads(in_refs, total_ref, out_ref, 2 * BLOCK, send)
    for move in moves:
        move.wait()


def add_grads(in_refs, total_ref, out_ref, size, send=None):
    back_ref, *in_refs = in_refs
    pairs = len(in_refs) // 2
    table_refs, slope_refs = in_refs[:pairs], in_refs[pairs:]
    rows_dev, own_cols = out_ref.shape
    core = lax.axis_index("wave")
    lefts = []
    for pair in range(pairs):
        lane = 2 * pair * FOCAL
        real, imag = back_ref[:, lane : lane + FOCAL], back_ref[:, lane + FOCAL : lane + 2 * FOCAL]
        above = jnp.where(core == 1, imag, -imag)
        below = jnp.where(core == 1, -real, real)
        lefts.append(
            jnp.concatenate(
                [jnp.concatenate([real, above], axis=1), jnp.concatenate([imag, below], axis=1)], axis=0
            )
        )
    for start in range(0, own_cols, size):
        place = slice(start, start + size)
        total = jnp.zeros((rows_dev, size), jnp.float32) if total_ref is None else total_ref[:, place]
        for left, table_ref, slope_ref in zip(lefts, table_refs, slope_refs):
            grad = jnp.dot(left, table_ref[:, place], preferred_element_type=jnp.float32)
            total += grad[:rows_dev] * slope_ref[0, :, place]
            total += grad[rows_dev:] * slope_ref[1, :, place]
        if send is None:
            out_ref[:, place] = total
        else:
            send(start, total)


VMEM = pl.BlockSpec(memory_space=pltpu.VMEM)
SMEM = pl.BlockSpec(memory_space=pltpu.SMEM)
ANY = pl.BlockSpec(memory_space=pl.ANY)
HBM = pl.BlockSpec(memory_space=pltpu.HBM)


def call(kernel, name, outs, in_specs, out_specs, scratch, flops, moved):
    return pl.pallas_call(
        kernel,
        name=name,
        out_shape=outs,
        in_specs=in_specs,
        out_specs=out_specs,
        scratch_shapes=scratch,
        cost_estimate=pl.CostEstimate(flops=flops, bytes_accessed=moved, transcendentals=0),
        compiler_params=pltpu.CompilerParams(vmem_limit_bytes=VMEM_LIMIT),
    )


def on_device(widths, coef_table, wave_ids, angle_ids, targets):
    rows_dev, cols = widths.shape
    pairs_dev = wave_ids.shape[0]
    peers = lax.axis_size("aperture")
    copies = lax.axis_size("wave")
    rows = rows_dev * peers
    pairs = pairs_dev * copies
    own_cols = cols // copies
    lanes = 2 * pairs_dev * FOCAL
    f32, bf16 = jnp.float32, jnp.bfloat16
    shape = jax.ShapeDtypeStruct

    def in_hbm(value):
        return pltpu.with_memory_space_constraint(value, pltpu.HBM)

    def exchange(value, step):
        return lax.ppermute(value, "aperture", [(index, index ^ step) for index in range(peers)])

    def to_core(value):
        return lax.ppermute(value, "wave", [(index, (index + 1) % copies) for index in range(copies)])

    waves = [
        pltpu.VMEM((pairs_dev, 2, BLOCK, FOCAL), f32),
        pltpu.VMEM((pairs_dev, 2, 8, FOCAL), f32),
    ]
    mine, info, own = call(
        forward_kernel, "forward",
        (
            shape((rows_dev, lanes), bf16),
            shape((pairs_dev, INFO_ROWS, FOCAL), f32), shape((rows_dev, own_cols), f32),
        ),
        [HBM] * 5, (VMEM,) * 3,
        [
            pltpu.SMEM(wave_ids.shape, jnp.int32),
            pltpu.SMEM(angle_ids.shape, jnp.int32),
            pltpu.SMEM(targets.shape, jnp.int32),
            pltpu.VMEM(coef_table.shape[::-1], f32),
            pltpu.VMEM(widths.shape, f32),
            *waves,
            pltpu.VMEM((pairs_dev, 2 * TERMS, SUBLANES, LANES), f32),
            pltpu.VMEM((pairs_dev, 4 * rows_dev, own_cols), bf16),
            pltpu.VMEM((pairs_dev, own_cols, 2 * FOCAL), bf16),
            pltpu.VMEM((pairs_dev, 4 * rows_dev, 2 * FOCAL), f32),
            pltpu.SemaphoreType.DMA((5,)),
        ],
        10**9, 10**7,
    )(*(in_hbm(value) for value in (wave_ids, angle_ids, targets, coef_table.T, widths)))
    far_info = to_core(info)

    tall, flat, spots, gains = call(
        row_kernel, "row_tables",
        (
            shape((pairs_dev, 2 * FOCAL, rows), bf16), shape((pairs_dev, rows_dev, 2 * FOCAL), bf16),
            shape((pairs_dev, FOCAL, FOCAL), f32), shape((pairs_dev, 8, 128), f32),
        ),
        [VMEM], (VMEM,) * 4, [], 10**8, 10**6,
    )(info)
    if peers <= DIRECT:
        steps = list(range(peers - 2, 0, -2))
        got = [exchange(mine, step) for step in steps]
        near = exchange(mine, 1)
        first, flat = lax.optimization_barrier((got[0], flat))
        joined = call(join_kernel, "join", shape(((len(steps) - 1) * rows_dev, lanes), bf16),
                      [VMEM] * (len(steps) - 1), VMEM, [], 10**6, 10**6)(*got[1:])
        sections = [mine, near, first, joined, exchange(first, 1), exchange(joined, 1)]
        steps = [0, 1, *steps, *(step ^ 1 for step in steps)]
        after = [near, joined]
    else:
        blocks = jnp.tile(mine[None], (peers, 1, 1))
        blocks = lax.all_to_all(blocks, "aperture", 0, 0, tiled=True)
        sections, steps, after = [blocks.reshape(rows, lanes)], None, []
    outs = [shape((2 * FOCAL, own_cols), bf16)] * pairs + [shape((2, rows_dev, own_cols), f32)] * pairs
    made = call(
        functools.partial(table_kernel, math.sqrt(rows * cols), cols), "column_tables",
        outs, [VMEM] * 3 + [ANY] * len(after), [VMEM] * len(outs),
        [
            pltpu.VMEM((pairs, 2, BLOCK, FOCAL), f32),
            pltpu.VMEM((pairs, 2, 8, FOCAL), f32),
            pltpu.VMEM((pairs, 2, FOCAL, BLOCK), f32),
            pltpu.VMEM((pairs, 2 * TERMS, SUBLANES, LANES), f32),
        ],
        30 * 10**8, 30 * 10**6,
    )(info, far_info, own, *after)
    tables, slopes = made[:pairs], made[pairs:]

    back, scores = call(
        functools.partial(focus_kernel, steps), "focus",
        (shape((rows_dev, lanes), bf16), shape((pairs_dev, SUBLANES, LANES), f32)),
        [VMEM] * 4 + [ANY] + [VMEM] * len(sections), (VMEM, VMEM),
        [
            pltpu.VMEM((rows, lanes), bf16),
            pltpu.VMEM((pairs_dev, 2 * FOCAL, 2 * FOCAL), f32),
            pltpu.VMEM((pairs_dev, 2, FOCAL, FOCAL), f32),
            pltpu.VMEM((pairs_dev, 2 * FOCAL, 2 * FOCAL), bf16),
        ],
        10**8, 10**6,
    )(tall, flat, spots, gains, slopes[0], *sections)

    out = shape((rows_dev, own_cols), f32)
    ins = [back, *tables[:pairs_dev], *slopes[:pairs_dev]]
    grad = call(
        own_grad_kernel, "gradient_own", out, [VMEM] * len(ins), VMEM, [], 10**9, 10**7,
    )(*ins)
    ins = [to_core(back), *tables[pairs_dev:], *slopes[pairs_dev:], grad, scores]
    grad, scores = call(
        last_grad_kernel, "gradient_far", (out, shape((pairs_dev,), f32)), [VMEM] * len(ins), (HBM, HBM),
        [
            pltpu.VMEM(out.shape, f32),
            pltpu.SMEM((pairs_dev,), f32),
            pltpu.SemaphoreType.DMA((own_cols // (2 * BLOCK) + 1,)),
        ],
        10**9, 10**7,
    )(*ins)
    return grad, scores


def solution(mesh):
    in_specs = (
        P(("group", "aperture"), None),
        P(),
        P(("group", "wave")),
        P(("group", "wave")),
        P(("group", "wave"), None),
    )
    out_specs = (P(("group", "aperture"), "wave"), P(("group", "wave")))
    return jax.shard_map(
        on_device, mesh=mesh, in_specs=in_specs, out_specs=out_specs, check_vma=False
    )
```

```python
import functools
import itertools
import math

import jax
import jax.numpy as jnp
from jax import lax
from jax.experimental import pallas as pl
from jax.experimental.pallas import tpu as pltpu
from jax.sharding import PartitionSpec as P

FOCAL = 256
SPOT = 4
SHIFT = 32
TERMS = 8
BLOCK = 256
GRAIN = 16
LANES = 128
PIECE = 16
SUBLANES = 8
VMEM_LIMIT = 16 * 1024 * 1024
WAVE_ROW, ANGLE_ROW, AIM_ROW, INFO_ROWS = 16, 17, 18, 24
CUBE = 8

COS = (
    1.0, -19.7392088015709, 64.93939395773512, -85.45681453397417, 60.24458621302471,
    -26.425616460281425, 7.8991596631575085, -1.6968741456712442, 0.2437618617467591,
)
SIN = (
    6.2831853071792665, -41.34170224019464, 81.60524925425943, -76.70585885700535,
    42.05867547580699, -15.094428387947755, 3.818490079304055, -0.7122771247541972,
    0.09149844789363434,
)


def horner(terms, u):
    value = terms[-1] * u + terms[-2]
    for term in terms[-3::-1]:
        value = value * u + term
    return value


def unit_waves(counts, period):
    half = period // 2
    centred = ((counts + half) & (period - 1)) - half
    t = centred.astype(jnp.float32) * (1.0 / period)
    u = t * t
    return horner(COS, u), -(t * horner(SIN, u))


def iota(shape, axis):
    return lax.broadcasted_iota(jnp.int32, shape, axis)


def pick_coef(table, wave):
    chosen = jnp.where(iota(table.shape, 1) == wave, table, 0.0)
    return jnp.sum(chosen, axis=1, keepdims=True)


def column_freq(info_ref, pair):
    wave = info_ref[pair, WAVE_ROW : WAVE_ROW + 1, :].astype(jnp.int32)
    angle = info_ref[pair, ANGLE_ROW : ANGLE_ROW + 1, :].astype(jnp.int32)
    return (iota((1, FOCAL), 1) - FOCAL // 2 + SHIFT * angle) * (BLOCK + wave)


def fill_base(freq, shift, period, base_ref, centre_ref):
    low_r, low_i = unit_waves(iota((GRAIN, 1), 0) * freq, period)
    steps = BLOCK // GRAIN
    high_r, high_i = unit_waves((iota((steps, 1), 0) * GRAIN - BLOCK // 2 + shift) * freq, period)
    for step in range(steps):
        one_r, one_i = high_r[step : step + 1], high_i[step : step + 1]
        rows = slice(step * GRAIN, (step + 1) * GRAIN)
        base_ref[0, rows, :] = one_r * low_r - one_i * low_i
        base_ref[1, rows, :] = one_r * low_i + one_i * low_r
    count = centre_ref.shape[1]
    cent_r, cent_i = unit_waves((iota((count, 1), 0) * BLOCK + BLOCK // 2) * freq, period)
    centre_ref[0] = cent_r
    centre_ref[1] = cent_i


def power_coefs(coef):
    before, current = [1], [0, 1]
    bases = [before, current]
    for _ in range(2, TERMS):
        doubled = [0] + [2 * term for term in current]
        before, current = current, [a - b for a, b in itertools.zip_longest(doubled, before, fillvalue=0)]
        bases.append(current)
    rows = []
    for part, power in itertools.product(range(2), range(TERMS)):
        row = None
        for order in range(power, TERMS, 2):
            place = part * TERMS + order
            term = coef[place : place + 1] * float(bases[order][power])
            row = term if row is None else row + term
        rows.append(row)
    return jnp.concatenate(rows, axis=0)


def as_tiles(rows):
    return jnp.broadcast_to(rows[:, None, :], (rows.shape[0], SUBLANES, rows.shape[1]))


def split_rows(value):
    return value.reshape(value.shape[0] // SUBLANES, SUBLANES, value.shape[1])


def join_rows(value):
    return value.reshape(value.shape[0] * SUBLANES, value.shape[2])


def near_fields(s, power_ref, pairs):
    s = split_rows(s)
    outs = []
    for pair, part in itertools.product(range(pairs), range(2)):
        row = (part + 1) * TERMS - 1
        value = power_ref[pair, row] * s + power_ref[pair, row - 1]
        for row in range(row - 2, part * TERMS - 1, -1):
            value = value * s + power_ref[pair, row]
        outs.append(join_rows(value))
    return [outs[2 * pair : 2 * pair + 2] for pair in range(pairs)]


def near_slopes(s, power_ref, pairs):
    s = split_rows(s)
    outs = []
    for pair, part in itertools.product(range(pairs), range(2)):
        row = (part + 1) * TERMS - 1
        value = power_ref[pair, row] * s + power_ref[pair, row - 1]
        for row in range(row - 2, part * TERMS, -1):
            value = value * s + power_ref[pair, row]
        outs.append(join_rows(value))
    return [outs[2 * pair : 2 * pair + 2] for pair in range(pairs)]


def turn_round(value):
    rows, cols = value.shape
    order = LANES - 1 - iota((rows, LANES), 1)
    parts = [
        jnp.take_along_axis(value[:, start : start + LANES], order, axis=1)
        for start in range(cols - LANES, -1, -LANES)
    ]
    return jnp.concatenate(parts, axis=1)


def side_pieces(width_ref, core):
    rows, cols = width_ref.shape
    half = cols // 2
    count = half // LANES
    lane = iota((rows, LANES), 1)
    shift = jnp.where(core == 1, 1, LANES - 1)
    edge = jnp.where(core == 1, 0, LANES - 1)

    @functools.cache
    def turned(piece):
        right = width_ref[:, half + piece * LANES : half + (piece + 1) * LANES]
        left = turn_round(width_ref[:, half - (piece + 1) * LANES : half - piece * LANES])
        other = pltpu.roll(jnp.where(core == 1, left, right), shift, 1)
        return jnp.where(core == 1, right, left), other

    def sides(piece):
        own, other = turned(piece)
        beside = jnp.where(core == 1, turned(max(piece - 1, 0))[1], turned(min(piece + 1, count - 1))[1])
        return own, jnp.where(lane == edge, beside, other)

    return sides


def block_starts(cols, index):
    return cols // 2 - (index + 1) * BLOCK, cols // 2 + index * BLOCK


def both_blocks(base_r, base_i, cent_r, cent_i):
    rr, ii = base_r * cent_r, base_i * cent_i
    ri, ir = base_r * cent_i, base_i * cent_r
    return (rr + ii, ir - ri), (rr - ii, ir + ri)


def own_waves(info_ref, pair, cols, base_ref, centre_ref):
    shift = cols // 4 + 1 - lax.axis_index("wave")
    fill_base(column_freq(info_ref, pair), shift, 256 * cols, base_ref, centre_ref)


def forward_kernel(
    wave_hbm, angle_hbm, aim_hbm, coef_hbm, width_hbm, mine_ref, info_ref, own_ref, base_ref, centre_ref, *refs
):
    pairs = info_ref.shape[0]
    (
        wave_ref, angle_ref, aim_ref, coef_ref, width_ref, power_ref, near_ref, table_ref, acc_ref, sems,
    ) = refs
    rows_dev, cols = width_ref.shape
    half = cols // 2
    moves = [
        pltpu.make_async_copy(source, target, sems.at[index])
        for index, (source, target) in enumerate((
            (width_hbm, width_ref), (wave_hbm, wave_ref), (angle_hbm, angle_ref),
            (coef_hbm, coef_ref), (aim_hbm, aim_ref),
        ))
    ]
    for move in moves:
        move.start()
    for move in moves[1:]:
        move.wait()
    for pair in range(pairs):
        coef = pick_coef(coef_ref[...], wave_ref[pair])
        coef = jnp.broadcast_to(coef, (WAVE_ROW, FOCAL))
        info_ref[pair, :WAVE_ROW, :] = coef
        power_ref[pair] = as_tiles(power_coefs(coef[:, :LANES]))
        row = iota((INFO_ROWS - WAVE_ROW, FOCAL), 0) + WAVE_ROW
        ids = jnp.where(row == WAVE_ROW, wave_ref[pair], 0)
        ids = jnp.where(row == ANGLE_ROW, angle_ref[pair], ids)
        ids = jnp.where(row == AIM_ROW, aim_ref[pair, 0], ids)
        ids = jnp.where(row == AIM_ROW + 1, aim_ref[pair, 1], ids)
        info_ref[pair, WAVE_ROW:, :] = ids.astype(jnp.float32)
    for pair in range(pairs):
        own_waves(info_ref, pair, cols, base_ref.at[pair], centre_ref.at[pair])
    core = lax.axis_index("wave")
    moves[0].wait()
    sides = side_pieces(width_ref, core)
    alone = jnp.where(core == 1, 0, half)
    column = width_ref[:, pl.ds(pl.multiple_of(alone, LANES), LANES)]
    columns = near_fields(column, power_ref, pairs)
    void = jnp.where(core == 1, 0, half - 1)
    for index in range(half // (2 * BLOCK)):
        starts = block_starts(half, index)
        for start in (start + step for start in starts for step in range(0, BLOCK, LANES)):
            both = sides(start // LANES)
            own_ref[:, start : start + LANES] = both[0]
            for side, widths in enumerate(both):
                outs = near_fields(widths, power_ref, pairs)
                if side and start in (0, half - LANES):
                    keep = iota((rows_dev, LANES), 1) + start != void
                    outs = [[jnp.where(keep, part, 0.0) for part in out] for out in outs]
                for pair, part in ((pair, part) for pair in range(pairs) for part in range(2)):
                    row = (2 * side + part) * rows_dev
                    near_ref[pair, row : row + rows_dev, start : start + LANES] = outs[pair][part].astype(jnp.bfloat16)
        for pair in range(pairs):
            cent_r, cent_i = (centre_ref[pair, part, index : index + 1, :] for part in range(2))
            for row in range(0, BLOCK, GRAIN):
                base_r, base_i = (base_ref[pair, part, row : row + GRAIN, :] for part in range(2))
                for start, table in zip(starts, both_blocks(base_r, base_i, cent_r, cent_i)):
                    rows = slice(start + row, start + row + GRAIN)
                    table_ref[pair, rows, :FOCAL] = table[0].astype(jnp.bfloat16)
                    table_ref[pair, rows, FOCAL:] = table[1].astype(jnp.bfloat16)
            product = jnp.dot(
                jnp.concatenate([near_ref[pair, :, start : start + BLOCK] for start in starts], axis=1),
                jnp.concatenate([table_ref[pair, start : start + BLOCK, :] for start in starts], axis=0),
                preferred_element_type=jnp.float32,
            )
            acc_ref[pair] = product if index == 0 else acc_ref[pair] + product
    for pair in range(pairs):
        acc = [acc_ref[pair, part * rows_dev : (part + 1) * rows_dev, :] for part in range(4)]
        (own_rr, own_ri), (own_ir, own_ii), (far_rr, far_ri), (far_ir, far_ii) = (
            (part[:, :FOCAL], part[:, FOCAL:]) for part in acc
        )
        cross_r, cross_i = far_ii - own_ii, own_ri - far_ri
        real = own_rr + far_rr + jnp.where(core == 1, cross_r, -cross_r)
        imag = own_ir + far_ir + jnp.where(core == 1, cross_i, -cross_i)
        near_r, near_i = (part[:, :1].astype(jnp.bfloat16).astype(jnp.float32) for part in columns[pair])
        wave_r, wave_i = (
            part.astype(jnp.bfloat16).astype(jnp.float32)
            for part in unit_waves((alone - half) * column_freq(info_ref, pair), 256 * cols)
        )
        real = real + (near_r * wave_r - near_i * wave_i)
        imag = imag + (near_r * wave_i + near_i * wave_r)
        for part, value in enumerate((real, imag)):
            lane = (2 * pair + part) * FOCAL
            mine_ref[:, lane : lane + FOCAL] = value.astype(jnp.bfloat16)


def spot_rows(info_ref, pair, first):
    aims = [info_ref[pair, row : row + 1, :] for row in (AIM_ROW, AIM_ROW + 1)]
    rows_off = (iota((PIECE, FOCAL), 0) + first).astype(jnp.float32) - aims[0]
    cols_off = iota((1, FOCAL), 1).astype(jnp.float32) - aims[1]
    return jnp.exp(-(rows_off * rows_off + cols_off * cols_off) / (2.0 * SPOT * SPOT))


def total_of(value):
    return jnp.sum(jnp.sum(value, axis=0, keepdims=True), axis=1, keepdims=True)


def row_kernel(info_ref, tall_ref, flat_ref, spot_ref, gain_ref):
    pairs, _, rows = tall_ref.shape
    rows_dev = flat_ref.shape[1]
    period = 256 * rows
    size = min(rows, FOCAL)
    for pair in range(pairs):
        wave = info_ref[pair, WAVE_ROW : WAVE_ROW + 1, :].astype(jnp.int32) + BLOCK
        focal = (iota((FOCAL, 1), 0) - FOCAL // 2) * wave

        def step(index, carry):
            start = pl.multiple_of(index * size, size)
            place = iota((1, size), 1) + (start - rows // 2)
            for row in range(0, FOCAL, PIECE):
                real, imag = unit_waves(focal[row : row + PIECE, :size] * place, period)
                tall_ref[pair, row : row + PIECE, pl.ds(start, size)] = real.astype(jnp.bfloat16)
                row += FOCAL
                tall_ref[pair, row : row + PIECE, pl.ds(start, size)] = imag.astype(jnp.bfloat16)
            return carry

        if rows == size:
            step(0, 0)
        else:
            lax.fori_loop(0, rows // size, step, 0)
        focal = (iota((1, FOCAL), 1) - FOCAL // 2) * wave
        first = lax.axis_index("aperture") * rows_dev - rows // 2
        real, imag = unit_waves((iota((rows_dev, 1), 0) + first) * focal, period)
        flat_ref[pair, :, :FOCAL] = real.astype(jnp.bfloat16)
        flat_ref[pair, :, FOCAL:] = imag.astype(jnp.bfloat16)
        total = jnp.zeros((PIECE, FOCAL), jnp.float32)
        for row in range(0, FOCAL, PIECE):
            spot = spot_rows(info_ref, pair, row)
            spot_ref[pair, row : row + PIECE, :] = spot
            total += spot
        gain_ref[pair] = jnp.broadcast_to(FOCAL * FOCAL / total_of(total), gain_ref.shape[1:])


def focus_kernel(steps, tall_ref, flat_ref, spot_ref, gain_ref, after_ref, *refs):
    del after_ref
    *sect_refs, back_ref, score_ref, rows_ref, mixed_ref, field_ref, stack_ref = refs
    pairs = tall_ref.shape[0]
    rows_dev = back_ref.shape[0]
    if steps is None:
        rows_ref = sect_refs[0]
    else:
        me = lax.axis_index("aperture")
        blocks = [
            ref[index * rows_dev : (index + 1) * rows_dev, :]
            for ref in sect_refs
            for index in range(ref.shape[0] // rows_dev)
        ]
        for step, block in zip(steps, blocks, strict=True):
            start = pl.multiple_of((me ^ step) * rows_dev, rows_dev)
            rows_ref[pl.ds(start, rows_dev), :] = block
    for pair in range(pairs):
        lane = 2 * pair * FOCAL
        section = rows_ref[:, lane : lane + 2 * FOCAL]
        mixed_ref[pair] = jnp.dot(tall_ref[pair], section, preferred_element_type=jnp.float32)
    pieces = [slice(row, row + PIECE) for row in range(0, FOCAL, PIECE)]
    sums = []
    for pair in range(pairs):
        totals = [jnp.zeros((PIECE, FOCAL), jnp.float32) for _ in range(2)]
        for rows in pieces:
            lower = slice(rows.start + FOCAL, rows.stop + FOCAL)
            real = mixed_ref[pair, rows, :FOCAL] - mixed_ref[pair, lower, FOCAL:]
            imag = mixed_ref[pair, rows, FOCAL:] + mixed_ref[pair, lower, :FOCAL]
            field_ref[pair, 0, rows, :] = real
            field_ref[pair, 1, rows, :] = imag
            power = real * real + imag * imag
            totals = [totals[0] + spot_ref[pair, rows, :] * power, totals[1] + power]
        sums.append((total_of(totals[0]), total_of(totals[1]) + 1e-06))
    for pair, (spot_power, all_power) in enumerate(sums):
        ratio = spot_power / all_power
        gain = gain_ref[pair, :1, :1]
        score_ref[pair] = jnp.broadcast_to(ratio * gain, score_ref.shape[1:])
        scale = gain * 2.0 / all_power
        for rows in pieces:
            lower = slice(rows.start + FOCAL, rows.stop + FOCAL)
            weight = scale * (spot_ref[pair, rows, :] - ratio)
            real = (weight * field_ref[pair, 0, rows, :]).astype(jnp.bfloat16)
            imag = (weight * field_ref[pair, 1, rows, :]).astype(jnp.bfloat16)
            stack_ref[pair, rows, :FOCAL] = real
            stack_ref[pair, rows, FOCAL:] = imag
            stack_ref[pair, lower, :FOCAL] = imag
            stack_ref[pair, lower, FOCAL:] = -real
        back = jnp.dot(flat_ref[pair], stack_ref[pair], preferred_element_type=jnp.float32)
        lane = 2 * pair * FOCAL
        back_ref[:, lane : lane + 2 * FOCAL] = back.astype(jnp.bfloat16)


def table_kernel(scale, cols, info_ref, far_info_ref, width_ref, own_base_ref, own_centre_ref, *refs):
    *out_refs, base_ref, centre_ref, turned_ref, power_ref = refs
    pairs = power_ref.shape[0]
    out_refs = out_refs[-2 * pairs :]
    table_refs, slope_refs = out_refs[:pairs], out_refs[pairs:]
    own_cols = width_ref.shape[1]
    sources = [(ref, pair) for ref in (info_ref, far_info_ref) for pair in range(pairs // 2)]
    centres = []
    for pair, (ref, source) in enumerate(sources):
        power = power_coefs(ref[source, : 2 * TERMS, :LANES])
        power_ref[pair] = as_tiles(power * ((iota(power.shape, 0) % TERMS).astype(jnp.float32) * scale))
        if ref is info_ref:
            bases, middles = own_base_ref.at[source], own_centre_ref.at[source]
        else:
            bases, middles = base_ref.at[source], centre_ref.at[source]
            own_waves(ref, source, cols, bases, middles)
        for part, row, lane in itertools.product(range(2), range(0, BLOCK, LANES), range(0, FOCAL, LANES)):
            tile = bases[part, row : row + LANES, lane : lane + LANES]
            turned_ref[pair, part, lane : lane + LANES, row : row + LANES] = tile.T
        centres.append([middles[part].T for part in range(2)])
    for index in range(own_cols // (2 * BLOCK)):
        starts = block_starts(own_cols, index)
        for pair in range(pairs):
            for row in range(0, FOCAL, GRAIN):
                rows = slice(row, row + GRAIN)
                cent_r, cent_i = (centre[rows, index : index + 1] for centre in centres[pair])
                base_r, base_i = (turned_ref[pair, part, rows, :] for part in range(2))
                for start, table in zip(starts, both_blocks(base_r, base_i, cent_r, cent_i)):
                    for part, value in enumerate(table):
                        place = slice(row + part * FOCAL, row + part * FOCAL + GRAIN)
                        table_refs[pair][place, start : start + BLOCK] = value.astype(jnp.bfloat16)
        for start in (start + step for start in starts for step in range(0, BLOCK, LANES)):
            place = slice(start, start + LANES)
            slopes = near_slopes(width_ref[:, place], power_ref, pairs)
            for ref, slope in zip(slope_refs, slopes):
                ref[0, :, place] = slope[0]
                ref[1, :, place] = slope[1]


def own_grad_kernel(*refs):
    *in_refs, out_ref = refs
    add_grads(in_refs, None, out_ref, 2 * BLOCK)


def last_grad_kernel(*refs):
    *in_refs, total_ref, tile_ref, out_hbm, score_hbm, out_ref, score_ref, sems = refs
    own_cols = out_ref.shape[1]
    core = lax.axis_index("wave")
    for pair in range(score_ref.shape[0]):
        score_ref[pair] = jnp.sum(tile_ref[pair, :1, :1])
    moves = [pltpu.make_async_copy(score_ref, score_hbm, sems.at[own_cols // (2 * BLOCK)])]
    moves[0].start()

    def send(start, total):
        size = total.shape[1]
        place = pl.multiple_of(jnp.where(core == 1, start, own_cols - size - start), size)
        place = pl.ds(place, size)
        out_ref[:, place] = jnp.where(core == 1, total, turn_round(total))
        index = start // size
        moves.append(pltpu.make_async_copy(out_ref.at[:, place], out_hbm.at[:, place], sems.at[index]))
        moves[-1].start()

    add_grads(in_refs, total_ref, out_ref, 2 * BLOCK, send)
    for move in moves:
        move.wait()


def add_grads(in_refs, total_ref, out_ref, size, send=None):
    back_ref, *in_refs = in_refs
    pairs = len(in_refs) // 2
    table_refs, slope_refs = in_refs[:pairs], in_refs[pairs:]
    rows_dev, own_cols = out_ref.shape
    core = lax.axis_index("wave")
    lefts = []
    for pair in range(pairs):
        lane = 2 * pair * FOCAL
        real, imag = back_ref[:, lane : lane + FOCAL], back_ref[:, lane + FOCAL : lane + 2 * FOCAL]
        above = jnp.where(core == 1, imag, -imag)
        below = jnp.where(core == 1, -real, real)
        lefts.append(
            jnp.concatenate(
                [jnp.concatenate([real, above], axis=1), jnp.concatenate([imag, below], axis=1)], axis=0
            )
        )
    for start in range(0, own_cols, size):
        place = slice(start, start + size)
        total = jnp.zeros((rows_dev, size), jnp.float32) if total_ref is None else total_ref[:, place]
        for left, table_ref, slope_ref in zip(lefts, table_refs, slope_refs):
            grad = jnp.dot(left, table_ref[:, place], preferred_element_type=jnp.float32)
            total += grad[:rows_dev] * slope_ref[0, :, place]
            total += grad[rows_dev:] * slope_ref[1, :, place]
        if send is None:
            out_ref[:, place] = total
        else:
            send(start, total)


VMEM = pl.BlockSpec(memory_space=pltpu.VMEM)
SMEM = pl.BlockSpec(memory_space=pltpu.SMEM)
ANY = pl.BlockSpec(memory_space=pl.ANY)
HBM = pl.BlockSpec(memory_space=pltpu.HBM)


def call(kernel, name, outs, in_specs, out_specs, scratch, flops, moved):
    return pl.pallas_call(
        kernel,
        name=name,
        out_shape=outs,
        in_specs=in_specs,
        out_specs=out_specs,
        scratch_shapes=scratch,
        cost_estimate=pl.CostEstimate(flops=flops, bytes_accessed=moved, transcendentals=0),
        compiler_params=pltpu.CompilerParams(vmem_limit_bytes=VMEM_LIMIT),
    )


def on_device(widths, coef_table, wave_ids, angle_ids, targets):
    rows_dev, cols = widths.shape
    pairs_dev = wave_ids.shape[0]
    peers = lax.axis_size("aperture")
    copies = lax.axis_size("wave")
    rows = rows_dev * peers
    pairs = pairs_dev * copies
    own_cols = cols // copies
    lanes = 2 * pairs_dev * FOCAL
    f32, bf16 = jnp.float32, jnp.bfloat16
    shape = jax.ShapeDtypeStruct

    def in_hbm(value):
        return pltpu.with_memory_space_constraint(value, pltpu.HBM)

    def exchange(value, step):
        return lax.ppermute(value, "aperture", [(index, index ^ step) for index in range(peers)])

    def to_core(value):
        return lax.ppermute(value, "wave", [(index, (index + 1) % copies) for index in range(copies)])

    waves = [
        pltpu.VMEM((pairs_dev, 2, BLOCK, FOCAL), f32),
        pltpu.VMEM((pairs_dev, 2, 8, FOCAL), f32),
    ]
    mine, info, own, base, centre = call(
        forward_kernel, "forward",
        (
            shape((rows_dev, lanes), bf16),
            shape((pairs_dev, INFO_ROWS, FOCAL), f32), shape((rows_dev, own_cols), f32),
            *(shape(ref.shape, f32) for ref in waves),
        ),
        [HBM] * 5, (VMEM,) * 5,
        [
            pltpu.SMEM(wave_ids.shape, jnp.int32),
            pltpu.SMEM(angle_ids.shape, jnp.int32),
            pltpu.SMEM(targets.shape, jnp.int32),
            pltpu.VMEM(coef_table.shape[::-1], f32),
            pltpu.VMEM(widths.shape, f32),
            pltpu.VMEM((pairs_dev, 2 * TERMS, SUBLANES, LANES), f32),
            pltpu.VMEM((pairs_dev, 4 * rows_dev, own_cols), bf16),
            pltpu.VMEM((pairs_dev, own_cols, 2 * FOCAL), bf16),
            pltpu.VMEM((pairs_dev, 4 * rows_dev, 2 * FOCAL), f32),
            pltpu.SemaphoreType.DMA((5,)),
        ],
        10**9, 10**7,
    )(*(in_hbm(value) for value in (wave_ids, angle_ids, targets, coef_table.T, widths)))
    far_info = to_core(info)

    tall, flat, spots, gains = call(
        row_kernel, "row_tables",
        (
            shape((pairs_dev, 2 * FOCAL, rows), bf16), shape((pairs_dev, rows_dev, 2 * FOCAL), bf16),
            shape((pairs_dev, FOCAL, FOCAL), f32), shape((pairs_dev, 8, 128), f32),
        ),
        [VMEM], (VMEM,) * 4, [], 10**8, 10**6,
    )(info)
    if peers == CUBE:
        last, middle, beside = (exchange(mine, step) for step in (6, 4, 2))
        near = exchange(mine, 1)
        corner = exchange(mine, 3)
        last, flat = lax.optimization_barrier((last, flat))
        sections = [mine, near, last, middle, beside, corner, exchange(last, 1), exchange(middle, 1)]
        steps = [0, 1, 6, 4, 2, 3, 7, 5]
        after = [near, corner, middle, beside]
    else:
        blocks = jnp.tile(mine[None], (peers, 1, 1))
        blocks = lax.all_to_all(blocks, "aperture", 0, 0, tiled=True)
        sections, steps, after = [blocks.reshape(rows, lanes)], None, []
    outs = [shape((2 * FOCAL, own_cols), bf16)] * pairs + [shape((2, rows_dev, own_cols), f32)] * pairs
    made = call(
        functools.partial(table_kernel, math.sqrt(rows * cols), cols), "column_tables",
        outs, [VMEM] * 5 + [ANY] * len(after), [VMEM] * len(outs),
        [
            *waves,
            pltpu.VMEM((pairs, 2, FOCAL, BLOCK), f32),
            pltpu.VMEM((pairs, 2 * TERMS, SUBLANES, LANES), f32),
        ],
        30 * 10**8, 30 * 10**6,
    )(info, far_info, own, base, centre, *after)
    tables, slopes = made[:pairs], made[pairs:]

    back, scores = call(
        functools.partial(focus_kernel, steps), "focus",
        (shape((rows_dev, lanes), bf16), shape((pairs_dev, SUBLANES, LANES), f32)),
        [VMEM] * 4 + [ANY] + [VMEM] * len(sections), (VMEM, VMEM),
        [
            pltpu.VMEM((rows, lanes), bf16),
            pltpu.VMEM((pairs_dev, 2 * FOCAL, 2 * FOCAL), f32),
            pltpu.VMEM((pairs_dev, 2, FOCAL, FOCAL), f32),
            pltpu.VMEM((pairs_dev, 2 * FOCAL, 2 * FOCAL), bf16),
        ],
        10**8, 10**6,
    )(tall, flat, spots, gains, slopes[0], *sections)

    out = shape((rows_dev, own_cols), f32)
    ins = [back, *tables[:pairs_dev], *slopes[:pairs_dev]]
    grad = call(
        own_grad_kernel, "gradient_own", out, [VMEM] * len(ins), VMEM, [], 10**9, 10**7,
    )(*ins)
    ins = [to_core(back), *tables[pairs_dev:], *slopes[pairs_dev:], grad, scores]
    grad, scores = call(
        last_grad_kernel, "gradient_far", (out, shape((pairs_dev,), f32)), [VMEM] * len(ins), (HBM, HBM),
        [
            pltpu.VMEM(out.shape, f32),
            pltpu.SMEM((pairs_dev,), f32),
            pltpu.SemaphoreType.DMA((own_cols // (2 * BLOCK) + 1,)),
        ],
        10**9, 10**7,
    )(*ins)
    return grad, scores


def solution(mesh):
    in_specs = (
        P(("group", "aperture"), None),
        P(),
        P(("group", "wave")),
        P(("group", "wave")),
        P(("group", "wave"), None),
    )
    out_specs = (P(("group", "aperture"), "wave"), P(("group", "wave")))
    return jax.shard_map(
        on_device, mesh=mesh, in_specs=in_specs, out_specs=out_specs, check_vma=False
    )
```

```python
import functools
import itertools
import math

import jax
import jax.numpy as jnp
from jax import lax
from jax.experimental import pallas as pl
from jax.experimental.pallas import tpu as pltpu
from jax.sharding import PartitionSpec as P

FOCAL = 256
SPOT = 4
SHIFT = 32
TERMS = 8
BLOCK = 256
GRAIN = 16
LANES = 128
PIECE = 16
SUBLANES = 8
VMEM_LIMIT = 16 * 1024 * 1024
WAVE_ROW, ANGLE_ROW, AIM_ROW, INFO_ROWS = 16, 17, 18, 24
CUBE = 8

COS = (
    1.0, -19.7392088015709, 64.93939395773512, -85.45681453397417, 60.24458621302471,
    -26.425616460281425, 7.8991596631575085, -1.6968741456712442, 0.2437618617467591,
)
SIN = (
    6.2831853071792665, -41.34170224019464, 81.60524925425943, -76.70585885700535,
    42.05867547580699, -15.094428387947755, 3.818490079304055, -0.7122771247541972,
    0.09149844789363434,
)


def horner(terms, u):
    value = terms[-1] * u + terms[-2]
    for term in terms[-3::-1]:
        value = value * u + term
    return value


def unit_waves(counts, period):
    half = period // 2
    centred = ((counts + half) & (period - 1)) - half
    t = centred.astype(jnp.float32) * (1.0 / period)
    u = t * t
    return horner(COS, u), -(t * horner(SIN, u))


def iota(shape, axis):
    return lax.broadcasted_iota(jnp.int32, shape, axis)


def pick_coef(table, wave):
    chosen = jnp.where(iota(table.shape, 1) == wave, table, 0.0)
    return jnp.sum(chosen, axis=1, keepdims=True)


def column_freq(info_ref, pair):
    wave = info_ref[pair, WAVE_ROW : WAVE_ROW + 1, :].astype(jnp.int32)
    angle = info_ref[pair, ANGLE_ROW : ANGLE_ROW + 1, :].astype(jnp.int32)
    return (iota((1, FOCAL), 1) - FOCAL // 2 + SHIFT * angle) * (BLOCK + wave)


def fill_base(freq, shift, period, base_ref, centre_ref):
    low_r, low_i = unit_waves(iota((GRAIN, 1), 0) * freq, period)
    steps = BLOCK // GRAIN
    high_r, high_i = unit_waves((iota((steps, 1), 0) * GRAIN - BLOCK // 2 + shift) * freq, period)
    for step in range(steps):
        one_r, one_i = high_r[step : step + 1], high_i[step : step + 1]
        rows = slice(step * GRAIN, (step + 1) * GRAIN)
        base_ref[0, rows, :] = one_r * low_r - one_i * low_i
        base_ref[1, rows, :] = one_r * low_i + one_i * low_r
    count = centre_ref.shape[1]
    cent_r, cent_i = unit_waves((iota((count, 1), 0) * BLOCK + BLOCK // 2) * freq, period)
    centre_ref[0] = cent_r
    centre_ref[1] = cent_i


def power_coefs(coef):
    before, current = [1], [0, 1]
    bases = [before, current]
    for _ in range(2, TERMS):
        doubled = [0] + [2 * term for term in current]
        before, current = current, [a - b for a, b in itertools.zip_longest(doubled, before, fillvalue=0)]
        bases.append(current)
    rows = []
    for part, power in itertools.product(range(2), range(TERMS)):
        row = None
        for order in range(power, TERMS, 2):
            place = part * TERMS + order
            term = coef[place : place + 1] * float(bases[order][power])
            row = term if row is None else row + term
        rows.append(row)
    return jnp.concatenate(rows, axis=0)


def as_tiles(rows):
    return jnp.broadcast_to(rows[:, None, :], (rows.shape[0], SUBLANES, rows.shape[1]))


def split_rows(value):
    return value.reshape(value.shape[0] // SUBLANES, SUBLANES, value.shape[1])


def join_rows(value):
    return value.reshape(value.shape[0] * SUBLANES, value.shape[2])


def near_fields(s, power_ref, pairs):
    s = split_rows(s)
    outs = []
    for pair, part in itertools.product(range(pairs), range(2)):
        row = (part + 1) * TERMS - 1
        value = power_ref[pair, row] * s + power_ref[pair, row - 1]
        for row in range(row - 2, part * TERMS - 1, -1):
            value = value * s + power_ref[pair, row]
        outs.append(join_rows(value))
    return [outs[2 * pair : 2 * pair + 2] for pair in range(pairs)]


def near_slopes(s, power_ref, pairs):
    s = split_rows(s)
    outs = []
    for pair, part in itertools.product(range(pairs), range(2)):
        row = (part + 1) * TERMS - 1
        value = power_ref[pair, row] * s + power_ref[pair, row - 1]
        for row in range(row - 2, part * TERMS, -1):
            value = value * s + power_ref[pair, row]
        outs.append(join_rows(value))
    return [outs[2 * pair : 2 * pair + 2] for pair in range(pairs)]


def turn_round(value):
    rows, cols = value.shape
    order = LANES - 1 - iota((rows, LANES), 1)
    parts = [
        jnp.take_along_axis(value[:, start : start + LANES], order, axis=1)
        for start in range(cols - LANES, -1, -LANES)
    ]
    return jnp.concatenate(parts, axis=1)


def side_pieces(width_ref, core):
    rows, cols = width_ref.shape
    half = cols // 2
    count = half // LANES
    lane = iota((rows, LANES), 1)
    shift = jnp.where(core == 1, 1, LANES - 1)
    edge = jnp.where(core == 1, 0, LANES - 1)

    @functools.cache
    def turned(piece):
        right = width_ref[:, half + piece * LANES : half + (piece + 1) * LANES]
        left = turn_round(width_ref[:, half - (piece + 1) * LANES : half - piece * LANES])
        other = pltpu.roll(jnp.where(core == 1, left, right), shift, 1)
        return jnp.where(core == 1, right, left), other

    def sides(piece):
        own, other = turned(piece)
        beside = jnp.where(core == 1, turned(max(piece - 1, 0))[1], turned(min(piece + 1, count - 1))[1])
        return own, jnp.where(lane == edge, beside, other)

    return sides


def block_starts(cols, index):
    return cols // 2 - (index + 1) * BLOCK, cols // 2 + index * BLOCK


def both_blocks(base_r, base_i, cent_r, cent_i):
    rr, ii = base_r * cent_r, base_i * cent_i
    ri, ir = base_r * cent_i, base_i * cent_r
    return (rr + ii, ir - ri), (rr - ii, ir + ri)


def own_waves(info_ref, pair, cols, base_ref, centre_ref):
    shift = cols // 4 + 1 - lax.axis_index("wave")
    fill_base(column_freq(info_ref, pair), shift, 256 * cols, base_ref, centre_ref)


def forward_kernel(
    wave_hbm, angle_hbm, aim_hbm, coef_hbm, width_hbm, mine_ref, info_ref, own_ref, base_ref, centre_ref, *refs
):
    pairs = info_ref.shape[0]
    (
        wave_ref, angle_ref, aim_ref, coef_ref, width_ref, power_ref, near_ref, table_ref, acc_ref, sems,
    ) = refs
    rows_dev, cols = width_ref.shape
    half = cols // 2
    moves = [
        pltpu.make_async_copy(source, target, sems.at[index])
        for index, (source, target) in enumerate((
            (width_hbm, width_ref), (wave_hbm, wave_ref), (angle_hbm, angle_ref),
            (coef_hbm, coef_ref), (aim_hbm, aim_ref),
        ))
    ]
    for move in moves:
        move.start()
    for move in moves[1:]:
        move.wait()
    for pair in range(pairs):
        coef = pick_coef(coef_ref[...], wave_ref[pair])
        coef = jnp.broadcast_to(coef, (WAVE_ROW, FOCAL))
        info_ref[pair, :WAVE_ROW, :] = coef
        power_ref[pair] = as_tiles(power_coefs(coef[:, :LANES]))
        row = iota((INFO_ROWS - WAVE_ROW, FOCAL), 0) + WAVE_ROW
        ids = jnp.where(row == WAVE_ROW, wave_ref[pair], 0)
        ids = jnp.where(row == ANGLE_ROW, angle_ref[pair], ids)
        ids = jnp.where(row == AIM_ROW, aim_ref[pair, 0], ids)
        ids = jnp.where(row == AIM_ROW + 1, aim_ref[pair, 1], ids)
        info_ref[pair, WAVE_ROW:, :] = ids.astype(jnp.float32)
    for pair in range(pairs):
        own_waves(info_ref, pair, cols, base_ref.at[pair], centre_ref.at[pair])
    core = lax.axis_index("wave")
    moves[0].wait()
    sides = side_pieces(width_ref, core)
    alone = jnp.where(core == 1, 0, half)
    column = width_ref[:, pl.ds(pl.multiple_of(alone, LANES), LANES)]
    columns = near_fields(column, power_ref, pairs)
    void = jnp.where(core == 1, 0, half - 1)
    for index in range(half // (2 * BLOCK)):
        starts = block_starts(half, index)
        for start in (start + step for start in starts for step in range(0, BLOCK, LANES)):
            both = sides(start // LANES)
            own_ref[:, start : start + LANES] = both[0]
            for side, widths in enumerate(both):
                outs = near_fields(widths, power_ref, pairs)
                if side and start in (0, half - LANES):
                    keep = iota((rows_dev, LANES), 1) + start != void
                    outs = [[jnp.where(keep, part, 0.0) for part in out] for out in outs]
                for pair, part in ((pair, part) for pair in range(pairs) for part in range(2)):
                    row = (2 * side + part) * rows_dev
                    near_ref[pair, row : row + rows_dev, start : start + LANES] = outs[pair][part].astype(jnp.bfloat16)
        for pair in range(pairs):
            cent_r, cent_i = (centre_ref[pair, part, index : index + 1, :] for part in range(2))
            for row in range(0, BLOCK, GRAIN):
                base_r, base_i = (base_ref[pair, part, row : row + GRAIN, :] for part in range(2))
                for start, table in zip(starts, both_blocks(base_r, base_i, cent_r, cent_i)):
                    rows = slice(start + row, start + row + GRAIN)
                    table_ref[pair, rows, :FOCAL] = table[0].astype(jnp.bfloat16)
                    table_ref[pair, rows, FOCAL:] = table[1].astype(jnp.bfloat16)
            product = jnp.dot(
                jnp.concatenate([near_ref[pair, :, start : start + BLOCK] for start in starts], axis=1),
                jnp.concatenate([table_ref[pair, start : start + BLOCK, :] for start in starts], axis=0),
                preferred_element_type=jnp.float32,
            )
            acc_ref[pair] = product if index == 0 else acc_ref[pair] + product
    for pair in range(pairs):
        acc = [acc_ref[pair, part * rows_dev : (part + 1) * rows_dev, :] for part in range(4)]
        (own_rr, own_ri), (own_ir, own_ii), (far_rr, far_ri), (far_ir, far_ii) = (
            (part[:, :FOCAL], part[:, FOCAL:]) for part in acc
        )
        cross_r, cross_i = far_ii - own_ii, own_ri - far_ri
        real = own_rr + far_rr + jnp.where(core == 1, cross_r, -cross_r)
        imag = own_ir + far_ir + jnp.where(core == 1, cross_i, -cross_i)
        near_r, near_i = (part[:, :1].astype(jnp.bfloat16).astype(jnp.float32) for part in columns[pair])
        wave_r, wave_i = (
            part.astype(jnp.bfloat16).astype(jnp.float32)
            for part in unit_waves((alone - half) * column_freq(info_ref, pair), 256 * cols)
        )
        real = real + (near_r * wave_r - near_i * wave_i)
        imag = imag + (near_r * wave_i + near_i * wave_r)
        for part, value in enumerate((real, imag)):
            lane = (2 * pair + part) * FOCAL
            mine_ref[:, lane : lane + FOCAL] = value.astype(jnp.bfloat16)


def spot_rows(info_ref, pair, first):
    aims = [info_ref[pair, row : row + 1, :] for row in (AIM_ROW, AIM_ROW + 1)]
    rows_off = (iota((PIECE, FOCAL), 0) + first).astype(jnp.float32) - aims[0]
    cols_off = iota((1, FOCAL), 1).astype(jnp.float32) - aims[1]
    return jnp.exp(-(rows_off * rows_off + cols_off * cols_off) / (2.0 * SPOT * SPOT))


def total_of(value):
    return jnp.sum(jnp.sum(value, axis=0, keepdims=True), axis=1, keepdims=True)


def row_kernel(info_ref, tall_ref, flat_ref, spot_ref, gain_ref):
    pairs, _, rows = tall_ref.shape
    rows_dev = flat_ref.shape[1]
    period = 256 * rows
    size = min(rows, FOCAL)
    for pair in range(pairs):
        wave = info_ref[pair, WAVE_ROW : WAVE_ROW + 1, :].astype(jnp.int32) + BLOCK
        focal = (iota((FOCAL, 1), 0) - FOCAL // 2) * wave

        def step(index, carry):
            start = pl.multiple_of(index * size, size)
            place = iota((1, size), 1) + (start - rows // 2)
            for row in range(0, FOCAL, PIECE):
                real, imag = unit_waves(focal[row : row + PIECE, :size] * place, period)
                tall_ref[pair, row : row + PIECE, pl.ds(start, size)] = real.astype(jnp.bfloat16)
                row += FOCAL
                tall_ref[pair, row : row + PIECE, pl.ds(start, size)] = imag.astype(jnp.bfloat16)
            return carry

        if rows == size:
            step(0, 0)
        else:
            lax.fori_loop(0, rows // size, step, 0)
        focal = (iota((1, FOCAL), 1) - FOCAL // 2) * wave
        first = lax.axis_index("aperture") * rows_dev - rows // 2
        real, imag = unit_waves((iota((rows_dev, 1), 0) + first) * focal, period)
        flat_ref[pair, :, :FOCAL] = real.astype(jnp.bfloat16)
        flat_ref[pair, :, FOCAL:] = imag.astype(jnp.bfloat16)
        total = jnp.zeros((PIECE, FOCAL), jnp.float32)
        for row in range(0, FOCAL, PIECE):
            spot = spot_rows(info_ref, pair, row)
            spot_ref[pair, row : row + PIECE, :] = spot
            total += spot
        gain_ref[pair] = jnp.broadcast_to(FOCAL * FOCAL / total_of(total), gain_ref.shape[1:])


def focus_kernel(steps, tall_ref, flat_ref, spot_ref, gain_ref, after_ref, *refs):
    del after_ref
    *sect_refs, back_ref, score_ref, rows_ref, mixed_ref, field_ref, stack_ref = refs
    pairs = tall_ref.shape[0]
    rows_dev = back_ref.shape[0]
    if steps is None:
        rows_ref = sect_refs[0]
    else:
        me = lax.axis_index("aperture")
        blocks = [
            ref[index * rows_dev : (index + 1) * rows_dev, :]
            for ref in sect_refs
            for index in range(ref.shape[0] // rows_dev)
        ]
        for step, block in zip(steps, blocks, strict=True):
            start = pl.multiple_of((me ^ step) * rows_dev, rows_dev)
            rows_ref[pl.ds(start, rows_dev), :] = block
    for pair in range(pairs):
        lane = 2 * pair * FOCAL
        section = rows_ref[:, lane : lane + 2 * FOCAL]
        mixed_ref[pair] = jnp.dot(tall_ref[pair], section, preferred_element_type=jnp.float32)
    pieces = [slice(row, row + PIECE) for row in range(0, FOCAL, PIECE)]
    sums = []
    for pair in range(pairs):
        totals = [jnp.zeros((PIECE, FOCAL), jnp.float32) for _ in range(2)]
        for rows in pieces:
            lower = slice(rows.start + FOCAL, rows.stop + FOCAL)
            real = mixed_ref[pair, rows, :FOCAL] - mixed_ref[pair, lower, FOCAL:]
            imag = mixed_ref[pair, rows, FOCAL:] + mixed_ref[pair, lower, :FOCAL]
            field_ref[pair, 0, rows, :] = real
            field_ref[pair, 1, rows, :] = imag
            power = real * real + imag * imag
            totals = [totals[0] + spot_ref[pair, rows, :] * power, totals[1] + power]
        sums.append((total_of(totals[0]), total_of(totals[1]) + 1e-06))
    for pair, (spot_power, all_power) in enumerate(sums):
        ratio = spot_power / all_power
        gain = gain_ref[pair, :1, :1]
        score_ref[pair] = jnp.broadcast_to(ratio * gain, score_ref.shape[1:])
        scale = gain * 2.0 / all_power
        for rows in pieces:
            lower = slice(rows.start + FOCAL, rows.stop + FOCAL)
            weight = scale * (spot_ref[pair, rows, :] - ratio)
            real = (weight * field_ref[pair, 0, rows, :]).astype(jnp.bfloat16)
            imag = (weight * field_ref[pair, 1, rows, :]).astype(jnp.bfloat16)
            stack_ref[pair, rows, :FOCAL] = real
            stack_ref[pair, rows, FOCAL:] = imag
            stack_ref[pair, lower, :FOCAL] = imag
            stack_ref[pair, lower, FOCAL:] = -real
        back = jnp.dot(flat_ref[pair], stack_ref[pair], preferred_element_type=jnp.float32)
        lane = 2 * pair * FOCAL
        back_ref[:, lane : lane + 2 * FOCAL] = back.astype(jnp.bfloat16)


def table_kernel(scale, cols, info_ref, far_info_ref, width_ref, own_base_ref, own_centre_ref, *refs):
    *out_refs, base_ref, centre_ref, turned_ref, power_ref = refs
    pairs = power_ref.shape[0]
    out_refs = out_refs[-2 * pairs :]
    table_refs, slope_refs = out_refs[:pairs], out_refs[pairs:]
    own_cols = width_ref.shape[1]
    sources = [(ref, pair) for ref in (info_ref, far_info_ref) for pair in range(pairs // 2)]
    centres = []
    for pair, (ref, source) in enumerate(sources):
        power = power_coefs(ref[source, : 2 * TERMS, :LANES])
        power_ref[pair] = as_tiles(power * ((iota(power.shape, 0) % TERMS).astype(jnp.float32) * scale))
        if ref is info_ref:
            bases, middles = own_base_ref.at[source], own_centre_ref.at[source]
        else:
            bases, middles = base_ref.at[source], centre_ref.at[source]
            own_waves(ref, source, cols, bases, middles)
        for part, row, lane in itertools.product(range(2), range(0, BLOCK, LANES), range(0, FOCAL, LANES)):
            tile = bases[part, row : row + LANES, lane : lane + LANES]
            turned_ref[pair, part, lane : lane + LANES, row : row + LANES] = tile.T
        centres.append([middles[part].T for part in range(2)])
    for index in range(own_cols // (2 * BLOCK)):
        starts = block_starts(own_cols, index)
        for pair in range(pairs):
            for row in range(0, FOCAL, GRAIN):
                rows = slice(row, row + GRAIN)
                cent_r, cent_i = (centre[rows, index : index + 1] for centre in centres[pair])
                base_r, base_i = (turned_ref[pair, part, rows, :] for part in range(2))
                for start, table in zip(starts, both_blocks(base_r, base_i, cent_r, cent_i)):
                    for part, value in enumerate(table):
                        place = slice(row + part * FOCAL, row + part * FOCAL + GRAIN)
                        table_refs[pair][place, start : start + BLOCK] = value.astype(jnp.bfloat16)
        for start in (start + step for start in starts for step in range(0, BLOCK, LANES)):
            place = slice(start, start + LANES)
            slopes = near_slopes(width_ref[:, place], power_ref, pairs)
            for ref, slope in zip(slope_refs, slopes):
                ref[0, :, place] = slope[0]
                ref[1, :, place] = slope[1]


def own_grad_kernel(*refs):
    *in_refs, out_ref = refs
    add_grads(in_refs, None, out_ref, 2 * BLOCK)


def last_grad_kernel(*refs):
    *in_refs, total_ref, tile_ref, out_hbm, score_hbm, out_ref, score_ref, sems = refs
    own_cols = out_ref.shape[1]
    core = lax.axis_index("wave")
    for pair in range(score_ref.shape[0]):
        score_ref[pair] = jnp.sum(tile_ref[pair, :1, :1])
    moves = [pltpu.make_async_copy(score_ref, score_hbm, sems.at[own_cols // (2 * BLOCK)])]
    moves[0].start()

    def send(start, total):
        size = total.shape[1]
        place = pl.multiple_of(jnp.where(core == 1, start, own_cols - size - start), size)
        place = pl.ds(place, size)
        out_ref[:, place] = jnp.where(core == 1, total, turn_round(total))
        index = start // size
        moves.append(pltpu.make_async_copy(out_ref.at[:, place], out_hbm.at[:, place], sems.at[index]))
        moves[-1].start()

    add_grads(in_refs, total_ref, out_ref, 2 * BLOCK, send)
    for move in moves:
        move.wait()


def add_grads(in_refs, total_ref, out_ref, size, send=None):
    back_ref, *in_refs = in_refs
    pairs = len(in_refs) // 2
    table_refs, slope_refs = in_refs[:pairs], in_refs[pairs:]
    rows_dev, own_cols = out_ref.shape
    core = lax.axis_index("wave")
    lefts = []
    for pair in range(pairs):
        lane = 2 * pair * FOCAL
        real, imag = back_ref[:, lane : lane + FOCAL], back_ref[:, lane + FOCAL : lane + 2 * FOCAL]
        above = jnp.where(core == 1, imag, -imag)
        below = jnp.where(core == 1, -real, real)
        lefts.append(
            jnp.concatenate(
                [jnp.concatenate([real, above], axis=1), jnp.concatenate([imag, below], axis=1)], axis=0
            )
        )
    for start in range(0, own_cols, size):
        place = slice(start, start + size)
        total = jnp.zeros((rows_dev, size), jnp.float32) if total_ref is None else total_ref[:, place]
        for left, table_ref, slope_ref in zip(lefts, table_refs, slope_refs):
            grad = jnp.dot(left, table_ref[:, place], preferred_element_type=jnp.float32)
            total += grad[:rows_dev] * slope_ref[0, :, place]
            total += grad[rows_dev:] * slope_ref[1, :, place]
        if send is None:
            out_ref[:, place] = total
        else:
            send(start, total)


VMEM = pl.BlockSpec(memory_space=pltpu.VMEM)
SMEM = pl.BlockSpec(memory_space=pltpu.SMEM)
ANY = pl.BlockSpec(memory_space=pl.ANY)
HBM = pl.BlockSpec(memory_space=pltpu.HBM)


def call(kernel, name, outs, in_specs, out_specs, scratch, flops, moved):
    return pl.pallas_call(
        kernel,
        name=name,
        out_shape=outs,
        in_specs=in_specs,
        out_specs=out_specs,
        scratch_shapes=scratch,
        cost_estimate=pl.CostEstimate(flops=flops, bytes_accessed=moved, transcendentals=0),
        compiler_params=pltpu.CompilerParams(vmem_limit_bytes=VMEM_LIMIT),
    )


def on_device(widths, coef_table, wave_ids, angle_ids, targets):
    rows_dev, cols = widths.shape
    pairs_dev = wave_ids.shape[0]
    peers = lax.axis_size("aperture")
    copies = lax.axis_size("wave")
    rows = rows_dev * peers
    pairs = pairs_dev * copies
    own_cols = cols // copies
    lanes = 2 * pairs_dev * FOCAL
    f32, bf16 = jnp.float32, jnp.bfloat16
    shape = jax.ShapeDtypeStruct

    def in_hbm(value):
        return pltpu.with_memory_space_constraint(value, pltpu.HBM)

    def exchange(value, step):
        return lax.ppermute(value, "aperture", [(index, index ^ step) for index in range(peers)])

    def to_core(value):
        return lax.ppermute(value, "wave", [(index, (index + 1) % copies) for index in range(copies)])

    waves = [
        pltpu.VMEM((pairs_dev, 2, BLOCK, FOCAL), f32),
        pltpu.VMEM((pairs_dev, 2, 8, FOCAL), f32),
    ]
    mine, info, own, base, centre = call(
        forward_kernel, "forward",
        (
            shape((rows_dev, lanes), bf16),
            shape((pairs_dev, INFO_ROWS, FOCAL), f32), shape((rows_dev, own_cols), f32),
            *(shape(ref.shape, f32) for ref in waves),
        ),
        [HBM] * 5, (VMEM,) * 5,
        [
            pltpu.SMEM(wave_ids.shape, jnp.int32),
            pltpu.SMEM(angle_ids.shape, jnp.int32),
            pltpu.SMEM(targets.shape, jnp.int32),
            pltpu.VMEM(coef_table.shape[::-1], f32),
            pltpu.VMEM(widths.shape, f32),
            pltpu.VMEM((pairs_dev, 2 * TERMS, SUBLANES, LANES), f32),
            pltpu.VMEM((pairs_dev, 4 * rows_dev, own_cols), bf16),
            pltpu.VMEM((pairs_dev, own_cols, 2 * FOCAL), bf16),
            pltpu.VMEM((pairs_dev, 4 * rows_dev, 2 * FOCAL), f32),
            pltpu.SemaphoreType.DMA((5,)),
        ],
        10**9, 10**7,
    )(*(in_hbm(value) for value in (wave_ids, angle_ids, targets, coef_table.T, widths)))
    far_info = to_core(info)

    tall, flat, spots, gains = call(
        row_kernel, "row_tables",
        (
            shape((pairs_dev, 2 * FOCAL, rows), bf16), shape((pairs_dev, rows_dev, 2 * FOCAL), bf16),
            shape((pairs_dev, FOCAL, FOCAL), f32), shape((pairs_dev, 8, 128), f32),
        ),
        [VMEM], (VMEM,) * 4, [], 10**8, 10**6,
    )(info)
    if peers == CUBE:
        last, middle, beside = (exchange(mine, step) for step in (6, 4, 2))
        near = exchange(mine, 1)
        corner = exchange(mine, 3)
        last, flat = lax.optimization_barrier((last, flat))
        sections = [mine, near, last, middle, beside, corner, exchange(last, 1), exchange(middle, 1)]
        steps = [0, 1, 6, 4, 2, 3, 7, 5]
        after = [near, middle]
    else:
        blocks = jnp.tile(mine[None], (peers, 1, 1))
        blocks = lax.all_to_all(blocks, "aperture", 0, 0, tiled=True)
        sections, steps, after = [blocks.reshape(rows, lanes)], None, []
    outs = [shape((2 * FOCAL, own_cols), bf16)] * pairs + [shape((2, rows_dev, own_cols), f32)] * pairs
    made = call(
        functools.partial(table_kernel, math.sqrt(rows * cols), cols), "column_tables",
        outs, [VMEM] * 5 + [ANY] * len(after), [VMEM] * len(outs),
        [
            *waves,
            pltpu.VMEM((pairs, 2, FOCAL, BLOCK), f32),
            pltpu.VMEM((pairs, 2 * TERMS, SUBLANES, LANES), f32),
        ],
        30 * 10**8, 30 * 10**6,
    )(info, far_info, own, base, centre, *after)
    tables, slopes = made[:pairs], made[pairs:]

    back, scores = call(
        functools.partial(focus_kernel, steps), "focus",
        (shape((rows_dev, lanes), bf16), shape((pairs_dev, SUBLANES, LANES), f32)),
        [VMEM] * 4 + [ANY] + [VMEM] * len(sections), (VMEM, VMEM),
        [
            pltpu.VMEM((rows, lanes), bf16),
            pltpu.VMEM((pairs_dev, 2 * FOCAL, 2 * FOCAL), f32),
            pltpu.VMEM((pairs_dev, 2, FOCAL, FOCAL), f32),
            pltpu.VMEM((pairs_dev, 2 * FOCAL, 2 * FOCAL), bf16),
        ],
        10**8, 10**6,
    )(tall, flat, spots, gains, slopes[0], *sections)

    out = shape((rows_dev, own_cols), f32)
    ins = [back, *tables[:pairs_dev], *slopes[:pairs_dev]]
    grad = call(
        own_grad_kernel, "gradient_own", out, [VMEM] * len(ins), VMEM, [], 10**9, 10**7,
    )(*ins)
    ins = [to_core(back), *tables[pairs_dev:], *slopes[pairs_dev:], grad, scores]
    grad, scores = call(
        last_grad_kernel, "gradient_far", (out, shape((pairs_dev,), f32)), [VMEM] * len(ins), (HBM, HBM),
        [
            pltpu.VMEM(out.shape, f32),
            pltpu.SMEM((pairs_dev,), f32),
            pltpu.SemaphoreType.DMA((own_cols // (2 * BLOCK) + 1,)),
        ],
        10**9, 10**7,
    )(*ins)
    return grad, scores


def solution(mesh):
    in_specs = (
        P(("group", "aperture"), None),
        P(),
        P(("group", "wave")),
        P(("group", "wave")),
        P(("group", "wave"), None),
    )
    out_specs = (P(("group", "aperture"), "wave"), P(("group", "wave")))
    return jax.shard_map(
        on_device, mesh=mesh, in_specs=in_specs, out_specs=out_specs, check_vma=False
    )
```

```python
import functools
import itertools
import math

import jax
import jax.numpy as jnp
from jax import lax
from jax.experimental import pallas as pl
from jax.experimental.pallas import tpu as pltpu
from jax.sharding import PartitionSpec as P

FOCAL = 256
SPOT = 4
SHIFT = 32
TERMS = 8
BLOCK = 256
GRAIN = 16
LANES = 128
PIECE = 16
SUBLANES = 8
VMEM_LIMIT = 16 * 1024 * 1024
WAVE_ROW, ANGLE_ROW, AIM_ROW, INFO_ROWS = 16, 17, 18, 24
DIRECT = 16

COS = (
    1.0, -19.7392088015709, 64.93939395773512, -85.45681453397417, 60.24458621302471,
    -26.425616460281425, 7.8991596631575085, -1.6968741456712442, 0.2437618617467591,
)
SIN = (
    6.2831853071792665, -41.34170224019464, 81.60524925425943, -76.70585885700535,
    42.05867547580699, -15.094428387947755, 3.818490079304055, -0.7122771247541972,
    0.09149844789363434,
)


def horner(terms, u):
    value = terms[-1] * u + terms[-2]
    for term in terms[-3::-1]:
        value = value * u + term
    return value


def unit_waves(counts, period):
    half = period // 2
    centred = ((counts + half) & (period - 1)) - half
    t = centred.astype(jnp.float32) * (1.0 / period)
    u = t * t
    return horner(COS, u), -(t * horner(SIN, u))


def iota(shape, axis):
    return lax.broadcasted_iota(jnp.int32, shape, axis)


def pick_coef(table, wave):
    chosen = jnp.where(iota(table.shape, 1) == wave, table, 0.0)
    return jnp.sum(chosen, axis=1, keepdims=True)


def column_freq(info_ref, pair):
    wave = info_ref[pair, WAVE_ROW : WAVE_ROW + 1, :].astype(jnp.int32)
    angle = info_ref[pair, ANGLE_ROW : ANGLE_ROW + 1, :].astype(jnp.int32)
    return (iota((1, FOCAL), 1) - FOCAL // 2 + SHIFT * angle) * (BLOCK + wave)


def fill_base(freq, shift, period, base_ref, centre_ref):
    low_r, low_i = unit_waves(iota((GRAIN, 1), 0) * freq, period)
    steps = BLOCK // GRAIN
    high_r, high_i = unit_waves((iota((steps, 1), 0) * GRAIN - BLOCK // 2 + shift) * freq, period)
    for step in range(steps):
        one_r, one_i = high_r[step : step + 1], high_i[step : step + 1]
        rows = slice(step * GRAIN, (step + 1) * GRAIN)
        base_ref[0, rows, :] = one_r * low_r - one_i * low_i
        base_ref[1, rows, :] = one_r * low_i + one_i * low_r
    count = centre_ref.shape[1]
    cent_r, cent_i = unit_waves((iota((count, 1), 0) * BLOCK + BLOCK // 2) * freq, period)
    centre_ref[0] = cent_r
    centre_ref[1] = cent_i


def power_coefs(coef):
    before, current = [1], [0, 1]
    bases = [before, current]
    for _ in range(2, TERMS):
        doubled = [0] + [2 * term for term in current]
        before, current = current, [a - b for a, b in itertools.zip_longest(doubled, before, fillvalue=0)]
        bases.append(current)
    rows = []
    for part, power in itertools.product(range(2), range(TERMS)):
        row = None
        for order in range(power, TERMS, 2):
            place = part * TERMS + order
            term = coef[place : place + 1] * float(bases[order][power])
            row = term if row is None else row + term
        rows.append(row)
    return jnp.concatenate(rows, axis=0)


def as_tiles(rows):
    return jnp.broadcast_to(rows[:, None, :], (rows.shape[0], SUBLANES, rows.shape[1]))


def split_rows(value):
    return value.reshape(value.shape[0] // SUBLANES, SUBLANES, value.shape[1])


def join_rows(value):
    return value.reshape(value.shape[0] * SUBLANES, value.shape[2])


def near_fields(s, power_ref, pairs):
    s = split_rows(s)
    outs = []
    for pair, part in itertools.product(range(pairs), range(2)):
        row = (part + 1) * TERMS - 1
        value = power_ref[pair, row] * s + power_ref[pair, row - 1]
        for row in range(row - 2, part * TERMS - 1, -1):
            value = value * s + power_ref[pair, row]
        outs.append(join_rows(value))
    return [outs[2 * pair : 2 * pair + 2] for pair in range(pairs)]


def near_slopes(s, power_ref, pairs):
    s = split_rows(s)
    outs = []
    for pair, part in itertools.product(range(pairs), range(2)):
        row = (part + 1) * TERMS - 1
        value = power_ref[pair, row] * s + power_ref[pair, row - 1]
        for row in range(row - 2, part * TERMS, -1):
            value = value * s + power_ref[pair, row]
        outs.append(join_rows(value))
    return [outs[2 * pair : 2 * pair + 2] for pair in range(pairs)]


def turn_round(value):
    rows, cols = value.shape
    order = LANES - 1 - iota((rows, LANES), 1)
    parts = [
        jnp.take_along_axis(value[:, start : start + LANES], order, axis=1)
        for start in range(cols - LANES, -1, -LANES)
    ]
    return jnp.concatenate(parts, axis=1)


def side_pieces(width_ref, core):
    rows, cols = width_ref.shape
    half = cols // 2
    count = half // LANES
    lane = iota((rows, LANES), 1)
    shift = jnp.where(core == 1, 1, LANES - 1)
    edge = jnp.where(core == 1, 0, LANES - 1)

    @functools.cache
    def turned(piece):
        right = width_ref[:, half + piece * LANES : half + (piece + 1) * LANES]
        left = turn_round(width_ref[:, half - (piece + 1) * LANES : half - piece * LANES])
        other = pltpu.roll(jnp.where(core == 1, left, right), shift, 1)
        return jnp.where(core == 1, right, left), other

    def sides(piece):
        own, other = turned(piece)
        beside = jnp.where(core == 1, turned(max(piece - 1, 0))[1], turned(min(piece + 1, count - 1))[1])
        return own, jnp.where(lane == edge, beside, other)

    return sides


def block_starts(cols, index):
    return cols // 2 - (index + 1) * BLOCK, cols // 2 + index * BLOCK


def both_blocks(base_r, base_i, cent_r, cent_i):
    rr, ii = base_r * cent_r, base_i * cent_i
    ri, ir = base_r * cent_i, base_i * cent_r
    return (rr + ii, ir - ri), (rr - ii, ir + ri)


def own_waves(info_ref, pair, cols, base_ref, centre_ref):
    shift = cols // 4 + 1 - lax.axis_index("wave")
    fill_base(column_freq(info_ref, pair), shift, 256 * cols, base_ref, centre_ref)


def forward_kernel(
    wave_hbm, angle_hbm, aim_hbm, coef_hbm, width_hbm, mine_ref, info_ref, own_ref, *refs
):
    pairs = info_ref.shape[0]
    (
        wave_ref, angle_ref, aim_ref, coef_ref, width_ref, base_ref, centre_ref, power_ref, near_ref, table_ref,
        acc_ref, sems,
    ) = refs
    rows_dev, cols = width_ref.shape
    half = cols // 2
    moves = [
        pltpu.make_async_copy(source, target, sems.at[index])
        for index, (source, target) in enumerate((
            (width_hbm, width_ref), (wave_hbm, wave_ref), (angle_hbm, angle_ref),
            (coef_hbm, coef_ref), (aim_hbm, aim_ref),
        ))
    ]
    for move in moves:
        move.start()
    for move in moves[1:]:
        move.wait()
    for pair in range(pairs):
        coef = pick_coef(coef_ref[...], wave_ref[pair])
        coef = jnp.broadcast_to(coef, (WAVE_ROW, FOCAL))
        info_ref[pair, :WAVE_ROW, :] = coef
        power_ref[pair] = as_tiles(power_coefs(coef[:, :LANES]))
        row = iota((INFO_ROWS - WAVE_ROW, FOCAL), 0) + WAVE_ROW
        ids = jnp.where(row == WAVE_ROW, wave_ref[pair], 0)
        ids = jnp.where(row == ANGLE_ROW, angle_ref[pair], ids)
        ids = jnp.where(row == AIM_ROW, aim_ref[pair, 0], ids)
        ids = jnp.where(row == AIM_ROW + 1, aim_ref[pair, 1], ids)
        info_ref[pair, WAVE_ROW:, :] = ids.astype(jnp.float32)
    for pair in range(pairs):
        own_waves(info_ref, pair, cols, base_ref.at[pair], centre_ref.at[pair])
    core = lax.axis_index("wave")
    moves[0].wait()
    sides = side_pieces(width_ref, core)
    alone = jnp.where(core == 1, 0, half)
    column = width_ref[:, pl.ds(pl.multiple_of(alone, LANES), LANES)]
    columns = near_fields(column, power_ref, pairs)
    void = jnp.where(core == 1, 0, half - 1)
    for index in range(half // (2 * BLOCK)):
        starts = block_starts(half, index)
        for start in (start + step for start in starts for step in range(0, BLOCK, LANES)):
            both = sides(start // LANES)
            own_ref[:, start : start + LANES] = both[0]
            for side, widths in enumerate(both):
                outs = near_fields(widths, power_ref, pairs)
                if side and start in (0, half - LANES):
                    keep = iota((rows_dev, LANES), 1) + start != void
                    outs = [[jnp.where(keep, part, 0.0) for part in out] for out in outs]
                for pair, part in ((pair, part) for pair in range(pairs) for part in range(2)):
                    row = (2 * side + part) * rows_dev
                    near_ref[pair, row : row + rows_dev, start : start + LANES] = outs[pair][part].astype(jnp.bfloat16)
        for pair in range(pairs):
            cent_r, cent_i = (centre_ref[pair, part, index : index + 1, :] for part in range(2))
            for row in range(0, BLOCK, GRAIN):
                base_r, base_i = (base_ref[pair, part, row : row + GRAIN, :] for part in range(2))
                for start, table in zip(starts, both_blocks(base_r, base_i, cent_r, cent_i)):
                    rows = slice(start + row, start + row + GRAIN)
                    table_ref[pair, rows, :FOCAL] = table[0].astype(jnp.bfloat16)
                    table_ref[pair, rows, FOCAL:] = table[1].astype(jnp.bfloat16)
            product = jnp.dot(
                jnp.concatenate([near_ref[pair, :, start : start + BLOCK] for start in starts], axis=1),
                jnp.concatenate([table_ref[pair, start : start + BLOCK, :] for start in starts], axis=0),
                preferred_element_type=jnp.float32,
            )
            acc_ref[pair] = product if index == 0 else acc_ref[pair] + product
    for pair in range(pairs):
        acc = [acc_ref[pair, part * rows_dev : (part + 1) * rows_dev, :] for part in range(4)]
        (own_rr, own_ri), (own_ir, own_ii), (far_rr, far_ri), (far_ir, far_ii) = (
            (part[:, :FOCAL], part[:, FOCAL:]) for part in acc
        )
        cross_r, cross_i = far_ii - own_ii, own_ri - far_ri
        real = own_rr + far_rr + jnp.where(core == 1, cross_r, -cross_r)
        imag = own_ir + far_ir + jnp.where(core == 1, cross_i, -cross_i)
        near_r, near_i = (part[:, :1].astype(jnp.bfloat16).astype(jnp.float32) for part in columns[pair])
        wave_r, wave_i = (
            part.astype(jnp.bfloat16).astype(jnp.float32)
            for part in unit_waves((alone - half) * column_freq(info_ref, pair), 256 * cols)
        )
        real = real + (near_r * wave_r - near_i * wave_i)
        imag = imag + (near_r * wave_i + near_i * wave_r)
        for part, value in enumerate((real, imag)):
            lane = (2 * pair + part) * FOCAL
            mine_ref[:, lane : lane + FOCAL] = value.astype(jnp.bfloat16)


def spot_rows(info_ref, pair, first):
    aims = [info_ref[pair, row : row + 1, :] for row in (AIM_ROW, AIM_ROW + 1)]
    rows_off = (iota((PIECE, FOCAL), 0) + first).astype(jnp.float32) - aims[0]
    cols_off = iota((1, FOCAL), 1).astype(jnp.float32) - aims[1]
    return jnp.exp(-(rows_off * rows_off + cols_off * cols_off) / (2.0 * SPOT * SPOT))


def total_of(value):
    return jnp.sum(jnp.sum(value, axis=0, keepdims=True), axis=1, keepdims=True)


def row_kernel(info_ref, tall_ref, flat_ref, spot_ref, gain_ref):
    pairs, _, rows = tall_ref.shape
    rows_dev = flat_ref.shape[1]
    period = 256 * rows
    size = min(rows, FOCAL)
    for pair in range(pairs):
        wave = info_ref[pair, WAVE_ROW : WAVE_ROW + 1, :].astype(jnp.int32) + BLOCK
        focal = (iota((FOCAL, 1), 0) - FOCAL // 2) * wave

        def step(index, carry):
            start = pl.multiple_of(index * size, size)
            place = iota((1, size), 1) + (start - rows // 2)
            for row in range(0, FOCAL, PIECE):
                real, imag = unit_waves(focal[row : row + PIECE, :size] * place, period)
                tall_ref[pair, row : row + PIECE, pl.ds(start, size)] = real.astype(jnp.bfloat16)
                row += FOCAL
                tall_ref[pair, row : row + PIECE, pl.ds(start, size)] = imag.astype(jnp.bfloat16)
            return carry

        if rows == size:
            step(0, 0)
        else:
            lax.fori_loop(0, rows // size, step, 0)
        focal = (iota((1, FOCAL), 1) - FOCAL // 2) * wave
        first = lax.axis_index("aperture") * rows_dev - rows // 2
        real, imag = unit_waves((iota((rows_dev, 1), 0) + first) * focal, period)
        flat_ref[pair, :, :FOCAL] = real.astype(jnp.bfloat16)
        flat_ref[pair, :, FOCAL:] = imag.astype(jnp.bfloat16)
        total = jnp.zeros((PIECE, FOCAL), jnp.float32)
        for row in range(0, FOCAL, PIECE):
            spot = spot_rows(info_ref, pair, row)
            spot_ref[pair, row : row + PIECE, :] = spot
            total += spot
        gain_ref[pair] = jnp.broadcast_to(FOCAL * FOCAL / total_of(total), gain_ref.shape[1:])


def join_kernel(*refs):
    *in_refs, out_ref = refs
    count = in_refs[0].shape[0]
    for index, ref in enumerate(in_refs):
        out_ref[index * count : (index + 1) * count, :] = ref[...]


def focus_kernel(steps, tall_ref, flat_ref, spot_ref, gain_ref, after_ref, *refs):
    del after_ref
    *sect_refs, back_ref, score_ref, rows_ref, mixed_ref, field_ref, stack_ref = refs
    pairs = tall_ref.shape[0]
    rows_dev = back_ref.shape[0]
    if steps is None:
        rows_ref = sect_refs[0]
    else:
        me = lax.axis_index("aperture")
        blocks = [
            ref[index * rows_dev : (index + 1) * rows_dev, :]
            for ref in sect_refs
            for index in range(ref.shape[0] // rows_dev)
        ]
        for step, block in zip(steps, blocks, strict=True):
            start = pl.multiple_of((me ^ step) * rows_dev, rows_dev)
            rows_ref[pl.ds(start, rows_dev), :] = block
    for pair in range(pairs):
        lane = 2 * pair * FOCAL
        section = rows_ref[:, lane : lane + 2 * FOCAL]
        mixed_ref[pair] = jnp.dot(tall_ref[pair], section, preferred_element_type=jnp.float32)
    pieces = [slice(row, row + PIECE) for row in range(0, FOCAL, PIECE)]
    sums = []
    for pair in range(pairs):
        totals = [jnp.zeros((PIECE, FOCAL), jnp.float32) for _ in range(2)]
        for rows in pieces:
            lower = slice(rows.start + FOCAL, rows.stop + FOCAL)
            real = mixed_ref[pair, rows, :FOCAL] - mixed_ref[pair, lower, FOCAL:]
            imag = mixed_ref[pair, rows, FOCAL:] + mixed_ref[pair, lower, :FOCAL]
            field_ref[pair, 0, rows, :] = real
            field_ref[pair, 1, rows, :] = imag
            power = real * real + imag * imag
            totals = [totals[0] + spot_ref[pair, rows, :] * power, totals[1] + power]
        sums.append((total_of(totals[0]), total_of(totals[1]) + 1e-06))
    for pair, (spot_power, all_power) in enumerate(sums):
        ratio = spot_power / all_power
        gain = gain_ref[pair, :1, :1]
        score_ref[pair] = jnp.broadcast_to(ratio * gain, score_ref.shape[1:])
        scale = gain * 2.0 / all_power
        for rows in pieces:
            lower = slice(rows.start + FOCAL, rows.stop + FOCAL)
            weight = scale * (spot_ref[pair, rows, :] - ratio)
            real = (weight * field_ref[pair, 0, rows, :]).astype(jnp.bfloat16)
            imag = (weight * field_ref[pair, 1, rows, :]).astype(jnp.bfloat16)
            stack_ref[pair, rows, :FOCAL] = real
            stack_ref[pair, rows, FOCAL:] = imag
            stack_ref[pair, lower, :FOCAL] = imag
            stack_ref[pair, lower, FOCAL:] = -real
        back = jnp.dot(flat_ref[pair], stack_ref[pair], preferred_element_type=jnp.float32)
        lane = 2 * pair * FOCAL
        back_ref[:, lane : lane + 2 * FOCAL] = back.astype(jnp.bfloat16)


def table_kernel(scale, cols, info_ref, far_info_ref, width_ref, *refs):
    *out_refs, base_ref, centre_ref, turned_ref, power_ref = refs
    pairs = power_ref.shape[0]
    out_refs = out_refs[-2 * pairs :]
    table_refs, slope_refs = out_refs[:pairs], out_refs[pairs:]
    own_cols = width_ref.shape[1]
    sources = [(ref, pair) for ref in (info_ref, far_info_ref) for pair in range(pairs // 2)]
    centres = []
    for pair, (ref, source) in enumerate(sources):
        power = power_coefs(ref[source, : 2 * TERMS, :LANES])
        power_ref[pair] = as_tiles(power * ((iota(power.shape, 0) % TERMS).astype(jnp.float32) * scale))
        own_waves(ref, source, cols, base_ref.at[pair], centre_ref.at[pair])
        for part, row, lane in itertools.product(range(2), range(0, BLOCK, LANES), range(0, FOCAL, LANES)):
            tile = base_ref[pair, part, row : row + LANES, lane : lane + LANES]
            turned_ref[pair, part, lane : lane + LANES, row : row + LANES] = tile.T
        centres.append([centre_ref[pair, part].T for part in range(2)])
    for index in range(own_cols // (2 * BLOCK)):
        starts = block_starts(own_cols, index)
        for pair in range(pairs):
            for row in range(0, FOCAL, GRAIN):
                rows = slice(row, row + GRAIN)
                cent_r, cent_i = (centre[rows, index : index + 1] for centre in centres[pair])
                base_r, base_i = (turned_ref[pair, part, rows, :] for part in range(2))
                for start, table in zip(starts, both_blocks(base_r, base_i, cent_r, cent_i)):
                    for part, value in enumerate(table):
                        place = slice(row + part * FOCAL, row + part * FOCAL + GRAIN)
                        table_refs[pair][place, start : start + BLOCK] = value.astype(jnp.bfloat16)
        for start in (start + step for start in starts for step in range(0, BLOCK, LANES)):
            place = slice(start, start + LANES)
            slopes = near_slopes(width_ref[:, place], power_ref, pairs)
            for ref, slope in zip(slope_refs, slopes):
                ref[0, :, place] = slope[0]
                ref[1, :, place] = slope[1]


def own_grad_kernel(*refs):
    *in_refs, out_ref = refs
    add_grads(in_refs, None, out_ref, 2 * BLOCK)


def last_grad_kernel(*refs):
    *in_refs, total_ref, tile_ref, out_hbm, score_hbm, out_ref, score_ref, sems = refs
    own_cols = out_ref.shape[1]
    core = lax.axis_index("wave")
    for pair in range(score_ref.shape[0]):
        score_ref[pair] = jnp.sum(tile_ref[pair, :1, :1])
    moves = [pltpu.make_async_copy(score_ref, score_hbm, sems.at[0])]
    moves[0].start()

    def send(start, total):
        size = total.shape[1]
        place = pl.multiple_of(jnp.where(core == 1, start, own_cols - size - start), size)
        place = pl.ds(place, size)
        out_ref[:, place] = jnp.where(core == 1, total, turn_round(total))
        moves.append(pltpu.make_async_copy(out_ref.at[:, place], out_hbm.at[:, place], sems.at[len(moves)]))
        moves[-1].start()

    add_grads(in_refs, total_ref, out_ref, 2 * BLOCK, send)
    for move in moves:
        move.wait()


def add_grads(in_refs, total_ref, out_ref, size, send=None):
    back_ref, *in_refs = in_refs
    pairs = len(in_refs) // 2
    table_refs, slope_refs = in_refs[:pairs], in_refs[pairs:]
    rows_dev, own_cols = out_ref.shape
    core = lax.axis_index("wave")
    lefts = []
    for pair in range(pairs):
        lane = 2 * pair * FOCAL
        real, imag = back_ref[:, lane : lane + FOCAL], back_ref[:, lane + FOCAL : lane + 2 * FOCAL]
        above = jnp.where(core == 1, imag, -imag)
        below = jnp.where(core == 1, -real, real)
        lefts.append(
            jnp.concatenate(
                [jnp.concatenate([real, above], axis=1), jnp.concatenate([imag, below], axis=1)], axis=0
            )
        )
    starts = list(range(0, own_cols, size))
    if send is not None:
        starts.append(own_cols - size // 2)
    for start, stop in zip(starts, [*starts[1:], own_cols]):
        place = slice(start, stop)
        total = jnp.zeros((rows_dev, stop - start), jnp.float32) if total_ref is None else total_ref[:, place]
        for left, table_ref, slope_ref in zip(lefts, table_refs, slope_refs):
            grad = jnp.dot(left, table_ref[:, place], preferred_element_type=jnp.float32)
            total += grad[:rows_dev] * slope_ref[0, :, place]
            total += grad[rows_dev:] * slope_ref[1, :, place]
        if send is None:
            out_ref[:, place] = total
        else:
            send(start, total)


VMEM = pl.BlockSpec(memory_space=pltpu.VMEM)
SMEM = pl.BlockSpec(memory_space=pltpu.SMEM)
ANY = pl.BlockSpec(memory_space=pl.ANY)
HBM = pl.BlockSpec(memory_space=pltpu.HBM)


def call(kernel, name, outs, in_specs, out_specs, scratch, flops, moved):
    return pl.pallas_call(
        kernel,
        name=name,
        out_shape=outs,
        in_specs=in_specs,
        out_specs=out_specs,
        scratch_shapes=scratch,
        cost_estimate=pl.CostEstimate(flops=flops, bytes_accessed=moved, transcendentals=0),
        compiler_params=pltpu.CompilerParams(vmem_limit_bytes=VMEM_LIMIT),
    )


def on_device(widths, coef_table, wave_ids, angle_ids, targets):
    rows_dev, cols = widths.shape
    pairs_dev = wave_ids.shape[0]
    peers = lax.axis_size("aperture")
    copies = lax.axis_size("wave")
    rows = rows_dev * peers
    pairs = pairs_dev * copies
    own_cols = cols // copies
    lanes = 2 * pairs_dev * FOCAL
    f32, bf16 = jnp.float32, jnp.bfloat16
    shape = jax.ShapeDtypeStruct

    def in_hbm(value):
        return pltpu.with_memory_space_constraint(value, pltpu.HBM)

    def exchange(value, step):
        return lax.ppermute(value, "aperture", [(index, index ^ step) for index in range(peers)])

    def to_core(value):
        return lax.ppermute(value, "wave", [(index, (index + 1) % copies) for index in range(copies)])

    waves = [
        pltpu.VMEM((pairs_dev, 2, BLOCK, FOCAL), f32),
        pltpu.VMEM((pairs_dev, 2, 8, FOCAL), f32),
    ]
    mine, info, own = call(
        forward_kernel, "forward",
        (
            shape((rows_dev, lanes), bf16),
            shape((pairs_dev, INFO_ROWS, FOCAL), f32), shape((rows_dev, own_cols), f32),
        ),
        [HBM] * 5, (VMEM,) * 3,
        [
            pltpu.SMEM(wave_ids.shape, jnp.int32),
            pltpu.SMEM(angle_ids.shape, jnp.int32),
            pltpu.SMEM(targets.shape, jnp.int32),
            pltpu.VMEM(coef_table.shape[::-1], f32),
            pltpu.VMEM(widths.shape, f32),
            *waves,
            pltpu.VMEM((pairs_dev, 2 * TERMS, SUBLANES, LANES), f32),
            pltpu.VMEM((pairs_dev, 4 * rows_dev, own_cols), bf16),
            pltpu.VMEM((pairs_dev, own_cols, 2 * FOCAL), bf16),
            pltpu.VMEM((pairs_dev, 4 * rows_dev, 2 * FOCAL), f32),
            pltpu.SemaphoreType.DMA((5,)),
        ],
        10**9, 10**7,
    )(*(in_hbm(value) for value in (wave_ids, angle_ids, targets, coef_table.T, widths)))
    far_info = to_core(info)

    tall, flat, spots, gains = call(
        row_kernel, "row_tables",
        (
            shape((pairs_dev, 2 * FOCAL, rows), bf16), shape((pairs_dev, rows_dev, 2 * FOCAL), bf16),
            shape((pairs_dev, FOCAL, FOCAL), f32), shape((pairs_dev, 8, 128), f32),
        ),
        [VMEM], (VMEM,) * 4, [], 10**8, 10**6,
    )(info)
    if peers <= DIRECT:
        steps = list(range(peers - 2, 0, -2))
        got = [exchange(mine, step) for step in steps]
        near = exchange(mine, 1)
        first, flat = lax.optimization_barrier((got[0], flat))
        joined = call(join_kernel, "join", shape(((len(steps) - 1) * rows_dev, lanes), bf16),
                      [VMEM] * (len(steps) - 1), VMEM, [], 10**6, 10**6)(*got[1:])
        sections = [mine, near, first, joined, exchange(first, 1), exchange(joined, 1)]
        steps = [0, 1, *steps, *(step ^ 1 for step in steps)]
        after = [near, joined]
    else:
        blocks = jnp.tile(mine[None], (peers, 1, 1))
        blocks = lax.all_to_all(blocks, "aperture", 0, 0, tiled=True)
        sections, steps, after = [blocks.reshape(rows, lanes)], None, []
    outs = [shape((2 * FOCAL, own_cols), bf16)] * pairs + [shape((2, rows_dev, own_cols), f32)] * pairs
    made = call(
        functools.partial(table_kernel, math.sqrt(rows * cols), cols), "column_tables",
        outs, [VMEM] * 3 + [ANY] * len(after), [VMEM] * len(outs),
        [
            pltpu.VMEM((pairs, 2, BLOCK, FOCAL), f32),
            pltpu.VMEM((pairs, 2, 8, FOCAL), f32),
            pltpu.VMEM((pairs, 2, FOCAL, BLOCK), f32),
            pltpu.VMEM((pairs, 2 * TERMS, SUBLANES, LANES), f32),
        ],
        30 * 10**8, 30 * 10**6,
    )(info, far_info, own, *after)
    tables, slopes = made[:pairs], made[pairs:]

    back, scores = call(
        functools.partial(focus_kernel, steps), "focus",
        (shape((rows_dev, lanes), bf16), shape((pairs_dev, SUBLANES, LANES), f32)),
        [VMEM] * 4 + [ANY] + [VMEM] * len(sections), (VMEM, VMEM),
        [
            pltpu.VMEM((rows, lanes), bf16),
            pltpu.VMEM((pairs_dev, 2 * FOCAL, 2 * FOCAL), f32),
            pltpu.VMEM((pairs_dev, 2, FOCAL, FOCAL), f32),
            pltpu.VMEM((pairs_dev, 2 * FOCAL, 2 * FOCAL), bf16),
        ],
        10**8, 10**6,
    )(tall, flat, spots, gains, slopes[0], *sections)

    out = shape((rows_dev, own_cols), f32)
    ins = [back, *tables[:pairs_dev], *slopes[:pairs_dev]]
    grad = call(
        own_grad_kernel, "gradient_own", out, [VMEM] * len(ins), VMEM, [], 10**9, 10**7,
    )(*ins)
    ins = [to_core(back), *tables[pairs_dev:], *slopes[pairs_dev:], grad, scores]
    grad, scores = call(
        last_grad_kernel, "gradient_far", (out, shape((pairs_dev,), f32)), [VMEM] * len(ins), (HBM, HBM),
        [
            pltpu.VMEM(out.shape, f32),
            pltpu.SMEM((pairs_dev,), f32),
            pltpu.SemaphoreType.DMA((own_cols // (2 * BLOCK) + 2,)),
        ],
        10**9, 10**7,
    )(*ins)
    return grad, scores


def solution(mesh):
    in_specs = (
        P(("group", "aperture"), None),
        P(),
        P(("group", "wave")),
        P(("group", "wave")),
        P(("group", "wave"), None),
    )
    out_specs = (P(("group", "aperture"), "wave"), P(("group", "wave")))
    return jax.shard_map(
        on_device, mesh=mesh, in_specs=in_specs, out_specs=out_specs, check_vma=False
    )
```
